32 devices in a mesh: group: 2 (over x), gx: 16 (over z, y, core).
Axes of the slice: x: 2, y: 2, z: 4, core: 2. Of those that a mesh axis runs over, the one named last changes fastest.
Arguments:
- hidden: bfloat16 [2, 64, 16384], P(None, ('group', 'gx')), parts along dimension 1, may hold values from -6 to 6
- norm_gain: bfloat16 [16384], replicated, may hold values from 0.5 to 1.5
- w_query: bfloat16 [16384, 8192], P(None, 'gx'), may hold values from -0.046875 to 0.046875
- w_keyval: bfloat16 [2, 16384, 512], P(None, 'gx'), may hold values from -0.046875 to 0.046875
- w_out: bfloat16 [8192, 16384], P(None, 'gx'), may hold values from -0.5 to 0.5
- kv_cache: bfloat16 [2, 64, 1024, 512], P(None, ('group', 'gx')), parts along dimension 1, may hold values from -1700 to 1700
- lengths: int32 [64], P(('group', 'gx')), parts along dimension 0, may hold values from 1 to 1024, as said below
Outputs:
- attended: bfloat16 [2, 64, 16384], P(None, ('group', 'gx')), parts along dimension 1
The draws below stay inside these ranges and needn't reach their ends.
There are 2 independent parts, one for each index of `group`. The reference program is written for one: setup_inputs(seed, part) draws one part's arguments, and reference() takes and returns one part's arrays. A program takes and returns all parts, laid end to end along the dimension named above; an argument that names none is the same for every part. Nothing has to cross between parts.
Inputs may be any that keep to these rules, and one draw needn't show every extreme that they name: `lengths`: some row has exactly 1024 valid entries in every draw.
All inputs are finite; a program needn't handle non-finite values.
Results may differ from the reference program's by a relative error of at most 0.0055.
The reference program's roundings to bfloat16 on the way count: a program that leaves them out, or rounds other values in their place, can miss the bound.
Values may be sent and summed in bfloat16 or wider, within the bound.
No kernel may reach another device: no remote copies, remote signals or barrier semaphores. Data moves between devices by JAX's collectives and lax.ppermute only.
A program may use at most 192 MiB of HBM per device.

```python
import math
import jax
import jax.numpy as jnp
from jax import lax

D = 16384
HD = 128
HQ = 64
HK = 4
STEPS = 2
L = 1024
ROWS = 32


def draw_lengths(key, part):
    key = jax.random.fold_in(key, 11)
    first_key, second_key, third_key = jax.random.split(key, 3)
    first_draw = jax.random.randint(first_key, (ROWS,), 0, L)
    second_draw = jax.random.randint(second_key, (ROWS,), 0, L)
    spread = 1 + first_draw * second_draw // L
    longest = jax.random.randint(third_key, (), 0, ROWS)
    return jnp.where(jnp.arange(ROWS) == longest, L, spread).astype(jnp.int32)


def draw_kv_cache(key, part):
    key = jax.random.fold_in(key, 5)
    base_key = jax.random.fold_in(key, 0)
    shape = (2, ROWS, L, HK * HD)
    base = jnp.clip(jax.random.normal(base_key, shape, jnp.float32), -6.0, 6.0)
    return base.astype(jnp.bfloat16)


def block_levels(own_key, dims, shards, smallest, largest):
    def one(dim, parts):
        draws = jax.random.uniform(jax.random.fold_in(jax.random.fold_in(own_key, 6), dim), (parts,), jnp.float32, smallest / len(shards), largest / len(shards))
        return jnp.repeat(jnp.exp(draws), dims[dim] // parts).reshape((-1,) + (1,) * (len(dims) - dim - 1))

    loudness = one(*shards[0])
    for cut in shards[1:]:
        loudness = loudness * one(*cut)
    return loudness


def scatter_about(own_key, dims, scale, reach, pieces=(), kind=jnp.bfloat16):
    array = scale * jax.random.normal(own_key, dims, jnp.float32)
    if pieces:
        array = array * block_levels(own_key, dims, pieces, -0.22, 0.18)
    return jnp.clip(array, -reach, reach).astype(kind)


def setup_inputs(seed: int = 0, part: int = 0) -> dict:
    key_of = jax.random.split(jax.random.key(seed), 8)
    own_keys = jax.random.split(jax.random.fold_in(key_of[7], part), 8)
    return {
        "hidden": scatter_about(own_keys[0], (STEPS, ROWS, D), 1.0, 6.0, ((1, 16),)),
        "norm_gain": jnp.clip(1.0 + 0.1 * jax.random.normal(key_of[1], (D,), jnp.float32), 0.5, 1.5).astype(jnp.bfloat16),
        "w_query": scatter_about(key_of[2], (D, HQ * HD), D ** -0.5, 0.046875, ((1, 16),)),
        "w_keyval": scatter_about(key_of[3], (2, D, HK * HD), D ** -0.5, 0.046875, ((1, 16),)),
        "w_out": scatter_about(key_of[4], (HQ * HD, D), HD ** -0.5, 0.5, ((1, 16),)),
        "kv_cache": draw_kv_cache(jax.random.fold_in(jax.random.fold_in(key_of[7], part), 71), part),
        "lengths": draw_lengths(jax.random.fold_in(jax.random.fold_in(key_of[7], part), 71), part),
    }


ROPE_BASE = 500000.0
EPSILON = 1e-05

def rotate(values, positions):
    row_total, head_count, head_width = values.shape
    half_width = head_width // 2
    frequency = ROPE_BASE ** (-2.0 * jnp.arange(half_width, dtype=jnp.float32) / head_width)
    angles = positions[:, None, None] * frequency[None, None, :]
    cosine = jnp.cos(angles)
    sine_part = jnp.sin(angles)
    paired = values.reshape(row_total, head_count, half_width, 2)
    first_half = paired[..., 0]
    second_half = paired[..., 1]
    turned = jnp.stack([first_half * cosine - second_half * sine_part, first_half * sine_part + second_half * cosine], -1)
    return turned.reshape(row_total, head_count, head_width)

def normalize(hidden, norm_gain):
    states = hidden.astype(jnp.float32)
    scaled = states * lax.rsqrt(lax.optimization_barrier(jnp.mean(states * states, -1, keepdims=True)) + EPSILON)
    return (scaled * norm_gain.astype(jnp.float32)).astype(jnp.bfloat16)

def widen(probs):
    return lax.optimization_barrier(probs.astype(jnp.bfloat16)).astype(jnp.float32)

def attend_row(queries, cache_keys, cache_values, length, fresh_keys, fresh_values):
    score_scale = 1.0 / math.sqrt(HD)
    cached = jnp.einsum('kgd,lkd->kgl', queries.astype(jnp.float32), cache_keys.astype(jnp.float32)) * score_scale
    in_range = jnp.arange(cache_keys.shape[0]) < length
    cached = jnp.where(in_range[None, None, :], cached, -jnp.inf)
    fresh_scores = jnp.einsum('kgd,skd->kgs', queries.astype(jnp.float32), fresh_keys.astype(jnp.float32)) * score_scale
    row_peak = jnp.maximum(cached.max(-1), fresh_scores.max(-1))
    cached_exp = jnp.exp(cached - row_peak[..., None])
    fresh_exp = jnp.exp(fresh_scores - row_peak[..., None])
    denominator = cached_exp.sum(-1) + fresh_exp.sum(-1)
    mixed = jnp.einsum('kgl,lkd->kgd', widen(cached_exp), cache_values.astype(jnp.float32))
    mixed = mixed + jnp.einsum('kgs,skd->kgd', widen(fresh_exp), fresh_values.astype(jnp.float32))
    return (mixed / denominator[..., None]).astype(jnp.bfloat16)

def reference(hidden, norm_gain, w_query, w_keyval, w_out, kv_cache, lengths):
    cache_keys = kv_cache[0].reshape(ROWS, L, HK, HD)
    cache_values = kv_cache[1].reshape(ROWS, L, HK, HD)
    normed = normalize(hidden, norm_gain)
    new_keys = []
    new_values = []
    outputs = []
    for step_index in range(STEPS):
        positions = (lengths + step_index).astype(jnp.float32)
        queries = jnp.dot(normed[step_index], w_query, preferred_element_type=jnp.float32).reshape(ROWS, HQ, HD)
        key_new = jnp.dot(normed[step_index], w_keyval[0], preferred_element_type=jnp.float32).reshape(ROWS, HK, HD)
        value_new = jnp.dot(normed[step_index], w_keyval[1], preferred_element_type=jnp.float32).reshape(ROWS, HK, HD)
        queries = rotate(queries, positions).astype(jnp.bfloat16).reshape(ROWS, HK, HQ // HK, HD)
        new_keys.append(rotate(key_new, positions).astype(jnp.bfloat16))
        new_values.append(value_new.astype(jnp.bfloat16))
        fresh_keys = jnp.stack(new_keys, 1)
        fresh_values = jnp.stack(new_values, 1)
        mixed = lax.map(lambda row_items: attend_row(*row_items), (queries, cache_keys, cache_values, lengths, fresh_keys, fresh_values))
        outputs.append(jnp.dot(mixed.reshape(ROWS, HQ * HD), w_out, preferred_element_type=jnp.float32).astype(jnp.bfloat16))
    return jnp.stack(outputs)
```

```python
import functools
import math

import jax
import jax.numpy as jnp
import numpy as np
from jax import lax
from jax.experimental import pallas as pl
from jax.experimental.pallas import tpu as pltpu
from jax.sharding import PartitionSpec as P

HD = 128
ROPE_BASE = 500000.0
EPSILON = 1e-05
TAG = 128
VMEM_LIMIT = 32 * 1024 * 1024


class Item:
    def __init__(self, block, source, part=0, parts=1):
        self.block, self.source, self.part, self.parts = block, source, part, parts

    def send(self, target):
        source = np.empty_like(self.source)
        source[target] = self.source
        pairs = [(int(i), int(t)) for i, t in enumerate(target)]
        return Item(lax.ppermute(self.block, "gx", pairs), source, self.part, self.parts)

    def half(self, which):
        width = self.block.shape[1] // 2
        piece = self.block[:, which * width : (which + 1) * width]
        return Item(piece, self.source, 2 * self.part + which, 2 * self.parts)


def ring_order(size):
    if size > 4:
        return list(range(size))
    return list(range(0, size, 2)) + list(range(1, size, 2))[::-1]


def grid_of(devices):
    chips = devices // 2
    inner = 1
    while inner * inner * 4 <= chips and chips % (inner * 2) == 0:
        inner *= 2
    return chips // inner, inner, 2


def moves(devices):
    sizes = grid_of(devices)
    place = np.arange(devices).reshape(sizes)
    result = []
    for axis, size in enumerate(sizes):
        order = ring_order(size)
        after = np.empty(size, int)
        for here, there in zip(order, order[1:] + order[:1]):
            after[here] = there
        before = np.argsort(after)
        result.append((size, np.take(place, after, axis).ravel(), np.take(place, before, axis).ravel()))
    return result


def ring(item, size, following, preceding):
    stages = [[item]]
    forward = backward = item
    for _ in range((size - 1) // 2):
        forward, backward = forward.send(following), backward.send(preceding)
        stages.append([forward, backward])
    if size == 2:
        stages.append([item.send(following)])
    elif size % 2 == 0:
        stages.append([forward.half(0).send(following), backward.half(1).send(preceding)])
    return stages


def gather_blocks(block, devices):
    outer, inner, core = moves(devices)
    groups = []
    for outer_stage in ring(Item(block, np.arange(devices)), *outer):
        spread = [ring(item, *inner) for item in outer_stage]
        for inner_stage in zip(*spread):
            items = [item for stage in inner_stage for item in stage]
            groups.append(items + [item.send(core[1]) for item in items])
    return groups


def product_kernel(widths, with_sum, finish, extra_count, *refs):
    count = len(widths)
    starts, blocks, weights = refs[0], refs[1 : 1 + count], refs[1 + count]
    place = 2 + count
    total_in = None
    if with_sum:
        total_in, place = refs[place], place + 1
    extras, out = refs[place : place + extra_count], refs[place + extra_count]
    slots, arrived = refs[place + extra_count + 1 : place + extra_count + 1 + count], refs[place + extra_count + 1 + count]
    copies = []
    for index, width in enumerate(widths):
        start = pl.multiple_of(starts[index], width)
        copies.append(pltpu.make_async_copy(weights.at[pl.ds(start, width), :], slots[index], arrived.at[index]))
        copies[-1].start()
    total = total_in[...] if with_sum else None
    for index in range(count):
        copies[index].wait()
        term = jnp.dot(blocks[index][...], slots[index][...], preferred_element_type=jnp.float32)
        total = term if total is None else total + term
    finish(total, out, *extras)


def keep(total, out):
    out[...] = total


def keep_rounded(total, out):
    out[...] = total.astype(out.dtype)


def turn(values, cosine, sine):
    lanes = values.shape[-1]
    even = lax.broadcasted_iota(jnp.int32, values.shape, 1) % 2 == 0
    swapped = jnp.where(even, pltpu.roll(values, lanes - 1, 1), pltpu.roll(values, 1, 1))
    return values * cosine + swapped * sine


def rotate_and_pack(total, out, cosine, sine, packed):
    devices, heads = out.shape[0], total.shape[1] // HD
    for head in range(heads):
        turned = turn(total[:, head * HD : (head + 1) * HD], cosine[...], sine[...])
        for dev in range(devices):
            for row in range(2):
                packed[dev, row * 2 * heads + head * 2 : row * 2 * heads + head * 2 + 2, :] = turned[
                    dev * 4 + row * 2 : dev * 4 + row * 2 + 2, :
                ]
    out[...] = packed[...].astype(out.dtype)


def product(items, weights, total, devices, finish=keep, extras=(), out_shape=None, scratch=(), me=None):
    depth = weights.shape[0] // devices
    table = np.stack([item.source * depth + item.part * (depth // item.parts) for item in items], 1).astype(np.int32)
    starts = lax.dynamic_index_in_dim(jnp.asarray(table), me, 0, keepdims=False)
    widths = [item.block.shape[1] for item in items]
    rows, columns = items[0].block.shape[0], weights.shape[1]
    vmem = pl.BlockSpec(memory_space=pltpu.VMEM)
    operands = [starts] + [item.block for item in items] + [weights]
    specs = [pl.BlockSpec(memory_space=pltpu.SMEM)] + [vmem] * len(items) + [pl.BlockSpec(memory_space=pl.ANY)]
    if total is not None:
        operands.append(total)
        specs.append(vmem)
    operands += list(extras)
    specs += [vmem] * len(extras)
    if out_shape is None:
        out_shape = jax.ShapeDtypeStruct((rows, columns), jnp.float32)

    def kernel(*refs):
        extra_scratch = refs[len(refs) - len(scratch) :] if scratch else ()
        main = refs[: len(refs) - len(scratch)] if scratch else refs
        end = functools.partial(call_finish, finish, extra_scratch)
        product_kernel(widths, total is not None, end, len(extras), *main)

    return pl.pallas_call(
        kernel,
        out_shape=out_shape,
        in_specs=specs,
        out_specs=vmem,
        scratch_shapes=[pltpu.VMEM((width, columns), weights.dtype) for width in widths]
        + [pltpu.SemaphoreType.DMA((len(items),))]
        + list(scratch),
        compiler_params=pltpu.CompilerParams(vmem_limit_bytes=VMEM_LIMIT),
        cost_estimate=pl.CostEstimate(
            flops=2 * rows * columns * sum(widths), bytes_accessed=2 * columns * sum(widths), transcendentals=0
        ),
    )(*operands)


def call_finish(finish, extra_scratch, total, out, *extras):
    finish(total, out, *extras, *extra_scratch)


def attend_kernel(devices, kv_heads, length, lengths, queries, fresh, cosine, sine, cache, out, keys, values, mixed, arrived):
    padded = keys.shape[1]
    width = kv_heads * HD
    per_head = devices // kv_heads * 8
    scale = 1.0 / math.sqrt(HD)
    copies = []
    for row in range(2):
        for which, target in enumerate((keys, values)):
            copies.append(
                pltpu.make_async_copy(cache.at[which, row], target.at[row, pl.ds(0, length), :], arrived.at[2 * row + which])
            )
            copies[-1].start()
    total = fresh[0]
    for dev in range(1, devices):
        total = total + fresh[dev]
    new_values = total[:, width:]
    new_keys = jnp.concatenate(
        [turn(total[:, head * HD : (head + 1) * HD], cosine[...], sine[...]) for head in range(kv_heads)], 1
    )
    place = lax.broadcasted_iota(jnp.int32, (padded - length, width), 0)
    for row in range(2):
        for new, target in ((new_keys, keys), (new_values, values)):
            spread = jnp.where(place == 0, new[2 * row : 2 * row + 1, :], 0.0)
            spread = jnp.where(place == 1, new[2 * row + 1 : 2 * row + 2, :], spread)
            target[row, length:, :] = spread.astype(target.dtype)
    every = queries[...].astype(jnp.float32)
    column = lax.broadcasted_iota(jnp.int32, (kv_heads * per_head, padded), 1)
    step = lax.broadcasted_iota(jnp.int32, (kv_heads * per_head, padded), 0) % 2
    for row in range(2):
        mine = every[:, row * 8 : row * 8 + 8, :].reshape(kv_heads * per_head, HD)
        spread = jnp.concatenate([mine] * kv_heads, 1)
        own_row = lax.broadcasted_iota(jnp.int32, spread.shape, 0) // per_head
        own_lane = lax.broadcasted_iota(jnp.int32, spread.shape, 1) // HD
        spread = jnp.where(own_row == own_lane, spread, 0.0).astype(jnp.bfloat16)
        copies[2 * row].wait()
        scores = (
            lax.dot_general(spread, keys[row], (((1,), (1,)), ((), ())), preferred_element_type=jnp.float32) * scale
        )
        valid = (column < lengths[row]) | ((column >= length) & (column <= length + step))
        scores = jnp.where(valid, scores, -jnp.inf)
        peak = jnp.max(scores, 1, keepdims=True)
        weight = jnp.exp(scores - peak)
        denominator = jnp.sum(weight, 1, keepdims=True)
        copies[2 * row + 1].wait()
        result = jnp.dot(weight.astype(jnp.bfloat16), values[row], preferred_element_type=jnp.float32)
        for head in range(kv_heads):
            rows = slice(head * per_head, (head + 1) * per_head)
            part = result[rows, head * HD : (head + 1) * HD] / denominator[rows]
            first = head * (devices // kv_heads)
            mixed[first : first + devices // kv_heads, row * 8 : row * 8 + 8, :] = part.reshape(-1, 8, HD)
    out[...] = mixed[...].astype(out.dtype)


def attend(queries, fresh, cosine, sine, cache, lengths):
    devices = queries.shape[0]
    length, width = cache.shape[2], cache.shape[3]
    padded = length + HD
    vmem = pl.BlockSpec(memory_space=pltpu.VMEM)
    return pl.pallas_call(
        functools.partial(attend_kernel, devices, width // HD, length),
        out_shape=jax.ShapeDtypeStruct(queries.shape, jnp.bfloat16),
        in_specs=[pl.BlockSpec(memory_space=pltpu.SMEM)] + [vmem] * 4 + [pl.BlockSpec(memory_space=pl.ANY)],
        out_specs=vmem,
        scratch_shapes=[
            pltpu.VMEM((2, padded, width), cache.dtype),
            pltpu.VMEM((2, padded, width), cache.dtype),
            pltpu.VMEM(queries.shape, jnp.float32),
            pltpu.SemaphoreType.DMA((4,)),
        ],
        compiler_params=pltpu.CompilerParams(vmem_limit_bytes=VMEM_LIMIT),
        cost_estimate=pl.CostEstimate(
            flops=8 * 128 * padded * width, bytes_accessed=8 * length * width, transcendentals=256 * padded
        ),
    )(lengths, queries, fresh, cosine, sine, cache)


def turns(positions):
    frequency = ROPE_BASE ** (-2.0 * jnp.arange(HD // 2, dtype=jnp.float32) / HD)
    angles = positions[:, None] * jnp.repeat(frequency, 2)[None, :]
    sign = jnp.where(jnp.arange(HD) % 2 == 0, -1.0, 1.0)
    return jnp.cos(angles), jnp.sin(angles) * sign


def exchange(pieces):
    return lax.all_to_all(pieces, "gx", split_axis=0, concat_axis=0, tiled=True)


def body(hidden, norm_gain, w_query, w_keyval, w_out, kv_cache, lengths):
    steps, rows_dev, model_width = hidden.shape
    devices = lax.axis_size("gx")
    me = lax.axis_index("gx")
    slab = model_width // devices
    own = rows_dev * steps
    query_cols = w_query.shape[1]
    heads_dev = query_cols // HD

    states = jnp.transpose(hidden.astype(jnp.float32), (1, 0, 2)).reshape(own, model_width)
    scaled = states * lax.rsqrt(jnp.mean(states * states, -1, keepdims=True) + EPSILON)
    normed = (scaled * norm_gain.astype(jnp.float32)).astype(jnp.bfloat16)
    own_positions = jnp.repeat(lengths, steps) + jnp.tile(jnp.arange(steps, dtype=jnp.int32), rows_dev)
    lane = jnp.arange(TAG)[None, :]
    tag = jnp.where(lane == 0, own_positions[:, None] // 32, jnp.where(lane == 1, own_positions[:, None] % 32, 0))
    tag = jnp.broadcast_to(tag.astype(jnp.bfloat16)[None], (devices, own, TAG))
    pieces = jnp.transpose(normed.reshape(own, devices, slab), (1, 0, 2))
    received = exchange(jnp.concatenate([pieces, tag], 2)).reshape(devices * own, slab + TAG)
    block = received[:, :slab]
    positions = received[:, slab].astype(jnp.float32) * 32.0 + received[:, slab + 1].astype(jnp.float32)

    fresh = jnp.concatenate(
        [jnp.dot(block, w_keyval[which], preferred_element_type=jnp.float32) for which in range(2)], 1
    )
    fresh = exchange(fresh.reshape(devices, own, 2 * w_keyval.shape[2]))

    groups = gather_blocks(block, devices)
    total = None
    for group in groups[:-1]:
        total = product(group, w_query, total, devices, me=me)
    packed_shape = (devices, own * heads_dev, HD)
    queries = product(
        groups[-1],
        w_query,
        total,
        devices,
        finish=rotate_and_pack,
        extras=turns(positions),
        out_shape=jax.ShapeDtypeStruct(packed_shape, jnp.bfloat16),
        scratch=[pltpu.VMEM(packed_shape, jnp.float32)],
        me=me,
    )
    queries = exchange(queries)

    mixed = attend(queries, fresh, *turns(own_positions.astype(jnp.float32)), kv_cache, lengths)
    mixed = exchange(mixed).reshape(devices, rows_dev, heads_dev, steps, HD)
    block = jnp.transpose(mixed, (0, 1, 3, 2, 4)).reshape(devices * own, query_cols)

    groups = gather_blocks(block, devices)
    total = None
    for group in groups[:-1]:
        total = product(group, w_out, total, devices, me=me)
    out_cols = w_out.shape[1]
    columns = product(
        groups[-1],
        w_out,
        total,
        devices,
        finish=keep_rounded,
        out_shape=jax.ShapeDtypeStruct((devices * own, out_cols), jnp.bfloat16),
        me=me,
    )
    outputs = exchange(columns.reshape(devices, own, out_cols)).reshape(devices, rows_dev, steps, out_cols)
    return jnp.transpose(outputs, (2, 1, 0, 3)).reshape(steps, rows_dev, devices * out_cols)
def rotate(values, positions):
    row_total, head_count, head_width = values.shape
    half_width = head_width // 2
    frequency = ROPE_BASE ** (-2.0 * jnp.arange(half_width, dtype=jnp.float32) / head_width)
    angles = positions[:, None, None] * frequency[None, None, :]
    cosine = jnp.cos(angles)
    sine_part = jnp.sin(angles)
    paired = values.reshape(row_total, head_count, half_width, 2)
    first_half = paired[..., 0]
    second_half = paired[..., 1]
    turned = jnp.stack(
        [
            first_half * cosine - second_half * sine_part,
            first_half * sine_part + second_half * cosine,
        ],
        -1,
    )
    return turned.reshape(row_total, head_count, head_width)


def attend_split_heads(queries, cache_keys, cache_values, lengths, fresh_keys, fresh_values):
    score_scale = 1.0 / math.sqrt(HD)
    fresh_scores = (
        jnp.einsum("rkgd,rskd->rkgs", queries, fresh_keys, preferred_element_type=jnp.float32)
        * score_scale
    )
    cached = (
        jnp.einsum("rkgd,rlkd->rkgl", queries, cache_keys, preferred_element_type=jnp.float32)
        * score_scale
    )
    in_range = jnp.arange(cache_keys.shape[1])[None, :] < lengths[:, None]
    cached = jnp.where(in_range[:, None, None, :], cached, -jnp.inf)
    row_peak = jnp.maximum(cached.max(-1), fresh_scores.max(-1))
    cached_exp = jnp.exp(cached - row_peak[..., None])
    fresh_exp = jnp.exp(fresh_scores - row_peak[..., None])
    denominator = cached_exp.sum(-1) + fresh_exp.sum(-1)
    mixed = jnp.einsum(
        "rkgl,rlkd->rkgd",
        cached_exp.astype(jnp.bfloat16),
        cache_values,
        preferred_element_type=jnp.float32,
    )
    mixed = mixed + jnp.einsum(
        "rkgs,rskd->rkgd",
        fresh_exp.astype(jnp.bfloat16),
        fresh_values,
        preferred_element_type=jnp.float32,
    )
    return (mixed / denominator[..., None]).astype(jnp.bfloat16)


def body_split_heads(hidden, norm_gain, w_query, w_keyval, w_out, kv_cache, lengths):
    step_count, rows_dev, model_width = hidden.shape
    devices = lax.axis_size("gx")
    device_index = lax.axis_index("gx")
    row_slab = w_keyval.shape[1]
    kv_width = w_keyval.shape[2]
    query_cols = w_query.shape[1]
    heads_width = query_cols * devices
    head_count = heads_width // HD
    kv_heads = kv_width // HD
    kv_both = jnp.concatenate([w_keyval[0], w_keyval[1]], 1)
    cache_keys = kv_cache[0].reshape(rows_dev, kv_cache.shape[2], kv_heads, HD)
    cache_values = kv_cache[1].reshape(rows_dev, kv_cache.shape[2], kv_heads, HD)
    states = hidden.astype(jnp.float32)
    scaled = states * lax.rsqrt(jnp.mean(states * states, -1, keepdims=True) + EPSILON)
    normed = (scaled * norm_gain.astype(jnp.float32)).astype(jnp.bfloat16)
    new_keys = []
    new_values = []
    outputs = []
    for step_index in range(step_count):
        shard_piece = lax.all_gather(normed[step_index], "gx", axis=0, tiled=True)
        queries = jnp.dot(shard_piece, w_query, preferred_element_type=jnp.float32)
        own_slab = lax.dynamic_slice_in_dim(shard_piece, device_index * row_slab, row_slab, 1)
        partial_kv = jnp.dot(own_slab, kv_both, preferred_element_type=jnp.float32)
        joined = jnp.concatenate([queries, partial_kv], 1)
        project_query_rows = lax.all_to_all(
            joined[:, :query_cols], "gx", split_axis=0, concat_axis=1, tiled=True
        )
        project_keyval = lax.psum_scatter(
            joined[:, query_cols:], "gx", scatter_dimension=0, tiled=True
        )
        positions = (lengths + step_index).astype(jnp.float32)
        prepare_queries = rotate(
            project_query_rows.reshape(rows_dev, head_count, HD), positions
        ).astype(jnp.bfloat16)
        prepare_queries = prepare_queries.reshape(rows_dev, kv_heads, head_count // kv_heads, HD)
        key_new = rotate(
            project_keyval[:, :kv_width].reshape(rows_dev, kv_heads, HD), positions
        ).astype(jnp.bfloat16)
        value_new = (
            project_keyval[:, kv_width:].reshape(rows_dev, kv_heads, HD).astype(jnp.bfloat16)
        )
        queries, key_new, value_new = (prepare_queries, key_new, value_new)
        new_keys.append(key_new)
        new_values.append(value_new)
        mixed = attend_split_heads(
            queries,
            cache_keys,
            cache_values,
            lengths,
            jnp.stack(new_keys, 1),
            jnp.stack(new_values, 1),
        )
        out_cols = jnp.dot(
            lax.all_gather(mixed.reshape(rows_dev, heads_width), "gx", axis=0, tiled=True),
            w_out,
            preferred_element_type=jnp.float32,
        ).astype(jnp.bfloat16)
        outputs.append(lax.all_to_all(out_cols, "gx", split_axis=0, concat_axis=1, tiled=True))
    return jnp.stack(outputs)


def solution(mesh):
    devices = mesh.shape["gx"]

    def run(*arrays):
        whole_heads = arrays[2].shape[1] % HD == 0 and devices % 2 == 0
        return (body if whole_heads else body_split_heads)(*arrays)

    in_specs = (
        P(None, ("group", "gx"), None),
        P(),
        P(None, "gx"),
        P(None, "gx", None),
        P(None, "gx"),
        P(None, ("group", "gx"), None, None),
        P(("group", "gx")),
    )
    out_specs = P(None, ("group", "gx"), None)
    return jax.shard_map(run, mesh=mesh, in_specs=in_specs, out_specs=out_specs, check_vma=False)
```

```python
import functools
import math

import jax
import jax.numpy as jnp
import numpy as np
from jax import lax
from jax.experimental import pallas as pl
from jax.experimental.pallas import tpu as pltpu
from jax.sharding import PartitionSpec as P

HD = 128
ROPE_BASE = 500000.0
EPSILON = 1e-05
TAG = 128
VMEM_LIMIT = 48 * 1024 * 1024
VMEM = pl.BlockSpec(memory_space=pltpu.VMEM)
SMEM = pl.BlockSpec(memory_space=pltpu.SMEM)
HBM = pl.BlockSpec(memory_space=pltpu.HBM)


def permute(block, target):
    return lax.ppermute(block, "gx", [(int(i), int(t)) for i, t in enumerate(target)])


def moved(source, target):
    result = np.empty_like(source)
    result[target] = source
    return result


class Slot:
    def __init__(self, parts, source):
        self.parts, self.source = parts, source

    def send(self, target):
        return Slot([permute(part, target) for part in self.parts], moved(self.source, target))


def halves(block, middle):
    return block[:, :middle], block[:, middle:]


def ring_order(size):
    if size > 4:
        return list(range(size))
    return list(range(0, size, 2)) + list(range(1, size, 2))[::-1]


def axes_of(devices):
    chips, inner = devices // 2, 1
    while inner * inner * 4 <= chips and chips % (inner * 2) == 0:
        inner *= 2
    sizes = (chips // inner, inner, 2)
    place = np.arange(devices).reshape(sizes)
    result = []
    for axis, size in enumerate(sizes):
        order = ring_order(size)
        after = np.empty(size, int)
        for here, there in zip(order, order[1:] + order[:1]):
            after[here] = there
        before = np.argsort(after)
        result.append((size, np.take(place, after, axis).ravel(), np.take(place, before, axis).ravel()))
    return result


def ring(slot, axis, middle):
    size, following, preceding = axis
    slots = [slot]
    forward = backward = slot
    for _ in range((size - 1) // 2):
        forward, backward = forward.send(following), backward.send(preceding)
        slots += [forward, backward]
    if size == 2:
        slots.append(slot.send(following))
    elif size % 2 == 0:
        low, high = halves(forward.parts[0], middle)[0], halves(backward.parts[0], middle)[1]
        slots.append(Slot([permute(low, following), permute(high, preceding)], moved(forward.source, following)))
    return slots


def slot_sources(devices):
    result = []
    for size, following, preceding in axes_of(devices):
        here = np.arange(devices)
        sources = [here]
        forward = backward = here
        for _ in range((size - 1) // 2):
            forward, backward = moved(forward, following), moved(backward, preceding)
            sources += [forward, backward]
        if size % 2 == 0:
            sources.append(moved(forward, following))
        result.append(sources)
    return result


def gather(block, devices, middle):
    outer, inner, core = axes_of(devices)
    along = ring(Slot([block], np.arange(devices)), outer, middle)
    spread = [ring(slot, inner, middle) for slot in along]
    chip = [spread[z][y] for y in range(inner[0]) for z in range(outer[0])]
    return chip + [slot.send(core[1]) for slot in chip]


def give_back(pieces, devices, add):
    outer, inner, core = slot_sources(devices)
    pieces = pieces[None]
    sources = [np.arange(devices)]
    for slots in (core, inner, outer):
        came = [pieces[:, 0]] + [permute(pieces[:, s], target) for s, target in enumerate(slots) if s]
        if add:
            pieces = functools.reduce(jnp.add, came)
        else:
            pieces = jnp.concatenate(came, 0)
            sources = [moved(source, target) for target in slots for source in sources]
    return pieces[0] if add else (pieces, sources)


def norm_kernel(hidden, gain, tag, out):
    states = hidden[...].astype(jnp.float32)
    scale = lax.rsqrt(jnp.mean(states * states, -1, keepdims=True) + EPSILON)
    normed = states * scale * gain[...].astype(jnp.float32)
    steps, rows, width = normed.shape
    rows = [normed[step, row : row + 1] for row in range(rows) for step in range(steps)]
    out[:, :width] = jnp.concatenate(rows, 0).astype(out.dtype)
    out[:, width:] = tag[...].astype(out.dtype)


def norm(hidden, gain, tag):
    steps, rows, width = hidden.shape
    return pl.pallas_call(
        norm_kernel,
        out_shape=jax.ShapeDtypeStruct((steps * rows, width + TAG), jnp.bfloat16),
        in_specs=[VMEM] * 3,
        out_specs=VMEM,
        compiler_params=pltpu.CompilerParams(vmem_limit_bytes=VMEM_LIMIT),
        cost_estimate=pl.CostEstimate(flops=6 * steps * rows * width, bytes_accessed=4 * steps * rows * width, transcendentals=0),
    )(hidden, gain.reshape(1, width), tag)


def assemble(slots, first, width):
    pieces = []
    for parts in slots:
        ref, base = parts
        pieces.append(ref[:, pl.ds(pl.multiple_of(first - base, 128), width)].astype(jnp.float32))
    return jnp.concatenate(pieces, 0).astype(jnp.bfloat16)


def split_refs(shape_of_slots, refs, middle):
    low, high, place = [], [], 0
    for count in shape_of_slots:
        if count == 1:
            low.append((refs[place], 0))
            high.append((refs[place], 0))
        else:
            low.append((refs[place], 0))
            high.append((refs[place + 1], middle))
        place += count
    return low, high


def stream(weights, buffers, arrived, depth):
    def start(index, carry):
        rows = pl.ds(pl.multiple_of(index * depth, depth), depth)
        pltpu.make_async_copy(weights.at[rows, :], buffers.at[index], arrived.at[index]).start()
        return carry

    lax.fori_loop(0, buffers.shape[0], start, 0)


def multiply(low, high, weights, buffers, arrived, depth, total, kept=None):
    chunks = buffers.shape[0]
    total[...] = jnp.zeros_like(total)
    for which, slots in ((0, low), (1, high)):

        def step(index, carry):
            block = assemble(slots, index * depth, depth)
            if kept is not None:
                kept[index] = block
            rows = pl.ds(pl.multiple_of(index * depth, depth), depth)
            pltpu.make_async_copy(weights.at[rows, :], buffers.at[index], arrived.at[index]).wait()
            total[...] += jnp.dot(block, buffers[index], preferred_element_type=jnp.float32)
            return carry

        lax.fori_loop(which * (chunks // 2), (which + 1) * (chunks // 2), step, 0)


def turns(positions):
    shape = (positions.shape[0], HD)
    lane = lax.broadcasted_iota(jnp.int32, shape, 1)
    pair = (lane // 2).astype(jnp.float32)
    angles = positions * jnp.exp(pair * (-2.0 * math.log(ROPE_BASE) / HD))
    return jnp.cos(angles), jnp.where(lane % 2 == 0, -1.0, 1.0) * jnp.sin(angles)


def turn(values, cosine, sine):
    lanes = values.shape[-1]
    even = lax.broadcasted_iota(jnp.int32, values.shape, 1) % 2 == 0
    swapped = jnp.where(even, pltpu.roll(values, lanes - 1, 1), pltpu.roll(values, 1, 1))
    return values * cosine + swapped * sine


def project_kernel(layout, middle, width, me, *refs):
    count = sum(layout)
    low, high = split_refs(layout, refs, middle)
    weights, keyval, queries, fresh, buffers, small, kept, total, packed, arrived, came = refs[count:]
    depth = buffers.shape[1]
    for which in range(2):
        pltpu.make_async_copy(keyval.at[which], small.at[which], came.at[which]).start()
    stream(weights, buffers, arrived, depth)
    tags = jnp.concatenate([ref[:, width - base :].astype(jnp.float32) for ref, base in high], 0)
    cosine, sine = turns(tags[:, 0:1] * 32.0 + tags[:, 1:2])
    multiply(low, high, weights, buffers, arrived, depth, total, kept)
    own = kept[me[0]]
    kv_width = keyval.shape[2]
    for which in range(2):
        pltpu.make_async_copy(keyval.at[which], small.at[which], came.at[which]).wait()
        fresh[:, which * kv_width : (which + 1) * kv_width] = jnp.dot(
            own, small[which], preferred_element_type=jnp.float32
        )
    heads = total.shape[1] // HD
    for head in range(heads):
        turned = turn(total[:, head * HD : (head + 1) * HD], cosine, sine)
        for slot in range(packed.shape[0]):
            for row in range(2):
                place, at = row * 2 * heads + head * 2, slot * 4 + row * 2
                packed[slot, place : place + 2, :] = turned[at : at + 2, :]
    queries[...] = packed[...].astype(queries.dtype)


def project(slots, w_query, w_keyval, me, middle):
    devices = len(slots)
    width, columns = w_query.shape
    depth = w_keyval.shape[1]
    rows = devices * slots[0].parts[0].shape[0]
    parts = [part for slot in slots for part in slot.parts]
    packed = (devices, rows // devices * (columns // HD), HD)
    kv_width = w_keyval.shape[2]
    return pl.pallas_call(
        functools.partial(project_kernel, [len(slot.parts) for slot in slots], middle, width),
        out_shape=[
            jax.ShapeDtypeStruct(packed, jnp.bfloat16),
            jax.ShapeDtypeStruct((rows, 2 * kv_width), jnp.float32),
        ],
        in_specs=[SMEM] + [VMEM] * len(parts) + [HBM, HBM],
        out_specs=[VMEM, VMEM],
        scratch_shapes=[
            pltpu.VMEM((devices, depth, columns), w_query.dtype),
            pltpu.VMEM((2, depth, kv_width), w_keyval.dtype),
            pltpu.VMEM((devices, rows, depth), jnp.bfloat16),
            pltpu.VMEM((rows, columns), jnp.float32),
            pltpu.VMEM(packed, jnp.float32),
            pltpu.SemaphoreType.DMA((devices,)),
            pltpu.SemaphoreType.DMA((2,)),
        ],
        compiler_params=pltpu.CompilerParams(vmem_limit_bytes=VMEM_LIMIT),
        cost_estimate=pl.CostEstimate(
            flops=2 * rows * columns * width, bytes_accessed=2 * columns * width, transcendentals=2 * rows * HD
        ),
    )(me, *parts, w_query, w_keyval)


def out_kernel(layout, middle, *refs):
    count = sum(layout)
    low, high = split_refs(layout, refs, middle)
    weights, out, buffers, total, arrived = refs[count:]
    depth = buffers.shape[1]
    stream(weights, buffers, arrived, depth)
    multiply(low, high, weights, buffers, arrived, depth, total)
    own = out.shape[1]
    for slot in range(out.shape[0]):
        out[slot] = total[slot * own : (slot + 1) * own].astype(out.dtype)


def project_out(slots, w_out, middle, chunks):
    devices = len(slots)
    width, columns = w_out.shape
    own = slots[0].parts[0].shape[0]
    parts = [part for slot in slots for part in slot.parts]
    return pl.pallas_call(
        functools.partial(out_kernel, [len(slot.parts) for slot in slots], middle),
        out_shape=jax.ShapeDtypeStruct((devices, own, columns), jnp.bfloat16),
        in_specs=[VMEM] * len(parts) + [HBM],
        out_specs=VMEM,
        scratch_shapes=[
            pltpu.VMEM((chunks, width // chunks, columns), w_out.dtype),
            pltpu.VMEM((devices * own, columns), jnp.float32),
            pltpu.SemaphoreType.DMA((chunks,)),
        ],
        compiler_params=pltpu.CompilerParams(vmem_limit_bytes=VMEM_LIMIT),
        cost_estimate=pl.CostEstimate(
            flops=2 * devices * own * columns * width, bytes_accessed=2 * columns * width, transcendentals=0
        ),
    )(*parts, w_out)


def attend_kernel(
    devices, kv_heads, length, lengths, sources, pieces, fresh, cache, out, keys, values, queries, mixed, arrived
):
    padded = keys.shape[1]
    width = kv_heads * HD
    tile = pieces.shape[1] // 2
    per_head = devices // kv_heads * tile
    scale = 1.0 / math.sqrt(HD)
    copies = []
    for row in range(2):
        for which, target in enumerate((keys, values)):
            copies.append(
                pltpu.make_async_copy(cache.at[which, row], target.at[row, pl.ds(0, length), :], arrived.at[2 * row + which])
            )
            copies[-1].start()
    for slot in range(devices):
        queries[sources[slot]] = pieces[slot].astype(jnp.float32)
    line = lax.broadcasted_iota(jnp.int32, (8, 1), 0)
    first = jnp.where(line < 2, lengths[0], lengths[1])
    cosine, sine = turns((first + line % 2).astype(jnp.float32))
    total = fresh[...]
    total = jnp.concatenate([total, total], 0)
    new_values = total[:, width:]
    new_keys = jnp.concatenate([turn(total[:, head * HD : (head + 1) * HD], cosine, sine) for head in range(kv_heads)], 1)
    place = lax.broadcasted_iota(jnp.int32, (padded - length, width), 0)
    for row in range(2):
        for new, target in ((new_keys, keys), (new_values, values)):
            spread = jnp.where(place == 0, new[2 * row : 2 * row + 1, :], 0.0)
            spread = jnp.where(place == 1, new[2 * row + 1 : 2 * row + 2, :], spread)
            target[row, length:, :] = spread.astype(target.dtype)
    every = queries[...]
    column = lax.broadcasted_iota(jnp.int32, (kv_heads * per_head, padded), 1)
    step = lax.broadcasted_iota(jnp.int32, (kv_heads * per_head, padded), 0) % 2
    for row in range(2):
        mine = every[:, row * tile : row * tile + tile, :].reshape(kv_heads * per_head, HD)
        spread = jnp.concatenate([mine] * kv_heads, 1)
        own_row = lax.broadcasted_iota(jnp.int32, spread.shape, 0) // per_head
        own_lane = lax.broadcasted_iota(jnp.int32, spread.shape, 1) // HD
        spread = jnp.where(own_row == own_lane, spread, 0.0).astype(jnp.bfloat16)
        copies[2 * row].wait()
        scores = lax.dot_general(spread, keys[row], (((1,), (1,)), ((), ())), preferred_element_type=jnp.float32) * scale
        valid = (column < lengths[row]) | ((column >= length) & (column <= length + step))
        scores = jnp.where(valid, scores, -jnp.inf)
        peak = jnp.max(scores, 1, keepdims=True)
        weight = jnp.exp(scores - peak)
        denominator = jnp.sum(weight, 1, keepdims=True)
        copies[2 * row + 1].wait()
        result = jnp.dot(weight.astype(jnp.bfloat16), values[row], preferred_element_type=jnp.float32)
        for head in range(kv_heads):
            rows = slice(head * per_head, (head + 1) * per_head)
            part = result[rows, head * HD : (head + 1) * HD] / denominator[rows]
            for query in range(per_head // 2):
                lanes = slice((head * per_head // 2 + query) * HD, (head * per_head // 2 + query + 1) * HD)
                for at in range(2):
                    mixed[at * 2 + row : at * 2 + row + 1, lanes] = part[2 * query + at : 2 * query + at + 1]
    out[...] = mixed[...].astype(out.dtype)


def attend(pieces, fresh, cache, lengths, sources):
    devices = pieces.shape[0]
    length, width = cache.shape[2], cache.shape[3]
    padded = length + HD
    rows, heads = fresh.shape[0], devices * pieces.shape[1] // fresh.shape[0]
    return pl.pallas_call(
        functools.partial(attend_kernel, devices, width // HD, length),
        out_shape=jax.ShapeDtypeStruct((rows, heads * HD), jnp.bfloat16),
        in_specs=[SMEM, SMEM, VMEM, VMEM, HBM],
        out_specs=VMEM,
        scratch_shapes=[
            pltpu.VMEM((2, padded, width), cache.dtype),
            pltpu.VMEM((2, padded, width), cache.dtype),
            pltpu.VMEM(pieces.shape, jnp.float32),
            pltpu.VMEM((rows, heads * HD), jnp.float32),
            pltpu.SemaphoreType.DMA((4,)),
        ],
        compiler_params=pltpu.CompilerParams(vmem_limit_bytes=VMEM_LIMIT),
        cost_estimate=pl.CostEstimate(
            flops=8 * 128 * padded * width, bytes_accessed=8 * length * width, transcendentals=256 * padded
        ),
    )(lengths, sources, pieces, fresh, cache)


def finish_kernel(sources, pieces, out):
    columns = pieces.shape[2]
    steps, rows = out.shape[:2]
    for slot in range(pieces.shape[0]):
        lanes = pl.ds(pl.multiple_of(sources[slot] * columns, columns), columns)
        piece = pieces[slot].astype(jnp.float32)
        for step in range(steps):
            out[step, :, lanes] = piece[step * rows : (step + 1) * rows].astype(out.dtype)


def finish(pieces, sources, steps):
    devices, own, columns = pieces.shape
    return pl.pallas_call(
        finish_kernel,
        out_shape=jax.ShapeDtypeStruct((steps, own // steps, devices * columns), jnp.bfloat16),
        in_specs=[SMEM, VMEM],
        out_specs=VMEM,
        compiler_params=pltpu.CompilerParams(vmem_limit_bytes=VMEM_LIMIT),
    )(sources, pieces)


def body(hidden, norm_gain, w_query, w_keyval, w_out, kv_cache, lengths):
    steps, rows, width = hidden.shape
    devices = lax.axis_size("gx")
    me = lax.axis_index("gx")
    outer, inner, core = axes_of(devices)
    grid = (core[0], inner[0], outer[0])

    positions = (lengths[:, None] + jnp.arange(steps, dtype=jnp.int32)[None, :]).reshape(rows * steps, 1)
    lane = jnp.arange(TAG)[None, :]
    tag = jnp.where(lane == 0, positions // 32, jnp.where(lane == 1, positions % 32, 0)).astype(jnp.float32)

    slots = gather(norm(hidden, norm_gain, tag), devices, width // 2)
    queries, fresh = project(slots, w_query, w_keyval, me.reshape(1), width // 2)
    queries, order = give_back(queries.reshape(*grid, *queries.shape[1:]), devices, False)
    fresh = give_back(fresh.reshape(*grid, rows * steps, fresh.shape[1]), devices, True)
    sources = lax.dynamic_index_in_dim(jnp.asarray(np.stack(order, 1).astype(np.int32)), me, 0, keepdims=False)

    mixed = attend(queries, fresh, kv_cache, lengths, sources)
    slots = gather(mixed, devices, mixed.shape[1] // 2)
    columns = project_out(slots, w_out, mixed.shape[1] // 2, devices // 2)
    columns, _ = give_back(columns.reshape(*grid, *columns.shape[1:]), devices, False)
    return finish(columns, sources, steps)


def rotate(values, positions):
    row_total, head_count, head_width = values.shape
    half_width = head_width // 2
    frequency = ROPE_BASE ** (-2.0 * jnp.arange(half_width, dtype=jnp.float32) / head_width)
    angles = positions[:, None, None] * frequency[None, None, :]
    cosine = jnp.cos(angles)
    sine_part = jnp.sin(angles)
    paired = values.reshape(row_total, head_count, half_width, 2)
    first_half = paired[..., 0]
    second_half = paired[..., 1]
    turned = jnp.stack(
        [
            first_half * cosine - second_half * sine_part,
            first_half * sine_part + second_half * cosine,
        ],
        -1,
    )
    return turned.reshape(row_total, head_count, head_width)


def attend_split_heads(queries, cache_keys, cache_values, lengths, fresh_keys, fresh_values):
    score_scale = 1.0 / math.sqrt(HD)
    fresh_scores = (
        jnp.einsum("rkgd,rskd->rkgs", queries, fresh_keys, preferred_element_type=jnp.float32)
        * score_scale
    )
    cached = (
        jnp.einsum("rkgd,rlkd->rkgl", queries, cache_keys, preferred_element_type=jnp.float32)
        * score_scale
    )
    in_range = jnp.arange(cache_keys.shape[1])[None, :] < lengths[:, None]
    cached = jnp.where(in_range[:, None, None, :], cached, -jnp.inf)
    row_peak = jnp.maximum(cached.max(-1), fresh_scores.max(-1))
    cached_exp = jnp.exp(cached - row_peak[..., None])
    fresh_exp = jnp.exp(fresh_scores - row_peak[..., None])
    denominator = cached_exp.sum(-1) + fresh_exp.sum(-1)
    mixed = jnp.einsum(
        "rkgl,rlkd->rkgd",
        cached_exp.astype(jnp.bfloat16),
        cache_values,
        preferred_element_type=jnp.float32,
    )
    mixed = mixed + jnp.einsum(
        "rkgs,rskd->rkgd",
        fresh_exp.astype(jnp.bfloat16),
        fresh_values,
        preferred_element_type=jnp.float32,
    )
    return (mixed / denominator[..., None]).astype(jnp.bfloat16)


def body_split_heads(hidden, norm_gain, w_query, w_keyval, w_out, kv_cache, lengths):
    step_count, rows_dev, model_width = hidden.shape
    devices = lax.axis_size("gx")
    device_index = lax.axis_index("gx")
    row_slab = w_keyval.shape[1]
    kv_width = w_keyval.shape[2]
    query_cols = w_query.shape[1]
    heads_width = query_cols * devices
    head_count = heads_width // HD
    kv_heads = kv_width // HD
    kv_both = jnp.concatenate([w_keyval[0], w_keyval[1]], 1)
    cache_keys = kv_cache[0].reshape(rows_dev, kv_cache.shape[2], kv_heads, HD)
    cache_values = kv_cache[1].reshape(rows_dev, kv_cache.shape[2], kv_heads, HD)
    states = hidden.astype(jnp.float32)
    scaled = states * lax.rsqrt(jnp.mean(states * states, -1, keepdims=True) + EPSILON)
    normed = (scaled * norm_gain.astype(jnp.float32)).astype(jnp.bfloat16)
    new_keys = []
    new_values = []
    outputs = []
    for step_index in range(step_count):
        shard_piece = lax.all_gather(normed[step_index], "gx", axis=0, tiled=True)
        queries = jnp.dot(shard_piece, w_query, preferred_element_type=jnp.float32)
        own_slab = lax.dynamic_slice_in_dim(shard_piece, device_index * row_slab, row_slab, 1)
        partial_kv = jnp.dot(own_slab, kv_both, preferred_element_type=jnp.float32)
        joined = jnp.concatenate([queries, partial_kv], 1)
        project_query_rows = lax.all_to_all(
            joined[:, :query_cols], "gx", split_axis=0, concat_axis=1, tiled=True
        )
        project_keyval = lax.psum_scatter(
            joined[:, query_cols:], "gx", scatter_dimension=0, tiled=True
        )
        positions = (lengths + step_index).astype(jnp.float32)
        prepare_queries = rotate(
            project_query_rows.reshape(rows_dev, head_count, HD), positions
        ).astype(jnp.bfloat16)
        prepare_queries = prepare_queries.reshape(rows_dev, kv_heads, head_count // kv_heads, HD)
        key_new = rotate(
            project_keyval[:, :kv_width].reshape(rows_dev, kv_heads, HD), positions
        ).astype(jnp.bfloat16)
        value_new = (
            project_keyval[:, kv_width:].reshape(rows_dev, kv_heads, HD).astype(jnp.bfloat16)
        )
        queries, key_new, value_new = (prepare_queries, key_new, value_new)
        new_keys.append(key_new)
        new_values.append(value_new)
        mixed = attend_split_heads(
            queries,
            cache_keys,
            cache_values,
            lengths,
            jnp.stack(new_keys, 1),
            jnp.stack(new_values, 1),
        )
        out_cols = jnp.dot(
            lax.all_gather(mixed.reshape(rows_dev, heads_width), "gx", axis=0, tiled=True),
            w_out,
            preferred_element_type=jnp.float32,
        ).astype(jnp.bfloat16)
        outputs.append(lax.all_to_all(out_cols, "gx", split_axis=0, concat_axis=1, tiled=True))
    return jnp.stack(outputs)


def solution(mesh):
    devices = mesh.shape["gx"]

    def run(*arrays):
        whole_heads = arrays[2].shape[1] % HD == 0 and devices % 2 == 0
        return (body if whole_heads else body_split_heads)(*arrays)

    in_specs = (
        P(None, ("group", "gx"), None),
        P(),
        P(None, "gx"),
        P(None, "gx", None),
        P(None, "gx"),
        P(None, ("group", "gx"), None, None),
        P(("group", "gx")),
    )
    out_specs = P(None, ("group", "gx"), None)
    return jax.shard_map(run, mesh=mesh, in_specs=in_specs, out_specs=out_specs, check_vma=False)
```

```python
import functools
import math

import jax
import jax.numpy as jnp
import numpy as np
from jax import lax
from jax.experimental import pallas as pl
from jax.experimental.pallas import tpu as pltpu
from jax.sharding import PartitionSpec as P

HD = 128
ROPE_BASE = 500000.0
EPSILON = 1e-05
TAG = 128
VMEM_LIMIT = 48 * 1024 * 1024
VMEM = pl.BlockSpec(memory_space=pltpu.VMEM)
SMEM = pl.BlockSpec(memory_space=pltpu.SMEM)
HBM = pl.BlockSpec(memory_space=pltpu.HBM)


def permute(block, target):
    return lax.ppermute(block, "gx", [(int(i), int(t)) for i, t in enumerate(target)])


def moved(source, target):
    result = np.empty_like(source)
    result[target] = source
    return result


class Group:
    def __init__(self, blocks, sources, crossed=False):
        self.blocks, self.sources, self.crossed = blocks, sources, crossed

    def send(self, target, crossed=False):
        return Group(permute(self.blocks, target), [moved(source, target) for source in self.sources], crossed)


def join(groups):
    if len(groups) == 1:
        return groups[0]
    return Group(jnp.concatenate([g.blocks for g in groups], 0), [source for g in groups for source in g.sources])


def ring_order(size):
    if size > 4:
        return list(range(size))
    return list(range(0, size, 2)) + list(range(1, size, 2))[::-1]


def axes_of(devices):
    chips, inner = devices // 2, 1
    while inner * inner * 4 <= chips and chips % (inner * 2) == 0:
        inner *= 2
    sizes = (chips // inner, inner, 2)
    place = np.arange(devices).reshape(sizes)
    result = []
    for axis, size in enumerate(sizes):
        order = ring_order(size)
        after = np.empty(size, int)
        for here, there in zip(order, order[1:] + order[:1]):
            after[here] = there
        before = np.argsort(after)
        result.append((size, np.take(place, after, axis).ravel(), np.take(place, before, axis).ravel()))
    return result


def ring(group, axis):
    size, following, preceding = axis
    stages = [[group]]
    forward = backward = group
    for step in range(1, size // 2 + 1):
        forward = forward.send(following)
        arrived = [forward]
        if 2 * step < size:
            backward = backward.send(preceding)
            arrived.append(backward)
        stages.append(arrived)
    return stages


def gather(block, devices):
    outer, inner, core = axes_of(devices)
    own = Group(block[None], [np.arange(devices)])
    groups = []
    for arrived in ring(own, outer):
        chips = join(arrived)
        reached = [chips] + [group for stage in ring(chips, inner)[1:] for group in stage]
        groups += arrived + reached[1:]
        groups.append(join(reached).send(core[1], crossed=True))
    return groups


def swap_cores(block, devices):
    return permute(block, np.arange(devices) ^ 1)


def exchange(pieces, devices):
    same_core = [list(range(core, devices, 2)) for core in range(2)]
    return lax.all_to_all(pieces, "gx", 0, 0, axis_index_groups=same_core, tiled=True)


def places(groups, devices):
    here = np.arange(devices)
    chips = [source // 2 for group in groups for source in group.sources]
    columns = [chip * 2 + (here % 2 ^ other) for chip in range(devices // 2) for other in range(2)]
    return np.stack(chips + columns + [here], 1).astype(np.int32)


def norm_kernel(lengths, hidden, gain, out):
    states = hidden[...].astype(jnp.float32)
    scale = lax.rsqrt(jnp.mean(states * states, -1, keepdims=True) + EPSILON)
    normed = states * scale * gain[...].astype(jnp.float32)
    steps, rows, width = normed.shape
    lines = [normed[step, row : row + 1] for row in range(rows) for step in range(steps)]
    out[:, :width] = jnp.concatenate(lines, 0).astype(out.dtype)
    line = lax.broadcasted_iota(jnp.int32, (steps * rows, TAG), 0)
    lane = lax.broadcasted_iota(jnp.int32, (steps * rows, TAG), 1)
    position = line % steps
    for row in range(rows):
        position = jnp.where(line // steps == row, position + lengths[row], position)
    tag = jnp.where(lane == 0, position // 32, position % 32)
    out[:, width:] = tag.astype(jnp.float32).astype(out.dtype)


def norm(hidden, gain, lengths):
    steps, rows, width = hidden.shape
    return pl.pallas_call(
        norm_kernel,
        out_shape=jax.ShapeDtypeStruct((steps * rows, width + TAG), jnp.bfloat16),
        in_specs=[SMEM, VMEM, VMEM],
        out_specs=VMEM,
        compiler_params=pltpu.CompilerParams(vmem_limit_bytes=VMEM_LIMIT),
        cost_estimate=pl.CostEstimate(flops=6 * steps * rows * width, bytes_accessed=4 * steps * rows * width, transcendentals=0),
    )(lengths, hidden, gain.reshape(1, width))


def slots_of(refs, counts):
    return [(ref, at) for ref, count in zip(refs, counts) for at in range(count)]


def assemble(slots, first, width):
    lanes = pl.ds(pl.multiple_of(first, 128), width)
    return jnp.concatenate([ref[at, :, lanes].astype(jnp.float32) for ref, at in slots], 0).astype(jnp.bfloat16)


def stream(weights, buffers, arrived, depth):
    def start(index, carry):
        rows = pl.ds(pl.multiple_of(index * depth, depth), depth)
        pltpu.make_async_copy(weights.at[rows, :], buffers.at[index], arrived.at[index]).start()
        return carry

    lax.fori_loop(0, buffers.shape[0], start, 0)


def multiply(slots, weights, buffers, arrived, depth, total, kept=None):
    total[...] = jnp.zeros_like(total)

    def step(index, carry):
        block = assemble(slots, index * depth, depth)
        if kept is not None:
            kept[index] = block
        rows = pl.ds(pl.multiple_of(index * depth, depth), depth)
        pltpu.make_async_copy(weights.at[rows, :], buffers.at[index], arrived.at[index]).wait()
        total[...] += jnp.dot(block, buffers[index], preferred_element_type=jnp.float32)
        return carry

    lax.fori_loop(0, buffers.shape[0], step, 0)


def turns(positions):
    shape = (positions.shape[0], HD)
    lane = lax.broadcasted_iota(jnp.int32, shape, 1)
    pair = (lane // 2).astype(jnp.float32)
    angles = positions * jnp.exp(pair * (-2.0 * math.log(ROPE_BASE) / HD))
    return jnp.cos(angles), jnp.where(lane % 2 == 0, -1.0, 1.0) * jnp.sin(angles)


def turn(values, cosine, sine):
    lanes = values.shape[-1]
    even = lax.broadcasted_iota(jnp.int32, values.shape, 1) % 2 == 0
    swapped = jnp.where(even, pltpu.roll(values, lanes - 1, 1), pltpu.roll(values, 1, 1))
    return values * cosine + swapped * sine


def project_kernel(counts, crossed, width, place, *refs):
    slots = slots_of(refs, counts)
    weights, keyval, *outs = refs[len(counts) : len(counts) + 6]
    buffers, small, kept, total, packed, arrived, came = refs[len(counts) + 6 :]
    queries, fresh = outs[:2], outs[2:]
    depth = buffers.shape[1]
    for which in range(2):
        pltpu.make_async_copy(keyval.at[which], small.at[which], came.at[which]).start()
    stream(weights, buffers, arrived, depth)
    tags = jnp.concatenate([ref[at, :, width:].astype(jnp.float32) for ref, at in slots], 0)
    cosine, sine = turns(tags[:, 0:1] * 32.0 + tags[:, 1:2])
    multiply(slots, weights, buffers, arrived, depth, total, kept)
    own = kept[place[2 * len(slots)]]
    blocks = keyval.shape[2] // HD
    for which in range(2):
        pltpu.make_async_copy(keyval.at[which], small.at[which], came.at[which]).wait()
        term = jnp.dot(own, small[which], preferred_element_type=jnp.float32)
        for slot in range(len(slots)):
            for at in range(blocks):
                row = (which * blocks + at) * 4
                fresh[crossed[slot]][place[slot], row : row + 4, :] = term[
                    slot * 4 : slot * 4 + 4, at * HD : (at + 1) * HD
                ]
    heads = total.shape[1] // HD
    for head in range(heads):
        turned = turn(total[:, head * HD : (head + 1) * HD], cosine, sine)
        for slot in range(len(slots)):
            for row in range(2):
                line, at = row * 2 * heads + head * 2, slot * 4 + row * 2
                packed[slot, line : line + 2, :] = turned[at : at + 2, :]
    for slot in range(len(slots)):
        queries[crossed[slot]][place[slot]] = packed[slot].astype(jnp.bfloat16)


def group_shape(groups):
    counts = [len(group.sources) for group in groups]
    return counts, [int(group.crossed) for group, count in zip(groups, counts) for _ in range(count)]


def project(groups, w_query, w_keyval, place, devices):
    counts, crossed = group_shape(groups)
    width, columns = w_query.shape
    depth, kv_width = w_keyval.shape[1:]
    own = groups[0].blocks.shape[1]
    rows, tile = devices * own, own * (columns // HD)
    query = jax.ShapeDtypeStruct((devices // 2, tile, HD), jnp.bfloat16)
    fresh = jax.ShapeDtypeStruct((devices // 2, own * 2 * kv_width // HD, HD), jnp.float32)
    return pl.pallas_call(
        functools.partial(project_kernel, counts, crossed, width),
        out_shape=[query, query, fresh, fresh],
        in_specs=[SMEM] + [VMEM] * len(groups) + [HBM, HBM],
        out_specs=[VMEM] * 4,
        scratch_shapes=[
            pltpu.VMEM((devices, depth, columns), w_query.dtype),
            pltpu.VMEM((2, depth, kv_width), w_keyval.dtype),
            pltpu.VMEM((devices, rows, depth), jnp.bfloat16),
            pltpu.VMEM((rows, columns), jnp.float32),
            pltpu.VMEM((devices, tile, HD), jnp.float32),
            pltpu.SemaphoreType.DMA((devices,)),
            pltpu.SemaphoreType.DMA((2,)),
        ],
        compiler_params=pltpu.CompilerParams(vmem_limit_bytes=VMEM_LIMIT),
        cost_estimate=pl.CostEstimate(
            flops=2 * rows * columns * width, bytes_accessed=2 * columns * width, transcendentals=2 * rows * HD
        ),
    )(place, *[group.blocks for group in groups], w_query, w_keyval)


def pack_kernel(near, far, near_sum, far_sum, out):
    tile, lines = near.shape[1], near_sum.shape[1]
    out[:, :tile, :] = near[...]
    out[:, tile : 2 * tile, :] = far[...]
    total = near_sum[...] + far_sum[...]
    high = total.astype(jnp.bfloat16)
    out[:, 2 * tile : 2 * tile + lines, :] = high
    out[:, 2 * tile + lines :, :] = (total - high.astype(jnp.float32)).astype(jnp.bfloat16)


def pack(near, far, near_sum, far_sum):
    chips, tile, _ = near.shape
    return pl.pallas_call(
        pack_kernel,
        out_shape=jax.ShapeDtypeStruct((chips, 2 * tile + 2 * near_sum.shape[1], HD), jnp.bfloat16),
        in_specs=[VMEM] * 4,
        out_specs=VMEM,
        compiler_params=pltpu.CompilerParams(vmem_limit_bytes=VMEM_LIMIT),
    )(near, far, near_sum, far_sum)


def out_kernel(counts, crossed, place, *refs):
    slots = slots_of(refs, counts)
    weights, near, far, buffers, total, arrived = refs[len(counts) :]
    depth = buffers.shape[1]
    stream(weights, buffers, arrived, depth)
    multiply(slots, weights, buffers, arrived, depth, total)
    own = near.shape[1]
    for slot in range(len(slots)):
        (near, far)[crossed[slot]][place[slot]] = total[slot * own : (slot + 1) * own].astype(near.dtype)


def project_out(groups, w_out, place, devices):
    counts, crossed = group_shape(groups)
    width, columns = w_out.shape
    own = groups[0].blocks.shape[1]
    chunks = devices // 2
    piece = jax.ShapeDtypeStruct((devices // 2, own, columns), jnp.bfloat16)
    return pl.pallas_call(
        functools.partial(out_kernel, counts, crossed),
        out_shape=[piece, piece],
        in_specs=[SMEM] + [VMEM] * len(groups) + [HBM],
        out_specs=[VMEM, VMEM],
        scratch_shapes=[
            pltpu.VMEM((chunks, width // chunks, columns), w_out.dtype),
            pltpu.VMEM((devices * own, columns), jnp.float32),
            pltpu.SemaphoreType.DMA((chunks,)),
        ],
        compiler_params=pltpu.CompilerParams(vmem_limit_bytes=VMEM_LIMIT),
        cost_estimate=pl.CostEstimate(
            flops=2 * devices * own * columns * width, bytes_accessed=2 * columns * width, transcendentals=0
        ),
    )(place, *[group.blocks for group in groups], w_out)


def attend_kernel(devices, kv_heads, length, tile, lengths, place, pieces, cache, out, keys, values, queries, mixed, arrived):
    padded = keys.shape[1]
    width = kv_heads * HD
    half = tile // 2
    per_head = devices // kv_heads * half
    scale = 1.0 / math.sqrt(HD)
    copies = []
    for row in range(2):
        for which, target in enumerate((keys, values)):
            copies.append(
                pltpu.make_async_copy(cache.at[which, row], target.at[row, pl.ds(0, length), :], arrived.at[2 * row + which])
            )
            copies[-1].start()
    for chip in range(devices // 2):
        for other in range(2):
            piece = pieces[chip, other * tile : (other + 1) * tile, :]
            queries[place[devices + 2 * chip + other]] = piece.astype(jnp.float32)
    line = lax.broadcasted_iota(jnp.int32, (8, 1), 0)
    first = jnp.where(line % 4 < 2, lengths[0], lengths[1])
    cosine, sine = turns((first + line % 2).astype(jnp.float32))
    terms = pieces[:, 2 * tile :, :].astype(jnp.float32)
    total = jnp.sum(terms, 0)
    total = total[: total.shape[0] // 2] + total[total.shape[0] // 2 :]
    twice = [jnp.concatenate([total[4 * at : 4 * at + 4]] * 2, 0) for at in range(2 * kv_heads)]
    new_keys = jnp.concatenate([turn(part, cosine, sine) for part in twice[:kv_heads]], 1)
    new_values = jnp.concatenate(twice[kv_heads:], 1)
    spot = lax.broadcasted_iota(jnp.int32, (padded - length, width), 0)
    for row in range(2):
        for new, target in ((new_keys, keys), (new_values, values)):
            spread = jnp.where(spot == 0, new[2 * row : 2 * row + 1, :], 0.0)
            spread = jnp.where(spot == 1, new[2 * row + 1 : 2 * row + 2, :], spread)
            target[row, length:, :] = spread.astype(target.dtype)
    every = queries[...]
    column = lax.broadcasted_iota(jnp.int32, (kv_heads * per_head, padded), 1)
    step = lax.broadcasted_iota(jnp.int32, (kv_heads * per_head, padded), 0) % 2
    for row in range(2):
        mine = every[:, row * half : row * half + half, :].reshape(kv_heads * per_head, HD)
        spread = jnp.concatenate([mine] * kv_heads, 1)
        own_row = lax.broadcasted_iota(jnp.int32, spread.shape, 0) // per_head
        own_lane = lax.broadcasted_iota(jnp.int32, spread.shape, 1) // HD
        spread = jnp.where(own_row == own_lane, spread, 0.0).astype(jnp.bfloat16)
        copies[2 * row].wait()
        scores = lax.dot_general(spread, keys[row], (((1,), (1,)), ((), ())), preferred_element_type=jnp.float32) * scale
        valid = (column < lengths[row]) | ((column >= length) & (column <= length + step))
        scores = jnp.where(valid, scores, -jnp.inf)
        peak = jnp.max(scores, 1, keepdims=True)
        weight = jnp.exp(scores - peak)
        denominator = jnp.sum(weight, 1, keepdims=True)
        copies[2 * row + 1].wait()
        result = jnp.dot(weight.astype(jnp.bfloat16), values[row], preferred_element_type=jnp.float32)
        for head in range(kv_heads):
            rows = slice(head * per_head, (head + 1) * per_head)
            part = result[rows, head * HD : (head + 1) * HD] / denominator[rows]
            for query in range(per_head // 2):
                lanes = slice((head * per_head // 2 + query) * HD, (head * per_head // 2 + query + 1) * HD)
                for at in range(2):
                    mixed[at * 2 + row : at * 2 + row + 1, lanes] = part[2 * query + at : 2 * query + at + 1]
    out[...] = mixed[...].astype(out.dtype)


def attend(pieces, tile, cache, lengths, place, devices):
    length, width = cache.shape[2], cache.shape[3]
    padded = length + HD
    columns = devices * tile // 4 * HD
    return pl.pallas_call(
        functools.partial(attend_kernel, devices, width // HD, length, tile),
        out_shape=jax.ShapeDtypeStruct((4, columns), jnp.bfloat16),
        in_specs=[SMEM, SMEM, VMEM, HBM],
        out_specs=VMEM,
        scratch_shapes=[
            pltpu.VMEM((2, padded, width), cache.dtype),
            pltpu.VMEM((2, padded, width), cache.dtype),
            pltpu.VMEM((devices, tile, HD), jnp.float32),
            pltpu.VMEM((4, columns), jnp.float32),
            pltpu.SemaphoreType.DMA((4,)),
        ],
        compiler_params=pltpu.CompilerParams(vmem_limit_bytes=VMEM_LIMIT),
        cost_estimate=pl.CostEstimate(
            flops=8 * 128 * padded * width, bytes_accessed=8 * length * width, transcendentals=256 * padded
        ),
    )(lengths, place, pieces, cache)


def finish_kernel(devices, place, pieces, out):
    columns = pieces.shape[3]
    steps, rows = out.shape[:2]
    for chip in range(devices // 2):
        for other in range(2):
            source = place[devices + 2 * chip + other]
            lanes = pl.ds(pl.multiple_of(source * columns, columns), columns)
            piece = pieces[chip, other].astype(jnp.float32)
            for step in range(steps):
                out[step, :, lanes] = piece[step * rows : (step + 1) * rows].astype(out.dtype)


def finish(pieces, place, steps, devices):
    own, columns = pieces.shape[2:]
    return pl.pallas_call(
        functools.partial(finish_kernel, devices),
        out_shape=jax.ShapeDtypeStruct((steps, own // steps, devices * columns), jnp.bfloat16),
        in_specs=[SMEM, VMEM],
        out_specs=VMEM,
        compiler_params=pltpu.CompilerParams(vmem_limit_bytes=VMEM_LIMIT),
    )(place, pieces)


def body(hidden, norm_gain, w_query, w_keyval, w_out, kv_cache, lengths):
    steps = hidden.shape[0]
    devices = lax.axis_size("gx")

    groups = gather(norm(hidden, norm_gain, lengths), devices)
    table = jnp.asarray(places(groups, devices))
    place = lax.dynamic_index_in_dim(table, lax.axis_index("gx"), 0, keepdims=False)
    near, far, near_sum, far_sum = project(groups, w_query, w_keyval, place, devices)
    pieces = pack(near, swap_cores(far, devices), near_sum, swap_cores(far_sum, devices))

    mixed = attend(exchange(pieces, devices), near.shape[1], kv_cache, lengths, place, devices)
    near, far = project_out(gather(mixed, devices), w_out, place, devices)
    pieces = jnp.stack([near, swap_cores(far, devices)], 1)
    return finish(exchange(pieces, devices), place, steps, devices)


def rotate(values, positions):
    row_total, head_count, head_width = values.shape
    half_width = head_width // 2
    frequency = ROPE_BASE ** (-2.0 * jnp.arange(half_width, dtype=jnp.float32) / head_width)
    angles = positions[:, None, None] * frequency[None, None, :]
    cosine = jnp.cos(angles)
    sine_part = jnp.sin(angles)
    paired = values.reshape(row_total, head_count, half_width, 2)
    first_half = paired[..., 0]
    second_half = paired[..., 1]
    turned = jnp.stack(
        [
            first_half * cosine - second_half * sine_part,
            first_half * sine_part + second_half * cosine,
        ],
        -1,
    )
    return turned.reshape(row_total, head_count, head_width)


def attend_split_heads(queries, cache_keys, cache_values, lengths, fresh_keys, fresh_values):
    score_scale = 1.0 / math.sqrt(HD)
    fresh_scores = (
        jnp.einsum("rkgd,rskd->rkgs", queries, fresh_keys, preferred_element_type=jnp.float32)
        * score_scale
    )
    cached = (
        jnp.einsum("rkgd,rlkd->rkgl", queries, cache_keys, preferred_element_type=jnp.float32)
        * score_scale
    )
    in_range = jnp.arange(cache_keys.shape[1])[None, :] < lengths[:, None]
    cached = jnp.where(in_range[:, None, None, :], cached, -jnp.inf)
    row_peak = jnp.maximum(cached.max(-1), fresh_scores.max(-1))
    cached_exp = jnp.exp(cached - row_peak[..., None])
    fresh_exp = jnp.exp(fresh_scores - row_peak[..., None])
    denominator = cached_exp.sum(-1) + fresh_exp.sum(-1)
    mixed = jnp.einsum(
        "rkgl,rlkd->rkgd",
        cached_exp.astype(jnp.bfloat16),
        cache_values,
        preferred_element_type=jnp.float32,
    )
    mixed = mixed + jnp.einsum(
        "rkgs,rskd->rkgd",
        fresh_exp.astype(jnp.bfloat16),
        fresh_values,
        preferred_element_type=jnp.float32,
    )
    return (mixed / denominator[..., None]).astype(jnp.bfloat16)


def body_split_heads(hidden, norm_gain, w_query, w_keyval, w_out, kv_cache, lengths):
    step_count, rows_dev, model_width = hidden.shape
    devices = lax.axis_size("gx")
    device_index = lax.axis_index("gx")
    row_slab = w_keyval.shape[1]
    kv_width = w_keyval.shape[2]
    query_cols = w_query.shape[1]
    heads_width = query_cols * devices
    head_count = heads_width // HD
    kv_heads = kv_width // HD
    kv_both = jnp.concatenate([w_keyval[0], w_keyval[1]], 1)
    cache_keys = kv_cache[0].reshape(rows_dev, kv_cache.shape[2], kv_heads, HD)
    cache_values = kv_cache[1].reshape(rows_dev, kv_cache.shape[2], kv_heads, HD)
    states = hidden.astype(jnp.float32)
    scaled = states * lax.rsqrt(jnp.mean(states * states, -1, keepdims=True) + EPSILON)
    normed = (scaled * norm_gain.astype(jnp.float32)).astype(jnp.bfloat16)
    new_keys = []
    new_values = []
    outputs = []
    for step_index in range(step_count):
        shard_piece = lax.all_gather(normed[step_index], "gx", axis=0, tiled=True)
        queries = jnp.dot(shard_piece, w_query, preferred_element_type=jnp.float32)
        own_slab = lax.dynamic_slice_in_dim(shard_piece, device_index * row_slab, row_slab, 1)
        partial_kv = jnp.dot(own_slab, kv_both, preferred_element_type=jnp.float32)
        joined = jnp.concatenate([queries, partial_kv], 1)
        project_query_rows = lax.all_to_all(
            joined[:, :query_cols], "gx", split_axis=0, concat_axis=1, tiled=True
        )
        project_keyval = lax.psum_scatter(
            joined[:, query_cols:], "gx", scatter_dimension=0, tiled=True
        )
        positions = (lengths + step_index).astype(jnp.float32)
        prepare_queries = rotate(
            project_query_rows.reshape(rows_dev, head_count, HD), positions
        ).astype(jnp.bfloat16)
        prepare_queries = prepare_queries.reshape(rows_dev, kv_heads, head_count // kv_heads, HD)
        key_new = rotate(
            project_keyval[:, :kv_width].reshape(rows_dev, kv_heads, HD), positions
        ).astype(jnp.bfloat16)
        value_new = (
            project_keyval[:, kv_width:].reshape(rows_dev, kv_heads, HD).astype(jnp.bfloat16)
        )
        queries, key_new, value_new = (prepare_queries, key_new, value_new)
        new_keys.append(key_new)
        new_values.append(value_new)
        mixed = attend_split_heads(
            queries,
            cache_keys,
            cache_values,
            lengths,
            jnp.stack(new_keys, 1),
            jnp.stack(new_values, 1),
        )
        out_cols = jnp.dot(
            lax.all_gather(mixed.reshape(rows_dev, heads_width), "gx", axis=0, tiled=True),
            w_out,
            preferred_element_type=jnp.float32,
        ).astype(jnp.bfloat16)
        outputs.append(lax.all_to_all(out_cols, "gx", split_axis=0, concat_axis=1, tiled=True))
    return jnp.stack(outputs)


def solution(mesh):
    devices = mesh.shape["gx"]

    def run(*arrays):
        whole_heads = arrays[2].shape[1] % HD == 0 and devices % 2 == 0
        return (body if whole_heads else body_split_heads)(*arrays)

    in_specs = (
        P(None, ("group", "gx"), None),
        P(),
        P(None, "gx"),
        P(None, "gx", None),
        P(None, "gx"),
        P(None, ("group", "gx"), None, None),
        P(("group", "gx")),
    )
    out_specs = P(None, ("group", "gx"), None)
    return jax.shard_map(run, mesh=mesh, in_specs=in_specs, out_specs=out_specs, check_vma=False)
```

```python
import functools
import math

import jax
import jax.numpy as jnp
import numpy as np
from jax import lax
from jax.experimental import pallas as pl
from jax.experimental.pallas import tpu as pltpu
from jax.sharding import PartitionSpec as P

HD = 128
ROPE_BASE = 500000.0
EPSILON = 1e-05
TAG = 128
VMEM_LIMIT = 8 * 1024 * 1024
OUT_VMEM_LIMIT = 18 * 1024 * 1024
VMEM = pl.BlockSpec(memory_space=pltpu.VMEM)
SMEM = pl.BlockSpec(memory_space=pltpu.SMEM)
HBM = pl.BlockSpec(memory_space=pltpu.HBM)


def permute(block, target):
    return lax.ppermute(block, "gx", [(int(i), int(t)) for i, t in enumerate(target)])


def moved(source, target):
    result = np.empty_like(source)
    result[target] = source
    return result


class Group:
    def __init__(self, blocks, sources, crossed=False):
        self.blocks, self.sources, self.crossed = blocks, sources, crossed

    def send(self, target, crossed=False):
        return Group(permute(self.blocks, target), [moved(source, target) for source in self.sources], crossed)


def join(groups):
    if len(groups) == 1:
        return groups[0]
    return Group(jnp.concatenate([g.blocks for g in groups], 0), [source for g in groups for source in g.sources])


def ring_order(size):
    if size > 4:
        return list(range(size))
    return list(range(0, size, 2)) + list(range(1, size, 2))[::-1]


def axes_of(devices):
    chips, inner = devices // 2, 1
    while inner * inner * 4 <= chips and chips % (inner * 2) == 0:
        inner *= 2
    sizes = (chips // inner, inner, 2)
    place = np.arange(devices).reshape(sizes)
    result = []
    for axis, size in enumerate(sizes):
        order = ring_order(size)
        after = np.empty(size, int)
        for here, there in zip(order, order[1:] + order[:1]):
            after[here] = there
        before = np.argsort(after)
        result.append((size, np.take(place, after, axis).ravel(), np.take(place, before, axis).ravel()))
    return result


def ring(group, axis):
    size, following, preceding = axis
    groups = []
    forward = backward = group
    for step in range(1, size // 2 + 1):
        forward = forward.send(following)
        groups.append(forward)
        if 2 * step < size:
            backward = backward.send(preceding)
            groups.append(backward)
    return groups


def gather(block, devices, meanwhile=()):
    (size, following, preceding), inner, core = axes_of(devices)
    own = Group(block[None], [np.arange(devices)])
    near = ring(own, inner)
    groups = [own] + near + [join([own] + near).send(core[1], crossed=True)]
    forward = backward = own
    for step in range(1, size // 2 + 1):
        before = forward.blocks
        arrived = [forward.send(following)] + ([backward.send(preceding)] if 2 * step < size else [])
        forward, backward = arrived[0], arrived[-1]
        if step <= len(meanwhile):
            onward = (step < size // 2) + (2 * step + 2 < size)
            chips, *alone = hold(arrived, onward, meanwhile[step - 1](before))
            forward, backward = (alone + [forward])[0], (alone + [backward])[-1]
        else:
            chips = join(arrived)
        reached = [chips] + ring(chips, inner)
        groups += reached + [group.send(core[1], crossed=True) for group in reached]
    return groups


def hold_kernel(count, *refs):
    stacked, *alone = refs[count + 1 :]
    for at in range(count):
        stacked[at] = refs[at][0]
    for at in range(len(alone)):
        alone[at][...] = refs[at][...]


def hold(groups, onward, after):
    blocks = [group.blocks for group in groups]
    stacked, *alone = pl.pallas_call(
        functools.partial(hold_kernel, len(blocks)),
        out_shape=[jax.ShapeDtypeStruct((len(blocks), *blocks[0].shape[1:]), blocks[0].dtype)]
        + [jax.ShapeDtypeStruct(block.shape, block.dtype) for block in blocks[:onward]],
        in_specs=[VMEM] * len(blocks) + [pl.BlockSpec(memory_space=pl.ANY)],
        out_specs=[VMEM] * (onward + 1),
        compiler_params=pltpu.CompilerParams(vmem_limit_bytes=VMEM_LIMIT),
    )(*blocks, after)
    sources = [group.sources for group in groups]
    return [Group(stacked, sum(sources, []))] + [Group(block, source) for block, source in zip(alone, sources)]


def swap_cores(block, devices):
    return permute(block, np.arange(devices) ^ 1)


def exchange(pieces, devices):
    same_core = [list(range(core, devices, 2)) for core in range(2)]
    return lax.all_to_all(pieces, "gx", 0, 0, axis_index_groups=same_core, tiled=True)


def places(groups, devices):
    here = np.arange(devices)
    chips = [source // 2 for group in groups for source in group.sources]
    columns = [chip * 2 + (here % 2 ^ other) for chip in range(devices // 2) for other in range(2)]
    return np.stack(chips + columns + [here], 1).astype(np.int32)


def norm_kernel(lengths_far, hidden_far, gain_far, out, lengths, hidden, gain, arrived):
    copies = [
        pltpu.make_async_copy(far, near, arrived.at[at])
        for at, (far, near) in enumerate(((hidden_far, hidden), (gain_far, gain), (lengths_far, lengths)))
    ]
    for copy in copies:
        copy.start()
    copies[0].wait()
    states = hidden[...].astype(jnp.float32)
    scale = lax.rsqrt(jnp.mean(states * states, -1, keepdims=True) + EPSILON)
    copies[1].wait()
    normed = states * scale * gain[...].astype(jnp.float32).reshape(1, 1, gain.shape[0])
    steps, rows, width = normed.shape
    lines = [normed[step, row : row + 1] for row in range(rows) for step in range(steps)]
    out[:, :width] = jnp.concatenate(lines, 0).astype(out.dtype)
    line = lax.broadcasted_iota(jnp.int32, (steps * rows, TAG), 0)
    lane = lax.broadcasted_iota(jnp.int32, (steps * rows, TAG), 1)
    position = line % steps
    copies[2].wait()
    for row in range(rows):
        position = jnp.where(line // steps == row, position + lengths[row], position)
    tag = jnp.where(lane == 0, position // 32, position % 32)
    out[:, width:] = tag.astype(jnp.float32).astype(out.dtype)


def norm(hidden, gain, lengths):
    steps, rows, width = hidden.shape
    return pl.pallas_call(
        norm_kernel,
        out_shape=jax.ShapeDtypeStruct((steps * rows, width + TAG), jnp.bfloat16),
        in_specs=[HBM] * 3,
        out_specs=VMEM,
        scratch_shapes=[
            pltpu.SMEM(lengths.shape, lengths.dtype),
            pltpu.VMEM(hidden.shape, hidden.dtype),
            pltpu.VMEM(gain.shape, gain.dtype),
            pltpu.SemaphoreType.DMA((3,)),
        ],
        compiler_params=pltpu.CompilerParams(vmem_limit_bytes=VMEM_LIMIT),
        cost_estimate=pl.CostEstimate(flops=6 * steps * rows * width, bytes_accessed=4 * steps * rows * width, transcendentals=0),
    )(*[pltpu.with_memory_space_constraint(array, pltpu.HBM) for array in (lengths, hidden, gain)])


def fetch_kernel(firsts, chunks, *refs):
    copies, count, arrived = [], len(firsts), refs[-1]
    refs[-2][...] = jnp.zeros_like(refs[-2])
    for first, far, near in zip(firsts, refs[:count], refs[count + 1 : 2 * count + 1]):
        size = near.shape[0] // min(chunks, near.shape[0])
        for at in range(0, near.shape[0], size):
            source = far.at[pl.ds(first + at, size)]
            copies.append(pltpu.make_async_copy(source, near.at[pl.ds(at, size)], arrived.at[len(copies)]))
            copies[-1].start()
    for copy in copies:
        copy.wait()


def fetch(ranges, after):
    chunks = 8
    arrays = [array for array, _, _ in ranges]
    shapes = [(count, *array.shape[1:]) for array, _, count in ranges]
    return pl.pallas_call(
        functools.partial(fetch_kernel, [first for _, first, _ in ranges], chunks),
        out_shape=[pltpu.VMEM(shape, array.dtype) for shape, array in zip(shapes, arrays)]
        + [jax.ShapeDtypeStruct((8, HD), jnp.float32)],
        in_specs=[HBM] * len(arrays) + [pl.BlockSpec(memory_space=pl.ANY)],
        out_specs=[VMEM] * (len(arrays) + 1),
        scratch_shapes=[pltpu.SemaphoreType.DMA((chunks * len(arrays),))],
        compiler_params=pltpu.CompilerParams(vmem_limit_bytes=VMEM_LIMIT),
        cost_estimate=pl.CostEstimate(
            flops=0, bytes_accessed=sum(2 * math.prod(shape) for shape in shapes), transcendentals=0
        ),
    )(*[pltpu.with_memory_space_constraint(array, pltpu.HBM) for array in arrays], after)


def slots_of(refs, counts):
    return [(ref, at) for ref, count in zip(refs, counts) for at in range(count)]


def assemble(slots, first, width):
    lanes = slice(first, first + width)
    return jnp.concatenate([ref[at, :, lanes].astype(jnp.float32) for ref, at in slots], 0).astype(jnp.bfloat16)


def multiply(slots, weights, depth, total, kept):
    total[...] = jnp.zeros_like(total)
    chunk = 0
    for part, copies in weights:
        for at in range(part.shape[0] // depth):
            kept[chunk] = assemble(slots, chunk * depth, depth)
            if copies:
                copies[at].wait()
            total[...] += jnp.dot(kept[chunk], part[at * depth : (at + 1) * depth, :], preferred_element_type=jnp.float32)
            chunk += 1


def turns(positions):
    shape = (positions.shape[0], HD)
    lane = lax.broadcasted_iota(jnp.int32, shape, 1)
    pair = (lane // 2).astype(jnp.float32)
    angles = positions * jnp.exp(pair * (-2.0 * math.log(ROPE_BASE) / HD))
    return jnp.cos(angles), jnp.where(lane % 2 == 0, -1.0, 1.0) * jnp.sin(angles)


def turn(values, cosine, sine):
    lanes = values.shape[-1]
    even = lax.broadcasted_iota(jnp.int32, values.shape, 1) % 2 == 0
    swapped = jnp.where(even, pltpu.roll(values, lanes - 1, 1), pltpu.roll(values, 1, 1))
    return values * cosine + swapped * sine


def project_kernel(counts, crossed, width, place, *refs):
    slots = slots_of(refs, counts)
    weights, keyval, *outs = refs[len(counts) : len(counts) + 6]
    kept, total, packed = refs[len(counts) + 6 :]
    queries, fresh = outs[:2], outs[2:]
    depth = keyval.shape[1]
    tags = jnp.concatenate([ref[at, :, width:].astype(jnp.float32) for ref, at in slots], 0)
    cosine, sine = turns(tags[:, 0:1] * 32.0 + tags[:, 1:2])
    multiply(slots, [(weights, None)], depth, total, kept)
    own = kept[place[2 * len(slots)]]
    blocks = keyval.shape[2] // HD
    for which in range(2):
        term = jnp.dot(own, keyval[which], preferred_element_type=jnp.float32)
        for slot in range(len(slots)):
            for at in range(blocks):
                row = (which * blocks + at) * 4
                fresh[crossed[slot]][place[slot], row : row + 4, :] = term[
                    slot * 4 : slot * 4 + 4, at * HD : (at + 1) * HD
                ]
    heads = total.shape[1] // HD
    for head in range(heads):
        turned = turn(total[:, head * HD : (head + 1) * HD], cosine, sine)
        for slot in range(len(slots)):
            for row in range(2):
                line, at = row * 2 * heads + head * 2, slot * 4 + row * 2
                packed[slot, line : line + 2, :] = turned[at : at + 2, :]
    for slot in range(len(slots)):
        queries[crossed[slot]][place[slot]] = packed[slot].astype(jnp.bfloat16)


def group_shape(groups):
    counts = [len(group.sources) for group in groups]
    return counts, [int(group.crossed) for group, count in zip(groups, counts) for _ in range(count)]


def project(groups, w_query, w_keyval, place, devices):
    counts, crossed = group_shape(groups)
    width, columns = w_query.shape
    depth, kv_width = w_keyval.shape[1:]
    own = groups[0].blocks.shape[1]
    rows, tile = devices * own, own * (columns // HD)
    query = jax.ShapeDtypeStruct((devices // 2, tile, HD), jnp.bfloat16)
    fresh = jax.ShapeDtypeStruct((devices // 2, own * 2 * kv_width // HD, HD), jnp.float32)
    return pl.pallas_call(
        functools.partial(project_kernel, counts, crossed, width),
        out_shape=[query, query, fresh, fresh],
        in_specs=[SMEM] + [VMEM] * (len(groups) + 2),
        out_specs=[VMEM] * 4,
        scratch_shapes=[
            pltpu.VMEM((devices, rows, depth), jnp.bfloat16),
            pltpu.VMEM((rows, columns), jnp.float32),
            pltpu.VMEM((devices, tile, HD), jnp.float32),
        ],
        compiler_params=pltpu.CompilerParams(vmem_limit_bytes=VMEM_LIMIT),
        cost_estimate=pl.CostEstimate(
            flops=2 * rows * columns * width, bytes_accessed=2 * columns * width, transcendentals=2 * rows * HD
        ),
    )(place, *[group.blocks for group in groups], w_query, w_keyval)


def pack_kernel(near, far, near_sum, far_sum, out):
    tile, lines = near.shape[1], near_sum.shape[1]
    out[:, :tile, :] = near[...]
    out[:, tile : 2 * tile, :] = far[...]
    total = near_sum[...] + far_sum[...]
    high = total.astype(jnp.bfloat16)
    out[:, 2 * tile : 2 * tile + lines, :] = high
    out[:, 2 * tile + lines :, :] = (total - high.astype(jnp.float32)).astype(jnp.bfloat16)


def pack(near, far, near_sum, far_sum):
    chips, tile, _ = near.shape
    return pl.pallas_call(
        pack_kernel,
        out_shape=jax.ShapeDtypeStruct((chips, 2 * tile + 2 * near_sum.shape[1], HD), jnp.bfloat16),
        in_specs=[VMEM] * 4,
        out_specs=VMEM,
        compiler_params=pltpu.CompilerParams(vmem_limit_bytes=VMEM_LIMIT),
    )(near, far, near_sum, far_sum)


def out_kernel(counts, crossed, place, *refs):
    slots = slots_of(refs, counts)
    upper, weights, near, far, lower, kept, total, arrived = refs[len(counts) :]
    depth, first = kept.shape[2], upper.shape[0]
    copies = []
    for at in range(lower.shape[0] // depth):
        source = weights.at[pl.ds(first + at * depth, depth)]
        copies.append(pltpu.make_async_copy(source, lower.at[pl.ds(at * depth, depth)], arrived.at[at]))
        copies[-1].start()
    multiply(slots, [(upper, None), (lower, copies)], depth, total, kept)
    own = near.shape[1]
    for slot in range(len(slots)):
        (near, far)[crossed[slot]][place[slot]] = total[slot * own : (slot + 1) * own].astype(near.dtype)


def project_out(groups, w_upper, w_out, place, devices):
    counts, crossed = group_shape(groups)
    columns = w_out.shape[1]
    own, width = groups[0].blocks.shape[1:]
    chunks = devices // 2
    piece = jax.ShapeDtypeStruct((devices // 2, own, columns), jnp.bfloat16)
    return pl.pallas_call(
        functools.partial(out_kernel, counts, crossed),
        out_shape=[piece, piece],
        in_specs=[SMEM] + [VMEM] * (len(groups) + 1) + [HBM],
        out_specs=[VMEM, VMEM],
        scratch_shapes=[
            pltpu.VMEM((width - w_upper.shape[0], columns), w_out.dtype),
            pltpu.VMEM((chunks, devices * own, width // chunks), jnp.bfloat16),
            pltpu.VMEM((devices * own, columns), jnp.float32),
            pltpu.SemaphoreType.DMA((chunks // 2,)),
        ],
        compiler_params=pltpu.CompilerParams(vmem_limit_bytes=OUT_VMEM_LIMIT),
        cost_estimate=pl.CostEstimate(
            flops=2 * devices * own * columns * width, bytes_accessed=2 * columns * width, transcendentals=0
        ),
    )(place, *[group.blocks for group in groups], w_upper, pltpu.with_memory_space_constraint(w_out, pltpu.HBM))


def attend_kernel(devices, kv_heads, tile, lengths, place, pieces, cache, out, fresh, queries, mixed):
    length, width = cache.shape[2:]
    extra = fresh.shape[2]
    half = tile // 2
    per_head = devices // kv_heads * half
    scale = 1.0 / math.sqrt(HD)
    for chip in range(devices // 2):
        for other in range(2):
            piece = pieces[chip, other * tile : (other + 1) * tile, :]
            queries[place[devices + 2 * chip + other]] = piece.astype(jnp.float32)
    line = lax.broadcasted_iota(jnp.int32, (8, 1), 0)
    first = jnp.where(line % 4 < 2, lengths[0], lengths[1])
    cosine, sine = turns((first + line % 2).astype(jnp.float32))
    terms = pieces[:, 2 * tile :, :].astype(jnp.float32)
    total = jnp.sum(terms, 0)
    total = total[: total.shape[0] // 2] + total[total.shape[0] // 2 :]
    twice = [jnp.concatenate([total[4 * at : 4 * at + 4]] * 2, 0) for at in range(2 * kv_heads)]
    new_keys = jnp.concatenate([turn(part, cosine, sine) for part in twice[:kv_heads]], 1)
    new_values = jnp.concatenate(twice[kv_heads:], 1)
    spot = lax.broadcasted_iota(jnp.int32, (extra, width), 0)
    for row in range(2):
        for which, new in enumerate((new_keys, new_values)):
            spread = jnp.where(spot == 0, new[2 * row : 2 * row + 1, :], 0.0)
            spread = jnp.where(spot == 1, new[2 * row + 1 : 2 * row + 2, :], spread)
            fresh[which, row] = spread.astype(fresh.dtype)
    every = queries[...]
    lines = kv_heads * per_head
    column = lax.broadcasted_iota(jnp.int32, (lines, length), 1)
    new_column = lax.broadcasted_iota(jnp.int32, (lines, extra), 1)
    step = lax.broadcasted_iota(jnp.int32, (lines, extra), 0) % 2
    across = (((1,), (1,)), ((), ()))
    for row in range(2):
        mine = every[:, row * half : row * half + half, :].reshape(lines, HD)
        spread = jnp.concatenate([mine] * kv_heads, 1)
        own_row = lax.broadcasted_iota(jnp.int32, spread.shape, 0) // per_head
        own_lane = lax.broadcasted_iota(jnp.int32, spread.shape, 1) // HD
        spread = jnp.where(own_row == own_lane, spread, 0.0).astype(jnp.bfloat16)
        scores = lax.dot_general(spread, cache[0, row], across, preferred_element_type=jnp.float32) * scale
        scores = jnp.where(column < lengths[row], scores, -jnp.inf)
        new_scores = lax.dot_general(spread, fresh[0, row], across, preferred_element_type=jnp.float32) * scale
        new_scores = jnp.where(new_column <= step, new_scores, -jnp.inf)
        peak = jnp.maximum(jnp.max(scores, 1, keepdims=True), jnp.max(new_scores, 1, keepdims=True))
        weight = jnp.exp(scores - peak)
        new_weight = jnp.exp(new_scores - peak)
        denominator = jnp.sum(weight, 1, keepdims=True) + jnp.sum(new_weight, 1, keepdims=True)
        result = jnp.dot(weight.astype(jnp.bfloat16), cache[1, row], preferred_element_type=jnp.float32)
        result += jnp.dot(new_weight.astype(jnp.bfloat16), fresh[1, row], preferred_element_type=jnp.float32)
        for head in range(kv_heads):
            rows = slice(head * per_head, (head + 1) * per_head)
            part = result[rows, head * HD : (head + 1) * HD] / denominator[rows]
            for query in range(per_head // 2):
                lanes = slice((head * per_head // 2 + query) * HD, (head * per_head // 2 + query + 1) * HD)
                for at in range(2):
                    mixed[at * 2 + row : at * 2 + row + 1, lanes] = part[2 * query + at : 2 * query + at + 1]
    out[...] = mixed[...].astype(out.dtype)


def attend(pieces, tile, cache, lengths, place, devices):
    length, width = cache.shape[2], cache.shape[3]
    columns = devices * tile // 4 * HD
    return pl.pallas_call(
        functools.partial(attend_kernel, devices, width // HD, tile),
        out_shape=jax.ShapeDtypeStruct((4, columns), jnp.bfloat16),
        in_specs=[SMEM, SMEM, VMEM, VMEM],
        out_specs=VMEM,
        scratch_shapes=[
            pltpu.VMEM((2, 2, HD, width), cache.dtype),
            pltpu.VMEM((devices, tile, HD), jnp.float32),
            pltpu.VMEM((4, columns), jnp.float32),
        ],
        compiler_params=pltpu.CompilerParams(vmem_limit_bytes=VMEM_LIMIT),
        cost_estimate=pl.CostEstimate(
            flops=8 * 128 * length * width, bytes_accessed=8 * length * width, transcendentals=256 * length
        ),
    )(lengths, place, pieces, cache)


def finish_kernel(devices, place, pieces, out):
    columns = pieces.shape[3]
    steps, rows = out.shape[:2]
    for chip in range(devices // 2):
        for other in range(2):
            source = place[devices + 2 * chip + other]
            lanes = pl.ds(pl.multiple_of(source * columns, columns), columns)
            piece = pieces[chip, other].astype(jnp.float32)
            for step in range(steps):
                out[step, :, lanes] = piece[step * rows : (step + 1) * rows].astype(out.dtype)


def finish(pieces, place, steps, devices):
    own, columns = pieces.shape[2:]
    return pl.pallas_call(
        functools.partial(finish_kernel, devices),
        out_shape=jax.ShapeDtypeStruct((steps, own // steps, devices * columns), jnp.bfloat16),
        in_specs=[SMEM, VMEM],
        out_specs=VMEM,
        compiler_params=pltpu.CompilerParams(vmem_limit_bytes=VMEM_LIMIT),
    )(place, pieces)


def body(hidden, norm_gain, w_query, w_keyval, w_out, kv_cache, lengths):
    steps = hidden.shape[0]
    devices = lax.axis_size("gx")

    normed = norm(hidden, norm_gain, lengths)
    half = w_out.shape[0] // 2
    fetched = []

    def bring(ranges, after):
        *arrays, done = fetch(ranges, after)
        fetched.append(arrays)
        return done

    groups = gather(
        normed,
        devices,
        [
            functools.partial(bring, [(w_query, 0, w_query.shape[0]), (w_keyval, 0, 2)]),
            functools.partial(bring, [(kv_cache, 0, 2), (w_out, 0, half)]),
        ],
    )
    (w_query, w_keyval), (kv_cache, w_upper) = fetched
    table = jnp.asarray(places(groups, devices))
    place = lax.dynamic_index_in_dim(table, lax.axis_index("gx"), 0, keepdims=False)
    near, far, near_sum, far_sum = project(groups, w_query, w_keyval, place, devices)
    pieces = pack(near, swap_cores(far, devices), near_sum, swap_cores(far_sum, devices))

    mixed = attend(exchange(pieces, devices), near.shape[1], kv_cache, lengths, place, devices)
    near, far = project_out(gather(mixed, devices), w_upper, w_out, place, devices)
    pieces = jnp.stack([near, swap_cores(far, devices)], 1)
    return finish(exchange(pieces, devices), place, steps, devices)


def rotate(values, positions):
    row_total, head_count, head_width = values.shape
    half_width = head_width // 2
    frequency = ROPE_BASE ** (-2.0 * jnp.arange(half_width, dtype=jnp.float32) / head_width)
    angles = positions[:, None, None] * frequency[None, None, :]
    cosine = jnp.cos(angles)
    sine_part = jnp.sin(angles)
    paired = values.reshape(row_total, head_count, half_width, 2)
    first_half = paired[..., 0]
    second_half = paired[..., 1]
    turned = jnp.stack(
        [
            first_half * cosine - second_half * sine_part,
            first_half * sine_part + second_half * cosine,
        ],
        -1,
    )
    return turned.reshape(row_total, head_count, head_width)


def attend_split_heads(queries, cache_keys, cache_values, lengths, fresh_keys, fresh_values):
    score_scale = 1.0 / math.sqrt(HD)
    fresh_scores = (
        jnp.einsum("rkgd,rskd->rkgs", queries, fresh_keys, preferred_element_type=jnp.float32)
        * score_scale
    )
    cached = (
        jnp.einsum("rkgd,rlkd->rkgl", queries, cache_keys, preferred_element_type=jnp.float32)
        * score_scale
    )
    in_range = jnp.arange(cache_keys.shape[1])[None, :] < lengths[:, None]
    cached = jnp.where(in_range[:, None, None, :], cached, -jnp.inf)
    row_peak = jnp.maximum(cached.max(-1), fresh_scores.max(-1))
    cached_exp = jnp.exp(cached - row_peak[..., None])
    fresh_exp = jnp.exp(fresh_scores - row_peak[..., None])
    denominator = cached_exp.sum(-1) + fresh_exp.sum(-1)
    mixed = jnp.einsum(
        "rkgl,rlkd->rkgd",
        cached_exp.astype(jnp.bfloat16),
        cache_values,
        preferred_element_type=jnp.float32,
    )
    mixed = mixed + jnp.einsum(
        "rkgs,rskd->rkgd",
        fresh_exp.astype(jnp.bfloat16),
        fresh_values,
        preferred_element_type=jnp.float32,
    )
    return (mixed / denominator[..., None]).astype(jnp.bfloat16)


def body_split_heads(hidden, norm_gain, w_query, w_keyval, w_out, kv_cache, lengths):
    step_count, rows_dev, model_width = hidden.shape
    devices = lax.axis_size("gx")
    device_index = lax.axis_index("gx")
    row_slab = w_keyval.shape[1]
    kv_width = w_keyval.shape[2]
    query_cols = w_query.shape[1]
    heads_width = query_cols * devices
    head_count = heads_width // HD
    kv_heads = kv_width // HD
    kv_both = jnp.concatenate([w_keyval[0], w_keyval[1]], 1)
    cache_keys = kv_cache[0].reshape(rows_dev, kv_cache.shape[2], kv_heads, HD)
    cache_values = kv_cache[1].reshape(rows_dev, kv_cache.shape[2], kv_heads, HD)
    states = hidden.astype(jnp.float32)
    scaled = states * lax.rsqrt(jnp.mean(states * states, -1, keepdims=True) + EPSILON)
    normed = (scaled * norm_gain.astype(jnp.float32)).astype(jnp.bfloat16)
    new_keys = []
    new_values = []
    outputs = []
    for step_index in range(step_count):
        shard_piece = lax.all_gather(normed[step_index], "gx", axis=0, tiled=True)
        queries = jnp.dot(shard_piece, w_query, preferred_element_type=jnp.float32)
        own_slab = lax.dynamic_slice_in_dim(shard_piece, device_index * row_slab, row_slab, 1)
        partial_kv = jnp.dot(own_slab, kv_both, preferred_element_type=jnp.float32)
        joined = jnp.concatenate([queries, partial_kv], 1)
        project_query_rows = lax.all_to_all(
            joined[:, :query_cols], "gx", split_axis=0, concat_axis=1, tiled=True
        )
        project_keyval = lax.psum_scatter(
            joined[:, query_cols:], "gx", scatter_dimension=0, tiled=True
        )
        positions = (lengths + step_index).astype(jnp.float32)
        prepare_queries = rotate(
            project_query_rows.reshape(rows_dev, head_count, HD), positions
        ).astype(jnp.bfloat16)
        prepare_queries = prepare_queries.reshape(rows_dev, kv_heads, head_count // kv_heads, HD)
        key_new = rotate(
            project_keyval[:, :kv_width].reshape(rows_dev, kv_heads, HD), positions
        ).astype(jnp.bfloat16)
        value_new = (
            project_keyval[:, kv_width:].reshape(rows_dev, kv_heads, HD).astype(jnp.bfloat16)
        )
        queries, key_new, value_new = (prepare_queries, key_new, value_new)
        new_keys.append(key_new)
        new_values.append(value_new)
        mixed = attend_split_heads(
            queries,
            cache_keys,
            cache_values,
            lengths,
            jnp.stack(new_keys, 1),
            jnp.stack(new_values, 1),
        )
        out_cols = jnp.dot(
            lax.all_gather(mixed.reshape(rows_dev, heads_width), "gx", axis=0, tiled=True),
            w_out,
            preferred_element_type=jnp.float32,
        ).astype(jnp.bfloat16)
        outputs.append(lax.all_to_all(out_cols, "gx", split_axis=0, concat_axis=1, tiled=True))
    return jnp.stack(outputs)


def solution(mesh):
    devices = mesh.shape["gx"]

    def run(*arrays):
        whole_heads = arrays[2].shape[1] % HD == 0 and devices % 2 == 0
        return (body if whole_heads else body_split_heads)(*arrays)

    in_specs = (
        P(None, ("group", "gx"), None),
        P(),
        P(None, "gx"),
        P(None, "gx", None),
        P(None, "gx"),
        P(None, ("group", "gx"), None, None),
        P(("group", "gx")),
    )
    out_specs = P(None, ("group", "gx"), None)
    return jax.shard_map(run, mesh=mesh, in_specs=in_specs, out_specs=out_specs, check_vma=False)
```

```python
import functools
import math

import jax
import jax.numpy as jnp
import numpy as np
from jax import lax
from jax.experimental import pallas as pl
from jax.experimental.pallas import tpu as pltpu
from jax.sharding import PartitionSpec as P

HD = 128
ROPE_BASE = 500000.0
EPSILON = 1e-05
TAG = 128
VMEM_LIMIT = 8 * 1024 * 1024
VMEM = pl.BlockSpec(memory_space=pltpu.VMEM)
SMEM = pl.BlockSpec(memory_space=pltpu.SMEM)
HBM = pl.BlockSpec(memory_space=pltpu.HBM)


def permute(block, target):
    return lax.ppermute(block, "gx", [(int(i), int(t)) for i, t in enumerate(target)])


def moved(source, target):
    result = np.empty_like(source)
    result[target] = source
    return result


class Group:
    def __init__(self, blocks, sources, crossed=False):
        self.blocks, self.sources, self.crossed = blocks, sources, crossed

    def send(self, target, crossed=False):
        return Group(permute(self.blocks, target), [moved(source, target) for source in self.sources], crossed)


def join(groups):
    if len(groups) == 1:
        return groups[0]
    return Group(jnp.concatenate([g.blocks for g in groups], 0), [source for g in groups for source in g.sources])


def ring_order(size):
    if size > 4:
        return list(range(size))
    return list(range(0, size, 2)) + list(range(1, size, 2))[::-1]


def axes_of(devices):
    chips, inner = devices // 2, 1
    while inner * inner * 4 <= chips and chips % (inner * 2) == 0:
        inner *= 2
    sizes = (chips // inner, inner, 2)
    place = np.arange(devices).reshape(sizes)
    result = []
    for axis, size in enumerate(sizes):
        order = ring_order(size)
        after = np.empty(size, int)
        for here, there in zip(order, order[1:] + order[:1]):
            after[here] = there
        before = np.argsort(after)
        result.append((size, np.take(place, after, axis).ravel(), np.take(place, before, axis).ravel()))
    return result


def ring(group, axis):
    size, following, preceding = axis
    groups = []
    forward = backward = group
    for step in range(1, size // 2 + 1):
        forward = forward.send(following)
        groups.append(forward)
        if 2 * step < size:
            backward = backward.send(preceding)
            groups.append(backward)
    return groups


def gather(block, devices, meanwhile=()):
    (size, following, preceding), inner, core = axes_of(devices)
    own = Group(block[None], [np.arange(devices)])
    near = ring(own, inner)
    groups = [own] + near + [join([own] + near).send(core[1], crossed=True)]
    forward = backward = own
    for step in range(1, size // 2 + 1):
        before = forward.blocks
        arrived = [forward.send(following)] + ([backward.send(preceding)] if 2 * step < size else [])
        forward, backward = arrived[0], arrived[-1]
        if step <= len(meanwhile):
            onward = (step < size // 2) + (2 * step + 2 < size)
            chips, *alone = hold(arrived, onward, meanwhile[step - 1](before))
            forward, backward = (alone + [forward])[0], (alone + [backward])[-1]
        else:
            chips = join(arrived)
        reached = [chips] + ring(chips, inner)
        if step == size // 2 < len(meanwhile):
            reached[-1:] = hold(reached[-1:], 0, meanwhile[step](chips.blocks))
        groups += reached + [group.send(core[1], crossed=True) for group in reached]
    return groups


def hold_kernel(count, *refs):
    stacked, *alone = refs[count + 1 :]
    for at in range(count):
        stacked[at] = refs[at][0]
    for at in range(len(alone)):
        alone[at][...] = refs[at][...]


def hold(groups, onward, after):
    blocks = [group.blocks for group in groups]
    stacked, *alone = pl.pallas_call(
        functools.partial(hold_kernel, len(blocks)),
        out_shape=[jax.ShapeDtypeStruct((len(blocks), *blocks[0].shape[1:]), blocks[0].dtype)]
        + [jax.ShapeDtypeStruct(block.shape, block.dtype) for block in blocks[:onward]],
        in_specs=[VMEM] * len(blocks) + [pl.BlockSpec(memory_space=pl.ANY)],
        out_specs=[VMEM] * (onward + 1),
        compiler_params=pltpu.CompilerParams(vmem_limit_bytes=VMEM_LIMIT),
    )(*blocks, after)
    sources = [group.sources for group in groups]
    return [Group(stacked, sum(sources, []))] + [Group(block, source) for block, source in zip(alone, sources)]


def swap_cores(block, devices):
    return permute(block, np.arange(devices) ^ 1)


def exchange(pieces, devices):
    same_core = [list(range(core, devices, 2)) for core in range(2)]
    return lax.all_to_all(pieces, "gx", 0, 0, axis_index_groups=same_core, tiled=True)


def places(groups, devices):
    here = np.arange(devices)
    chips = [source // 2 for group in groups for source in group.sources]
    columns = [chip * 2 + (here % 2 ^ other) for chip in range(devices // 2) for other in range(2)]
    return np.stack(chips + columns, 1).astype(np.int32)


def norm_kernel(lengths_far, hidden_far, gain_far, out, lengths, hidden, gain, arrived):
    copies = [
        pltpu.make_async_copy(far, near, arrived.at[at])
        for at, (far, near) in enumerate(((hidden_far, hidden), (gain_far, gain), (lengths_far, lengths)))
    ]
    for copy in copies:
        copy.start()
    copies[0].wait()
    states = hidden[...].astype(jnp.float32)
    scale = lax.rsqrt(jnp.mean(states * states, -1, keepdims=True) + EPSILON)
    copies[1].wait()
    normed = states * scale * gain[...].astype(jnp.float32).reshape(1, 1, gain.shape[0])
    steps, rows, width = normed.shape
    lines = [normed[step, row : row + 1] for row in range(rows) for step in range(steps)]
    out[:, :width] = jnp.concatenate(lines, 0).astype(out.dtype)
    line = lax.broadcasted_iota(jnp.int32, (steps * rows, TAG), 0)
    lane = lax.broadcasted_iota(jnp.int32, (steps * rows, TAG), 1)
    position = line % steps
    copies[2].wait()
    for row in range(rows):
        position = jnp.where(line // steps == row, position + lengths[row], position)
    tag = jnp.where(lane == 0, position // 32, position % 32)
    out[:, width:] = tag.astype(jnp.float32).astype(out.dtype)


def norm(hidden, gain, lengths):
    steps, rows, width = hidden.shape
    return pl.pallas_call(
        norm_kernel,
        out_shape=jax.ShapeDtypeStruct((steps * rows, width + TAG), jnp.bfloat16),
        in_specs=[HBM] * 3,
        out_specs=VMEM,
        scratch_shapes=[
            pltpu.SMEM(lengths.shape, lengths.dtype),
            pltpu.VMEM(hidden.shape, hidden.dtype),
            pltpu.VMEM(gain.shape, gain.dtype),
            pltpu.SemaphoreType.DMA((3,)),
        ],
        compiler_params=pltpu.CompilerParams(vmem_limit_bytes=VMEM_LIMIT),
        cost_estimate=pl.CostEstimate(flops=6 * steps * rows * width, bytes_accessed=4 * steps * rows * width, transcendentals=0),
    )(*[pltpu.with_memory_space_constraint(array, pltpu.HBM) for array in (lengths, hidden, gain)])


def fetch_kernel(firsts, chunks, *refs):
    copies, count, arrived = [], len(firsts), refs[-1]
    refs[-2][...] = jnp.zeros_like(refs[-2])
    for first, far, near in zip(firsts, refs[:count], refs[count + 1 : 2 * count + 1]):
        size = near.shape[0] // min(chunks, near.shape[0])
        for at in range(0, near.shape[0], size):
            source = far.at[pl.ds(first + at, size)]
            copies.append(pltpu.make_async_copy(source, near.at[pl.ds(at, size)], arrived.at[len(copies)]))
            copies[-1].start()
    for copy in copies:
        copy.wait()


def fetch(ranges, after):
    chunks = 8
    arrays = [array for array, _, _ in ranges]
    shapes = [(count, *array.shape[1:]) for array, _, count in ranges]
    return pl.pallas_call(
        functools.partial(fetch_kernel, [first for _, first, _ in ranges], chunks),
        out_shape=[pltpu.VMEM(shape, array.dtype) for shape, array in zip(shapes, arrays)]
        + [jax.ShapeDtypeStruct((8, HD), jnp.float32)],
        in_specs=[HBM] * len(arrays) + [pl.BlockSpec(memory_space=pl.ANY)],
        out_specs=[VMEM] * (len(arrays) + 1),
        scratch_shapes=[pltpu.SemaphoreType.DMA((chunks * len(arrays),))],
        compiler_params=pltpu.CompilerParams(vmem_limit_bytes=VMEM_LIMIT),
        cost_estimate=pl.CostEstimate(
            flops=0, bytes_accessed=sum(2 * math.prod(shape) for shape in shapes), transcendentals=0
        ),
    )(*[pltpu.with_memory_space_constraint(array, pltpu.HBM) for array in arrays], after)


def slots_of(refs, counts):
    return [(ref, at) for ref, count in zip(refs, counts) for at in range(count)]


def assemble(slots, first, width):
    lanes = slice(first, first + width)
    return jnp.concatenate([ref[at, :, lanes].astype(jnp.float32) for ref, at in slots], 0).astype(jnp.bfloat16)


def multiply(slots, weights, depth, total, kept):
    total[...] = jnp.zeros_like(total)
    chunk = 0
    for part in weights:
        for at in range(0, part.shape[0], depth):
            kept[chunk] = assemble(slots, chunk * depth, depth)
            total[...] += jnp.dot(kept[chunk], part[at : at + depth, :], preferred_element_type=jnp.float32)
            chunk += 1


def turns(positions):
    shape = (positions.shape[0], HD)
    lane = lax.broadcasted_iota(jnp.int32, shape, 1)
    pair = (lane // 2).astype(jnp.float32)
    angles = positions * jnp.exp(pair * (-2.0 * math.log(ROPE_BASE) / HD))
    return jnp.cos(angles), jnp.where(lane % 2 == 0, -1.0, 1.0) * jnp.sin(angles)


def turn(values, cosine, sine):
    lanes = values.shape[-1]
    even = lax.broadcasted_iota(jnp.int32, values.shape, 1) % 2 == 0
    swapped = jnp.where(even, pltpu.roll(values, lanes - 1, 1), pltpu.roll(values, 1, 1))
    return values * cosine + swapped * sine


def project_kernel(counts, crossed, width, place, *refs):
    slots = slots_of(refs, counts)
    first, second, keyval, *outs = refs[len(counts) : len(counts) + 7]
    kept, total, packed = refs[len(counts) + 7 :]
    queries, fresh = outs[:2], outs[2:]
    depth = keyval.shape[1]
    tags = jnp.concatenate([ref[at, :, width:].astype(jnp.float32) for ref, at in slots], 0)
    cosine, sine = turns(tags[:, 0:1] * 32.0 + tags[:, 1:2])
    multiply(slots, [first, second], depth, total, kept)
    me = lax.axis_index("gx")
    own = kept[me]
    blocks = keyval.shape[2] // HD
    for which in range(2):
        term = jnp.dot(own, keyval[which], preferred_element_type=jnp.float32)
        for slot in range(len(slots)):
            for at in range(blocks):
                row = (which * blocks + at) * 4
                fresh[crossed[slot]][place[me, slot], row : row + 4, :] = term[
                    slot * 4 : slot * 4 + 4, at * HD : (at + 1) * HD
                ]
    heads = total.shape[1] // HD
    for head in range(heads):
        turned = turn(total[:, head * HD : (head + 1) * HD], cosine, sine)
        for slot in range(len(slots)):
            for row in range(2):
                line, at = row * 2 * heads + head * 2, slot * 4 + row * 2
                packed[slot, line : line + 2, :] = turned[at : at + 2, :]
    for slot in range(len(slots)):
        queries[crossed[slot]][place[me, slot]] = packed[slot].astype(jnp.bfloat16)


def group_shape(groups):
    counts = [len(group.sources) for group in groups]
    return counts, [int(group.crossed) for group, count in zip(groups, counts) for _ in range(count)]


def project(groups, w_query, w_keyval, place, devices):
    counts, crossed = group_shape(groups)
    columns = w_query[0].shape[1]
    depth, kv_width = w_keyval.shape[1:]
    own, width = groups[0].blocks.shape[1], devices * depth
    rows, tile = devices * own, own * (columns // HD)
    query = jax.ShapeDtypeStruct((devices // 2, tile, HD), jnp.bfloat16)
    fresh = jax.ShapeDtypeStruct((devices // 2, own * 2 * kv_width // HD, HD), jnp.float32)
    return pl.pallas_call(
        functools.partial(project_kernel, counts, crossed, width),
        out_shape=[query, query, fresh, fresh],
        in_specs=[SMEM] + [VMEM] * (len(groups) + 3),
        out_specs=[VMEM] * 4,
        scratch_shapes=[
            pltpu.VMEM((devices, rows, depth), jnp.bfloat16),
            pltpu.VMEM((rows, columns), jnp.float32),
            pltpu.VMEM((devices, tile, HD), jnp.float32),
        ],
        compiler_params=pltpu.CompilerParams(vmem_limit_bytes=VMEM_LIMIT),
        cost_estimate=pl.CostEstimate(
            flops=2 * rows * columns * width, bytes_accessed=2 * columns * width, transcendentals=2 * rows * HD
        ),
    )(place, *[group.blocks for group in groups], *w_query, w_keyval)


def pack_kernel(near, far, near_sum, far_sum, out):
    tile, lines = near.shape[1], near_sum.shape[1]
    out[:, :tile, :] = near[...]
    out[:, tile : 2 * tile, :] = far[...]
    total = near_sum[...] + far_sum[...]
    high = total.astype(jnp.bfloat16)
    out[:, 2 * tile : 2 * tile + lines, :] = high
    out[:, 2 * tile + lines :, :] = (total - high.astype(jnp.float32)).astype(jnp.bfloat16)


def pack(near, far, near_sum, far_sum):
    chips, tile, _ = near.shape
    return pl.pallas_call(
        pack_kernel,
        out_shape=jax.ShapeDtypeStruct((chips, 2 * tile + 2 * near_sum.shape[1], HD), jnp.bfloat16),
        in_specs=[VMEM] * 4,
        out_specs=VMEM,
        compiler_params=pltpu.CompilerParams(vmem_limit_bytes=VMEM_LIMIT),
    )(near, far, near_sum, far_sum)


def out_kernel(counts, crossed, place, *refs):
    slots = slots_of(refs, counts)
    weights, near, far, kept, total = refs[len(counts) :]
    multiply(slots, [weights], kept.shape[2], total, kept)
    own, me = near.shape[1], lax.axis_index("gx")
    for slot in range(len(slots)):
        (near, far)[crossed[slot]][place[me, slot]] = total[slot * own : (slot + 1) * own].astype(near.dtype)


def project_out(groups, w_out, place, devices):
    counts, crossed = group_shape(groups)
    columns = w_out.shape[1]
    own, width = groups[0].blocks.shape[1:]
    chunks = devices // 2
    piece = jax.ShapeDtypeStruct((devices // 2, own, columns), jnp.bfloat16)
    return pl.pallas_call(
        functools.partial(out_kernel, counts, crossed),
        out_shape=[piece, piece],
        in_specs=[SMEM] + [VMEM] * (len(groups) + 1),
        out_specs=[VMEM, VMEM],
        scratch_shapes=[
            pltpu.VMEM((chunks, devices * own, width // chunks), jnp.bfloat16),
            pltpu.VMEM((devices * own, columns), jnp.float32),
        ],
        compiler_params=pltpu.CompilerParams(vmem_limit_bytes=VMEM_LIMIT),
        cost_estimate=pl.CostEstimate(
            flops=2 * devices * own * columns * width, bytes_accessed=2 * columns * width, transcendentals=0
        ),
    )(place, *[group.blocks for group in groups], w_out)


def attend_kernel(devices, kv_heads, tile, lengths, place, pieces, cache, _, out, fresh, queries, mixed):
    length, width = cache.shape[2:]
    extra = fresh.shape[2]
    half = tile // 2
    per_head = devices // kv_heads * half
    scale = 1.0 / math.sqrt(HD)
    for chip in range(devices // 2):
        for other in range(2):
            piece = pieces[chip, other * tile : (other + 1) * tile, :]
            queries[place[lax.axis_index("gx"), devices + 2 * chip + other]] = piece.astype(jnp.float32)
    line = lax.broadcasted_iota(jnp.int32, (8, 1), 0)
    first = jnp.where(line % 4 < 2, lengths[0], lengths[1])
    cosine, sine = turns((first + line % 2).astype(jnp.float32))
    terms = pieces[:, 2 * tile :, :].astype(jnp.float32)
    total = jnp.sum(terms, 0)
    total = total[: total.shape[0] // 2] + total[total.shape[0] // 2 :]
    twice = [jnp.concatenate([total[4 * at : 4 * at + 4]] * 2, 0) for at in range(2 * kv_heads)]
    new_keys = jnp.concatenate([turn(part, cosine, sine) for part in twice[:kv_heads]], 1)
    new_values = jnp.concatenate(twice[kv_heads:], 1)
    spot = lax.broadcasted_iota(jnp.int32, (extra, width), 0)
    for row in range(2):
        for which, new in enumerate((new_keys, new_values)):
            spread = jnp.where(spot == 0, new[2 * row : 2 * row + 1, :], 0.0)
            spread = jnp.where(spot == 1, new[2 * row + 1 : 2 * row + 2, :], spread)
            fresh[which, row] = spread.astype(fresh.dtype)
    every = queries[...]
    lines = kv_heads * per_head
    column = lax.broadcasted_iota(jnp.int32, (lines, length), 1)
    new_column = lax.broadcasted_iota(jnp.int32, (lines, extra), 1)
    step = lax.broadcasted_iota(jnp.int32, (lines, extra), 0) % 2
    across = (((1,), (1,)), ((), ()))
    for row in range(2):
        mine = every[:, row * half : row * half + half, :].reshape(lines, HD)
        spread = jnp.concatenate([mine] * kv_heads, 1)
        own_row = lax.broadcasted_iota(jnp.int32, spread.shape, 0) // per_head
        own_lane = lax.broadcasted_iota(jnp.int32, spread.shape, 1) // HD
        spread = jnp.where(own_row == own_lane, spread, 0.0).astype(jnp.bfloat16)
        scores = lax.dot_general(spread, cache[0, row], across, preferred_element_type=jnp.float32) * scale
        scores = jnp.where(column < lengths[row], scores, -jnp.inf)
        new_scores = lax.dot_general(spread, fresh[0, row], across, preferred_element_type=jnp.float32) * scale
        new_scores = jnp.where(new_column <= step, new_scores, -jnp.inf)
        peak = jnp.maximum(jnp.max(scores, 1, keepdims=True), jnp.max(new_scores, 1, keepdims=True))
        weight = jnp.exp(scores - peak)
        new_weight = jnp.exp(new_scores - peak)
        denominator = jnp.sum(weight, 1, keepdims=True) + jnp.sum(new_weight, 1, keepdims=True)
        result = jnp.dot(weight.astype(jnp.bfloat16), cache[1, row], preferred_element_type=jnp.float32)
        result += jnp.dot(new_weight.astype(jnp.bfloat16), fresh[1, row], preferred_element_type=jnp.float32)
        for head in range(kv_heads):
            rows = slice(head * per_head, (head + 1) * per_head)
            part = result[rows, head * HD : (head + 1) * HD] / denominator[rows]
            for query in range(per_head // 2):
                lanes = slice((head * per_head // 2 + query) * HD, (head * per_head // 2 + query + 1) * HD)
                for at in range(2):
                    mixed[at * 2 + row : at * 2 + row + 1, lanes] = part[2 * query + at : 2 * query + at + 1]
    out[...] = mixed[...].astype(out.dtype)


def attend(pieces, tile, cache, lengths, place, after, devices):
    length, width = cache.shape[2], cache.shape[3]
    columns = devices * tile // 4 * HD
    return pl.pallas_call(
        functools.partial(attend_kernel, devices, width // HD, tile),
        out_shape=jax.ShapeDtypeStruct((4, columns), jnp.bfloat16),
        in_specs=[SMEM, SMEM, VMEM, VMEM, pl.BlockSpec(memory_space=pl.ANY)],
        out_specs=VMEM,
        scratch_shapes=[
            pltpu.VMEM((2, 2, HD, width), cache.dtype),
            pltpu.VMEM((devices, tile, HD), jnp.float32),
            pltpu.VMEM((4, columns), jnp.float32),
        ],
        compiler_params=pltpu.CompilerParams(vmem_limit_bytes=VMEM_LIMIT),
        cost_estimate=pl.CostEstimate(
            flops=8 * 128 * length * width, bytes_accessed=8 * length * width, transcendentals=256 * length
        ),
    )(lengths, place, pieces, cache, after)


def finish_kernel(devices, place, pieces, out):
    columns = pieces.shape[3]
    steps, rows = out.shape[:2]
    for chip in range(devices // 2):
        for other in range(2):
            source = place[lax.axis_index("gx"), devices + 2 * chip + other]
            lanes = pl.ds(pl.multiple_of(source * columns, columns), columns)
            piece = pieces[chip, other].astype(jnp.float32)
            for step in range(steps):
                out[step, :, lanes] = piece[step * rows : (step + 1) * rows].astype(out.dtype)


def finish(pieces, place, steps, devices):
    own, columns = pieces.shape[2:]
    return pl.pallas_call(
        functools.partial(finish_kernel, devices),
        out_shape=jax.ShapeDtypeStruct((steps, own // steps, devices * columns), jnp.bfloat16),
        in_specs=[SMEM, VMEM],
        out_specs=VMEM,
        compiler_params=pltpu.CompilerParams(vmem_limit_bytes=VMEM_LIMIT),
    )(place, pieces)


def body(hidden, norm_gain, w_query, w_keyval, w_out, kv_cache, lengths):
    steps = hidden.shape[0]
    devices = lax.axis_size("gx")

    normed = norm(hidden, norm_gain, lengths)
    first = w_query.shape[0] * 3 // 4
    fetched = []

    def bring(ranges, after):
        *arrays, done = fetch(ranges, after)
        fetched.append(arrays)
        return done

    groups = gather(
        normed,
        devices,
        [
            functools.partial(bring, [(w_query, 0, first)]),
            functools.partial(bring, [(w_keyval, 0, 2), (kv_cache, 0, 2)]),
            functools.partial(bring, [(w_query, first, w_query.shape[0] - first)]),
        ],
    )
    (w_first,), (w_keyval, kv_cache), (w_second,) = fetched
    place = jnp.asarray(places(groups, devices))
    near, far, near_sum, far_sum = project(groups, [w_first, w_second], w_keyval, place, devices)
    pieces = pack(near, swap_cores(far, devices), near_sum, swap_cores(far_sum, devices))
    w_out, done = fetch([(w_out, 0, w_out.shape[0])], pieces)

    mixed = attend(exchange(pieces, devices), near.shape[1], kv_cache, lengths, place, done, devices)
    near, far = project_out(gather(mixed, devices), w_out, place, devices)
    pieces = jnp.stack([near, swap_cores(far, devices)], 1)
    return finish(exchange(pieces, devices), place, steps, devices)


def rotate(values, positions):
    row_total, head_count, head_width = values.shape
    half_width = head_width // 2
    frequency = ROPE_BASE ** (-2.0 * jnp.arange(half_width, dtype=jnp.float32) / head_width)
    angles = positions[:, None, None] * frequency[None, None, :]
    cosine = jnp.cos(angles)
    sine_part = jnp.sin(angles)
    paired = values.reshape(row_total, head_count, half_width, 2)
    first_half = paired[..., 0]
    second_half = paired[..., 1]
    turned = jnp.stack(
        [
            first_half * cosine - second_half * sine_part,
            first_half * sine_part + second_half * cosine,
        ],
        -1,
    )
    return turned.reshape(row_total, head_count, head_width)


def attend_split_heads(queries, cache_keys, cache_values, lengths, fresh_keys, fresh_values):
    score_scale = 1.0 / math.sqrt(HD)
    fresh_scores = (
        jnp.einsum("rkgd,rskd->rkgs", queries, fresh_keys, preferred_element_type=jnp.float32)
        * score_scale
    )
    cached = (
        jnp.einsum("rkgd,rlkd->rkgl", queries, cache_keys, preferred_element_type=jnp.float32)
        * score_scale
    )
    in_range = jnp.arange(cache_keys.shape[1])[None, :] < lengths[:, None]
    cached = jnp.where(in_range[:, None, None, :], cached, -jnp.inf)
    row_peak = jnp.maximum(cached.max(-1), fresh_scores.max(-1))
    cached_exp = jnp.exp(cached - row_peak[..., None])
    fresh_exp = jnp.exp(fresh_scores - row_peak[..., None])
    denominator = cached_exp.sum(-1) + fresh_exp.sum(-1)
    mixed = jnp.einsum(
        "rkgl,rlkd->rkgd",
        cached_exp.astype(jnp.bfloat16),
        cache_values,
        preferred_element_type=jnp.float32,
    )
    mixed = mixed + jnp.einsum(
        "rkgs,rskd->rkgd",
        fresh_exp.astype(jnp.bfloat16),
        fresh_values,
        preferred_element_type=jnp.float32,
    )
    return (mixed / denominator[..., None]).astype(jnp.bfloat16)


def body_split_heads(hidden, norm_gain, w_query, w_keyval, w_out, kv_cache, lengths):
    step_count, rows_dev, model_width = hidden.shape
    devices = lax.axis_size("gx")
    device_index = lax.axis_index("gx")
    row_slab = w_keyval.shape[1]
    kv_width = w_keyval.shape[2]
    query_cols = w_query.shape[1]
    heads_width = query_cols * devices
    head_count = heads_width // HD
    kv_heads = kv_width // HD
    kv_both = jnp.concatenate([w_keyval[0], w_keyval[1]], 1)
    cache_keys = kv_cache[0].reshape(rows_dev, kv_cache.shape[2], kv_heads, HD)
    cache_values = kv_cache[1].reshape(rows_dev, kv_cache.shape[2], kv_heads, HD)
    states = hidden.astype(jnp.float32)
    scaled = states * lax.rsqrt(jnp.mean(states * states, -1, keepdims=True) + EPSILON)
    normed = (scaled * norm_gain.astype(jnp.float32)).astype(jnp.bfloat16)
    new_keys = []
    new_values = []
    outputs = []
    for step_index in range(step_count):
        shard_piece = lax.all_gather(normed[step_index], "gx", axis=0, tiled=True)
        queries = jnp.dot(shard_piece, w_query, preferred_element_type=jnp.float32)
        own_slab = lax.dynamic_slice_in_dim(shard_piece, device_index * row_slab, row_slab, 1)
        partial_kv = jnp.dot(own_slab, kv_both, preferred_element_type=jnp.float32)
        joined = jnp.concatenate([queries, partial_kv], 1)
        project_query_rows = lax.all_to_all(
            joined[:, :query_cols], "gx", split_axis=0, concat_axis=1, tiled=True
        )
        project_keyval = lax.psum_scatter(
            joined[:, query_cols:], "gx", scatter_dimension=0, tiled=True
        )
        positions = (lengths + step_index).astype(jnp.float32)
        prepare_queries = rotate(
            project_query_rows.reshape(rows_dev, head_count, HD), positions
        ).astype(jnp.bfloat16)
        prepare_queries = prepare_queries.reshape(rows_dev, kv_heads, head_count // kv_heads, HD)
        key_new = rotate(
            project_keyval[:, :kv_width].reshape(rows_dev, kv_heads, HD), positions
        ).astype(jnp.bfloat16)
        value_new = (
            project_keyval[:, kv_width:].reshape(rows_dev, kv_heads, HD).astype(jnp.bfloat16)
        )
        queries, key_new, value_new = (prepare_queries, key_new, value_new)
        new_keys.append(key_new)
        new_values.append(value_new)
        mixed = attend_split_heads(
            queries,
            cache_keys,
            cache_values,
            lengths,
            jnp.stack(new_keys, 1),
            jnp.stack(new_values, 1),
        )
        out_cols = jnp.dot(
            lax.all_gather(mixed.reshape(rows_dev, heads_width), "gx", axis=0, tiled=True),
            w_out,
            preferred_element_type=jnp.float32,
        ).astype(jnp.bfloat16)
        outputs.append(lax.all_to_all(out_cols, "gx", split_axis=0, concat_axis=1, tiled=True))
    return jnp.stack(outputs)


def solution(mesh):
    devices = mesh.shape["gx"]

    def run(*arrays):
        whole_heads = arrays[2].shape[1] % HD == 0 and devices % 2 == 0
        return (body if whole_heads else body_split_heads)(*arrays)

    in_specs = (
        P(None, ("group", "gx"), None),
        P(),
        P(None, "gx"),
        P(None, "gx", None),
        P(None, "gx"),
        P(None, ("group", "gx"), None, None),
        P(("group", "gx")),
    )
    out_specs = P(None, ("group", "gx"), None)
    return jax.shard_map(run, mesh=mesh, in_specs=in_specs, out_specs=out_specs, check_vma=False)
```

```python
import functools
import math

import jax
import jax.numpy as jnp
import numpy as np
from jax import lax
from jax.experimental import pallas as pl
from jax.experimental.pallas import tpu as pltpu
from jax.sharding import PartitionSpec as P

HD = 128
ROPE_BASE = 500000.0
EPSILON = 1e-05
TAG = 128
VMEM_LIMIT = 8 * 1024 * 1024
VMEM = pl.BlockSpec(memory_space=pltpu.VMEM)
SMEM = pl.BlockSpec(memory_space=pltpu.SMEM)
HBM = pl.BlockSpec(memory_space=pltpu.HBM)


def permute(block, target):
    return lax.ppermute(block, "gx", [(int(i), int(t)) for i, t in enumerate(target)])


def moved(source, target):
    result = np.empty_like(source)
    result[target] = source
    return result


class Group:
    def __init__(self, blocks, sources, crossed=False):
        self.blocks, self.sources, self.crossed = blocks, sources, crossed

    def send(self, target, crossed=False):
        return Group(permute(self.blocks, target), [moved(source, target) for source in self.sources], crossed)


def join(groups):
    if len(groups) == 1:
        return groups[0]
    return Group(jnp.concatenate([g.blocks for g in groups], 0), [source for g in groups for source in g.sources])


def ring_order(size):
    if size > 4:
        return list(range(size))
    return list(range(0, size, 2)) + list(range(1, size, 2))[::-1]


def axes_of(devices):
    chips, inner = devices // 2, 1
    while inner * inner * 4 <= chips and chips % (inner * 2) == 0:
        inner *= 2
    sizes = (chips // inner, inner, 2)
    place = np.arange(devices).reshape(sizes)
    result = []
    for axis, size in enumerate(sizes):
        order = ring_order(size)
        after = np.empty(size, int)
        for here, there in zip(order, order[1:] + order[:1]):
            after[here] = there
        before = np.argsort(after)
        result.append((size, np.take(place, after, axis).ravel(), np.take(place, before, axis).ravel()))
    return result


def ring(group, axis):
    size, following, preceding = axis
    groups = []
    forward = backward = group
    for step in range(1, size // 2 + 1):
        forward = forward.send(following)
        groups.append(forward)
        if 2 * step < size:
            backward = backward.send(preceding)
            groups.append(backward)
    return groups


def gather(block, devices, meanwhile=()):
    (size, following, preceding), inner, core = axes_of(devices)
    own = Group(block[None], [np.arange(devices)])
    near = ring(own, inner)
    groups = [own] + near + [join([own] + near).send(core[1], crossed=True)]
    forward = backward = own
    for step in range(1, size // 2 + 1):
        before = forward.blocks
        arrived = [forward.send(following)] + ([backward.send(preceding)] if 2 * step < size else [])
        forward, backward = arrived[0], arrived[-1]
        if step <= len(meanwhile):
            onward = (step < size // 2) + (2 * step + 2 < size)
            chips, *alone = hold(arrived, onward, meanwhile[step - 1](before))
            forward, backward = (alone + [forward])[0], (alone + [backward])[-1]
        else:
            chips = join(arrived)
        reached = [chips] + ring(chips, inner)
        if step == size // 2 < len(meanwhile):
            reached[-1:] = hold(reached[-1:], 0, meanwhile[step](chips.blocks))
        groups += reached + [group.send(core[1], crossed=True) for group in reached]
    return groups


def hold_kernel(count, *refs):
    stacked, *alone = refs[count + 1 :]
    for at in range(count):
        stacked[at] = refs[at][0]
    for at in range(len(alone)):
        alone[at][...] = refs[at][...]


def hold(groups, onward, after):
    blocks = [group.blocks for group in groups]
    stacked, *alone = pl.pallas_call(
        functools.partial(hold_kernel, len(blocks)),
        out_shape=[jax.ShapeDtypeStruct((len(blocks), *blocks[0].shape[1:]), blocks[0].dtype)]
        + [jax.ShapeDtypeStruct(block.shape, block.dtype) for block in blocks[:onward]],
        in_specs=[VMEM] * len(blocks) + [pl.BlockSpec(memory_space=pl.ANY)],
        out_specs=[VMEM] * (onward + 1),
        compiler_params=pltpu.CompilerParams(vmem_limit_bytes=VMEM_LIMIT),
    )(*blocks, after)
    sources = [group.sources for group in groups]
    return [Group(stacked, sum(sources, []))] + [Group(block, source) for block, source in zip(alone, sources)]


def swap_cores(block, devices):
    return permute(block, np.arange(devices) ^ 1)


def exchange(pieces, devices):
    same_core = [list(range(core, devices, 2)) for core in range(2)]
    return lax.all_to_all(pieces, "gx", 0, 0, axis_index_groups=same_core, tiled=True)


def places(groups, devices):
    here = np.arange(devices)
    chips = [source // 2 for group in groups for source in group.sources]
    columns = [chip * 2 + (here % 2 ^ other) for chip in range(devices // 2) for other in range(2)]
    return np.stack(chips + columns, 1).astype(np.int32)


def norm_kernel(lengths_far, hidden_far, gain_far, out, lengths, hidden, gain, arrived):
    copies = [
        pltpu.make_async_copy(far, near, arrived.at[at])
        for at, (far, near) in enumerate(((hidden_far, hidden), (gain_far, gain), (lengths_far, lengths)))
    ]
    for copy in copies:
        copy.start()
    copies[0].wait()
    states = hidden[...].astype(jnp.float32)
    scale = lax.rsqrt(jnp.mean(states * states, -1, keepdims=True) + EPSILON)
    copies[1].wait()
    normed = states * scale * gain[...].astype(jnp.float32).reshape(1, 1, gain.shape[0])
    steps, rows, width = normed.shape
    lines = [normed[step, row : row + 1] for row in range(rows) for step in range(steps)]
    out[:, :width] = jnp.concatenate(lines, 0).astype(out.dtype)
    line = lax.broadcasted_iota(jnp.int32, (steps * rows, TAG), 0)
    lane = lax.broadcasted_iota(jnp.int32, (steps * rows, TAG), 1)
    position = line % steps
    copies[2].wait()
    for row in range(rows):
        position = jnp.where(line // steps == row, position + lengths[row], position)
    tag = jnp.where(lane == 0, position // 32, position % 32)
    out[:, width:] = tag.astype(jnp.float32).astype(out.dtype)


def norm(hidden, gain, lengths):
    steps, rows, width = hidden.shape
    return pl.pallas_call(
        norm_kernel,
        out_shape=jax.ShapeDtypeStruct((steps * rows, width + TAG), jnp.bfloat16),
        in_specs=[HBM] * 3,
        out_specs=VMEM,
        scratch_shapes=[
            pltpu.SMEM(lengths.shape, lengths.dtype),
            pltpu.VMEM(hidden.shape, hidden.dtype),
            pltpu.VMEM(gain.shape, gain.dtype),
            pltpu.SemaphoreType.DMA((3,)),
        ],
        compiler_params=pltpu.CompilerParams(vmem_limit_bytes=VMEM_LIMIT),
        cost_estimate=pl.CostEstimate(flops=6 * steps * rows * width, bytes_accessed=4 * steps * rows * width, transcendentals=0),
    )(*[pltpu.with_memory_space_constraint(array, pltpu.HBM) for array in (lengths, hidden, gain)])


def fetch_kernel(firsts, chunks, *refs):
    copies, count, arrived = [], len(firsts), refs[-1]
    refs[-2][...] = jnp.zeros_like(refs[-2])
    for first, far, near in zip(firsts, refs[:count], refs[count + 1 : 2 * count + 1]):
        size = near.shape[0] // min(chunks, near.shape[0])
        for at in range(0, near.shape[0], size):
            source = far.at[pl.ds(first + at, size)]
            copies.append(pltpu.make_async_copy(source, near.at[pl.ds(at, size)], arrived.at[len(copies)]))
            copies[-1].start()
    for copy in copies:
        copy.wait()


def fetch(ranges, after):
    chunks = 8
    arrays = [array for array, _, _ in ranges]
    shapes = [(count, *array.shape[1:]) for array, _, count in ranges]
    return pl.pallas_call(
        functools.partial(fetch_kernel, [first for _, first, _ in ranges], chunks),
        out_shape=[pltpu.VMEM(shape, array.dtype) for shape, array in zip(shapes, arrays)]
        + [jax.ShapeDtypeStruct((8, HD), jnp.float32)],
        in_specs=[HBM] * len(arrays) + [pl.BlockSpec(memory_space=pl.ANY)],
        out_specs=[VMEM] * (len(arrays) + 1),
        scratch_shapes=[pltpu.SemaphoreType.DMA((chunks * len(arrays),))],
        compiler_params=pltpu.CompilerParams(vmem_limit_bytes=VMEM_LIMIT),
        cost_estimate=pl.CostEstimate(
            flops=0, bytes_accessed=sum(2 * math.prod(shape) for shape in shapes), transcendentals=0
        ),
    )(*[pltpu.with_memory_space_constraint(array, pltpu.HBM) for array in arrays], after)


def slots_of(refs, counts):
    return [(ref, at) for ref, count in zip(refs, counts) for at in range(count)]


def assemble(slots, first, width):
    lanes = slice(first, first + width)
    return jnp.concatenate([ref[at, :, lanes].astype(jnp.float32) for ref, at in slots], 0).astype(jnp.bfloat16)


def multiply(slots, weights, depth, total, kept):
    total[...] = jnp.zeros_like(total)
    chunk = 0
    for part in weights:
        for at in range(0, part.shape[0], depth):
            kept[chunk] = assemble(slots, chunk * depth, depth)
            total[...] += jnp.dot(kept[chunk], part[at : at + depth, :], preferred_element_type=jnp.float32)
            chunk += 1


def turns(positions):
    shape = (positions.shape[0], HD)
    lane = lax.broadcasted_iota(jnp.int32, shape, 1)
    pair = (lane // 2).astype(jnp.float32)
    angles = positions * jnp.exp(pair * (-2.0 * math.log(ROPE_BASE) / HD))
    return jnp.cos(angles), jnp.where(lane % 2 == 0, -1.0, 1.0) * jnp.sin(angles)


def turn(values, cosine, sine):
    lanes = values.shape[-1]
    even = lax.broadcasted_iota(jnp.int32, values.shape, 1) % 2 == 0
    swapped = jnp.where(even, pltpu.roll(values, lanes - 1, 1), pltpu.roll(values, 1, 1))
    return values * cosine + swapped * sine


def project_kernel(counts, crossed, width, place, *refs):
    slots = slots_of(refs, counts)
    first, second, keyval, *outs = refs[len(counts) : len(counts) + 7]
    kept, total, packed = refs[len(counts) + 7 :]
    queries, fresh = outs[:2], outs[2:]
    depth = keyval.shape[1]
    tags = jnp.concatenate([ref[at, :, width:].astype(jnp.float32) for ref, at in slots], 0)
    cosine, sine = turns(tags[:, 0:1] * 32.0 + tags[:, 1:2])
    multiply(slots, [first, second], depth, total, kept)
    me = lax.axis_index("gx")
    own = kept[me]
    blocks = keyval.shape[2] // HD
    for which in range(2):
        term = jnp.dot(own, keyval[which], preferred_element_type=jnp.float32)
        for slot in range(len(slots)):
            for at in range(blocks):
                row = (which * blocks + at) * 4
                fresh[crossed[slot]][place[me, slot], row : row + 4, :] = term[
                    slot * 4 : slot * 4 + 4, at * HD : (at + 1) * HD
                ]
    heads = total.shape[1] // HD
    for head in range(heads):
        turned = turn(total[:, head * HD : (head + 1) * HD], cosine, sine)
        for slot in range(len(slots)):
            for row in range(2):
                line, at = row * 2 * heads + head * 2, slot * 4 + row * 2
                packed[slot, line : line + 2, :] = turned[at : at + 2, :]
    for slot in range(len(slots)):
        queries[crossed[slot]][place[me, slot]] = packed[slot].astype(jnp.bfloat16)


def group_shape(groups):
    counts = [len(group.sources) for group in groups]
    return counts, [int(group.crossed) for group, count in zip(groups, counts) for _ in range(count)]


def project(groups, w_query, w_keyval, place, devices):
    counts, crossed = group_shape(groups)
    columns = w_query[0].shape[1]
    depth, kv_width = w_keyval.shape[1:]
    own, width = groups[0].blocks.shape[1], devices * depth
    rows, tile = devices * own, own * (columns // HD)
    query = jax.ShapeDtypeStruct((devices // 2, tile, HD), jnp.bfloat16)
    fresh = jax.ShapeDtypeStruct((devices // 2, own * 2 * kv_width // HD, HD), jnp.float32)
    return pl.pallas_call(
        functools.partial(project_kernel, counts, crossed, width),
        out_shape=[query, query, fresh, fresh],
        in_specs=[SMEM] + [VMEM] * (len(groups) + 3),
        out_specs=[VMEM] * 4,
        scratch_shapes=[
            pltpu.VMEM((devices, rows, depth), jnp.bfloat16),
            pltpu.VMEM((rows, columns), jnp.float32),
            pltpu.VMEM((devices, tile, HD), jnp.float32),
        ],
        compiler_params=pltpu.CompilerParams(vmem_limit_bytes=VMEM_LIMIT),
        cost_estimate=pl.CostEstimate(
            flops=2 * rows * columns * width, bytes_accessed=2 * columns * width, transcendentals=2 * rows * HD
        ),
    )(place, *[group.blocks for group in groups], *w_query, w_keyval)


def pack_kernel(near, far, near_sum, far_sum, out):
    tile, lines = near.shape[1], near_sum.shape[1]
    out[:, :tile, :] = near[...]
    out[:, tile : 2 * tile, :] = far[...]
    total = near_sum[...] + far_sum[...]
    high = total.astype(jnp.bfloat16)
    out[:, 2 * tile : 2 * tile + lines, :] = high
    out[:, 2 * tile + lines :, :] = (total - high.astype(jnp.float32)).astype(jnp.bfloat16)


def pack(near, far, near_sum, far_sum):
    chips, tile, _ = near.shape
    return pl.pallas_call(
        pack_kernel,
        out_shape=jax.ShapeDtypeStruct((chips, 2 * tile + 2 * near_sum.shape[1], HD), jnp.bfloat16),
        in_specs=[VMEM] * 4,
        out_specs=VMEM,
        compiler_params=pltpu.CompilerParams(vmem_limit_bytes=VMEM_LIMIT),
    )(near, far, near_sum, far_sum)


def out_kernel(counts, crossed, place, *refs):
    slots = slots_of(refs, counts)
    *weights, near, far, kept, total = refs[len(counts) :]
    multiply(slots, weights, kept.shape[2], total, kept)
    own, me = near.shape[1], lax.axis_index("gx")
    for slot in range(len(slots)):
        (near, far)[crossed[slot]][place[me, slot]] = total[slot * own : (slot + 1) * own].astype(near.dtype)


def project_out(groups, w_out, place, devices):
    counts, crossed = group_shape(groups)
    columns = w_out[0].shape[1]
    own, width = groups[0].blocks.shape[1:]
    chunks = devices // 2
    piece = jax.ShapeDtypeStruct((devices // 2, own, columns), jnp.bfloat16)
    return pl.pallas_call(
        functools.partial(out_kernel, counts, crossed),
        out_shape=[piece, piece],
        in_specs=[SMEM] + [VMEM] * (len(groups) + len(w_out)),
        out_specs=[VMEM, VMEM],
        scratch_shapes=[
            pltpu.VMEM((chunks, devices * own, width // chunks), jnp.bfloat16),
            pltpu.VMEM((devices * own, columns), jnp.float32),
        ],
        compiler_params=pltpu.CompilerParams(vmem_limit_bytes=VMEM_LIMIT),
        cost_estimate=pl.CostEstimate(
            flops=2 * devices * own * columns * width, bytes_accessed=2 * columns * width, transcendentals=0
        ),
    )(place, *[group.blocks for group in groups], *w_out)


def attend_kernel(devices, kv_heads, tile, lengths, place, pieces, cache, out, fresh, queries, mixed):
    length, width = cache.shape[2:]
    extra = fresh.shape[2]
    half = tile // 2
    per_head = devices // kv_heads * half
    scale = 1.0 / math.sqrt(HD)
    for chip in range(devices // 2):
        for other in range(2):
            piece = pieces[chip, other * tile : (other + 1) * tile, :]
            queries[place[lax.axis_index("gx"), devices + 2 * chip + other]] = piece.astype(jnp.float32)
    line = lax.broadcasted_iota(jnp.int32, (8, 1), 0)
    first = jnp.where(line % 4 < 2, lengths[0], lengths[1])
    cosine, sine = turns((first + line % 2).astype(jnp.float32))
    terms = pieces[:, 2 * tile :, :].astype(jnp.float32)
    total = jnp.sum(terms, 0)
    total = total[: total.shape[0] // 2] + total[total.shape[0] // 2 :]
    twice = [jnp.concatenate([total[4 * at : 4 * at + 4]] * 2, 0) for at in range(2 * kv_heads)]
    new_keys = jnp.concatenate([turn(part, cosine, sine) for part in twice[:kv_heads]], 1)
    new_values = jnp.concatenate(twice[kv_heads:], 1)
    spot = lax.broadcasted_iota(jnp.int32, (extra, width), 0)
    for row in range(2):
        for which, new in enumerate((new_keys, new_values)):
            spread = jnp.where(spot == 0, new[2 * row : 2 * row + 1, :], 0.0)
            spread = jnp.where(spot == 1, new[2 * row + 1 : 2 * row + 2, :], spread)
            fresh[which, row] = spread.astype(fresh.dtype)
    every = queries[...]
    lines = kv_heads * per_head
    column = lax.broadcasted_iota(jnp.int32, (lines, length), 1)
    new_column = lax.broadcasted_iota(jnp.int32, (lines, extra), 1)
    step = lax.broadcasted_iota(jnp.int32, (lines, extra), 0) % 2
    across = (((1,), (1,)), ((), ()))
    for row in range(2):
        mine = every[:, row * half : row * half + half, :].reshape(lines, HD)
        spread = jnp.concatenate([mine] * kv_heads, 1)
        own_row = lax.broadcasted_iota(jnp.int32, spread.shape, 0) // per_head
        own_lane = lax.broadcasted_iota(jnp.int32, spread.shape, 1) // HD
        spread = jnp.where(own_row == own_lane, spread, 0.0).astype(jnp.bfloat16)
        scores = lax.dot_general(spread, cache[0, row], across, preferred_element_type=jnp.float32) * scale
        scores = jnp.where(column < lengths[row], scores, -jnp.inf)
        new_scores = lax.dot_general(spread, fresh[0, row], across, preferred_element_type=jnp.float32) * scale
        new_scores = jnp.where(new_column <= step, new_scores, -jnp.inf)
        peak = jnp.maximum(jnp.max(scores, 1, keepdims=True), jnp.max(new_scores, 1, keepdims=True))
        weight = jnp.exp(scores - peak)
        new_weight = jnp.exp(new_scores - peak)
        denominator = jnp.sum(weight, 1, keepdims=True) + jnp.sum(new_weight, 1, keepdims=True)
        result = jnp.dot(weight.astype(jnp.bfloat16), cache[1, row], preferred_element_type=jnp.float32)
        result += jnp.dot(new_weight.astype(jnp.bfloat16), fresh[1, row], preferred_element_type=jnp.float32)
        for head in range(kv_heads):
            rows = slice(head * per_head, (head + 1) * per_head)
            part = result[rows, head * HD : (head + 1) * HD] / denominator[rows]
            for query in range(per_head // 2):
                lanes = slice((head * per_head // 2 + query) * HD, (head * per_head // 2 + query + 1) * HD)
                for at in range(2):
                    mixed[at * 2 + row : at * 2 + row + 1, lanes] = part[2 * query + at : 2 * query + at + 1]
    out[...] = mixed[...].astype(out.dtype)


def attend(pieces, tile, cache, lengths, place, devices):
    length, width = cache.shape[2], cache.shape[3]
    columns = devices * tile // 4 * HD
    return pl.pallas_call(
        functools.partial(attend_kernel, devices, width // HD, tile),
        out_shape=jax.ShapeDtypeStruct((4, columns), jnp.bfloat16),
        in_specs=[SMEM, SMEM, VMEM, VMEM],
        out_specs=VMEM,
        scratch_shapes=[
            pltpu.VMEM((2, 2, HD, width), cache.dtype),
            pltpu.VMEM((devices, tile, HD), jnp.float32),
            pltpu.VMEM((4, columns), jnp.float32),
        ],
        compiler_params=pltpu.CompilerParams(vmem_limit_bytes=VMEM_LIMIT),
        cost_estimate=pl.CostEstimate(
            flops=8 * 128 * length * width, bytes_accessed=8 * length * width, transcendentals=256 * length
        ),
    )(lengths, place, pieces, cache)


def finish_kernel(devices, place, pieces, out):
    columns = pieces.shape[3]
    steps, rows = out.shape[:2]
    for chip in range(devices // 2):
        for other in range(2):
            source = place[lax.axis_index("gx"), devices + 2 * chip + other]
            lanes = pl.ds(pl.multiple_of(source * columns, columns), columns)
            piece = pieces[chip, other].astype(jnp.float32)
            for step in range(steps):
                out[step, :, lanes] = piece[step * rows : (step + 1) * rows].astype(out.dtype)


def finish(pieces, place, steps, devices):
    own, columns = pieces.shape[2:]
    return pl.pallas_call(
        functools.partial(finish_kernel, devices),
        out_shape=jax.ShapeDtypeStruct((steps, own // steps, devices * columns), jnp.bfloat16),
        in_specs=[SMEM, VMEM],
        out_specs=VMEM,
        compiler_params=pltpu.CompilerParams(vmem_limit_bytes=VMEM_LIMIT),
    )(place, pieces)


def body(hidden, norm_gain, w_query, w_keyval, w_out, kv_cache, lengths):
    steps = hidden.shape[0]
    devices = lax.axis_size("gx")

    normed = norm(hidden, norm_gain, lengths)
    cut = w_query.shape[0] * 3 // 4
    fetched = []

    def bring(*ranges):
        def start(after):
            *arrays, done = fetch(ranges, after)
            fetched.extend(arrays)
            return done

        return start

    waits = [bring((w_query, 0, cut)), bring((w_keyval, 0, 2), (kv_cache, 0, 2)), bring((w_query, cut, w_query.shape[0] - cut))]
    groups = gather(normed, devices, waits)
    w_first, w_keyval, kv_cache, w_second = fetched
    place = jnp.asarray(places(groups, devices))
    near, far, near_sum, far_sum = project(groups, [w_first, w_second], w_keyval, place, devices)
    pieces = pack(near, swap_cores(far, devices), near_sum, swap_cores(far_sum, devices))

    mixed = attend(exchange(pieces, devices), near.shape[1], kv_cache, lengths, place, devices)
    fetched = []
    part = w_out.shape[0] // 8
    waits = [bring((w_out, first * part, count * part)) for first, count in ((0, 3), (3, 3), (6, 2))]
    groups = gather(mixed, devices, waits)
    near, far = project_out(groups, fetched, place, devices)
    pieces = jnp.stack([near, swap_cores(far, devices)], 1)
    return finish(exchange(pieces, devices), place, steps, devices)


def rotate(values, positions):
    row_total, head_count, head_width = values.shape
    half_width = head_width // 2
    frequency = ROPE_BASE ** (-2.0 * jnp.arange(half_width, dtype=jnp.float32) / head_width)
    angles = positions[:, None, None] * frequency[None, None, :]
    cosine = jnp.cos(angles)
    sine_part = jnp.sin(angles)
    paired = values.reshape(row_total, head_count, half_width, 2)
    first_half = paired[..., 0]
    second_half = paired[..., 1]
    turned = jnp.stack(
        [
            first_half * cosine - second_half * sine_part,
            first_half * sine_part + second_half * cosine,
        ],
        -1,
    )
    return turned.reshape(row_total, head_count, head_width)


def attend_split_heads(queries, cache_keys, cache_values, lengths, fresh_keys, fresh_values):
    score_scale = 1.0 / math.sqrt(HD)
    fresh_scores = (
        jnp.einsum("rkgd,rskd->rkgs", queries, fresh_keys, preferred_element_type=jnp.float32)
        * score_scale
    )
    cached = (
        jnp.einsum("rkgd,rlkd->rkgl", queries, cache_keys, preferred_element_type=jnp.float32)
        * score_scale
    )
    in_range = jnp.arange(cache_keys.shape[1])[None, :] < lengths[:, None]
    cached = jnp.where(in_range[:, None, None, :], cached, -jnp.inf)
    row_peak = jnp.maximum(cached.max(-1), fresh_scores.max(-1))
    cached_exp = jnp.exp(cached - row_peak[..., None])
    fresh_exp = jnp.exp(fresh_scores - row_peak[..., None])
    denominator = cached_exp.sum(-1) + fresh_exp.sum(-1)
    mixed = jnp.einsum(
        "rkgl,rlkd->rkgd",
        cached_exp.astype(jnp.bfloat16),
        cache_values,
        preferred_element_type=jnp.float32,
    )
    mixed = mixed + jnp.einsum(
        "rkgs,rskd->rkgd",
        fresh_exp.astype(jnp.bfloat16),
        fresh_values,
        preferred_element_type=jnp.float32,
    )
    return (mixed / denominator[..., None]).astype(jnp.bfloat16)


def body_split_heads(hidden, norm_gain, w_query, w_keyval, w_out, kv_cache, lengths):
    step_count, rows_dev, model_width = hidden.shape
    devices = lax.axis_size("gx")
    device_index = lax.axis_index("gx")
    row_slab = w_keyval.shape[1]
    kv_width = w_keyval.shape[2]
    query_cols = w_query.shape[1]
    heads_width = query_cols * devices
    head_count = heads_width // HD
    kv_heads = kv_width // HD
    kv_both = jnp.concatenate([w_keyval[0], w_keyval[1]], 1)
    cache_keys = kv_cache[0].reshape(rows_dev, kv_cache.shape[2], kv_heads, HD)
    cache_values = kv_cache[1].reshape(rows_dev, kv_cache.shape[2], kv_heads, HD)
    states = hidden.astype(jnp.float32)
    scaled = states * lax.rsqrt(jnp.mean(states * states, -1, keepdims=True) + EPSILON)
    normed = (scaled * norm_gain.astype(jnp.float32)).astype(jnp.bfloat16)
    new_keys = []
    new_values = []
    outputs = []
    for step_index in range(step_count):
        shard_piece = lax.all_gather(normed[step_index], "gx", axis=0, tiled=True)
        queries = jnp.dot(shard_piece, w_query, preferred_element_type=jnp.float32)
        own_slab = lax.dynamic_slice_in_dim(shard_piece, device_index * row_slab, row_slab, 1)
        partial_kv = jnp.dot(own_slab, kv_both, preferred_element_type=jnp.float32)
        joined = jnp.concatenate([queries, partial_kv], 1)
        project_query_rows = lax.all_to_all(
            joined[:, :query_cols], "gx", split_axis=0, concat_axis=1, tiled=True
        )
        project_keyval = lax.psum_scatter(
            joined[:, query_cols:], "gx", scatter_dimension=0, tiled=True
        )
        positions = (lengths + step_index).astype(jnp.float32)
        prepare_queries = rotate(
            project_query_rows.reshape(rows_dev, head_count, HD), positions
        ).astype(jnp.bfloat16)
        prepare_queries = prepare_queries.reshape(rows_dev, kv_heads, head_count // kv_heads, HD)
        key_new = rotate(
            project_keyval[:, :kv_width].reshape(rows_dev, kv_heads, HD), positions
        ).astype(jnp.bfloat16)
        value_new = (
            project_keyval[:, kv_width:].reshape(rows_dev, kv_heads, HD).astype(jnp.bfloat16)
        )
        queries, key_new, value_new = (prepare_queries, key_new, value_new)
        new_keys.append(key_new)
        new_values.append(value_new)
        mixed = attend_split_heads(
            queries,
            cache_keys,
            cache_values,
            lengths,
            jnp.stack(new_keys, 1),
            jnp.stack(new_values, 1),
        )
        out_cols = jnp.dot(
            lax.all_gather(mixed.reshape(rows_dev, heads_width), "gx", axis=0, tiled=True),
            w_out,
            preferred_element_type=jnp.float32,
        ).astype(jnp.bfloat16)
        outputs.append(lax.all_to_all(out_cols, "gx", split_axis=0, concat_axis=1, tiled=True))
    return jnp.stack(outputs)


def solution(mesh):
    devices = mesh.shape["gx"]

    def run(*arrays):
        whole_heads = arrays[2].shape[1] % HD == 0 and devices % 2 == 0
        return (body if whole_heads else body_split_heads)(*arrays)

    in_specs = (
        P(None, ("group", "gx"), None),
        P(),
        P(None, "gx"),
        P(None, "gx", None),
        P(None, "gx"),
        P(None, ("group", "gx"), None, None),
        P(("group", "gx")),
    )
    out_specs = P(None, ("group", "gx"), None)
    return jax.shard_map(run, mesh=mesh, in_specs=in_specs, out_specs=out_specs, check_vma=False)
```

```python
import functools
import math

import jax
import jax.numpy as jnp
import numpy as np
from jax import lax
from jax.experimental import pallas as pl
from jax.experimental.pallas import tpu as pltpu
from jax.sharding import PartitionSpec as P

HD = 128
ROPE_BASE = 500000.0
EPSILON = 1e-05
TAG = 128
VMEM_LIMIT = 8 * 1024 * 1024
VMEM = pl.BlockSpec(memory_space=pltpu.VMEM)
SMEM = pl.BlockSpec(memory_space=pltpu.SMEM)
HBM = pl.BlockSpec(memory_space=pltpu.HBM)


def permute(block, target):
    return lax.ppermute(block, "gx", [(int(i), int(t)) for i, t in enumerate(target)])


def moved(source, target):
    result = np.empty_like(source)
    result[target] = source
    return result


class Group:
    def __init__(self, blocks, sources, crossed=False):
        self.blocks, self.sources, self.crossed = blocks, sources, crossed

    def send(self, target, crossed=False):
        return Group(permute(self.blocks, target), [moved(source, target) for source in self.sources], crossed)


def join(groups):
    if len(groups) == 1:
        return groups[0]
    return Group(jnp.concatenate([g.blocks for g in groups], 0), [source for g in groups for source in g.sources])


def ring_order(size):
    if size > 4:
        return list(range(size))
    return list(range(0, size, 2)) + list(range(1, size, 2))[::-1]


def axes_of(devices):
    chips, inner = devices // 2, 1
    while inner * inner * 4 <= chips and chips % (inner * 2) == 0:
        inner *= 2
    sizes = (chips // inner, inner, 2)
    place = np.arange(devices).reshape(sizes)
    result = []
    for axis, size in enumerate(sizes):
        order = ring_order(size)
        after = np.empty(size, int)
        for here, there in zip(order, order[1:] + order[:1]):
            after[here] = there
        before = np.argsort(after)
        result.append((size, np.take(place, after, axis).ravel(), np.take(place, before, axis).ravel()))
    return result


def ring(group, axis):
    size, following, preceding = axis
    groups = []
    forward = backward = group
    for step in range(1, size // 2 + 1):
        forward = forward.send(following)
        groups.append(forward)
        if 2 * step < size:
            backward = backward.send(preceding)
            groups.append(backward)
    return groups


def gather(block, devices, meanwhile=()):
    (size, following, preceding), inner, core = axes_of(devices)
    own = Group(block[None], [np.arange(devices)])
    near = ring(own, inner)
    groups = [own] + near + [join([own] + near).send(core[1], crossed=True)]
    forward = backward = own
    for step in range(1, size // 2 + 1):
        before = forward.blocks
        arrived = [forward.send(following)] + ([backward.send(preceding)] if 2 * step < size else [])
        forward, backward = arrived[0], arrived[-1]
        if step <= len(meanwhile):
            onward = (step < size // 2) + (2 * step + 2 < size)
            chips, *alone = hold(arrived, onward, meanwhile[step - 1](before))
            forward, backward = (alone + [forward])[0], (alone + [backward])[-1]
        else:
            chips = join(arrived)
        reached = [chips] + ring(chips, inner)
        if step == size // 2 < len(meanwhile):
            reached[-1:] = hold(reached[-1:], 0, meanwhile[step](chips.blocks))
        groups += reached + [group.send(core[1], crossed=True) for group in reached]
    return groups


def hold_kernel(count, *refs):
    stacked, *alone = refs[count + 1 :]
    for at in range(count):
        stacked[at] = refs[at][0]
    for at in range(len(alone)):
        alone[at][...] = refs[at][...]


def hold(groups, onward, after):
    blocks = [group.blocks for group in groups]
    stacked, *alone = pl.pallas_call(
        functools.partial(hold_kernel, len(blocks)),
        out_shape=[jax.ShapeDtypeStruct((len(blocks), *blocks[0].shape[1:]), blocks[0].dtype)]
        + [jax.ShapeDtypeStruct(block.shape, block.dtype) for block in blocks[:onward]],
        in_specs=[VMEM] * len(blocks) + [pl.BlockSpec(memory_space=pl.ANY)],
        out_specs=[VMEM] * (onward + 1),
        compiler_params=pltpu.CompilerParams(vmem_limit_bytes=VMEM_LIMIT),
    )(*blocks, after)
    sources = [group.sources for group in groups]
    return [Group(stacked, sum(sources, []))] + [Group(block, source) for block, source in zip(alone, sources)]


def swap_cores(block, devices):
    return permute(block, np.arange(devices) ^ 1)


def origins(groups):
    return [source for group in groups if not group.crossed for source in group.sources]


def give_back(pieces, groups):
    return [pieces[0]] + [permute(piece, origin) for piece, origin in zip(pieces[1:], origins(groups)[1:])]


def places(groups, devices):
    here = np.arange(devices)
    senders = [moved(here, origin) for origin in origins(groups)]
    return np.stack([sender ^ other for sender in senders for other in range(2)], 1).astype(np.int32)


def norm_kernel(lengths_far, hidden_far, gain_far, out, lengths, hidden, gain, arrived):
    copies = [
        pltpu.make_async_copy(far, near, arrived.at[at])
        for at, (far, near) in enumerate(((hidden_far, hidden), (gain_far, gain), (lengths_far, lengths)))
    ]
    for copy in copies:
        copy.start()
    copies[0].wait()
    states = hidden[...].astype(jnp.float32)
    scale = lax.rsqrt(jnp.mean(states * states, -1, keepdims=True) + EPSILON)
    copies[1].wait()
    normed = states * scale * gain[...].astype(jnp.float32).reshape(1, 1, gain.shape[0])
    steps, rows, width = normed.shape
    lines = [normed[step, row : row + 1] for row in range(rows) for step in range(steps)]
    out[:, :width] = jnp.concatenate(lines, 0).astype(out.dtype)
    line = lax.broadcasted_iota(jnp.int32, (steps * rows, TAG), 0)
    lane = lax.broadcasted_iota(jnp.int32, (steps * rows, TAG), 1)
    position = line % steps
    copies[2].wait()
    for row in range(rows):
        position = jnp.where(line // steps == row, position + lengths[row], position)
    tag = jnp.where(lane == 0, position // 32, position % 32)
    out[:, width:] = tag.astype(jnp.float32).astype(out.dtype)


def norm(hidden, gain, lengths):
    steps, rows, width = hidden.shape
    return pl.pallas_call(
        norm_kernel,
        out_shape=jax.ShapeDtypeStruct((steps * rows, width + TAG), jnp.bfloat16),
        in_specs=[HBM] * 3,
        out_specs=VMEM,
        scratch_shapes=[
            pltpu.SMEM(lengths.shape, lengths.dtype),
            pltpu.VMEM(hidden.shape, hidden.dtype),
            pltpu.VMEM(gain.shape, gain.dtype),
            pltpu.SemaphoreType.DMA((3,)),
        ],
        compiler_params=pltpu.CompilerParams(vmem_limit_bytes=VMEM_LIMIT),
        cost_estimate=pl.CostEstimate(flops=6 * steps * rows * width, bytes_accessed=4 * steps * rows * width, transcendentals=0),
    )(*[pltpu.with_memory_space_constraint(array, pltpu.HBM) for array in (lengths, hidden, gain)])


def fetch_kernel(firsts, chunks, *refs):
    copies, count, arrived = [], len(firsts), refs[-1]
    refs[-2][...] = jnp.zeros_like(refs[-2])
    for first, far, near in zip(firsts, refs[:count], refs[count + 1 : 2 * count + 1]):
        size = near.shape[0] // min(chunks, near.shape[0])
        for at in range(0, near.shape[0], size):
            source = far.at[pl.ds(first + at, size)]
            copies.append(pltpu.make_async_copy(source, near.at[pl.ds(at, size)], arrived.at[len(copies)]))
            copies[-1].start()
    for copy in copies:
        copy.wait()


def fetch(ranges, after):
    chunks = 8
    arrays = [array for array, _, _ in ranges]
    shapes = [(count, *array.shape[1:]) for array, _, count in ranges]
    return pl.pallas_call(
        functools.partial(fetch_kernel, [first for _, first, _ in ranges], chunks),
        out_shape=[pltpu.VMEM(shape, array.dtype) for shape, array in zip(shapes, arrays)]
        + [jax.ShapeDtypeStruct((8, HD), jnp.float32)],
        in_specs=[HBM] * len(arrays) + [pl.BlockSpec(memory_space=pl.ANY)],
        out_specs=[VMEM] * (len(arrays) + 1),
        scratch_shapes=[pltpu.SemaphoreType.DMA((chunks * len(arrays),))],
        compiler_params=pltpu.CompilerParams(vmem_limit_bytes=VMEM_LIMIT),
        cost_estimate=pl.CostEstimate(
            flops=0, bytes_accessed=sum(2 * math.prod(shape) for shape in shapes), transcendentals=0
        ),
    )(*[pltpu.with_memory_space_constraint(array, pltpu.HBM) for array in arrays], after)


def slots_of(refs, counts):
    return [(ref, at) for ref, count in zip(refs, counts) for at in range(count)]


def assemble(slots, first, width):
    lanes = slice(first, first + width)
    return jnp.concatenate([ref[at, :, lanes].astype(jnp.float32) for ref, at in slots], 0).astype(jnp.bfloat16)


def multiply(slots, weights, depth, total, kept):
    total[...] = jnp.zeros_like(total)
    chunk = 0
    for part in weights:
        for at in range(0, part.shape[0], depth):
            kept[chunk] = assemble(slots, chunk * depth, depth)
            total[...] += jnp.dot(kept[chunk], part[at : at + depth, :], preferred_element_type=jnp.float32)
            chunk += 1


def turns(positions):
    shape = (positions.shape[0], HD)
    lane = lax.broadcasted_iota(jnp.int32, shape, 1)
    pair = (lane // 2).astype(jnp.float32)
    angles = positions * jnp.exp(pair * (-2.0 * math.log(ROPE_BASE) / HD))
    return jnp.cos(angles), jnp.where(lane % 2 == 0, -1.0, 1.0) * jnp.sin(angles)


def turn(values, cosine, sine):
    lanes = values.shape[-1]
    even = lax.broadcasted_iota(jnp.int32, values.shape, 1) % 2 == 0
    swapped = jnp.where(even, pltpu.roll(values, lanes - 1, 1), pltpu.roll(values, 1, 1))
    return values * cosine + swapped * sine


def project_kernel(counts, crossed, width, *refs):
    slots = slots_of(refs, counts)
    first, second, keyval, *outs = refs[len(counts) : len(counts) + 7]
    kept, total, packed = refs[len(counts) + 7 :]
    queries, fresh = outs[:2], outs[2:]
    depth = keyval.shape[1]
    tags = jnp.concatenate([ref[at, :, width:].astype(jnp.float32) for ref, at in slots], 0)
    cosine, sine = turns(tags[:, 0:1] * 32.0 + tags[:, 1:2])
    multiply(slots, [first, second], depth, total, kept)
    own = kept[lax.axis_index("gx")]
    blocks = keyval.shape[2] // HD
    for which in range(2):
        term = jnp.dot(own, keyval[which], preferred_element_type=jnp.float32)
        for slot in range(len(slots)):
            for at in range(blocks):
                row = (which * blocks + at) * 4
                fresh[crossed[slot][0]][crossed[slot][1], row : row + 4, :] = term[
                    slot * 4 : slot * 4 + 4, at * HD : (at + 1) * HD
                ]
    heads = total.shape[1] // HD
    for head in range(heads):
        turned = turn(total[:, head * HD : (head + 1) * HD], cosine, sine)
        for slot in range(len(slots)):
            for row in range(2):
                line, at = row * 2 * heads + head * 2, slot * 4 + row * 2
                packed[slot, line : line + 2, :] = turned[at : at + 2, :]
    for slot in range(len(slots)):
        queries[crossed[slot][0]][crossed[slot][1]] = packed[slot].astype(jnp.bfloat16)


def group_shape(groups):
    counts = [len(group.sources) for group in groups]
    seen, order = [0, 0], []
    for group, count in zip(groups, counts):
        for _ in range(count):
            order.append((int(group.crossed), seen[group.crossed]))
            seen[group.crossed] += 1
    return counts, order


def project(groups, w_query, w_keyval, devices):
    counts, crossed = group_shape(groups)
    columns = w_query[0].shape[1]
    depth, kv_width = w_keyval.shape[1:]
    own, width = groups[0].blocks.shape[1], devices * depth
    rows, tile = devices * own, own * (columns // HD)
    query = jax.ShapeDtypeStruct((devices // 2, tile, HD), jnp.bfloat16)
    fresh = jax.ShapeDtypeStruct((devices // 2, own * 2 * kv_width // HD, HD), jnp.float32)
    return pl.pallas_call(
        functools.partial(project_kernel, counts, crossed, width),
        out_shape=[query, query, fresh, fresh],
        in_specs=[VMEM] * (len(groups) + 3),
        out_specs=[VMEM] * 4,
        scratch_shapes=[
            pltpu.VMEM((devices, rows, depth), jnp.bfloat16),
            pltpu.VMEM((rows, columns), jnp.float32),
            pltpu.VMEM((devices, tile, HD), jnp.float32),
        ],
        compiler_params=pltpu.CompilerParams(vmem_limit_bytes=VMEM_LIMIT),
        cost_estimate=pl.CostEstimate(
            flops=2 * rows * columns * width, bytes_accessed=2 * columns * width, transcendentals=2 * rows * HD
        ),
    )(*[group.blocks for group in groups], *w_query, w_keyval)


def pack_kernel(near, far, near_sum, far_sum, *outs):
    tile, lines = near.shape[1], near_sum.shape[1]
    for chip, out in enumerate(outs):
        out[:tile, :] = near[chip]
        out[tile : 2 * tile, :] = far[chip]
        total = near_sum[chip] + far_sum[chip]
        high = total.astype(jnp.bfloat16)
        out[2 * tile : 2 * tile + lines, :] = high
        out[2 * tile + lines :, :] = (total - high.astype(jnp.float32)).astype(jnp.bfloat16)


def pack(near, far, near_sum, far_sum):
    chips, tile, _ = near.shape
    piece = jax.ShapeDtypeStruct((2 * tile + 2 * near_sum.shape[1], HD), jnp.bfloat16)
    return pl.pallas_call(
        pack_kernel,
        out_shape=[piece] * chips,
        in_specs=[VMEM] * 4,
        out_specs=[VMEM] * chips,
        compiler_params=pltpu.CompilerParams(vmem_limit_bytes=VMEM_LIMIT),
    )(near, far, near_sum, far_sum)


def pair_kernel(near, far, *outs):
    for chip, out in enumerate(outs):
        out[0] = near[chip]
        out[1] = far[chip]


def pair(near, far):
    chips = near.shape[0]
    return pl.pallas_call(
        pair_kernel,
        out_shape=[jax.ShapeDtypeStruct((2, *near.shape[1:]), near.dtype)] * chips,
        in_specs=[VMEM] * 2,
        out_specs=[VMEM] * chips,
        compiler_params=pltpu.CompilerParams(vmem_limit_bytes=VMEM_LIMIT),
    )(near, far)


def out_kernel(counts, crossed, *refs):
    slots = slots_of(refs, counts)
    *weights, near, far, kept, total = refs[len(counts) :]
    multiply(slots, weights, kept.shape[2], total, kept)
    own = near.shape[1]
    for slot in range(len(slots)):
        (near, far)[crossed[slot][0]][crossed[slot][1]] = total[slot * own : (slot + 1) * own].astype(near.dtype)


def project_out(groups, w_out, devices):
    counts, crossed = group_shape(groups)
    columns = w_out[0].shape[1]
    own, width = groups[0].blocks.shape[1:]
    chunks = devices // 2
    piece = jax.ShapeDtypeStruct((devices // 2, own, columns), jnp.bfloat16)
    return pl.pallas_call(
        functools.partial(out_kernel, counts, crossed),
        out_shape=[piece, piece],
        in_specs=[VMEM] * (len(groups) + len(w_out)),
        out_specs=[VMEM, VMEM],
        scratch_shapes=[
            pltpu.VMEM((chunks, devices * own, width // chunks), jnp.bfloat16),
            pltpu.VMEM((devices * own, columns), jnp.float32),
        ],
        compiler_params=pltpu.CompilerParams(vmem_limit_bytes=VMEM_LIMIT),
        cost_estimate=pl.CostEstimate(
            flops=2 * devices * own * columns * width, bytes_accessed=2 * columns * width, transcendentals=0
        ),
    )(*[group.blocks for group in groups], *w_out)


def attend_kernel(devices, kv_heads, tile, lengths, place, cache, *refs):
    pieces, (out, fresh, queries, mixed) = refs[:-4], refs[-4:]
    length, width = cache.shape[2:]
    extra = fresh.shape[2]
    half = tile // 2
    per_head = devices // kv_heads * half
    scale = 1.0 / math.sqrt(HD)
    for chip in range(devices // 2):
        for other in range(2):
            piece = pieces[chip][other * tile : (other + 1) * tile, :]
            queries[place[lax.axis_index("gx"), 2 * chip + other]] = piece.astype(jnp.float32)
    line = lax.broadcasted_iota(jnp.int32, (8, 1), 0)
    first = jnp.where(line % 4 < 2, lengths[0], lengths[1])
    cosine, sine = turns((first + line % 2).astype(jnp.float32))
    total = pieces[0][2 * tile :, :].astype(jnp.float32)
    for piece in pieces[1:]:
        total += piece[2 * tile :, :].astype(jnp.float32)
    total = total[: total.shape[0] // 2] + total[total.shape[0] // 2 :]
    twice = [jnp.concatenate([total[4 * at : 4 * at + 4]] * 2, 0) for at in range(2 * kv_heads)]
    new_keys = jnp.concatenate([turn(part, cosine, sine) for part in twice[:kv_heads]], 1)
    new_values = jnp.concatenate(twice[kv_heads:], 1)
    spot = lax.broadcasted_iota(jnp.int32, (extra, width), 0)
    for row in range(2):
        for which, new in enumerate((new_keys, new_values)):
            spread = jnp.where(spot == 0, new[2 * row : 2 * row + 1, :], 0.0)
            spread = jnp.where(spot == 1, new[2 * row + 1 : 2 * row + 2, :], spread)
            fresh[which, row] = spread.astype(fresh.dtype)
    every = queries[...]
    lines = kv_heads * per_head
    column = lax.broadcasted_iota(jnp.int32, (lines, length), 1)
    new_column = lax.broadcasted_iota(jnp.int32, (lines, extra), 1)
    step = lax.broadcasted_iota(jnp.int32, (lines, extra), 0) % 2
    across = (((1,), (1,)), ((), ()))
    for row in range(2):
        mine = every[:, row * half : row * half + half, :].reshape(lines, HD)
        spread = jnp.concatenate([mine] * kv_heads, 1)
        own_row = lax.broadcasted_iota(jnp.int32, spread.shape, 0) // per_head
        own_lane = lax.broadcasted_iota(jnp.int32, spread.shape, 1) // HD
        spread = jnp.where(own_row == own_lane, spread, 0.0).astype(jnp.bfloat16)
        scores = lax.dot_general(spread, cache[0, row], across, preferred_element_type=jnp.float32) * scale
        scores = jnp.where(column < lengths[row], scores, -jnp.inf)
        new_scores = lax.dot_general(spread, fresh[0, row], across, preferred_element_type=jnp.float32) * scale
        new_scores = jnp.where(new_column <= step, new_scores, -jnp.inf)
        peak = jnp.maximum(jnp.max(scores, 1, keepdims=True), jnp.max(new_scores, 1, keepdims=True))
        weight = jnp.exp(scores - peak)
        new_weight = jnp.exp(new_scores - peak)
        denominator = jnp.sum(weight, 1, keepdims=True) + jnp.sum(new_weight, 1, keepdims=True)
        result = jnp.dot(weight.astype(jnp.bfloat16), cache[1, row], preferred_element_type=jnp.float32)
        result += jnp.dot(new_weight.astype(jnp.bfloat16), fresh[1, row], preferred_element_type=jnp.float32)
        for head in range(kv_heads):
            rows = slice(head * per_head, (head + 1) * per_head)
            part = result[rows, head * HD : (head + 1) * HD] / denominator[rows]
            for query in range(per_head // 2):
                lanes = slice((head * per_head // 2 + query) * HD, (head * per_head // 2 + query + 1) * HD)
                for at in range(2):
                    mixed[at * 2 + row : at * 2 + row + 1, lanes] = part[2 * query + at : 2 * query + at + 1]
    out[...] = mixed[...].astype(out.dtype)


def attend(pieces, tile, cache, lengths, place, devices):
    length, width = cache.shape[2], cache.shape[3]
    columns = devices * tile // 4 * HD
    return pl.pallas_call(
        functools.partial(attend_kernel, devices, width // HD, tile),
        out_shape=jax.ShapeDtypeStruct((4, columns), jnp.bfloat16),
        in_specs=[SMEM, SMEM] + [VMEM] * (len(pieces) + 1),
        out_specs=VMEM,
        scratch_shapes=[
            pltpu.VMEM((2, 2, HD, width), cache.dtype),
            pltpu.VMEM((devices, tile, HD), jnp.float32),
            pltpu.VMEM((4, columns), jnp.float32),
        ],
        compiler_params=pltpu.CompilerParams(vmem_limit_bytes=VMEM_LIMIT),
        cost_estimate=pl.CostEstimate(
            flops=8 * 128 * length * width, bytes_accessed=8 * length * width, transcendentals=256 * length
        ),
    )(lengths, place, cache, *pieces)


def finish_kernel(devices, place, *refs):
    *pieces, out = refs
    columns = pieces[0].shape[2]
    steps, rows = out.shape[:2]
    for chip in range(devices // 2):
        for other in range(2):
            source = place[lax.axis_index("gx"), 2 * chip + other]
            lanes = pl.ds(pl.multiple_of(source * columns, columns), columns)
            piece = pieces[chip][other].astype(jnp.float32)
            for step in range(steps):
                out[step, :, lanes] = piece[step * rows : (step + 1) * rows].astype(out.dtype)


def finish(pieces, place, steps, devices):
    own, columns = pieces[0].shape[1:]
    return pl.pallas_call(
        functools.partial(finish_kernel, devices),
        out_shape=jax.ShapeDtypeStruct((steps, own // steps, devices * columns), jnp.bfloat16),
        in_specs=[SMEM] + [VMEM] * len(pieces),
        out_specs=VMEM,
        compiler_params=pltpu.CompilerParams(vmem_limit_bytes=VMEM_LIMIT),
    )(place, *pieces)


def body(hidden, norm_gain, w_query, w_keyval, w_out, kv_cache, lengths):
    steps = hidden.shape[0]
    devices = lax.axis_size("gx")

    normed = norm(hidden, norm_gain, lengths)
    cut = w_query.shape[0] * 3 // 4
    fetched = []

    def bring(*ranges):
        def start(after):
            *arrays, done = fetch(ranges, after)
            fetched.extend(arrays)
            return done

        return start

    waits = [bring((w_query, 0, cut)), bring((w_keyval, 0, 2), (kv_cache, 0, 2)), bring((w_query, cut, w_query.shape[0] - cut))]
    groups = gather(normed, devices, waits)
    w_first, w_keyval, kv_cache, w_second = fetched
    place = jnp.asarray(places(groups, devices))
    near, far, near_sum, far_sum = project(groups, [w_first, w_second], w_keyval, devices)
    pieces = pack(near, swap_cores(far, devices), near_sum, swap_cores(far_sum, devices))

    mixed = attend(give_back(pieces, groups), near.shape[1], kv_cache, lengths, place, devices)
    fetched = []
    part = w_out.shape[0] // 8
    waits = [bring((w_out, first * part, count * part)) for first, count in ((0, 3), (3, 3), (6, 2))]
    groups = gather(mixed, devices, waits)
    near, far = project_out(groups, fetched, devices)
    pieces = pair(near, swap_cores(far, devices))
    return finish(give_back(pieces, groups), place, steps, devices)


def rotate(values, positions):
    row_total, head_count, head_width = values.shape
    half_width = head_width // 2
    frequency = ROPE_BASE ** (-2.0 * jnp.arange(half_width, dtype=jnp.float32) / head_width)
    angles = positions[:, None, None] * frequency[None, None, :]
    cosine = jnp.cos(angles)
    sine_part = jnp.sin(angles)
    paired = values.reshape(row_total, head_count, half_width, 2)
    first_half = paired[..., 0]
    second_half = paired[..., 1]
    turned = jnp.stack(
        [
            first_half * cosine - second_half * sine_part,
            first_half * sine_part + second_half * cosine,
        ],
        -1,
    )
    return turned.reshape(row_total, head_count, head_width)


def attend_split_heads(queries, cache_keys, cache_values, lengths, fresh_keys, fresh_values):
    score_scale = 1.0 / math.sqrt(HD)
    fresh_scores = (
        jnp.einsum("rkgd,rskd->rkgs", queries, fresh_keys, preferred_element_type=jnp.float32)
        * score_scale
    )
    cached = (
        jnp.einsum("rkgd,rlkd->rkgl", queries, cache_keys, preferred_element_type=jnp.float32)
        * score_scale
    )
    in_range = jnp.arange(cache_keys.shape[1])[None, :] < lengths[:, None]
    cached = jnp.where(in_range[:, None, None, :], cached, -jnp.inf)
    row_peak = jnp.maximum(cached.max(-1), fresh_scores.max(-1))
    cached_exp = jnp.exp(cached - row_peak[..., None])
    fresh_exp = jnp.exp(fresh_scores - row_peak[..., None])
    denominator = cached_exp.sum(-1) + fresh_exp.sum(-1)
    mixed = jnp.einsum(
        "rkgl,rlkd->rkgd",
        cached_exp.astype(jnp.bfloat16),
        cache_values,
        preferred_element_type=jnp.float32,
    )
    mixed = mixed + jnp.einsum(
        "rkgs,rskd->rkgd",
        fresh_exp.astype(jnp.bfloat16),
        fresh_values,
        preferred_element_type=jnp.float32,
    )
    return (mixed / denominator[..., None]).astype(jnp.bfloat16)


def body_split_heads(hidden, norm_gain, w_query, w_keyval, w_out, kv_cache, lengths):
    step_count, rows_dev, model_width = hidden.shape
    devices = lax.axis_size("gx")
    device_index = lax.axis_index("gx")
    row_slab = w_keyval.shape[1]
    kv_width = w_keyval.shape[2]
    query_cols = w_query.shape[1]
    heads_width = query_cols * devices
    head_count = heads_width // HD
    kv_heads = kv_width // HD
    kv_both = jnp.concatenate([w_keyval[0], w_keyval[1]], 1)
    cache_keys = kv_cache[0].reshape(rows_dev, kv_cache.shape[2], kv_heads, HD)
    cache_values = kv_cache[1].reshape(rows_dev, kv_cache.shape[2], kv_heads, HD)
    states = hidden.astype(jnp.float32)
    scaled = states * lax.rsqrt(jnp.mean(states * states, -1, keepdims=True) + EPSILON)
    normed = (scaled * norm_gain.astype(jnp.float32)).astype(jnp.bfloat16)
    new_keys = []
    new_values = []
    outputs = []
    for step_index in range(step_count):
        shard_piece = lax.all_gather(normed[step_index], "gx", axis=0, tiled=True)
        queries = jnp.dot(shard_piece, w_query, preferred_element_type=jnp.float32)
        own_slab = lax.dynamic_slice_in_dim(shard_piece, device_index * row_slab, row_slab, 1)
        partial_kv = jnp.dot(own_slab, kv_both, preferred_element_type=jnp.float32)
        joined = jnp.concatenate([queries, partial_kv], 1)
        project_query_rows = lax.all_to_all(
            joined[:, :query_cols], "gx", split_axis=0, concat_axis=1, tiled=True
        )
        project_keyval = lax.psum_scatter(
            joined[:, query_cols:], "gx", scatter_dimension=0, tiled=True
        )
        positions = (lengths + step_index).astype(jnp.float32)
        prepare_queries = rotate(
            project_query_rows.reshape(rows_dev, head_count, HD), positions
        ).astype(jnp.bfloat16)
        prepare_queries = prepare_queries.reshape(rows_dev, kv_heads, head_count // kv_heads, HD)
        key_new = rotate(
            project_keyval[:, :kv_width].reshape(rows_dev, kv_heads, HD), positions
        ).astype(jnp.bfloat16)
        value_new = (
            project_keyval[:, kv_width:].reshape(rows_dev, kv_heads, HD).astype(jnp.bfloat16)
        )
        queries, key_new, value_new = (prepare_queries, key_new, value_new)
        new_keys.append(key_new)
        new_values.append(value_new)
        mixed = attend_split_heads(
            queries,
            cache_keys,
            cache_values,
            lengths,
            jnp.stack(new_keys, 1),
            jnp.stack(new_values, 1),
        )
        out_cols = jnp.dot(
            lax.all_gather(mixed.reshape(rows_dev, heads_width), "gx", axis=0, tiled=True),
            w_out,
            preferred_element_type=jnp.float32,
        ).astype(jnp.bfloat16)
        outputs.append(lax.all_to_all(out_cols, "gx", split_axis=0, concat_axis=1, tiled=True))
    return jnp.stack(outputs)


def solution(mesh):
    devices = mesh.shape["gx"]

    def run(*arrays):
        whole_heads = arrays[2].shape[1] % HD == 0 and devices % 2 == 0
        return (body if whole_heads else body_split_heads)(*arrays)

    in_specs = (
        P(None, ("group", "gx"), None),
        P(),
        P(None, "gx"),
        P(None, "gx", None),
        P(None, "gx"),
        P(None, ("group", "gx"), None, None),
        P(("group", "gx")),
    )
    out_specs = P(None, ("group", "gx"), None)
    return jax.shard_map(run, mesh=mesh, in_specs=in_specs, out_specs=out_specs, check_vma=False)
```

```python
import functools
import math

import jax
import jax.numpy as jnp
import numpy as np
from jax import lax
from jax.experimental import pallas as pl
from jax.experimental.pallas import tpu as pltpu
from jax.sharding import PartitionSpec as P

HD = 128
ROPE_BASE = 500000.0
EPSILON = 1e-05
TAG = 128
VMEM_LIMIT = 8 * 1024 * 1024
VMEM = pl.BlockSpec(memory_space=pltpu.VMEM)
SMEM = pl.BlockSpec(memory_space=pltpu.SMEM)
HBM = pl.BlockSpec(memory_space=pltpu.HBM)


def permute(block, target):
    return lax.ppermute(block, "gx", [(int(i), int(t)) for i, t in enumerate(target)])


def moved(source, target):
    result = np.empty_like(source)
    result[target] = source
    return result


class Group:
    def __init__(self, blocks, sources, crossed=False):
        self.blocks, self.sources, self.crossed = blocks, sources, crossed

    def send(self, target, crossed=False):
        return Group(permute(self.blocks, target), [moved(source, target) for source in self.sources], crossed)


def join(groups):
    if len(groups) == 1:
        return groups[0]
    return Group(jnp.concatenate([g.blocks for g in groups], 0), [source for g in groups for source in g.sources])


def ring_order(size):
    if size > 4:
        return list(range(size))
    return list(range(0, size, 2)) + list(range(1, size, 2))[::-1]


def axes_of(devices):
    chips, inner = devices // 2, 1
    while inner * inner * 4 <= chips and chips % (inner * 2) == 0:
        inner *= 2
    sizes = (chips // inner, inner, 2)
    place = np.arange(devices).reshape(sizes)
    result = []
    for axis, size in enumerate(sizes):
        order = ring_order(size)
        after = np.empty(size, int)
        for here, there in zip(order, order[1:] + order[:1]):
            after[here] = there
        before = np.argsort(after)
        result.append((size, np.take(place, after, axis).ravel(), np.take(place, before, axis).ravel()))
    return result


def ring(group, axis):
    size, following, preceding = axis
    groups = []
    forward = backward = group
    for step in range(1, size // 2 + 1):
        forward = forward.send(following)
        groups.append(forward)
        if 2 * step < size:
            backward = backward.send(preceding)
            groups.append(backward)
    return groups


def gather(block, devices, meanwhile=()):
    (size, following, preceding), inner, core = axes_of(devices)
    own = Group(block[None], [np.arange(devices)])
    near = ring(own, inner)
    groups = [own] + near + [join([own] + near).send(core[1], crossed=True)]
    forward = backward = own
    for step in range(1, size // 2 + 1):
        before = forward.blocks
        arrived = [forward.send(following)] + ([backward.send(preceding)] if 2 * step < size else [])
        forward, backward = arrived[0], arrived[-1]
        if step <= len(meanwhile):
            onward = (step < size // 2) + (2 * step + 2 < size)
            chips, *alone = hold(arrived, onward, meanwhile[step - 1](before))
            forward, backward = (alone + [forward])[0], (alone + [backward])[-1]
        else:
            chips = join(arrived)
        reached = [chips] + ring(chips, inner)
        if step == size // 2 < len(meanwhile):
            reached[-1:] = hold(reached[-1:], 0, meanwhile[step](chips.blocks))
        groups += reached + [group.send(core[1], crossed=True) for group in reached]
    return groups


def hold_kernel(count, *refs):
    stacked, *alone = refs[count + 1 :]
    for at in range(count):
        stacked[at] = refs[at][0]
    for at in range(len(alone)):
        alone[at][...] = refs[at][...]


def hold(groups, onward, after):
    blocks = [group.blocks for group in groups]
    stacked, *alone = pl.pallas_call(
        functools.partial(hold_kernel, len(blocks)),
        out_shape=[jax.ShapeDtypeStruct((len(blocks), *blocks[0].shape[1:]), blocks[0].dtype)]
        + [jax.ShapeDtypeStruct(block.shape, block.dtype) for block in blocks[:onward]],
        in_specs=[VMEM] * len(blocks) + [pl.BlockSpec(memory_space=pl.ANY)],
        out_specs=[VMEM] * (onward + 1),
        compiler_params=pltpu.CompilerParams(vmem_limit_bytes=VMEM_LIMIT),
    )(*blocks, after)
    sources = [group.sources for group in groups]
    return [Group(stacked, sum(sources, []))] + [Group(block, source) for block, source in zip(alone, sources)]


def swap_cores(block, devices):
    return permute(block, np.arange(devices) ^ 1)


def exchange(pieces, devices):
    same_core = [list(range(core, devices, 2)) for core in range(2)]
    return lax.all_to_all(pieces, "gx", 0, 0, axis_index_groups=same_core, tiled=True)


def places(groups):
    origins = [source // 2 for group in groups if not group.crossed for source in group.sources]
    return np.stack(origins, 1).astype(np.int32)


def norm_kernel(lengths_far, hidden_far, gain_far, out, lengths, hidden, gain, arrived):
    copies = [
        pltpu.make_async_copy(far, near, arrived.at[at])
        for at, (far, near) in enumerate(((hidden_far, hidden), (gain_far, gain), (lengths_far, lengths)))
    ]
    for copy in copies:
        copy.start()
    copies[0].wait()
    states = hidden[...].astype(jnp.float32)
    scale = lax.rsqrt(jnp.mean(states * states, -1, keepdims=True) + EPSILON)
    copies[1].wait()
    normed = states * scale * gain[...].astype(jnp.float32).reshape(1, 1, gain.shape[0])
    steps, rows, width = normed.shape
    lines = [normed[step, row : row + 1] for row in range(rows) for step in range(steps)]
    out[:, :width] = jnp.concatenate(lines, 0).astype(out.dtype)
    line = lax.broadcasted_iota(jnp.int32, (steps * rows, TAG), 0)
    lane = lax.broadcasted_iota(jnp.int32, (steps * rows, TAG), 1)
    position = line % steps
    copies[2].wait()
    for row in range(rows):
        position = jnp.where(line // steps == row, position + lengths[row], position)
    tag = jnp.where(lane == 0, position // 32, position % 32)
    out[:, width:] = tag.astype(jnp.float32).astype(out.dtype)


def norm(hidden, gain, lengths):
    steps, rows, width = hidden.shape
    return pl.pallas_call(
        norm_kernel,
        out_shape=jax.ShapeDtypeStruct((steps * rows, width + TAG), jnp.bfloat16),
        in_specs=[HBM] * 3,
        out_specs=VMEM,
        scratch_shapes=[
            pltpu.SMEM(lengths.shape, lengths.dtype),
            pltpu.VMEM(hidden.shape, hidden.dtype),
            pltpu.VMEM(gain.shape, gain.dtype),
            pltpu.SemaphoreType.DMA((3,)),
        ],
        compiler_params=pltpu.CompilerParams(vmem_limit_bytes=VMEM_LIMIT),
        cost_estimate=pl.CostEstimate(flops=6 * steps * rows * width, bytes_accessed=4 * steps * rows * width, transcendentals=0),
    )(*[pltpu.with_memory_space_constraint(array, pltpu.HBM) for array in (lengths, hidden, gain)])


def fetch_kernel(firsts, chunks, *refs):
    copies, count, arrived = [], len(firsts), refs[-1]
    refs[-2][...] = jnp.zeros_like(refs[-2])
    for first, far, near in zip(firsts, refs[:count], refs[count + 1 : 2 * count + 1]):
        size = near.shape[0] // min(chunks, near.shape[0])
        for at in range(0, near.shape[0], size):
            source = far.at[pl.ds(first + at, size)]
            copies.append(pltpu.make_async_copy(source, near.at[pl.ds(at, size)], arrived.at[len(copies)]))
            copies[-1].start()
    for copy in copies:
        copy.wait()


def fetch(ranges, after):
    chunks = 8
    arrays = [array for array, _, _ in ranges]
    shapes = [(count, *array.shape[1:]) for array, _, count in ranges]
    return pl.pallas_call(
        functools.partial(fetch_kernel, [first for _, first, _ in ranges], chunks),
        out_shape=[pltpu.VMEM(shape, array.dtype) for shape, array in zip(shapes, arrays)]
        + [jax.ShapeDtypeStruct((8, HD), jnp.float32)],
        in_specs=[HBM] * len(arrays) + [pl.BlockSpec(memory_space=pl.ANY)],
        out_specs=[VMEM] * (len(arrays) + 1),
        scratch_shapes=[pltpu.SemaphoreType.DMA((chunks * len(arrays),))],
        compiler_params=pltpu.CompilerParams(vmem_limit_bytes=VMEM_LIMIT),
        cost_estimate=pl.CostEstimate(
            flops=0, bytes_accessed=sum(2 * math.prod(shape) for shape in shapes), transcendentals=0
        ),
    )(*[pltpu.with_memory_space_constraint(array, pltpu.HBM) for array in arrays], after)


def slots_of(refs, counts):
    return [(ref, at) for ref, count in zip(refs, counts) for at in range(count)]


def assemble(slots, first, width):
    lanes = slice(first, first + width)
    return jnp.concatenate([ref[at, :, lanes] for ref, at in slots], 0)


def multiply(slots, weights, depth, total, kept):
    total[...] = jnp.zeros_like(total)
    chunk = 0
    for part in weights:
        for at in range(0, part.shape[0], depth):
            kept[chunk] = assemble(slots, chunk * depth, depth)
            total[...] += jnp.dot(kept[chunk], part[at : at + depth, :], preferred_element_type=jnp.float32)
            chunk += 1


def turns(positions):
    shape = (positions.shape[0], HD)
    lane = lax.broadcasted_iota(jnp.int32, shape, 1)
    pair = (lane // 2).astype(jnp.float32)
    angles = positions * jnp.exp(pair * (-2.0 * math.log(ROPE_BASE) / HD))
    return jnp.cos(angles), jnp.where(lane % 2 == 0, -1.0, 1.0) * jnp.sin(angles)


def turn(values, cosine, sine):
    lanes = values.shape[-1]
    even = lax.broadcasted_iota(jnp.int32, values.shape, 1) % 2 == 0
    swapped = jnp.where(even, pltpu.roll(values, lanes - 1, 1), pltpu.roll(values, 1, 1))
    return values * cosine + swapped * sine


def project_kernel(counts, crossed, width, *refs):
    slots = slots_of(refs, counts)
    first, second, keyval, *outs = refs[len(counts) : len(counts) + 7]
    kept, total, packed = refs[len(counts) + 7 :]
    queries, fresh = outs[:2], outs[2:]
    depth = keyval.shape[1]
    tags = jnp.concatenate([ref[at, :, width:].astype(jnp.float32) for ref, at in slots], 0)
    cosine, sine = turns(tags[:, 0:1] * 32.0 + tags[:, 1:2])
    multiply(slots, [first, second], depth, total, kept)
    own = kept[lax.axis_index("gx")]
    blocks = keyval.shape[2] // HD
    for which in range(2):
        term = jnp.dot(own, keyval[which], preferred_element_type=jnp.float32)
        for slot in range(len(slots)):
            for at in range(blocks):
                row = (which * blocks + at) * 4
                fresh[crossed[slot][0]][crossed[slot][1], row : row + 4, :] = term[
                    slot * 4 : slot * 4 + 4, at * HD : (at + 1) * HD
                ]
    heads = total.shape[1] // HD
    for head in range(heads):
        turned = turn(total[:, head * HD : (head + 1) * HD], cosine, sine)
        for slot in range(len(slots)):
            for row in range(2):
                line, at = row * 2 * heads + head * 2, slot * 4 + row * 2
                packed[slot, line : line + 2, :] = turned[at : at + 2, :]
    for slot in range(len(slots)):
        queries[crossed[slot][0]][crossed[slot][1]] = packed[slot].astype(jnp.bfloat16)


def group_shape(groups):
    counts = [len(group.sources) for group in groups]
    seen, order = [0, 0], []
    for group, count in zip(groups, counts):
        for _ in range(count):
            order.append((int(group.crossed), seen[group.crossed]))
            seen[group.crossed] += 1
    return counts, order


def project(groups, w_query, w_keyval, devices):
    counts, crossed = group_shape(groups)
    columns = w_query[0].shape[1]
    depth, kv_width = w_keyval.shape[1:]
    own, width = groups[0].blocks.shape[1], devices * depth
    rows, tile = devices * own, own * (columns // HD)
    query = jax.ShapeDtypeStruct((devices // 2, tile, HD), jnp.bfloat16)
    fresh = jax.ShapeDtypeStruct((devices // 2, own * 2 * kv_width // HD, HD), jnp.float32)
    return pl.pallas_call(
        functools.partial(project_kernel, counts, crossed, width),
        out_shape=[query, query, fresh, fresh],
        in_specs=[VMEM] * (len(groups) + 3),
        out_specs=[VMEM] * 4,
        scratch_shapes=[
            pltpu.VMEM((devices, rows, depth), jnp.bfloat16),
            pltpu.VMEM((rows, columns), jnp.float32),
            pltpu.VMEM((devices, tile, HD), jnp.float32),
        ],
        compiler_params=pltpu.CompilerParams(vmem_limit_bytes=VMEM_LIMIT),
        cost_estimate=pl.CostEstimate(
            flops=2 * rows * columns * width, bytes_accessed=2 * columns * width, transcendentals=2 * rows * HD
        ),
    )(*[group.blocks for group in groups], *w_query, w_keyval)


def pack_kernel(place, near, far, near_sum, far_sum, out):
    tile, lines = near.shape[1], near_sum.shape[1]
    for slot in range(near.shape[0]):
        chip = place[lax.axis_index("gx"), slot]
        out[chip, :tile, :] = near[slot]
        out[chip, tile : 2 * tile, :] = far[slot]
        total = near_sum[slot] + far_sum[slot]
        high = total.astype(jnp.bfloat16)
        out[chip, 2 * tile : 2 * tile + lines, :] = high
        out[chip, 2 * tile + lines :, :] = (total - high.astype(jnp.float32)).astype(jnp.bfloat16)


def pack(place, near, far, near_sum, far_sum):
    chips, tile, _ = near.shape
    return pl.pallas_call(
        pack_kernel,
        out_shape=jax.ShapeDtypeStruct((chips, 2 * tile + 2 * near_sum.shape[1], HD), jnp.bfloat16),
        in_specs=[SMEM] + [VMEM] * 4,
        out_specs=VMEM,
        compiler_params=pltpu.CompilerParams(vmem_limit_bytes=VMEM_LIMIT),
    )(place, near, far, near_sum, far_sum)


def pair_kernel(place, near, far, out):
    for slot in range(near.shape[0]):
        chip = place[lax.axis_index("gx"), slot]
        out[chip, 0] = near[slot]
        out[chip, 1] = far[slot]


def pair(place, near, far):
    return pl.pallas_call(
        pair_kernel,
        out_shape=jax.ShapeDtypeStruct((near.shape[0], 2, *near.shape[1:]), near.dtype),
        in_specs=[SMEM] + [VMEM] * 2,
        out_specs=VMEM,
        compiler_params=pltpu.CompilerParams(vmem_limit_bytes=VMEM_LIMIT),
    )(place, near, far)


def out_kernel(counts, crossed, *refs):
    slots = slots_of(refs, counts)
    *weights, near, far, kept, total = refs[len(counts) :]
    multiply(slots, weights, kept.shape[2], total, kept)
    own = near.shape[1]
    for slot in range(len(slots)):
        (near, far)[crossed[slot][0]][crossed[slot][1]] = total[slot * own : (slot + 1) * own].astype(near.dtype)


def project_out(groups, w_out, devices):
    counts, crossed = group_shape(groups)
    columns = w_out[0].shape[1]
    own, width = groups[0].blocks.shape[1:]
    chunks = devices // 2
    piece = jax.ShapeDtypeStruct((devices // 2, own, columns), jnp.bfloat16)
    return pl.pallas_call(
        functools.partial(out_kernel, counts, crossed),
        out_shape=[piece, piece],
        in_specs=[VMEM] * (len(groups) + len(w_out)),
        out_specs=[VMEM, VMEM],
        scratch_shapes=[
            pltpu.VMEM((chunks, devices * own, width // chunks), jnp.bfloat16),
            pltpu.VMEM((devices * own, columns), jnp.float32),
        ],
        compiler_params=pltpu.CompilerParams(vmem_limit_bytes=VMEM_LIMIT),
        cost_estimate=pl.CostEstimate(
            flops=2 * devices * own * columns * width, bytes_accessed=2 * columns * width, transcendentals=0
        ),
    )(*[group.blocks for group in groups], *w_out)


def attend_kernel(devices, kv_heads, tile, lengths, pieces, cache, out, fresh, queries, mixed):
    length, width = cache.shape[2:]
    extra = fresh.shape[2]
    half = tile // 2
    per_head = devices // kv_heads * half
    scale = 1.0 / math.sqrt(HD)
    for chip in range(devices // 2):
        for other in range(2):
            piece = pieces[chip, other * tile : (other + 1) * tile, :]
            queries[2 * chip + (lax.axis_index("gx") % 2 + other) % 2] = piece.astype(jnp.float32)
    line = lax.broadcasted_iota(jnp.int32, (8, 1), 0)
    first = jnp.where(line % 4 < 2, lengths[0], lengths[1])
    cosine, sine = turns((first + line % 2).astype(jnp.float32))
    total = jnp.sum(pieces[:, 2 * tile :, :].astype(jnp.float32), 0)
    total = total[: total.shape[0] // 2] + total[total.shape[0] // 2 :]
    twice = [jnp.concatenate([total[4 * at : 4 * at + 4]] * 2, 0) for at in range(2 * kv_heads)]
    new_keys = jnp.concatenate([turn(part, cosine, sine) for part in twice[:kv_heads]], 1)
    new_values = jnp.concatenate(twice[kv_heads:], 1)
    spot = lax.broadcasted_iota(jnp.int32, (extra, width), 0)
    for row in range(2):
        for which, new in enumerate((new_keys, new_values)):
            spread = jnp.where(spot == 0, new[2 * row : 2 * row + 1, :], 0.0)
            spread = jnp.where(spot == 1, new[2 * row + 1 : 2 * row + 2, :], spread)
            fresh[which, row] = spread.astype(fresh.dtype)
    every = queries[...]
    lines = kv_heads * per_head
    column = lax.broadcasted_iota(jnp.int32, (lines, length), 1)
    new_column = lax.broadcasted_iota(jnp.int32, (lines, extra), 1)
    step = lax.broadcasted_iota(jnp.int32, (lines, extra), 0) % 2
    across = (((1,), (1,)), ((), ()))
    for row in range(2):
        mine = every[:, row * half : row * half + half, :].reshape(lines, HD)
        spread = jnp.concatenate([mine] * kv_heads, 1)
        own_row = lax.broadcasted_iota(jnp.int32, spread.shape, 0) // per_head
        own_lane = lax.broadcasted_iota(jnp.int32, spread.shape, 1) // HD
        spread = jnp.where(own_row == own_lane, spread, 0.0).astype(jnp.bfloat16)
        scores = lax.dot_general(spread, cache[0, row], across, preferred_element_type=jnp.float32) * scale
        scores = jnp.where(column < lengths[row], scores, -jnp.inf)
        new_scores = lax.dot_general(spread, fresh[0, row], across, preferred_element_type=jnp.float32) * scale
        new_scores = jnp.where(new_column <= step, new_scores, -jnp.inf)
        peak = jnp.maximum(jnp.max(scores, 1, keepdims=True), jnp.max(new_scores, 1, keepdims=True))
        weight = jnp.exp(scores - peak)
        new_weight = jnp.exp(new_scores - peak)
        denominator = jnp.sum(weight, 1, keepdims=True) + jnp.sum(new_weight, 1, keepdims=True)
        result = jnp.dot(weight.astype(jnp.bfloat16), cache[1, row], preferred_element_type=jnp.float32)
        result += jnp.dot(new_weight.astype(jnp.bfloat16), fresh[1, row], preferred_element_type=jnp.float32)
        for head in range(kv_heads):
            rows = slice(head * per_head, (head + 1) * per_head)
            part = result[rows, head * HD : (head + 1) * HD] / denominator[rows]
            for query in range(per_head // 2):
                lanes = slice((head * per_head // 2 + query) * HD, (head * per_head // 2 + query + 1) * HD)
                for at in range(2):
                    mixed[at * 2 + row : at * 2 + row + 1, lanes] = part[2 * query + at : 2 * query + at + 1]
    out[...] = mixed[...].astype(out.dtype)


def attend(pieces, tile, cache, lengths, devices):
    length, width = cache.shape[2], cache.shape[3]
    columns = devices * tile // 4 * HD
    return pl.pallas_call(
        functools.partial(attend_kernel, devices, width // HD, tile),
        out_shape=jax.ShapeDtypeStruct((4, columns), jnp.bfloat16),
        in_specs=[SMEM, VMEM, VMEM],
        out_specs=VMEM,
        scratch_shapes=[
            pltpu.VMEM((2, 2, HD, width), cache.dtype),
            pltpu.VMEM((devices, tile, HD), jnp.float32),
            pltpu.VMEM((4, columns), jnp.float32),
        ],
        compiler_params=pltpu.CompilerParams(vmem_limit_bytes=VMEM_LIMIT),
        cost_estimate=pl.CostEstimate(
            flops=8 * 128 * length * width, bytes_accessed=8 * length * width, transcendentals=256 * length
        ),
    )(lengths, pieces, cache)


def finish_kernel(devices, pieces, out):
    columns = pieces.shape[3]
    steps, rows = out.shape[:2]
    for chip in range(devices // 2):
        for other in range(2):
            source = 2 * chip + (lax.axis_index("gx") % 2 + other) % 2
            lanes = pl.ds(pl.multiple_of(source * columns, columns), columns)
            piece = pieces[chip, other].astype(jnp.float32)
            for step in range(steps):
                out[step, :, lanes] = piece[step * rows : (step + 1) * rows].astype(out.dtype)


def finish(pieces, steps, devices):
    own, columns = pieces.shape[2:]
    return pl.pallas_call(
        functools.partial(finish_kernel, devices),
        out_shape=jax.ShapeDtypeStruct((steps, own // steps, devices * columns), jnp.bfloat16),
        in_specs=[VMEM],
        out_specs=VMEM,
        compiler_params=pltpu.CompilerParams(vmem_limit_bytes=VMEM_LIMIT),
    )(pieces)


def body(hidden, norm_gain, w_query, w_keyval, w_out, kv_cache, lengths):
    steps = hidden.shape[0]
    devices = lax.axis_size("gx")

    normed = norm(hidden, norm_gain, lengths)
    cut = w_query.shape[0] * 3 // 4
    fetched = []

    def bring(*ranges):
        def start(after):
            *arrays, done = fetch(ranges, after)
            fetched.extend(arrays)
            return done

        return start

    part = w_out.shape[0] // 8
    waits = [
        bring((w_query, 0, cut)),
        bring((w_keyval, 0, 2), (kv_cache, 0, 2)),
        bring((w_query, cut, w_query.shape[0] - cut), (w_out, 0, part)),
    ]
    groups = gather(normed, devices, waits)
    w_first, w_keyval, kv_cache, w_second, w_out_first = fetched
    place = jnp.asarray(places(groups))
    near, far, near_sum, far_sum = project(groups, [w_first, w_second], w_keyval, devices)
    pieces = pack(place, near, swap_cores(far, devices), near_sum, swap_cores(far_sum, devices))

    mixed = attend(exchange(pieces, devices), near.shape[1], kv_cache, lengths, devices)
    fetched = [w_out_first]
    waits = [bring((w_out, first * part, count * part)) for first, count in ((1, 2), (3, 3), (6, 2))]
    groups = gather(mixed, devices, waits)
    near, far = project_out(groups, fetched, devices)
    pieces = pair(place, near, swap_cores(far, devices))
    return finish(exchange(pieces, devices), steps, devices)


def rotate(values, positions):
    row_total, head_count, head_width = values.shape
    half_width = head_width // 2
    frequency = ROPE_BASE ** (-2.0 * jnp.arange(half_width, dtype=jnp.float32) / head_width)
    angles = positions[:, None, None] * frequency[None, None, :]
    cosine = jnp.cos(angles)
    sine_part = jnp.sin(angles)
    paired = values.reshape(row_total, head_count, half_width, 2)
    first_half = paired[..., 0]
    second_half = paired[..., 1]
    turned = jnp.stack(
        [
            first_half * cosine - second_half * sine_part,
            first_half * sine_part + second_half * cosine,
        ],
        -1,
    )
    return turned.reshape(row_total, head_count, head_width)


def attend_split_heads(queries, cache_keys, cache_values, lengths, fresh_keys, fresh_values):
    score_scale = 1.0 / math.sqrt(HD)
    fresh_scores = (
        jnp.einsum("rkgd,rskd->rkgs", queries, fresh_keys, preferred_element_type=jnp.float32)
        * score_scale
    )
    cached = (
        jnp.einsum("rkgd,rlkd->rkgl", queries, cache_keys, preferred_element_type=jnp.float32)
        * score_scale
    )
    in_range = jnp.arange(cache_keys.shape[1])[None, :] < lengths[:, None]
    cached = jnp.where(in_range[:, None, None, :], cached, -jnp.inf)
    row_peak = jnp.maximum(cached.max(-1), fresh_scores.max(-1))
    cached_exp = jnp.exp(cached - row_peak[..., None])
    fresh_exp = jnp.exp(fresh_scores - row_peak[..., None])
    denominator = cached_exp.sum(-1) + fresh_exp.sum(-1)
    mixed = jnp.einsum(
        "rkgl,rlkd->rkgd",
        cached_exp.astype(jnp.bfloat16),
        cache_values,
        preferred_element_type=jnp.float32,
    )
    mixed = mixed + jnp.einsum(
        "rkgs,rskd->rkgd",
        fresh_exp.astype(jnp.bfloat16),
        fresh_values,
        preferred_element_type=jnp.float32,
    )
    return (mixed / denominator[..., None]).astype(jnp.bfloat16)


def body_split_heads(hidden, norm_gain, w_query, w_keyval, w_out, kv_cache, lengths):
    step_count, rows_dev, model_width = hidden.shape
    devices = lax.axis_size("gx")
    device_index = lax.axis_index("gx")
    row_slab = w_keyval.shape[1]
    kv_width = w_keyval.shape[2]
    query_cols = w_query.shape[1]
    heads_width = query_cols * devices
    head_count = heads_width // HD
    kv_heads = kv_width // HD
    kv_both = jnp.concatenate([w_keyval[0], w_keyval[1]], 1)
    cache_keys = kv_cache[0].reshape(rows_dev, kv_cache.shape[2], kv_heads, HD)
    cache_values = kv_cache[1].reshape(rows_dev, kv_cache.shape[2], kv_heads, HD)
    states = hidden.astype(jnp.float32)
    scaled = states * lax.rsqrt(jnp.mean(states * states, -1, keepdims=True) + EPSILON)
    normed = (scaled * norm_gain.astype(jnp.float32)).astype(jnp.bfloat16)
    new_keys = []
    new_values = []
    outputs = []
    for step_index in range(step_count):
        shard_piece = lax.all_gather(normed[step_index], "gx", axis=0, tiled=True)
        queries = jnp.dot(shard_piece, w_query, preferred_element_type=jnp.float32)
        own_slab = lax.dynamic_slice_in_dim(shard_piece, device_index * row_slab, row_slab, 1)
        partial_kv = jnp.dot(own_slab, kv_both, preferred_element_type=jnp.float32)
        joined = jnp.concatenate([queries, partial_kv], 1)
        project_query_rows = lax.all_to_all(
            joined[:, :query_cols], "gx", split_axis=0, concat_axis=1, tiled=True
        )
        project_keyval = lax.psum_scatter(
            joined[:, query_cols:], "gx", scatter_dimension=0, tiled=True
        )
        positions = (lengths + step_index).astype(jnp.float32)
        prepare_queries = rotate(
            project_query_rows.reshape(rows_dev, head_count, HD), positions
        ).astype(jnp.bfloat16)
        prepare_queries = prepare_queries.reshape(rows_dev, kv_heads, head_count // kv_heads, HD)
        key_new = rotate(
            project_keyval[:, :kv_width].reshape(rows_dev, kv_heads, HD), positions
        ).astype(jnp.bfloat16)
        value_new = (
            project_keyval[:, kv_width:].reshape(rows_dev, kv_heads, HD).astype(jnp.bfloat16)
        )
        queries, key_new, value_new = (prepare_queries, key_new, value_new)
        new_keys.append(key_new)
        new_values.append(value_new)
        mixed = attend_split_heads(
            queries,
            cache_keys,
            cache_values,
            lengths,
            jnp.stack(new_keys, 1),
            jnp.stack(new_values, 1),
        )
        out_cols = jnp.dot(
            lax.all_gather(mixed.reshape(rows_dev, heads_width), "gx", axis=0, tiled=True),
            w_out,
            preferred_element_type=jnp.float32,
        ).astype(jnp.bfloat16)
        outputs.append(lax.all_to_all(out_cols, "gx", split_axis=0, concat_axis=1, tiled=True))
    return jnp.stack(outputs)


def solution(mesh):
    devices = mesh.shape["gx"]

    def run(*arrays):
        whole_heads = arrays[2].shape[1] % HD == 0 and devices % 2 == 0
        return (body if whole_heads else body_split_heads)(*arrays)

    in_specs = (
        P(None, ("group", "gx"), None),
        P(),
        P(None, "gx"),
        P(None, "gx", None),
        P(None, "gx"),
        P(None, ("group", "gx"), None, None),
        P(("group", "gx")),
    )
    out_specs = P(None, ("group", "gx"), None)
    return jax.shard_map(run, mesh=mesh, in_specs=in_specs, out_specs=out_specs, check_vma=False)
```

```python
import functools
import math

import jax
import jax.numpy as jnp
import numpy as np
from jax import lax
from jax.experimental import pallas as pl
from jax.experimental.pallas import tpu as pltpu
from jax.sharding import PartitionSpec as P

HD = 128
ROPE_BASE = 500000.0
EPSILON = 1e-05
TAG = 128
VMEM_LIMIT = 10 * 1024 * 1024
VMEM = pl.BlockSpec(memory_space=pltpu.VMEM)
SMEM = pl.BlockSpec(memory_space=pltpu.SMEM)
HBM = pl.BlockSpec(memory_space=pltpu.HBM)


def permute(block, target):
    return lax.ppermute(block, "gx", [(int(i), int(t)) for i, t in enumerate(target)])


def moved(source, target):
    result = np.empty_like(source)
    result[target] = source
    return result


class Group:
    def __init__(self, blocks, sources, crossed=False):
        self.blocks, self.sources, self.crossed = blocks, sources, crossed

    def send(self, target, crossed=False):
        return Group(permute(self.blocks, target), [moved(source, target) for source in self.sources], crossed)


def join(groups):
    if len(groups) == 1:
        return groups[0]
    return Group(jnp.concatenate([g.blocks for g in groups], 0), [source for g in groups for source in g.sources])


def ring_order(size):
    if size > 4:
        return list(range(size))
    return list(range(0, size, 2)) + list(range(1, size, 2))[::-1]


def axes_of(devices):
    chips, inner = devices // 2, 1
    while inner * inner * 4 <= chips and chips % (inner * 2) == 0:
        inner *= 2
    sizes = (chips // inner, inner, 2)
    place = np.arange(devices).reshape(sizes)
    result = []
    for axis, size in enumerate(sizes):
        order = ring_order(size)
        after = np.empty(size, int)
        for here, there in zip(order, order[1:] + order[:1]):
            after[here] = there
        before = np.argsort(after)
        result.append((size, np.take(place, after, axis).ravel(), np.take(place, before, axis).ravel()))
    return result


def ring(group, axis):
    size, following, preceding = axis
    groups = []
    forward = backward = group
    for step in range(1, size // 2 + 1):
        forward = forward.send(following)
        groups.append(forward)
        if 2 * step < size:
            backward = backward.send(preceding)
            groups.append(backward)
    return groups


def gather(block, devices, meanwhile=(), inner_first=False):
    (size, following, preceding), inner, core = axes_of(devices)
    own = Group(block[None], [np.arange(devices)])
    near = ring(own, inner)
    chip_pair = join([own] + near)
    groups = [own] + near + [chip_pair.send(core[1], crossed=True)]
    forward = backward = own
    for step in range(1, size // 2 + 1):
        before = forward.blocks
        arrived = [forward.send(following)] + ([backward.send(preceding)] if 2 * step < size else [])
        forward, backward = arrived[0], arrived[-1]
        if step <= len(meanwhile):
            onward = (step < size // 2) + (2 * step + 2 < size)
            chips, *alone = hold(arrived, 0 if inner_first else onward, meanwhile[step - 1](before))
            if inner_first:
                alone = [hold([group], 0, chip_pair.blocks)[0] for group in arrived[:onward]]
            forward, backward = (alone + [forward])[0], (alone + [backward])[-1]
        else:
            chips = join(arrived)
        reached = [chips] + ring(chips, inner)
        if step == size // 2 < len(meanwhile):
            reached[-1:] = hold(reached[-1:], 0, meanwhile[step](chips.blocks))
        groups += reached + [group.send(core[1], crossed=True) for group in reached]
    return groups


def hold_kernel(count, *refs):
    stacked, *alone = refs[count + 1 :]
    for at in range(count):
        stacked[at] = refs[at][0]
    for at in range(len(alone)):
        alone[at][...] = refs[at][...]


def hold(groups, onward, after):
    blocks = [group.blocks for group in groups]
    stacked, *alone = pl.pallas_call(
        functools.partial(hold_kernel, len(blocks)),
        out_shape=[jax.ShapeDtypeStruct((len(blocks), *blocks[0].shape[1:]), blocks[0].dtype)]
        + [jax.ShapeDtypeStruct(block.shape, block.dtype) for block in blocks[:onward]],
        in_specs=[VMEM] * len(blocks) + [pl.BlockSpec(memory_space=pl.ANY)],
        out_specs=[VMEM] * (onward + 1),
        compiler_params=pltpu.CompilerParams(vmem_limit_bytes=VMEM_LIMIT),
    )(*blocks, after)
    sources = [group.sources for group in groups]
    return [Group(stacked, sum(sources, []))] + [Group(block, source) for block, source in zip(alone, sources)]


def swap_cores(block, devices):
    return permute(block, np.arange(devices) ^ 1)


def exchange(pieces, devices):
    same_core = [list(range(core, devices, 2)) for core in range(2)]
    return lax.all_to_all(pieces, "gx", 0, 0, axis_index_groups=same_core, tiled=True)


def places(groups):
    return [(source // 2)[::2] for group in groups if not group.crossed for source in group.sources]


def look_up(values):
    chip = lax.axis_index("gx") // 2
    found = jnp.int32(int(values[0]))
    for at in range(1, len(values)):
        found = jnp.where(chip == at, jnp.int32(int(values[at])), found)
    return found


def norm_kernel(lengths_far, hidden_far, gain_far, out, spread, lengths, hidden, gain, arrived):
    copies = [
        pltpu.make_async_copy(far, near, arrived.at[at])
        for at, (far, near) in enumerate(((hidden_far, hidden), (gain_far, gain), (lengths_far, lengths)))
    ]
    for copy in copies:
        copy.start()
    copies[0].wait()
    states = hidden[...].astype(jnp.float32)
    scale = lax.rsqrt(jnp.mean(states * states, -1, keepdims=True) + EPSILON)
    copies[1].wait()
    normed = states * scale * gain[...].astype(jnp.float32).reshape(1, 1, gain.shape[0])
    steps, rows, width = normed.shape
    lines = [normed[step, row : row + 1] for row in range(rows) for step in range(steps)]
    out[:, :width] = jnp.concatenate(lines, 0).astype(out.dtype)
    line = lax.broadcasted_iota(jnp.int32, (steps * rows, TAG), 0)
    lane = lax.broadcasted_iota(jnp.int32, (steps * rows, TAG), 1)
    position = line % steps
    copies[2].wait()
    for row in range(rows):
        position = jnp.where(line // steps == row, position + lengths[row], position)
    tag = jnp.where(lane == 0, position // 32, position % 32)
    out[:, width:] = tag.astype(jnp.float32).astype(out.dtype)
    for row in range(spread.shape[0]):
        spread[row] = jnp.full(spread.shape[1:], lengths[row], spread.dtype)


def norm(hidden, gain, lengths):
    steps, rows, width = hidden.shape
    return pl.pallas_call(
        norm_kernel,
        out_shape=[
            jax.ShapeDtypeStruct((steps * rows, width + TAG), jnp.bfloat16),
            jax.ShapeDtypeStruct((rows, 8, HD), jnp.int32),
        ],
        in_specs=[HBM] * 3,
        out_specs=[VMEM] * 2,
        scratch_shapes=[
            pltpu.SMEM(lengths.shape, lengths.dtype),
            pltpu.VMEM(hidden.shape, hidden.dtype),
            pltpu.VMEM(gain.shape, gain.dtype),
            pltpu.SemaphoreType.DMA((3,)),
        ],
        compiler_params=pltpu.CompilerParams(vmem_limit_bytes=VMEM_LIMIT),
        cost_estimate=pl.CostEstimate(flops=6 * steps * rows * width, bytes_accessed=4 * steps * rows * width, transcendentals=0),
    )(*[pltpu.with_memory_space_constraint(array, pltpu.HBM) for array in (lengths, hidden, gain)])


def fetch_kernel(firsts, chunks, *refs):
    copies, count, arrived = [], len(firsts), refs[-1]
    refs[-2][...] = jnp.zeros_like(refs[-2])
    for first, far, near in zip(firsts, refs[:count], refs[count + 1 : 2 * count + 1]):
        size = near.shape[0] // min(chunks, near.shape[0])
        for at in range(0, near.shape[0], size):
            source = far.at[pl.ds(first + at, size)]
            copies.append(pltpu.make_async_copy(source, near.at[pl.ds(at, size)], arrived.at[len(copies)]))
            copies[-1].start()
    for copy in copies:
        copy.wait()


def fetch(ranges, after):
    chunks = 8
    arrays = [array for array, _, _ in ranges]
    shapes = [(count, *array.shape[1:]) for array, _, count in ranges]
    return pl.pallas_call(
        functools.partial(fetch_kernel, [first for _, first, _ in ranges], chunks),
        out_shape=[pltpu.VMEM(shape, array.dtype) for shape, array in zip(shapes, arrays)]
        + [jax.ShapeDtypeStruct((8, HD), jnp.float32)],
        in_specs=[HBM] * len(arrays) + [pl.BlockSpec(memory_space=pl.ANY)],
        out_specs=[VMEM] * (len(arrays) + 1),
        scratch_shapes=[pltpu.SemaphoreType.DMA((chunks * len(arrays),))],
        compiler_params=pltpu.CompilerParams(vmem_limit_bytes=VMEM_LIMIT),
        cost_estimate=pl.CostEstimate(
            flops=0, bytes_accessed=sum(2 * math.prod(shape) for shape in shapes), transcendentals=0
        ),
    )(*[pltpu.with_memory_space_constraint(array, pltpu.HBM) for array in arrays], after)


def slots_of(refs, counts):
    return [(ref, at) for ref, count in zip(refs, counts) for at in range(count)]


def assemble(slots, first, width):
    lanes = slice(first, first + width)
    return jnp.concatenate([ref[at, :, lanes] for ref, at in slots], 0)


def multiply(slots, weights, depth, total, kept, copy=None):
    total[...] = jnp.zeros_like(total)
    chunk = 0
    for part in weights:
        if copy is not None and part is weights[-1]:
            copy.wait()
        for at in range(0, part.shape[0], depth):
            kept[chunk] = assemble(slots, chunk * depth, depth)
            total[...] += jnp.dot(kept[chunk], part[at : at + depth, :], preferred_element_type=jnp.float32)
            chunk += 1


def turns(positions):
    shape = (positions.shape[0], HD)
    lane = lax.broadcasted_iota(jnp.int32, shape, 1)
    pair = (lane // 2).astype(jnp.float32)
    angles = positions * jnp.exp(pair * (-2.0 * math.log(ROPE_BASE) / HD))
    return jnp.cos(angles), jnp.where(lane % 2 == 0, -1.0, 1.0) * jnp.sin(angles)


def turn(values, cosine, sine):
    lanes = values.shape[-1]
    even = lax.broadcasted_iota(jnp.int32, values.shape, 1) % 2 == 0
    swapped = jnp.where(even, pltpu.roll(values, lanes - 1, 1), pltpu.roll(values, 1, 1))
    return values * cosine + swapped * sine


def project_kernel(counts, crossed, width, *refs):
    slots = slots_of(refs, counts)
    first, second, keyval, *outs = refs[len(counts) : len(counts) + 7]
    kept, total, packed = refs[len(counts) + 7 :]
    queries, fresh = outs[:2], outs[2:]
    depth = keyval.shape[1]
    tags = jnp.concatenate([ref[at, :, width:].astype(jnp.float32) for ref, at in slots], 0)
    cosine, sine = turns(tags[:, 0:1] * 32.0 + tags[:, 1:2])
    multiply(slots, [first, second], depth, total, kept)
    own = kept[lax.axis_index("gx")]
    blocks = keyval.shape[2] // HD
    for which in range(2):
        term = jnp.dot(own, keyval[which], preferred_element_type=jnp.float32)
        for slot in range(len(slots)):
            for at in range(blocks):
                row = (which * blocks + at) * 4
                fresh[crossed[slot][0]][crossed[slot][1], row : row + 4, :] = term[
                    slot * 4 : slot * 4 + 4, at * HD : (at + 1) * HD
                ]
    heads = total.shape[1] // HD
    for head in range(heads):
        turned = turn(total[:, head * HD : (head + 1) * HD], cosine, sine)
        for slot in range(len(slots)):
            for row in range(2):
                line, at = row * 2 * heads + head * 2, slot * 4 + row * 2
                packed[slot, line : line + 2, :] = turned[at : at + 2, :]
    for slot in range(len(slots)):
        queries[crossed[slot][0]][crossed[slot][1]] = packed[slot].astype(jnp.bfloat16)


def group_shape(groups):
    counts = [len(group.sources) for group in groups]
    seen, order = [0, 0], []
    for group, count in zip(groups, counts):
        for _ in range(count):
            order.append((int(group.crossed), seen[group.crossed]))
            seen[group.crossed] += 1
    return counts, order


def project(groups, w_query, w_keyval, devices):
    counts, crossed = group_shape(groups)
    columns = w_query[0].shape[1]
    depth, kv_width = w_keyval.shape[1:]
    own, width = groups[0].blocks.shape[1], devices * depth
    rows, tile = devices * own, own * (columns // HD)
    query = jax.ShapeDtypeStruct((devices // 2, tile, HD), jnp.bfloat16)
    fresh = jax.ShapeDtypeStruct((devices // 2, own * 2 * kv_width // HD, HD), jnp.float32)
    return pl.pallas_call(
        functools.partial(project_kernel, counts, crossed, width),
        out_shape=[query, query, fresh, fresh],
        in_specs=[VMEM] * (len(groups) + 3),
        out_specs=[VMEM] * 4,
        scratch_shapes=[
            pltpu.VMEM((devices, rows, depth), jnp.bfloat16),
            pltpu.VMEM((rows, columns), jnp.float32),
            pltpu.VMEM((devices, tile, HD), jnp.float32),
        ],
        compiler_params=pltpu.CompilerParams(vmem_limit_bytes=VMEM_LIMIT),
        cost_estimate=pl.CostEstimate(
            flops=2 * rows * columns * width, bytes_accessed=2 * columns * width, transcendentals=2 * rows * HD
        ),
    )(*[group.blocks for group in groups], *w_query, w_keyval)


def pack_kernel(place, near, far, near_sum, far_sum, out):
    tile, lines = near.shape[1], near_sum.shape[1]
    for slot in range(near.shape[0]):
        chip = look_up(place[slot])
        out[chip, :tile, :] = near[slot]
        out[chip, tile : 2 * tile, :] = far[slot]
        total = near_sum[slot] + far_sum[slot]
        high = total.astype(jnp.bfloat16)
        out[chip, 2 * tile : 2 * tile + lines, :] = high
        out[chip, 2 * tile + lines :, :] = (total - high.astype(jnp.float32)).astype(jnp.bfloat16)


def pack(place, near, far, near_sum, far_sum):
    chips, tile, _ = near.shape
    return pl.pallas_call(
        functools.partial(pack_kernel, place),
        out_shape=jax.ShapeDtypeStruct((chips, 2 * tile + 2 * near_sum.shape[1], HD), jnp.bfloat16),
        in_specs=[VMEM] * 4,
        out_specs=VMEM,
        compiler_params=pltpu.CompilerParams(vmem_limit_bytes=VMEM_LIMIT),
    )(near, far, near_sum, far_sum)


def pair_kernel(place, near, far, out):
    for slot in range(near.shape[0]):
        chip = look_up(place[slot])
        out[chip, 0] = near[slot]
        out[chip, 1] = far[slot]


def pair(place, near, far):
    return pl.pallas_call(
        functools.partial(pair_kernel, place),
        out_shape=jax.ShapeDtypeStruct((near.shape[0], 2, *near.shape[1:]), near.dtype),
        in_specs=[VMEM] * 2,
        out_specs=VMEM,
        compiler_params=pltpu.CompilerParams(vmem_limit_bytes=VMEM_LIMIT),
    )(near, far)


def out_kernel(counts, crossed, *refs):
    slots = slots_of(refs, counts)
    *weights, rest, near, far, last, kept, total, arrived = refs[len(counts) :]
    copy = pltpu.make_async_copy(rest.at[pl.ds(rest.shape[0] - last.shape[0], last.shape[0])], last, arrived)
    copy.start()
    multiply(slots, weights + [last], kept.shape[2], total, kept, copy)
    own = near.shape[1]
    for slot in range(len(slots)):
        (near, far)[crossed[slot][0]][crossed[slot][1]] = total[slot * own : (slot + 1) * own].astype(near.dtype)


def project_out(groups, fetched, w_out, devices):
    counts, crossed = group_shape(groups)
    columns = w_out.shape[1]
    own, width = groups[0].blocks.shape[1:]
    chunks = devices // 2
    piece = jax.ShapeDtypeStruct((devices // 2, own, columns), jnp.bfloat16)
    return pl.pallas_call(
        functools.partial(out_kernel, counts, crossed),
        out_shape=[piece, piece],
        in_specs=[VMEM] * (len(groups) + len(fetched)) + [HBM],
        out_specs=[VMEM, VMEM],
        scratch_shapes=[
            pltpu.VMEM((width - sum(part.shape[0] for part in fetched), columns), w_out.dtype),
            pltpu.VMEM((chunks, devices * own, width // chunks), jnp.bfloat16),
            pltpu.VMEM((devices * own, columns), jnp.float32),
            pltpu.SemaphoreType.DMA(()),
        ],
        compiler_params=pltpu.CompilerParams(vmem_limit_bytes=VMEM_LIMIT),
        cost_estimate=pl.CostEstimate(
            flops=2 * devices * own * columns * width, bytes_accessed=2 * columns * width, transcendentals=0
        ),
    )(*[group.blocks for group in groups], *fetched, pltpu.with_memory_space_constraint(w_out, pltpu.HBM))


def attend_kernel(devices, kv_heads, tile, lengths, pieces, cache, out, fresh, queries, mixed):
    length, width = cache.shape[2:]
    extra = fresh.shape[2]
    half = tile // 2
    per_head = devices // kv_heads * half
    scale = 1.0 / math.sqrt(HD)
    for chip in range(devices // 2):
        for other in range(2):
            piece = pieces[chip, other * tile : (other + 1) * tile, :]
            queries[2 * chip + (lax.axis_index("gx") % 2 + other) % 2] = piece.astype(jnp.float32)
    line = lax.broadcasted_iota(jnp.int32, (8, 1), 0)
    first = jnp.where(line % 4 < 2, lengths[0, :, :1], lengths[1, :, :1])
    cosine, sine = turns((first + line % 2).astype(jnp.float32))
    total = jnp.sum(pieces[:, 2 * tile :, :].astype(jnp.float32), 0)
    total = total[: total.shape[0] // 2] + total[total.shape[0] // 2 :]
    twice = [jnp.concatenate([total[4 * at : 4 * at + 4]] * 2, 0) for at in range(2 * kv_heads)]
    new_keys = jnp.concatenate([turn(part, cosine, sine) for part in twice[:kv_heads]], 1)
    new_values = jnp.concatenate(twice[kv_heads:], 1)
    spot = lax.broadcasted_iota(jnp.int32, (extra, width), 0)
    for row in range(2):
        for which, new in enumerate((new_keys, new_values)):
            spread = jnp.where(spot == 0, new[2 * row : 2 * row + 1, :], 0.0)
            spread = jnp.where(spot == 1, new[2 * row + 1 : 2 * row + 2, :], spread)
            fresh[which, row] = spread.astype(fresh.dtype)
    every = queries[...]
    lines = kv_heads * per_head
    column = lax.broadcasted_iota(jnp.int32, (lines, length), 1)
    new_column = lax.broadcasted_iota(jnp.int32, (lines, extra), 1)
    step = lax.broadcasted_iota(jnp.int32, (lines, extra), 0) % 2
    across = (((1,), (1,)), ((), ()))
    for row in range(2):
        mine = every[:, row * half : row * half + half, :].reshape(lines, HD)
        spread = jnp.concatenate([mine] * kv_heads, 1)
        own_row = lax.broadcasted_iota(jnp.int32, spread.shape, 0) // per_head
        own_lane = lax.broadcasted_iota(jnp.int32, spread.shape, 1) // HD
        spread = jnp.where(own_row == own_lane, spread, 0.0).astype(jnp.bfloat16)
        scores = lax.dot_general(spread, cache[0, row], across, preferred_element_type=jnp.float32) * scale
        scores = jnp.where(column < lengths[row, :1, :1], scores, -jnp.inf)
        new_scores = lax.dot_general(spread, fresh[0, row], across, preferred_element_type=jnp.float32) * scale
        new_scores = jnp.where(new_column <= step, new_scores, -jnp.inf)
        peak = jnp.maximum(jnp.max(scores, 1, keepdims=True), jnp.max(new_scores, 1, keepdims=True))
        weight = jnp.exp(scores - peak)
        new_weight = jnp.exp(new_scores - peak)
        denominator = jnp.sum(weight, 1, keepdims=True) + jnp.sum(new_weight, 1, keepdims=True)
        result = jnp.dot(weight.astype(jnp.bfloat16), cache[1, row], preferred_element_type=jnp.float32)
        result += jnp.dot(new_weight.astype(jnp.bfloat16), fresh[1, row], preferred_element_type=jnp.float32)
        for head in range(kv_heads):
            rows = slice(head * per_head, (head + 1) * per_head)
            part = result[rows, head * HD : (head + 1) * HD] / denominator[rows]
            for query in range(per_head // 2):
                lanes = slice((head * per_head // 2 + query) * HD, (head * per_head // 2 + query + 1) * HD)
                for at in range(2):
                    mixed[at * 2 + row : at * 2 + row + 1, lanes] = part[2 * query + at : 2 * query + at + 1]
    out[...] = mixed[...].astype(out.dtype)


def attend(pieces, tile, cache, lengths, devices):
    length, width = cache.shape[2], cache.shape[3]
    columns = devices * tile // 4 * HD
    return pl.pallas_call(
        functools.partial(attend_kernel, devices, width // HD, tile),
        out_shape=jax.ShapeDtypeStruct((4, columns), jnp.bfloat16),
        in_specs=[VMEM] * 3,
        out_specs=VMEM,
        scratch_shapes=[
            pltpu.VMEM((2, 2, HD, width), cache.dtype),
            pltpu.VMEM((devices, tile, HD), jnp.float32),
            pltpu.VMEM((4, columns), jnp.float32),
        ],
        compiler_params=pltpu.CompilerParams(vmem_limit_bytes=VMEM_LIMIT),
        cost_estimate=pl.CostEstimate(
            flops=8 * 128 * length * width, bytes_accessed=8 * length * width, transcendentals=256 * length
        ),
    )(lengths, pieces, cache)


def finish_kernel(devices, pieces, out):
    columns = pieces.shape[3]
    steps, rows = out.shape[:2]
    for chip in range(devices // 2):
        for other in range(2):
            source = 2 * chip + (lax.axis_index("gx") % 2 + other) % 2
            lanes = pl.ds(pl.multiple_of(source * columns, columns), columns)
            piece = pieces[chip, other].astype(jnp.float32)
            for step in range(steps):
                out[step, :, lanes] = piece[step * rows : (step + 1) * rows].astype(out.dtype)


def finish(pieces, steps, devices):
    own, columns = pieces.shape[2:]
    return pl.pallas_call(
        functools.partial(finish_kernel, devices),
        out_shape=jax.ShapeDtypeStruct((steps, own // steps, devices * columns), jnp.bfloat16),
        in_specs=[VMEM],
        out_specs=VMEM,
        compiler_params=pltpu.CompilerParams(vmem_limit_bytes=VMEM_LIMIT),
    )(pieces)


def body(hidden, norm_gain, w_query, w_keyval, w_out, kv_cache, lengths):
    steps = hidden.shape[0]
    devices = lax.axis_size("gx")

    normed, lengths = norm(hidden, norm_gain, lengths)
    cut = w_query.shape[0] * 3 // 4
    fetched = []

    def bring(*ranges):
        def start(after):
            *arrays, done = fetch(ranges, after)
            fetched.extend(arrays)
            return done

        return start

    part = w_out.shape[0] // 8
    waits = [
        bring((w_query, 0, cut)),
        bring((w_keyval, 0, 2), (kv_cache, 0, 2)),
        bring((w_query, cut, w_query.shape[0] - cut), (w_out, 0, part)),
    ]
    groups = gather(normed, devices, waits, inner_first=True)
    w_first, w_keyval, kv_cache, w_second, w_out_first = fetched
    place = places(groups)
    near, far, near_sum, far_sum = project(groups, [w_first, w_second], w_keyval, devices)
    pieces = pack(place, near, swap_cores(far, devices), near_sum, swap_cores(far_sum, devices))

    mixed = attend(exchange(pieces, devices), near.shape[1], kv_cache, lengths, devices)
    fetched = [w_out_first]
    waits = [bring((w_out, first * part, count * part)) for first, count in ((1, 2), (3, 1), (4, 2))]
    groups = gather(mixed, devices, waits)
    near, far = project_out(groups, fetched, w_out, devices)
    pieces = pair(place, near, swap_cores(far, devices))
    return finish(exchange(pieces, devices), steps, devices)


def rotate(values, positions):
    row_total, head_count, head_width = values.shape
    half_width = head_width // 2
    frequency = ROPE_BASE ** (-2.0 * jnp.arange(half_width, dtype=jnp.float32) / head_width)
    angles = positions[:, None, None] * frequency[None, None, :]
    cosine = jnp.cos(angles)
    sine_part = jnp.sin(angles)
    paired = values.reshape(row_total, head_count, half_width, 2)
    first_half = paired[..., 0]
    second_half = paired[..., 1]
    turned = jnp.stack(
        [
            first_half * cosine - second_half * sine_part,
            first_half * sine_part + second_half * cosine,
        ],
        -1,
    )
    return turned.reshape(row_total, head_count, head_width)


def attend_split_heads(queries, cache_keys, cache_values, lengths, fresh_keys, fresh_values):
    score_scale = 1.0 / math.sqrt(HD)
    fresh_scores = (
        jnp.einsum("rkgd,rskd->rkgs", queries, fresh_keys, preferred_element_type=jnp.float32)
        * score_scale
    )
    cached = (
        jnp.einsum("rkgd,rlkd->rkgl", queries, cache_keys, preferred_element_type=jnp.float32)
        * score_scale
    )
    in_range = jnp.arange(cache_keys.shape[1])[None, :] < lengths[:, None]
    cached = jnp.where(in_range[:, None, None, :], cached, -jnp.inf)
    row_peak = jnp.maximum(cached.max(-1), fresh_scores.max(-1))
    cached_exp = jnp.exp(cached - row_peak[..., None])
    fresh_exp = jnp.exp(fresh_scores - row_peak[..., None])
    denominator = cached_exp.sum(-1) + fresh_exp.sum(-1)
    mixed = jnp.einsum(
        "rkgl,rlkd->rkgd",
        cached_exp.astype(jnp.bfloat16),
        cache_values,
        preferred_element_type=jnp.float32,
    )
    mixed = mixed + jnp.einsum(
        "rkgs,rskd->rkgd",
        fresh_exp.astype(jnp.bfloat16),
        fresh_values,
        preferred_element_type=jnp.float32,
    )
    return (mixed / denominator[..., None]).astype(jnp.bfloat16)


def body_split_heads(hidden, norm_gain, w_query, w_keyval, w_out, kv_cache, lengths):
    step_count, rows_dev, model_width = hidden.shape
    devices = lax.axis_size("gx")
    device_index = lax.axis_index("gx")
    row_slab = w_keyval.shape[1]
    kv_width = w_keyval.shape[2]
    query_cols = w_query.shape[1]
    heads_width = query_cols * devices
    head_count = heads_width // HD
    kv_heads = kv_width // HD
    kv_both = jnp.concatenate([w_keyval[0], w_keyval[1]], 1)
    cache_keys = kv_cache[0].reshape(rows_dev, kv_cache.shape[2], kv_heads, HD)
    cache_values = kv_cache[1].reshape(rows_dev, kv_cache.shape[2], kv_heads, HD)
    states = hidden.astype(jnp.float32)
    scaled = states * lax.rsqrt(jnp.mean(states * states, -1, keepdims=True) + EPSILON)
    normed = (scaled * norm_gain.astype(jnp.float32)).astype(jnp.bfloat16)
    new_keys = []
    new_values = []
    outputs = []
    for step_index in range(step_count):
        shard_piece = lax.all_gather(normed[step_index], "gx", axis=0, tiled=True)
        queries = jnp.dot(shard_piece, w_query, preferred_element_type=jnp.float32)
        own_slab = lax.dynamic_slice_in_dim(shard_piece, device_index * row_slab, row_slab, 1)
        partial_kv = jnp.dot(own_slab, kv_both, preferred_element_type=jnp.float32)
        joined = jnp.concatenate([queries, partial_kv], 1)
        project_query_rows = lax.all_to_all(
            joined[:, :query_cols], "gx", split_axis=0, concat_axis=1, tiled=True
        )
        project_keyval = lax.psum_scatter(
            joined[:, query_cols:], "gx", scatter_dimension=0, tiled=True
        )
        positions = (lengths + step_index).astype(jnp.float32)
        prepare_queries = rotate(
            project_query_rows.reshape(rows_dev, head_count, HD), positions
        ).astype(jnp.bfloat16)
        prepare_queries = prepare_queries.reshape(rows_dev, kv_heads, head_count // kv_heads, HD)
        key_new = rotate(
            project_keyval[:, :kv_width].reshape(rows_dev, kv_heads, HD), positions
        ).astype(jnp.bfloat16)
        value_new = (
            project_keyval[:, kv_width:].reshape(rows_dev, kv_heads, HD).astype(jnp.bfloat16)
        )
        queries, key_new, value_new = (prepare_queries, key_new, value_new)
        new_keys.append(key_new)
        new_values.append(value_new)
        mixed = attend_split_heads(
            queries,
            cache_keys,
            cache_values,
            lengths,
            jnp.stack(new_keys, 1),
            jnp.stack(new_values, 1),
        )
        out_cols = jnp.dot(
            lax.all_gather(mixed.reshape(rows_dev, heads_width), "gx", axis=0, tiled=True),
            w_out,
            preferred_element_type=jnp.float32,
        ).astype(jnp.bfloat16)
        outputs.append(lax.all_to_all(out_cols, "gx", split_axis=0, concat_axis=1, tiled=True))
    return jnp.stack(outputs)


def solution(mesh):
    devices = mesh.shape["gx"]

    def run(*arrays):
        whole_heads = arrays[2].shape[1] % HD == 0 and devices % 2 == 0
        return (body if whole_heads else body_split_heads)(*arrays)

    in_specs = (
        P(None, ("group", "gx"), None),
        P(),
        P(None, "gx"),
        P(None, "gx", None),
        P(None, "gx"),
        P(None, ("group", "gx"), None, None),
        P(("group", "gx")),
    )
    out_specs = P(None, ("group", "gx"), None)
    return jax.shard_map(run, mesh=mesh, in_specs=in_specs, out_specs=out_specs, check_vma=False)
```

```python
import functools
import math

import jax
import jax.numpy as jnp
import numpy as np
from jax import lax
from jax.experimental import pallas as pl
from jax.experimental.pallas import tpu as pltpu
from jax.sharding import PartitionSpec as P

HD = 128
ROPE_BASE = 500000.0
EPSILON = 1e-05
TAG = 128
VMEM_LIMIT = 10 * 1024 * 1024
VMEM = pl.BlockSpec(memory_space=pltpu.VMEM)
SMEM = pl.BlockSpec(memory_space=pltpu.SMEM)
HBM = pl.BlockSpec(memory_space=pltpu.HBM)


def permute(block, target):
    return lax.ppermute(block, "gx", [(int(i), int(t)) for i, t in enumerate(target)])


def moved(source, target):
    result = np.empty_like(source)
    result[target] = source
    return result


class Group:
    def __init__(self, blocks, sources, crossed=False):
        self.blocks, self.sources, self.crossed = blocks, sources, crossed

    def send(self, target, crossed=False):
        return Group(permute(self.blocks, target), [moved(source, target) for source in self.sources], crossed)


def join(groups):
    if len(groups) == 1:
        return groups[0]
    return Group(jnp.concatenate([g.blocks for g in groups], 0), [source for g in groups for source in g.sources])


def ring_order(size):
    if size > 4:
        return list(range(size))
    return list(range(0, size, 2)) + list(range(1, size, 2))[::-1]


def axes_of(devices):
    chips, inner = devices // 2, 1
    while inner * inner * 4 <= chips and chips % (inner * 2) == 0:
        inner *= 2
    sizes = (chips // inner, inner, 2)
    place = np.arange(devices).reshape(sizes)
    result = []
    for axis, size in enumerate(sizes):
        order = ring_order(size)
        after = np.empty(size, int)
        for here, there in zip(order, order[1:] + order[:1]):
            after[here] = there
        before = np.argsort(after)
        result.append((size, np.take(place, after, axis).ravel(), np.take(place, before, axis).ravel()))
    return result


def ring(group, axis):
    size, following, preceding = axis
    groups = []
    forward = backward = group
    for step in range(1, size // 2 + 1):
        forward = forward.send(following)
        groups.append(forward)
        if 2 * step < size:
            backward = backward.send(preceding)
            groups.append(backward)
    return groups


def gather(block, devices, meanwhile=(), inner_first=False):
    (size, following, preceding), inner, core = axes_of(devices)
    own = Group(block[None], [np.arange(devices)])
    near = ring(own, inner)
    chip_pair = join([own] + near)
    groups = [own] + near + [chip_pair.send(core[1], crossed=True)]
    forward = backward = own
    for step in range(1, size // 2 + 1):
        before = forward.blocks
        arrived = [forward.send(following)] + ([backward.send(preceding)] if 2 * step < size else [])
        forward, backward = arrived[0], arrived[-1]
        if step <= len(meanwhile):
            onward = (step < size // 2) + (2 * step + 2 < size)
            chips, *alone = hold(arrived, 0 if inner_first else onward, meanwhile[step - 1](before))
            if inner_first:
                alone = [hold([group], 0, chip_pair.blocks)[0] for group in arrived[:onward]]
            forward, backward = (alone + [forward])[0], (alone + [backward])[-1]
        else:
            chips = join(arrived)
        reached = [chips] + ring(chips, inner)
        if step == size // 2 < len(meanwhile):
            reached[-1:] = hold(reached[-1:], 0, meanwhile[step](chips.blocks))
        groups += reached + [group.send(core[1], crossed=True) for group in reached]
    return groups


def gather_direct(block, devices, meanwhile):
    (size, following, _), inner, core = axes_of(devices)
    own = Group(block[None], [np.arange(devices)])
    near = ring(own, inner)
    groups = [own] + near + [join([own] + near).send(core[1], crossed=True)]
    arrived, target = [], following
    for _ in range(size - 1):
        arrived.append(own.send(target))
        target = following[target]
    reached = hold(arrived, 0, meanwhile[0](block), *[group.blocks for group in near])
    beside = ring(reached[0], inner)
    if beside:
        beside[-1:] = hold(beside[-1:], 0, meanwhile[1](reached[0].blocks), groups[-1].blocks)
    reached += beside
    return groups + reached + [group.send(core[1], crossed=True) for group in reached]


def hold_kernel(count, waits, *refs):
    stacked, *alone = refs[count + waits :]
    first = 0
    for ref in refs[:count]:
        for at in range(ref.shape[0]):
            stacked[first + at] = ref[at]
        first += ref.shape[0]
    for at in range(len(alone)):
        alone[at][...] = refs[at][...]


def hold(groups, onward, *after):
    blocks = [group.blocks for group in groups]
    stacked, *alone = pl.pallas_call(
        functools.partial(hold_kernel, len(blocks), len(after)),
        out_shape=[jax.ShapeDtypeStruct((sum(block.shape[0] for block in blocks), *blocks[0].shape[1:]), blocks[0].dtype)]
        + [jax.ShapeDtypeStruct(block.shape, block.dtype) for block in blocks[:onward]],
        in_specs=[VMEM] * len(blocks) + [pl.BlockSpec(memory_space=pl.ANY)] * len(after),
        out_specs=[VMEM] * (onward + 1),
        compiler_params=pltpu.CompilerParams(vmem_limit_bytes=VMEM_LIMIT),
    )(*blocks, *after)
    sources = [group.sources for group in groups]
    return [Group(stacked, sum(sources, []))] + [Group(block, source) for block, source in zip(alone, sources)]


def swap_cores(block, devices):
    return permute(block, np.arange(devices) ^ 1)


def exchange(pieces, devices):
    same_core = [list(range(core, devices, 2)) for core in range(2)]
    return lax.all_to_all(pieces, "gx", 0, 0, axis_index_groups=same_core, tiled=True)


def places(groups):
    return [(source // 2)[::2] for group in groups if not group.crossed for source in group.sources]


def look_up(values):
    chip = lax.axis_index("gx") // 2
    found = jnp.int32(int(values[0]))
    for at in range(1, len(values)):
        found = jnp.where(chip == at, jnp.int32(int(values[at])), found)
    return found


def norm_kernel(lengths_far, hidden_far, gain_far, out, spread, lengths, hidden, gain, arrived):
    copies = [
        pltpu.make_async_copy(far, near, arrived.at[at])
        for at, (far, near) in enumerate(((hidden_far, hidden), (gain_far, gain), (lengths_far, lengths)))
    ]
    for copy in copies:
        copy.start()
    copies[0].wait()
    states = hidden[...].astype(jnp.float32)
    scale = lax.rsqrt(jnp.mean(states * states, -1, keepdims=True) + EPSILON)
    copies[1].wait()
    normed = states * scale * gain[...].astype(jnp.float32).reshape(1, 1, gain.shape[0])
    steps, rows, width = normed.shape
    lines = [normed[step, row : row + 1] for row in range(rows) for step in range(steps)]
    out[:, :width] = jnp.concatenate(lines, 0).astype(out.dtype)
    line = lax.broadcasted_iota(jnp.int32, (steps * rows, TAG), 0)
    lane = lax.broadcasted_iota(jnp.int32, (steps * rows, TAG), 1)
    position = line % steps
    copies[2].wait()
    for row in range(rows):
        position = jnp.where(line // steps == row, position + lengths[row], position)
    tag = jnp.where(lane == 0, position // 32, position % 32)
    out[:, width:] = tag.astype(jnp.float32).astype(out.dtype)
    for row in range(spread.shape[0]):
        spread[row] = jnp.full(spread.shape[1:], lengths[row], spread.dtype)


def norm(hidden, gain, lengths):
    steps, rows, width = hidden.shape
    return pl.pallas_call(
        norm_kernel,
        out_shape=[
            jax.ShapeDtypeStruct((steps * rows, width + TAG), jnp.bfloat16),
            jax.ShapeDtypeStruct((rows, 8, HD), jnp.int32),
        ],
        in_specs=[HBM] * 3,
        out_specs=[VMEM] * 2,
        scratch_shapes=[
            pltpu.SMEM(lengths.shape, lengths.dtype),
            pltpu.VMEM(hidden.shape, hidden.dtype),
            pltpu.VMEM(gain.shape, gain.dtype),
            pltpu.SemaphoreType.DMA((3,)),
        ],
        compiler_params=pltpu.CompilerParams(vmem_limit_bytes=VMEM_LIMIT),
        cost_estimate=pl.CostEstimate(flops=6 * steps * rows * width, bytes_accessed=4 * steps * rows * width, transcendentals=0),
    )(*[pltpu.with_memory_space_constraint(array, pltpu.HBM) for array in (lengths, hidden, gain)])


def fetch_kernel(firsts, chunks, *refs):
    copies, count, arrived = [], len(firsts), refs[-1]
    refs[-2][...] = jnp.zeros_like(refs[-2])
    for first, far, near in zip(firsts, refs[:count], refs[count + 1 : 2 * count + 1]):
        size = near.shape[0] // min(chunks, near.shape[0])
        for at in range(0, near.shape[0], size):
            source = far.at[pl.ds(first + at, size)]
            copies.append(pltpu.make_async_copy(source, near.at[pl.ds(at, size)], arrived.at[len(copies)]))
            copies[-1].start()
    for copy in copies:
        copy.wait()


def fetch(ranges, after):
    chunks = 8
    arrays = [array for array, _, _ in ranges]
    shapes = [(count, *array.shape[1:]) for array, _, count in ranges]
    return pl.pallas_call(
        functools.partial(fetch_kernel, [first for _, first, _ in ranges], chunks),
        out_shape=[pltpu.VMEM(shape, array.dtype) for shape, array in zip(shapes, arrays)]
        + [jax.ShapeDtypeStruct((8, HD), jnp.float32)],
        in_specs=[HBM] * len(arrays) + [pl.BlockSpec(memory_space=pl.ANY)],
        out_specs=[VMEM] * (len(arrays) + 1),
        scratch_shapes=[pltpu.SemaphoreType.DMA((chunks * len(arrays),))],
        compiler_params=pltpu.CompilerParams(vmem_limit_bytes=VMEM_LIMIT),
        cost_estimate=pl.CostEstimate(
            flops=0, bytes_accessed=sum(2 * math.prod(shape) for shape in shapes), transcendentals=0
        ),
    )(*[pltpu.with_memory_space_constraint(array, pltpu.HBM) for array in arrays], after)


def slots_of(refs, counts):
    return [(ref, at) for ref, count in zip(refs, counts) for at in range(count)]


def assemble(slots, first, width):
    lanes = slice(first, first + width)
    return jnp.concatenate([ref[at, :, lanes] for ref, at in slots], 0)


def multiply(slots, weights, depth, total, kept, copies=()):
    total[...] = jnp.zeros_like(total)
    chunk = 0
    for part in weights:
        for at in range(0, part.shape[0], depth):
            kept[chunk] = assemble(slots, chunk * depth, depth)
            if copies and part is weights[-1]:
                copies[at // depth].wait()
            total[...] += jnp.dot(kept[chunk], part[at : at + depth, :], preferred_element_type=jnp.float32)
            chunk += 1


def turns(positions):
    shape = (positions.shape[0], HD)
    lane = lax.broadcasted_iota(jnp.int32, shape, 1)
    pair = (lane // 2).astype(jnp.float32)
    angles = positions * jnp.exp(pair * (-2.0 * math.log(ROPE_BASE) / HD))
    return jnp.cos(angles), jnp.where(lane % 2 == 0, -1.0, 1.0) * jnp.sin(angles)


def turn(values, cosine, sine):
    lanes = values.shape[-1]
    even = lax.broadcasted_iota(jnp.int32, values.shape, 1) % 2 == 0
    swapped = jnp.where(even, pltpu.roll(values, lanes - 1, 1), pltpu.roll(values, 1, 1))
    return values * cosine + swapped * sine


def project_kernel(counts, crossed, width, *refs):
    slots = slots_of(refs, counts)
    first, second, keyval, *outs = refs[len(counts) : len(counts) + 7]
    kept, total, packed = refs[len(counts) + 7 :]
    queries, fresh = outs[:2], outs[2:]
    depth = keyval.shape[1]
    tags = jnp.concatenate([ref[at, :, width:].astype(jnp.float32) for ref, at in slots], 0)
    cosine, sine = turns(tags[:, 0:1] * 32.0 + tags[:, 1:2])
    multiply(slots, [first, second], depth, total, kept)
    own = kept[lax.axis_index("gx")]
    blocks = keyval.shape[2] // HD
    for which in range(2):
        term = jnp.dot(own, keyval[which], preferred_element_type=jnp.float32)
        for slot in range(len(slots)):
            for at in range(blocks):
                row = (which * blocks + at) * 4
                fresh[crossed[slot][0]][crossed[slot][1], row : row + 4, :] = term[
                    slot * 4 : slot * 4 + 4, at * HD : (at + 1) * HD
                ]
    heads = total.shape[1] // HD
    for head in range(heads):
        turned = turn(total[:, head * HD : (head + 1) * HD], cosine, sine)
        for slot in range(len(slots)):
            for row in range(2):
                line, at = row * 2 * heads + head * 2, slot * 4 + row * 2
                packed[slot, line : line + 2, :] = turned[at : at + 2, :]
    for slot in range(len(slots)):
        queries[crossed[slot][0]][crossed[slot][1]] = packed[slot].astype(jnp.bfloat16)


def group_shape(groups):
    counts = [len(group.sources) for group in groups]
    seen, order = [0, 0], []
    for group, count in zip(groups, counts):
        for _ in range(count):
            order.append((int(group.crossed), seen[group.crossed]))
            seen[group.crossed] += 1
    return counts, order


def project(groups, w_query, w_keyval, devices):
    counts, crossed = group_shape(groups)
    columns = w_query[0].shape[1]
    depth, kv_width = w_keyval.shape[1:]
    own, width = groups[0].blocks.shape[1], devices * depth
    rows, tile = devices * own, own * (columns // HD)
    query = jax.ShapeDtypeStruct((devices // 2, tile, HD), jnp.bfloat16)
    fresh = jax.ShapeDtypeStruct((devices // 2, own * 2 * kv_width // HD, HD), jnp.float32)
    return pl.pallas_call(
        functools.partial(project_kernel, counts, crossed, width),
        out_shape=[query, query, fresh, fresh],
        in_specs=[VMEM] * (len(groups) + 3),
        out_specs=[VMEM] * 4,
        scratch_shapes=[
            pltpu.VMEM((devices, rows, depth), jnp.bfloat16),
            pltpu.VMEM((rows, columns), jnp.float32),
            pltpu.VMEM((devices, tile, HD), jnp.float32),
        ],
        compiler_params=pltpu.CompilerParams(vmem_limit_bytes=VMEM_LIMIT),
        cost_estimate=pl.CostEstimate(
            flops=2 * rows * columns * width, bytes_accessed=2 * columns * width, transcendentals=2 * rows * HD
        ),
    )(*[group.blocks for group in groups], *w_query, w_keyval)


def pack_kernel(place, near, far, near_sum, far_sum, out):
    tile, lines = near.shape[1], near_sum.shape[1]
    for slot in range(near.shape[0]):
        chip = look_up(place[slot])
        out[chip, :tile, :] = near[slot]
        out[chip, tile : 2 * tile, :] = far[slot]
        total = near_sum[slot] + far_sum[slot]
        high = total.astype(jnp.bfloat16)
        out[chip, 2 * tile : 2 * tile + lines, :] = high
        out[chip, 2 * tile + lines :, :] = (total - high.astype(jnp.float32)).astype(jnp.bfloat16)


def pack(place, near, far, near_sum, far_sum):
    chips, tile, _ = near.shape
    return pl.pallas_call(
        functools.partial(pack_kernel, place),
        out_shape=jax.ShapeDtypeStruct((chips, 2 * tile + 2 * near_sum.shape[1], HD), jnp.bfloat16),
        in_specs=[VMEM] * 4,
        out_specs=VMEM,
        compiler_params=pltpu.CompilerParams(vmem_limit_bytes=VMEM_LIMIT),
    )(near, far, near_sum, far_sum)


def pair_kernel(place, near, far, out):
    for slot in range(near.shape[0]):
        chip = look_up(place[slot])
        out[chip, 0] = near[slot]
        out[chip, 1] = far[slot]


def pair(place, near, far):
    return pl.pallas_call(
        functools.partial(pair_kernel, place),
        out_shape=jax.ShapeDtypeStruct((near.shape[0], 2, *near.shape[1:]), near.dtype),
        in_specs=[VMEM] * 2,
        out_specs=VMEM,
        compiler_params=pltpu.CompilerParams(vmem_limit_bytes=VMEM_LIMIT),
    )(near, far)


def out_kernel(counts, crossed, *refs):
    slots = slots_of(refs, counts)
    *weights, rest, near, far, last, kept, total, arrived = refs[len(counts) :]
    depth, first, copies = kept.shape[2], rest.shape[0] - last.shape[0], []
    for at in range(last.shape[0] // depth):
        source = rest.at[pl.ds(first + at * depth, depth)]
        copies.append(pltpu.make_async_copy(source, last.at[pl.ds(at * depth, depth)], arrived.at[at]))
        copies[-1].start()
    multiply(slots, weights + [last], depth, total, kept, copies)
    own = near.shape[1]
    for slot in range(len(slots)):
        (near, far)[crossed[slot][0]][crossed[slot][1]] = total[slot * own : (slot + 1) * own].astype(near.dtype)


def project_out(groups, fetched, w_out, devices):
    counts, crossed = group_shape(groups)
    columns = w_out.shape[1]
    own, width = groups[0].blocks.shape[1:]
    chunks = devices // 2
    piece = jax.ShapeDtypeStruct((devices // 2, own, columns), jnp.bfloat16)
    return pl.pallas_call(
        functools.partial(out_kernel, counts, crossed),
        out_shape=[piece, piece],
        in_specs=[VMEM] * (len(groups) + len(fetched)) + [HBM],
        out_specs=[VMEM, VMEM],
        scratch_shapes=[
            pltpu.VMEM((width - sum(part.shape[0] for part in fetched), columns), w_out.dtype),
            pltpu.VMEM((chunks, devices * own, width // chunks), jnp.bfloat16),
            pltpu.VMEM((devices * own, columns), jnp.float32),
            pltpu.SemaphoreType.DMA((chunks,)),
        ],
        compiler_params=pltpu.CompilerParams(vmem_limit_bytes=VMEM_LIMIT),
        cost_estimate=pl.CostEstimate(
            flops=2 * devices * own * columns * width, bytes_accessed=2 * columns * width, transcendentals=0
        ),
    )(*[group.blocks for group in groups], *fetched, pltpu.with_memory_space_constraint(w_out, pltpu.HBM))


def attend_kernel(devices, kv_heads, tile, lengths, pieces, cache, out, fresh, queries, mixed):
    length, width = cache.shape[2:]
    extra = fresh.shape[2]
    half = tile // 2
    per_head = devices // kv_heads * half
    scale = 1.0 / math.sqrt(HD)
    for chip in range(devices // 2):
        for other in range(2):
            piece = pieces[chip, other * tile : (other + 1) * tile, :]
            queries[2 * chip + (lax.axis_index("gx") % 2 + other) % 2] = piece.astype(jnp.float32)
    line = lax.broadcasted_iota(jnp.int32, (8, 1), 0)
    first = jnp.where(line % 4 < 2, lengths[0, :, :1], lengths[1, :, :1])
    cosine, sine = turns((first + line % 2).astype(jnp.float32))
    total = jnp.sum(pieces[:, 2 * tile :, :].astype(jnp.float32), 0)
    total = total[: total.shape[0] // 2] + total[total.shape[0] // 2 :]
    twice = [jnp.concatenate([total[4 * at : 4 * at + 4]] * 2, 0) for at in range(2 * kv_heads)]
    new_keys = jnp.concatenate([turn(part, cosine, sine) for part in twice[:kv_heads]], 1)
    new_values = jnp.concatenate(twice[kv_heads:], 1)
    spot = lax.broadcasted_iota(jnp.int32, (extra, width), 0)
    for row in range(2):
        for which, new in enumerate((new_keys, new_values)):
            spread = jnp.where(spot == 0, new[2 * row : 2 * row + 1, :], 0.0)
            spread = jnp.where(spot == 1, new[2 * row + 1 : 2 * row + 2, :], spread)
            fresh[which, row] = spread.astype(fresh.dtype)
    every = queries[...]
    lines = kv_heads * per_head
    column = lax.broadcasted_iota(jnp.int32, (lines, length), 1)
    new_column = lax.broadcasted_iota(jnp.int32, (lines, extra), 1)
    step = lax.broadcasted_iota(jnp.int32, (lines, extra), 0) % 2
    across = (((1,), (1,)), ((), ()))
    for row in range(2):
        mine = every[:, row * half : row * half + half, :].reshape(lines, HD)
        spread = jnp.concatenate([mine] * kv_heads, 1)
        own_row = lax.broadcasted_iota(jnp.int32, spread.shape, 0) // per_head
        own_lane = lax.broadcasted_iota(jnp.int32, spread.shape, 1) // HD
        spread = jnp.where(own_row == own_lane, spread, 0.0).astype(jnp.bfloat16)
        scores = lax.dot_general(spread, cache[0, row], across, preferred_element_type=jnp.float32) * scale
        scores = jnp.where(column < lengths[row, :1, :1], scores, -jnp.inf)
        new_scores = lax.dot_general(spread, fresh[0, row], across, preferred_element_type=jnp.float32) * scale
        new_scores = jnp.where(new_column <= step, new_scores, -jnp.inf)
        peak = jnp.maximum(jnp.max(scores, 1, keepdims=True), jnp.max(new_scores, 1, keepdims=True))
        weight = jnp.exp(scores - peak)
        new_weight = jnp.exp(new_scores - peak)
        denominator = jnp.sum(weight, 1, keepdims=True) + jnp.sum(new_weight, 1, keepdims=True)
        result = jnp.dot(weight.astype(jnp.bfloat16), cache[1, row], preferred_element_type=jnp.float32)
        result += jnp.dot(new_weight.astype(jnp.bfloat16), fresh[1, row], preferred_element_type=jnp.float32)
        for head in range(kv_heads):
            rows = slice(head * per_head, (head + 1) * per_head)
            part = result[rows, head * HD : (head + 1) * HD] / denominator[rows]
            for query in range(per_head // 2):
                lanes = slice((head * per_head // 2 + query) * HD, (head * per_head // 2 + query + 1) * HD)
                for at in range(2):
                    mixed[at * 2 + row : at * 2 + row + 1, lanes] = part[2 * query + at : 2 * query + at + 1]
    out[...] = mixed[...].astype(out.dtype)


def attend(pieces, tile, cache, lengths, devices):
    length, width = cache.shape[2], cache.shape[3]
    columns = devices * tile // 4 * HD
    return pl.pallas_call(
        functools.partial(attend_kernel, devices, width // HD, tile),
        out_shape=jax.ShapeDtypeStruct((4, columns), jnp.bfloat16),
        in_specs=[VMEM] * 3,
        out_specs=VMEM,
        scratch_shapes=[
            pltpu.VMEM((2, 2, HD, width), cache.dtype),
            pltpu.VMEM((devices, tile, HD), jnp.float32),
            pltpu.VMEM((4, columns), jnp.float32),
        ],
        compiler_params=pltpu.CompilerParams(vmem_limit_bytes=VMEM_LIMIT),
        cost_estimate=pl.CostEstimate(
            flops=8 * 128 * length * width, bytes_accessed=8 * length * width, transcendentals=256 * length
        ),
    )(lengths, pieces, cache)


def finish_kernel(devices, pieces, out):
    columns = pieces.shape[3]
    steps, rows = out.shape[:2]
    for chip in range(devices // 2):
        for other in range(2):
            source = 2 * chip + (lax.axis_index("gx") % 2 + other) % 2
            lanes = pl.ds(pl.multiple_of(source * columns, columns), columns)
            piece = pieces[chip, other].astype(jnp.float32)
            for step in range(steps):
                out[step, :, lanes] = piece[step * rows : (step + 1) * rows].astype(out.dtype)


def finish(pieces, steps, devices):
    own, columns = pieces.shape[2:]
    return pl.pallas_call(
        functools.partial(finish_kernel, devices),
        out_shape=jax.ShapeDtypeStruct((steps, own // steps, devices * columns), jnp.bfloat16),
        in_specs=[VMEM],
        out_specs=VMEM,
        compiler_params=pltpu.CompilerParams(vmem_limit_bytes=VMEM_LIMIT),
    )(pieces)


def body(hidden, norm_gain, w_query, w_keyval, w_out, kv_cache, lengths):
    steps = hidden.shape[0]
    devices = lax.axis_size("gx")

    normed, lengths = norm(hidden, norm_gain, lengths)
    cut = w_query.shape[0] * 3 // 4
    fetched = []

    def bring(*ranges):
        def start(after):
            *arrays, done = fetch(ranges, after)
            fetched.extend(arrays)
            return done

        return start

    part = w_out.shape[0] // 8
    waits = [
        bring((w_query, 0, cut)),
        bring((w_keyval, 0, 2), (kv_cache, 0, 2)),
        bring((w_query, cut, w_query.shape[0] - cut), (w_out, 0, part)),
    ]
    groups = gather(normed, devices, waits, inner_first=True)
    w_first, w_keyval, kv_cache, w_second, w_out_first = fetched
    place = places(groups)
    near, far, near_sum, far_sum = project(groups, [w_first, w_second], w_keyval, devices)
    pieces = pack(place, near, swap_cores(far, devices), near_sum, swap_cores(far_sum, devices))

    mixed = attend(exchange(pieces, devices), near.shape[1], kv_cache, lengths, devices)
    fetched = [w_out_first]
    waits = [bring((w_out, first * part, count * part)) for first, count in ((1, 2), (3, 4))]
    groups = gather_direct(mixed, devices, waits)
    near, far = project_out(groups, fetched, w_out, devices)
    pieces = pair(places(groups), near, swap_cores(far, devices))
    return finish(exchange(pieces, devices), steps, devices)


def rotate(values, positions):
    row_total, head_count, head_width = values.shape
    half_width = head_width // 2
    frequency = ROPE_BASE ** (-2.0 * jnp.arange(half_width, dtype=jnp.float32) / head_width)
    angles = positions[:, None, None] * frequency[None, None, :]
    cosine = jnp.cos(angles)
    sine_part = jnp.sin(angles)
    paired = values.reshape(row_total, head_count, half_width, 2)
    first_half = paired[..., 0]
    second_half = paired[..., 1]
    turned = jnp.stack(
        [
            first_half * cosine - second_half * sine_part,
            first_half * sine_part + second_half * cosine,
        ],
        -1,
    )
    return turned.reshape(row_total, head_count, head_width)


def attend_split_heads(queries, cache_keys, cache_values, lengths, fresh_keys, fresh_values):
    score_scale = 1.0 / math.sqrt(HD)
    fresh_scores = (
        jnp.einsum("rkgd,rskd->rkgs", queries, fresh_keys, preferred_element_type=jnp.float32)
        * score_scale
    )
    cached = (
        jnp.einsum("rkgd,rlkd->rkgl", queries, cache_keys, preferred_element_type=jnp.float32)
        * score_scale
    )
    in_range = jnp.arange(cache_keys.shape[1])[None, :] < lengths[:, None]
    cached = jnp.where(in_range[:, None, None, :], cached, -jnp.inf)
    row_peak = jnp.maximum(cached.max(-1), fresh_scores.max(-1))
    cached_exp = jnp.exp(cached - row_peak[..., None])
    fresh_exp = jnp.exp(fresh_scores - row_peak[..., None])
    denominator = cached_exp.sum(-1) + fresh_exp.sum(-1)
    mixed = jnp.einsum(
        "rkgl,rlkd->rkgd",
        cached_exp.astype(jnp.bfloat16),
        cache_values,
        preferred_element_type=jnp.float32,
    )
    mixed = mixed + jnp.einsum(
        "rkgs,rskd->rkgd",
        fresh_exp.astype(jnp.bfloat16),
        fresh_values,
        preferred_element_type=jnp.float32,
    )
    return (mixed / denominator[..., None]).astype(jnp.bfloat16)


def body_split_heads(hidden, norm_gain, w_query, w_keyval, w_out, kv_cache, lengths):
    step_count, rows_dev, model_width = hidden.shape
    devices = lax.axis_size("gx")
    device_index = lax.axis_index("gx")
    row_slab = w_keyval.shape[1]
    kv_width = w_keyval.shape[2]
    query_cols = w_query.shape[1]
    heads_width = query_cols * devices
    head_count = heads_width // HD
    kv_heads = kv_width // HD
    kv_both = jnp.concatenate([w_keyval[0], w_keyval[1]], 1)
    cache_keys = kv_cache[0].reshape(rows_dev, kv_cache.shape[2], kv_heads, HD)
    cache_values = kv_cache[1].reshape(rows_dev, kv_cache.shape[2], kv_heads, HD)
    states = hidden.astype(jnp.float32)
    scaled = states * lax.rsqrt(jnp.mean(states * states, -1, keepdims=True) + EPSILON)
    normed = (scaled * norm_gain.astype(jnp.float32)).astype(jnp.bfloat16)
    new_keys = []
    new_values = []
    outputs = []
    for step_index in range(step_count):
        shard_piece = lax.all_gather(normed[step_index], "gx", axis=0, tiled=True)
        queries = jnp.dot(shard_piece, w_query, preferred_element_type=jnp.float32)
        own_slab = lax.dynamic_slice_in_dim(shard_piece, device_index * row_slab, row_slab, 1)
        partial_kv = jnp.dot(own_slab, kv_both, preferred_element_type=jnp.float32)
        joined = jnp.concatenate([queries, partial_kv], 1)
        project_query_rows = lax.all_to_all(
            joined[:, :query_cols], "gx", split_axis=0, concat_axis=1, tiled=True
        )
        project_keyval = lax.psum_scatter(
            joined[:, query_cols:], "gx", scatter_dimension=0, tiled=True
        )
        positions = (lengths + step_index).astype(jnp.float32)
        prepare_queries = rotate(
            project_query_rows.reshape(rows_dev, head_count, HD), positions
        ).astype(jnp.bfloat16)
        prepare_queries = prepare_queries.reshape(rows_dev, kv_heads, head_count // kv_heads, HD)
        key_new = rotate(
            project_keyval[:, :kv_width].reshape(rows_dev, kv_heads, HD), positions
        ).astype(jnp.bfloat16)
        value_new = (
            project_keyval[:, kv_width:].reshape(rows_dev, kv_heads, HD).astype(jnp.bfloat16)
        )
        queries, key_new, value_new = (prepare_queries, key_new, value_new)
        new_keys.append(key_new)
        new_values.append(value_new)
        mixed = attend_split_heads(
            queries,
            cache_keys,
            cache_values,
            lengths,
            jnp.stack(new_keys, 1),
            jnp.stack(new_values, 1),
        )
        out_cols = jnp.dot(
            lax.all_gather(mixed.reshape(rows_dev, heads_width), "gx", axis=0, tiled=True),
            w_out,
            preferred_element_type=jnp.float32,
        ).astype(jnp.bfloat16)
        outputs.append(lax.all_to_all(out_cols, "gx", split_axis=0, concat_axis=1, tiled=True))
    return jnp.stack(outputs)


def solution(mesh):
    devices = mesh.shape["gx"]

    def run(*arrays):
        whole_heads = arrays[2].shape[1] % HD == 0 and devices % 2 == 0
        return (body if whole_heads else body_split_heads)(*arrays)

    in_specs = (
        P(None, ("group", "gx"), None),
        P(),
        P(None, "gx"),
        P(None, "gx", None),
        P(None, "gx"),
        P(None, ("group", "gx"), None, None),
        P(("group", "gx")),
    )
    out_specs = P(None, ("group", "gx"), None)
    return jax.shard_map(run, mesh=mesh, in_specs=in_specs, out_specs=out_specs, check_vma=False)
```

```python
import functools
import math

import jax
import jax.numpy as jnp
import numpy as np
from jax import lax
from jax.experimental import pallas as pl
from jax.experimental.pallas import tpu as pltpu
from jax.sharding import PartitionSpec as P

HD = 128
ROPE_BASE = 500000.0
EPSILON = 1e-05
TAG = 128
VMEM_LIMIT = 8 * 1024 * 1024
VMEM = pl.BlockSpec(memory_space=pltpu.VMEM)
SMEM = pl.BlockSpec(memory_space=pltpu.SMEM)
HBM = pl.BlockSpec(memory_space=pltpu.HBM)


def permute(block, target):
    return lax.ppermute(block, "gx", [(int(i), int(t)) for i, t in enumerate(target)])


def moved(source, target):
    result = np.empty_like(source)
    result[target] = source
    return result


class Group:
    def __init__(self, blocks, sources, crossed=False):
        self.blocks, self.sources, self.crossed = blocks, sources, crossed

    def send(self, target, crossed=False):
        return Group(permute(self.blocks, target), [moved(source, target) for source in self.sources], crossed)


def join(groups):
    if len(groups) == 1:
        return groups[0]
    return Group(jnp.concatenate([g.blocks for g in groups], 0), [source for g in groups for source in g.sources])


def ring_order(size):
    if size > 4:
        return list(range(size))
    return list(range(0, size, 2)) + list(range(1, size, 2))[::-1]


def axes_of(devices):
    chips, inner = devices // 2, 1
    while inner * inner * 4 <= chips and chips % (inner * 2) == 0:
        inner *= 2
    sizes = (chips // inner, inner, 2)
    place = np.arange(devices).reshape(sizes)
    result = []
    for axis, size in enumerate(sizes):
        order = ring_order(size)
        after = np.empty(size, int)
        for here, there in zip(order, order[1:] + order[:1]):
            after[here] = there
        before = np.argsort(after)
        result.append((size, np.take(place, after, axis).ravel(), np.take(place, before, axis).ravel()))
    return result


def ring(group, axis):
    size, following, preceding = axis
    groups = []
    forward = backward = group
    for step in range(1, size // 2 + 1):
        forward = forward.send(following)
        groups.append(forward)
        if 2 * step < size:
            backward = backward.send(preceding)
            groups.append(backward)
    return groups


def gather(block, devices, meanwhile=(), inner_first=False):
    (size, following, preceding), inner, core = axes_of(devices)
    own = Group(block[None], [np.arange(devices)])
    near = ring(own, inner)
    chip_pair = join([own] + near)
    groups = [own] + near + [chip_pair.send(core[1], crossed=True)]
    forward = backward = own
    for step in range(1, size // 2 + 1):
        before = forward.blocks
        arrived = [forward.send(following)] + ([backward.send(preceding)] if 2 * step < size else [])
        forward, backward = arrived[0], arrived[-1]
        if step <= len(meanwhile):
            onward = (step < size // 2) + (2 * step + 2 < size)
            chips, *alone = hold(arrived, 0 if inner_first else onward, meanwhile[step - 1](before))
            if inner_first:
                alone = [hold([group], 0, chip_pair.blocks)[0] for group in arrived[:onward]]
            forward, backward = (alone + [forward])[0], (alone + [backward])[-1]
        else:
            chips = join(arrived)
        reached = [chips] + ring(chips, inner)
        if step == size // 2 < len(meanwhile):
            reached[-1:] = hold(reached[-1:], 0, meanwhile[step](chips.blocks))
        groups += reached + [group.send(core[1], crossed=True) for group in reached]
    return groups


def gather_direct(block, devices, meanwhile):
    (size, following, _), inner, core = axes_of(devices)
    own = Group(block[None], [np.arange(devices)])
    near = ring(own, inner)
    groups = [own] + near + [join([own] + near).send(core[1], crossed=True)]
    arrived, target = [], following
    for _ in range(size - 1):
        arrived.append(own.send(target))
        target = following[target]
    reached = hold(arrived, 0, meanwhile[0](block), *[group.blocks for group in near])
    beside = ring(reached[0], inner)
    if beside:
        beside[-1:] = hold(beside[-1:], 0, meanwhile[1](reached[0].blocks), groups[-1].blocks)
    reached += beside
    return groups + reached + [group.send(core[1], crossed=True) for group in reached]


def hold_kernel(count, waits, *refs):
    stacked, *alone = refs[count + waits :]
    first = 0
    for ref in refs[:count]:
        for at in range(ref.shape[0]):
            stacked[first + at] = ref[at]
        first += ref.shape[0]
    for at in range(len(alone)):
        alone[at][...] = refs[at][...]


def hold(groups, onward, *after):
    blocks = [group.blocks for group in groups]
    stacked, *alone = pl.pallas_call(
        functools.partial(hold_kernel, len(blocks), len(after)),
        out_shape=[jax.ShapeDtypeStruct((sum(block.shape[0] for block in blocks), *blocks[0].shape[1:]), blocks[0].dtype)]
        + [jax.ShapeDtypeStruct(block.shape, block.dtype) for block in blocks[:onward]],
        in_specs=[VMEM] * len(blocks) + [pl.BlockSpec(memory_space=pl.ANY)] * len(after),
        out_specs=[VMEM] * (onward + 1),
        compiler_params=pltpu.CompilerParams(vmem_limit_bytes=VMEM_LIMIT),
    )(*blocks, *after)
    sources = [group.sources for group in groups]
    return [Group(stacked, sum(sources, []))] + [Group(block, source) for block, source in zip(alone, sources)]


def swap_cores(block, devices):
    return permute(block, np.arange(devices) ^ 1)


def exchange(pieces, devices):
    same_core = [list(range(core, devices, 2)) for core in range(2)]
    return lax.all_to_all(pieces, "gx", 0, 0, axis_index_groups=same_core, tiled=True)


def places(groups):
    return [(source // 2)[::2] for group in groups if not group.crossed for source in group.sources]


def look_up(values):
    chip = lax.axis_index("gx") // 2
    found = jnp.int32(int(values[0]))
    for at in range(1, len(values)):
        found = jnp.where(chip == at, jnp.int32(int(values[at])), found)
    return found


def norm_kernel(lengths_far, hidden_far, gain_far, out, spread, lengths, hidden, gain, arrived):
    copies = [
        pltpu.make_async_copy(far, near, arrived.at[at])
        for at, (far, near) in enumerate(((hidden_far, hidden), (gain_far, gain), (lengths_far, lengths)))
    ]
    for copy in copies:
        copy.start()
    copies[0].wait()
    states = hidden[...].astype(jnp.float32)
    scale = lax.rsqrt(jnp.mean(states * states, -1, keepdims=True) + EPSILON)
    copies[1].wait()
    normed = states * scale * gain[...].astype(jnp.float32).reshape(1, 1, gain.shape[0])
    steps, rows, width = normed.shape
    lines = [normed[step, row : row + 1] for row in range(rows) for step in range(steps)]
    out[:, :width] = jnp.concatenate(lines, 0).astype(out.dtype)
    line = lax.broadcasted_iota(jnp.int32, (steps * rows, TAG), 0)
    lane = lax.broadcasted_iota(jnp.int32, (steps * rows, TAG), 1)
    position = line % steps
    copies[2].wait()
    for row in range(rows):
        position = jnp.where(line // steps == row, position + lengths[row], position)
    tag = jnp.where(lane == 0, position // 32, position % 32)
    out[:, width:] = tag.astype(jnp.float32).astype(out.dtype)
    for row in range(spread.shape[0]):
        spread[row] = jnp.full(spread.shape[1:], lengths[row], spread.dtype)


def norm(hidden, gain, lengths):
    steps, rows, width = hidden.shape
    return pl.pallas_call(
        norm_kernel,
        out_shape=[
            jax.ShapeDtypeStruct((steps * rows, width + TAG), jnp.bfloat16),
            jax.ShapeDtypeStruct((rows, 8, HD), jnp.int32),
        ],
        in_specs=[HBM] * 3,
        out_specs=[VMEM] * 2,
        scratch_shapes=[
            pltpu.SMEM(lengths.shape, lengths.dtype),
            pltpu.VMEM(hidden.shape, hidden.dtype),
            pltpu.VMEM(gain.shape, gain.dtype),
            pltpu.SemaphoreType.DMA((3,)),
        ],
        compiler_params=pltpu.CompilerParams(vmem_limit_bytes=VMEM_LIMIT),
        cost_estimate=pl.CostEstimate(flops=6 * steps * rows * width, bytes_accessed=4 * steps * rows * width, transcendentals=0),
    )(*[pltpu.with_memory_space_constraint(array, pltpu.HBM) for array in (lengths, hidden, gain)])


def fetch_kernel(firsts, chunks, *refs):
    copies, count, arrived = [], len(firsts), refs[-1]
    refs[-2][...] = jnp.zeros_like(refs[-2])
    for first, far, near in zip(firsts, refs[:count], refs[count + 1 : 2 * count + 1]):
        size = near.shape[0] // min(chunks, near.shape[0])
        for at in range(0, near.shape[0], size):
            source = far.at[pl.ds(first + at, size)]
            copies.append(pltpu.make_async_copy(source, near.at[pl.ds(at, size)], arrived.at[len(copies)]))
            copies[-1].start()
    for copy in copies:
        copy.wait()


def fetch(ranges, after):
    chunks = 8
    arrays = [array for array, _, _ in ranges]
    shapes = [(count, *array.shape[1:]) for array, _, count in ranges]
    return pl.pallas_call(
        functools.partial(fetch_kernel, [first for _, first, _ in ranges], chunks),
        out_shape=[pltpu.VMEM(shape, array.dtype) for shape, array in zip(shapes, arrays)]
        + [jax.ShapeDtypeStruct((8, HD), jnp.float32)],
        in_specs=[HBM] * len(arrays) + [pl.BlockSpec(memory_space=pl.ANY)],
        out_specs=[VMEM] * (len(arrays) + 1),
        scratch_shapes=[pltpu.SemaphoreType.DMA((chunks * len(arrays),))],
        compiler_params=pltpu.CompilerParams(vmem_limit_bytes=VMEM_LIMIT),
        cost_estimate=pl.CostEstimate(
            flops=0, bytes_accessed=sum(2 * math.prod(shape) for shape in shapes), transcendentals=0
        ),
    )(*[pltpu.with_memory_space_constraint(array, pltpu.HBM) for array in arrays], after)


def slots_of(refs, counts):
    return [(ref, at) for ref, count in zip(refs, counts) for at in range(count)]


def assemble(slots, first, width):
    lanes = slice(first, first + width)
    return jnp.concatenate([ref[at, :, lanes] for ref, at in slots], 0)


def multiply(slots, weights, depth, total, kept):
    total[...] = jnp.zeros_like(total)
    chunk = 0
    for part in weights:
        for at in range(0, part.shape[0], depth):
            kept[chunk] = assemble(slots, chunk * depth, depth)
            total[...] += jnp.dot(kept[chunk], part[at : at + depth, :], preferred_element_type=jnp.float32)
            chunk += 1


def turns(positions):
    shape = (positions.shape[0], HD)
    lane = lax.broadcasted_iota(jnp.int32, shape, 1)
    pair = (lane // 2).astype(jnp.float32)
    angles = positions * jnp.exp(pair * (-2.0 * math.log(ROPE_BASE) / HD))
    return jnp.cos(angles), jnp.where(lane % 2 == 0, -1.0, 1.0) * jnp.sin(angles)


def turn(values, cosine, sine):
    lanes = values.shape[-1]
    even = lax.broadcasted_iota(jnp.int32, values.shape, 1) % 2 == 0
    swapped = jnp.where(even, pltpu.roll(values, lanes - 1, 1), pltpu.roll(values, 1, 1))
    return values * cosine + swapped * sine


def project_kernel(counts, crossed, width, *refs):
    slots = slots_of(refs, counts)
    first, second, keyval, *outs = refs[len(counts) : len(counts) + 7]
    kept, total, packed = refs[len(counts) + 7 :]
    queries, fresh = outs[:2], outs[2:]
    depth = keyval.shape[1]
    tags = jnp.concatenate([ref[at, :, width:].astype(jnp.float32) for ref, at in slots], 0)
    cosine, sine = turns(tags[:, 0:1] * 32.0 + tags[:, 1:2])
    multiply(slots, [first, second], depth, total, kept)
    own = kept[lax.axis_index("gx")]
    blocks = keyval.shape[2] // HD
    for which in range(2):
        term = jnp.dot(own, keyval[which], preferred_element_type=jnp.float32)
        for slot in range(len(slots)):
            for at in range(blocks):
                row = (which * blocks + at) * 4
                fresh[crossed[slot][0]][crossed[slot][1], row : row + 4, :] = term[
                    slot * 4 : slot * 4 + 4, at * HD : (at + 1) * HD
                ]
    heads = total.shape[1] // HD
    for head in range(heads):
        turned = turn(total[:, head * HD : (head + 1) * HD], cosine, sine)
        for slot in range(len(slots)):
            for row in range(2):
                line, at = row * 2 * heads + head * 2, slot * 4 + row * 2
                packed[slot, line : line + 2, :] = turned[at : at + 2, :]
    for slot in range(len(slots)):
        queries[crossed[slot][0]][crossed[slot][1]] = packed[slot].astype(jnp.bfloat16)


def group_shape(groups):
    counts = [len(group.sources) for group in groups]
    seen, order = [0, 0], []
    for group, count in zip(groups, counts):
        for _ in range(count):
            order.append((int(group.crossed), seen[group.crossed]))
            seen[group.crossed] += 1
    return counts, order


def project(groups, w_query, w_keyval, devices):
    counts, crossed = group_shape(groups)
    columns = w_query[0].shape[1]
    depth, kv_width = w_keyval.shape[1:]
    own, width = groups[0].blocks.shape[1], devices * depth
    rows, tile = devices * own, own * (columns // HD)
    query = jax.ShapeDtypeStruct((devices // 2, tile, HD), jnp.bfloat16)
    fresh = jax.ShapeDtypeStruct((devices // 2, own * 2 * kv_width // HD, HD), jnp.float32)
    return pl.pallas_call(
        functools.partial(project_kernel, counts, crossed, width),
        out_shape=[query, query, fresh, fresh],
        in_specs=[VMEM] * (len(groups) + 3),
        out_specs=[VMEM] * 4,
        scratch_shapes=[
            pltpu.VMEM((devices, rows, depth), jnp.bfloat16),
            pltpu.VMEM((rows, columns), jnp.float32),
            pltpu.VMEM((devices, tile, HD), jnp.float32),
        ],
        compiler_params=pltpu.CompilerParams(vmem_limit_bytes=VMEM_LIMIT),
        cost_estimate=pl.CostEstimate(
            flops=2 * rows * columns * width, bytes_accessed=2 * columns * width, transcendentals=2 * rows * HD
        ),
    )(*[group.blocks for group in groups], *w_query, w_keyval)


def pack_kernel(place, near, far, near_sum, far_sum, out):
    tile, lines = near.shape[1], near_sum.shape[1]
    for slot in range(near.shape[0]):
        chip = look_up(place[slot])
        out[chip, :tile, :] = near[slot]
        out[chip, tile : 2 * tile, :] = far[slot]
        total = near_sum[slot] + far_sum[slot]
        high = total.astype(jnp.bfloat16)
        out[chip, 2 * tile : 2 * tile + lines, :] = high
        out[chip, 2 * tile + lines :, :] = (total - high.astype(jnp.float32)).astype(jnp.bfloat16)


def pack(place, near, far, near_sum, far_sum):
    chips, tile, _ = near.shape
    return pl.pallas_call(
        functools.partial(pack_kernel, place),
        out_shape=jax.ShapeDtypeStruct((chips, 2 * tile + 2 * near_sum.shape[1], HD), jnp.bfloat16),
        in_specs=[VMEM] * 4,
        out_specs=VMEM,
        compiler_params=pltpu.CompilerParams(vmem_limit_bytes=VMEM_LIMIT),
    )(near, far, near_sum, far_sum)


def pair_kernel(place, near, far, out):
    for slot in range(near.shape[0]):
        chip = look_up(place[slot])
        out[chip, 0] = near[slot]
        out[chip, 1] = far[slot]


def pair(place, near, far):
    return pl.pallas_call(
        functools.partial(pair_kernel, place),
        out_shape=jax.ShapeDtypeStruct((near.shape[0], 2, *near.shape[1:]), near.dtype),
        in_specs=[VMEM] * 2,
        out_specs=VMEM,
        compiler_params=pltpu.CompilerParams(vmem_limit_bytes=VMEM_LIMIT),
    )(near, far)


def out_kernel(counts, crossed, *refs):
    slots = slots_of(refs, counts)
    *weights, near, far, kept, total = refs[len(counts) :]
    multiply(slots, weights, kept.shape[2], total, kept)
    own = near.shape[1]
    for slot in range(len(slots)):
        (near, far)[crossed[slot][0]][crossed[slot][1]] = total[slot * own : (slot + 1) * own].astype(near.dtype)


def project_out(groups, w_out, devices):
    counts, crossed = group_shape(groups)
    columns = w_out[0].shape[1]
    own, width = groups[0].blocks.shape[1:]
    chunks = devices // 2
    piece = jax.ShapeDtypeStruct((devices // 2, own, columns), jnp.bfloat16)
    return pl.pallas_call(
        functools.partial(out_kernel, counts, crossed),
        out_shape=[piece, piece],
        in_specs=[VMEM] * (len(groups) + len(w_out)),
        out_specs=[VMEM, VMEM],
        scratch_shapes=[
            pltpu.VMEM((chunks, devices * own, width // chunks), jnp.bfloat16),
            pltpu.VMEM((devices * own, columns), jnp.float32),
        ],
        compiler_params=pltpu.CompilerParams(vmem_limit_bytes=VMEM_LIMIT),
        cost_estimate=pl.CostEstimate(
            flops=2 * devices * own * columns * width, bytes_accessed=2 * columns * width, transcendentals=0
        ),
    )(*[group.blocks for group in groups], *w_out)


def attend_kernel(devices, kv_heads, tile, lengths, pieces, cache, out, fresh, queries, mixed):
    length, width = cache.shape[2:]
    extra = fresh.shape[2]
    half = tile // 2
    per_head = devices // kv_heads * half
    scale = 1.0 / math.sqrt(HD)
    for chip in range(devices // 2):
        for other in range(2):
            piece = pieces[chip, other * tile : (other + 1) * tile, :]
            queries[2 * chip + (lax.axis_index("gx") % 2 + other) % 2] = piece.astype(jnp.float32)
    line = lax.broadcasted_iota(jnp.int32, (8, 1), 0)
    first = jnp.where(line % 4 < 2, lengths[0, :, :1], lengths[1, :, :1])
    cosine, sine = turns((first + line % 2).astype(jnp.float32))
    total = jnp.sum(pieces[:, 2 * tile :, :].astype(jnp.float32), 0)
    total = total[: total.shape[0] // 2] + total[total.shape[0] // 2 :]
    twice = [jnp.concatenate([total[4 * at : 4 * at + 4]] * 2, 0) for at in range(2 * kv_heads)]
    new_keys = jnp.concatenate([turn(part, cosine, sine) for part in twice[:kv_heads]], 1)
    new_values = jnp.concatenate(twice[kv_heads:], 1)
    spot = lax.broadcasted_iota(jnp.int32, (extra, width), 0)
    for row in range(2):
        for which, new in enumerate((new_keys, new_values)):
            spread = jnp.where(spot == 0, new[2 * row : 2 * row + 1, :], 0.0)
            spread = jnp.where(spot == 1, new[2 * row + 1 : 2 * row + 2, :], spread)
            fresh[which, row] = spread.astype(fresh.dtype)
    every = queries[...]
    lines = kv_heads * per_head
    column = lax.broadcasted_iota(jnp.int32, (lines, length), 1)
    new_column = lax.broadcasted_iota(jnp.int32, (lines, extra), 1)
    step = lax.broadcasted_iota(jnp.int32, (lines, extra), 0) % 2
    across = (((1,), (1,)), ((), ()))
    for row in range(2):
        mine = every[:, row * half : row * half + half, :].reshape(lines, HD)
        spread = jnp.concatenate([mine] * kv_heads, 1)
        own_row = lax.broadcasted_iota(jnp.int32, spread.shape, 0) // per_head
        own_lane = lax.broadcasted_iota(jnp.int32, spread.shape, 1) // HD
        spread = jnp.where(own_row == own_lane, spread, 0.0).astype(jnp.bfloat16)
        scores = lax.dot_general(spread, cache[0, row], across, preferred_element_type=jnp.float32) * scale
        scores = jnp.where(column < lengths[row, :1, :1], scores, -jnp.inf)
        new_scores = lax.dot_general(spread, fresh[0, row], across, preferred_element_type=jnp.float32) * scale
        new_scores = jnp.where(new_column <= step, new_scores, -jnp.inf)
        peak = jnp.maximum(jnp.max(scores, 1, keepdims=True), jnp.max(new_scores, 1, keepdims=True))
        weight = jnp.exp(scores - peak)
        new_weight = jnp.exp(new_scores - peak)
        denominator = jnp.sum(weight, 1, keepdims=True) + jnp.sum(new_weight, 1, keepdims=True)
        result = jnp.dot(weight.astype(jnp.bfloat16), cache[1, row], preferred_element_type=jnp.float32)
        result += jnp.dot(new_weight.astype(jnp.bfloat16), fresh[1, row], preferred_element_type=jnp.float32)
        for head in range(kv_heads):
            rows = slice(head * per_head, (head + 1) * per_head)
            part = result[rows, head * HD : (head + 1) * HD] / denominator[rows]
            for query in range(per_head // 2):
                lanes = slice((head * per_head // 2 + query) * HD, (head * per_head // 2 + query + 1) * HD)
                for at in range(2):
                    mixed[at * 2 + row : at * 2 + row + 1, lanes] = part[2 * query + at : 2 * query + at + 1]
    out[...] = mixed[...].astype(out.dtype)


def attend(pieces, tile, cache, lengths, devices):
    length, width = cache.shape[2], cache.shape[3]
    columns = devices * tile // 4 * HD
    return pl.pallas_call(
        functools.partial(attend_kernel, devices, width // HD, tile),
        out_shape=jax.ShapeDtypeStruct((4, columns), jnp.bfloat16),
        in_specs=[VMEM] * 3,
        out_specs=VMEM,
        scratch_shapes=[
            pltpu.VMEM((2, 2, HD, width), cache.dtype),
            pltpu.VMEM((devices, tile, HD), jnp.float32),
            pltpu.VMEM((4, columns), jnp.float32),
        ],
        compiler_params=pltpu.CompilerParams(vmem_limit_bytes=VMEM_LIMIT),
        cost_estimate=pl.CostEstimate(
            flops=8 * 128 * length * width, bytes_accessed=8 * length * width, transcendentals=256 * length
        ),
    )(lengths, pieces, cache)


def finish_kernel(devices, pieces, out):
    columns = pieces.shape[3]
    steps, rows = out.shape[:2]
    for chip in range(devices // 2):
        for other in range(2):
            source = 2 * chip + (lax.axis_index("gx") % 2 + other) % 2
            lanes = pl.ds(pl.multiple_of(source * columns, columns), columns)
            piece = pieces[chip, other].astype(jnp.float32)
            for step in range(steps):
                out[step, :, lanes] = piece[step * rows : (step + 1) * rows].astype(out.dtype)


def finish(pieces, steps, devices):
    own, columns = pieces.shape[2:]
    return pl.pallas_call(
        functools.partial(finish_kernel, devices),
        out_shape=jax.ShapeDtypeStruct((steps, own // steps, devices * columns), jnp.bfloat16),
        in_specs=[VMEM],
        out_specs=VMEM,
        compiler_params=pltpu.CompilerParams(vmem_limit_bytes=VMEM_LIMIT),
    )(pieces)


def body(hidden, norm_gain, w_query, w_keyval, w_out, kv_cache, lengths):
    steps = hidden.shape[0]
    devices = lax.axis_size("gx")

    normed, lengths = norm(hidden, norm_gain, lengths)
    cut = w_query.shape[0] * 3 // 4
    fetched = []

    def bring(*ranges):
        def start(after):
            *arrays, done = fetch(ranges, after)
            fetched.extend(arrays)
            return done

        return start

    part = w_out.shape[0] // 8
    waits = [
        bring((w_query, 0, cut)),
        bring((w_keyval, 0, 2), (kv_cache, 0, 2)),
        bring((w_query, cut, w_query.shape[0] - cut), (w_out, 0, 2 * part)),
    ]
    groups = gather(normed, devices, waits, inner_first=True)
    w_first, w_keyval, kv_cache, w_second, w_out_first = fetched
    place = places(groups)
    near, far, near_sum, far_sum = project(groups, [w_first, w_second], w_keyval, devices)
    pieces = pack(place, near, swap_cores(far, devices), near_sum, swap_cores(far_sum, devices))

    mixed = attend(exchange(pieces, devices), near.shape[1], kv_cache, lengths, devices)
    fetched = [w_out_first]
    waits = [bring((w_out, first * part, count * part)) for first, count in ((2, 2), (4, 4))]
    groups = gather_direct(mixed, devices, waits)
    near, far = project_out(groups, fetched, devices)
    pieces = pair(places(groups), near, swap_cores(far, devices))
    return finish(exchange(pieces, devices), steps, devices)


def rotate(values, positions):
    row_total, head_count, head_width = values.shape
    half_width = head_width // 2
    frequency = ROPE_BASE ** (-2.0 * jnp.arange(half_width, dtype=jnp.float32) / head_width)
    angles = positions[:, None, None] * frequency[None, None, :]
    cosine = jnp.cos(angles)
    sine_part = jnp.sin(angles)
    paired = values.reshape(row_total, head_count, half_width, 2)
    first_half = paired[..., 0]
    second_half = paired[..., 1]
    turned = jnp.stack(
        [
            first_half * cosine - second_half * sine_part,
            first_half * sine_part + second_half * cosine,
        ],
        -1,
    )
    return turned.reshape(row_total, head_count, head_width)


def attend_split_heads(queries, cache_keys, cache_values, lengths, fresh_keys, fresh_values):
    score_scale = 1.0 / math.sqrt(HD)
    fresh_scores = (
        jnp.einsum("rkgd,rskd->rkgs", queries, fresh_keys, preferred_element_type=jnp.float32)
        * score_scale
    )
    cached = (
        jnp.einsum("rkgd,rlkd->rkgl", queries, cache_keys, preferred_element_type=jnp.float32)
        * score_scale
    )
    in_range = jnp.arange(cache_keys.shape[1])[None, :] < lengths[:, None]
    cached = jnp.where(in_range[:, None, None, :], cached, -jnp.inf)
    row_peak = jnp.maximum(cached.max(-1), fresh_scores.max(-1))
    cached_exp = jnp.exp(cached - row_peak[..., None])
    fresh_exp = jnp.exp(fresh_scores - row_peak[..., None])
    denominator = cached_exp.sum(-1) + fresh_exp.sum(-1)
    mixed = jnp.einsum(
        "rkgl,rlkd->rkgd",
        cached_exp.astype(jnp.bfloat16),
        cache_values,
        preferred_element_type=jnp.float32,
    )
    mixed = mixed + jnp.einsum(
        "rkgs,rskd->rkgd",
        fresh_exp.astype(jnp.bfloat16),
        fresh_values,
        preferred_element_type=jnp.float32,
    )
    return (mixed / denominator[..., None]).astype(jnp.bfloat16)


def body_split_heads(hidden, norm_gain, w_query, w_keyval, w_out, kv_cache, lengths):
    step_count, rows_dev, model_width = hidden.shape
    devices = lax.axis_size("gx")
    device_index = lax.axis_index("gx")
    row_slab = w_keyval.shape[1]
    kv_width = w_keyval.shape[2]
    query_cols = w_query.shape[1]
    heads_width = query_cols * devices
    head_count = heads_width // HD
    kv_heads = kv_width // HD
    kv_both = jnp.concatenate([w_keyval[0], w_keyval[1]], 1)
    cache_keys = kv_cache[0].reshape(rows_dev, kv_cache.shape[2], kv_heads, HD)
    cache_values = kv_cache[1].reshape(rows_dev, kv_cache.shape[2], kv_heads, HD)
    states = hidden.astype(jnp.float32)
    scaled = states * lax.rsqrt(jnp.mean(states * states, -1, keepdims=True) + EPSILON)
    normed = (scaled * norm_gain.astype(jnp.float32)).astype(jnp.bfloat16)
    new_keys = []
    new_values = []
    outputs = []
    for step_index in range(step_count):
        shard_piece = lax.all_gather(normed[step_index], "gx", axis=0, tiled=True)
        queries = jnp.dot(shard_piece, w_query, preferred_element_type=jnp.float32)
        own_slab = lax.dynamic_slice_in_dim(shard_piece, device_index * row_slab, row_slab, 1)
        partial_kv = jnp.dot(own_slab, kv_both, preferred_element_type=jnp.float32)
        joined = jnp.concatenate([queries, partial_kv], 1)
        project_query_rows = lax.all_to_all(
            joined[:, :query_cols], "gx", split_axis=0, concat_axis=1, tiled=True
        )
        project_keyval = lax.psum_scatter(
            joined[:, query_cols:], "gx", scatter_dimension=0, tiled=True
        )
        positions = (lengths + step_index).astype(jnp.float32)
        prepare_queries = rotate(
            project_query_rows.reshape(rows_dev, head_count, HD), positions
        ).astype(jnp.bfloat16)
        prepare_queries = prepare_queries.reshape(rows_dev, kv_heads, head_count // kv_heads, HD)
        key_new = rotate(
            project_keyval[:, :kv_width].reshape(rows_dev, kv_heads, HD), positions
        ).astype(jnp.bfloat16)
        value_new = (
            project_keyval[:, kv_width:].reshape(rows_dev, kv_heads, HD).astype(jnp.bfloat16)
        )
        queries, key_new, value_new = (prepare_queries, key_new, value_new)
        new_keys.append(key_new)
        new_values.append(value_new)
        mixed = attend_split_heads(
            queries,
            cache_keys,
            cache_values,
            lengths,
            jnp.stack(new_keys, 1),
            jnp.stack(new_values, 1),
        )
        out_cols = jnp.dot(
            lax.all_gather(mixed.reshape(rows_dev, heads_width), "gx", axis=0, tiled=True),
            w_out,
            preferred_element_type=jnp.float32,
        ).astype(jnp.bfloat16)
        outputs.append(lax.all_to_all(out_cols, "gx", split_axis=0, concat_axis=1, tiled=True))
    return jnp.stack(outputs)


def solution(mesh):
    devices = mesh.shape["gx"]

    def run(*arrays):
        whole_heads = arrays[2].shape[1] % HD == 0 and devices % 2 == 0
        return (body if whole_heads else body_split_heads)(*arrays)

    in_specs = (
        P(None, ("group", "gx"), None),
        P(),
        P(None, "gx"),
        P(None, "gx", None),
        P(None, "gx"),
        P(None, ("group", "gx"), None, None),
        P(("group", "gx")),
    )
    out_specs = P(None, ("group", "gx"), None)
    return jax.shard_map(run, mesh=mesh, in_specs=in_specs, out_specs=out_specs, check_vma=False)
```

```python
import functools
import math

import jax
import jax.numpy as jnp
import numpy as np
from jax import lax
from jax.experimental import pallas as pl
from jax.experimental.pallas import tpu as pltpu
from jax.sharding import PartitionSpec as P

HD = 128
ROPE_BASE = 500000.0
EPSILON = 1e-05
TAG = 128
VMEM_LIMIT = 8 * 1024 * 1024
VMEM = pl.BlockSpec(memory_space=pltpu.VMEM)
SMEM = pl.BlockSpec(memory_space=pltpu.SMEM)
HBM = pl.BlockSpec(memory_space=pltpu.HBM)


def permute(block, target):
    return lax.ppermute(block, "gx", [(int(i), int(t)) for i, t in enumerate(target)])


def moved(source, target):
    result = np.empty_like(source)
    result[target] = source
    return result


class Group:
    def __init__(self, blocks, sources, crossed=False):
        self.blocks, self.sources, self.crossed = blocks, sources, crossed

    def send(self, target, crossed=False):
        return Group(permute(self.blocks, target), [moved(source, target) for source in self.sources], crossed)


def join(groups):
    if len(groups) == 1:
        return groups[0]
    return Group(jnp.concatenate([g.blocks for g in groups], 0), [source for g in groups for source in g.sources])


def ring_order(size):
    if size > 4:
        return list(range(size))
    return list(range(0, size, 2)) + list(range(1, size, 2))[::-1]


def axes_of(devices):
    chips, inner = devices // 2, 1
    while inner * inner * 4 <= chips and chips % (inner * 2) == 0:
        inner *= 2
    sizes = (chips // inner, inner, 2)
    place = np.arange(devices).reshape(sizes)
    result = []
    for axis, size in enumerate(sizes):
        order = ring_order(size)
        after = np.empty(size, int)
        for here, there in zip(order, order[1:] + order[:1]):
            after[here] = there
        before = np.argsort(after)
        result.append((size, np.take(place, after, axis).ravel(), np.take(place, before, axis).ravel()))
    return result


def ring(group, axis):
    size, following, preceding = axis
    groups = []
    forward = backward = group
    for step in range(1, size // 2 + 1):
        forward = forward.send(following)
        groups.append(forward)
        if 2 * step < size:
            backward = backward.send(preceding)
            groups.append(backward)
    return groups


def gather(block, devices, meanwhile=(), inner_first=False):
    (size, following, preceding), inner, core = axes_of(devices)
    own = Group(block[None], [np.arange(devices)])
    near = ring(own, inner)
    chip_pair = join([own] + near)
    groups = [own] + near + [chip_pair.send(core[1], crossed=True)]
    forward = backward = own
    for step in range(1, size // 2 + 1):
        before = forward.blocks
        arrived = [forward.send(following)] + ([backward.send(preceding)] if 2 * step < size else [])
        forward, backward = arrived[0], arrived[-1]
        if step <= len(meanwhile):
            onward = (step < size // 2) + (2 * step + 2 < size)
            chips, *alone = hold(arrived, 0 if inner_first else onward, meanwhile[step - 1](before))
            if inner_first:
                alone = [hold([group], 0, chip_pair.blocks)[0] for group in arrived[:onward]]
            forward, backward = (alone + [forward])[0], (alone + [backward])[-1]
        else:
            chips = join(arrived)
        reached = [chips] + ring(chips, inner)
        if step == size // 2 < len(meanwhile):
            reached[-1:] = hold(reached[-1:], 0, meanwhile[step](chips.blocks))
        groups += reached + [group.send(core[1], crossed=True) for group in reached]
    return groups


def gather_direct(block, devices, meanwhile):
    (size, following, _), inner, core = axes_of(devices)
    own = Group(block[None], [np.arange(devices)])
    near = ring(own, inner)
    groups = [own] + near + [join([own] + near).send(core[1], crossed=True)]
    arrived, target = [], following
    for _ in range(size - 1):
        arrived.append(own.send(target))
        target = following[target]
    reached = hold(arrived, 0, meanwhile[0](block), *[group.blocks for group in near])
    beside = ring(reached[0], inner)
    if beside:
        beside[-1:] = hold(beside[-1:], 0, meanwhile[1](reached[0].blocks), groups[-1].blocks)
    reached += beside
    return groups + reached + [group.send(core[1], crossed=True) for group in reached]


def hold_kernel(count, waits, *refs):
    stacked, *alone = refs[count + waits :]
    first = 0
    for ref in refs[:count]:
        for at in range(ref.shape[0]):
            stacked[first + at] = ref[at]
        first += ref.shape[0]
    for at in range(len(alone)):
        alone[at][...] = refs[at][...]


def hold(groups, onward, *after):
    blocks = [group.blocks for group in groups]
    stacked, *alone = pl.pallas_call(
        functools.partial(hold_kernel, len(blocks), len(after)),
        out_shape=[jax.ShapeDtypeStruct((sum(block.shape[0] for block in blocks), *blocks[0].shape[1:]), blocks[0].dtype)]
        + [jax.ShapeDtypeStruct(block.shape, block.dtype) for block in blocks[:onward]],
        in_specs=[VMEM] * len(blocks) + [pl.BlockSpec(memory_space=pl.ANY)] * len(after),
        out_specs=[VMEM] * (onward + 1),
        compiler_params=pltpu.CompilerParams(vmem_limit_bytes=VMEM_LIMIT),
    )(*blocks, *after)
    sources = [group.sources for group in groups]
    return [Group(stacked, sum(sources, []))] + [Group(block, source) for block, source in zip(alone, sources)]


def swap_cores(block, devices):
    return permute(block, np.arange(devices) ^ 1)


def exchange(pieces, devices):
    same_core = [list(range(core, devices, 2)) for core in range(2)]
    return lax.all_to_all(pieces, "gx", 0, 0, axis_index_groups=same_core, tiled=True)


def places(groups):
    return [(source // 2)[::2] for group in groups if not group.crossed for source in group.sources]


def look_up(values):
    chip = lax.axis_index("gx") // 2
    found = jnp.int32(int(values[0]))
    for at in range(1, len(values)):
        found = jnp.where(chip == at, jnp.int32(int(values[at])), found)
    return found


def norm_kernel(lengths_far, hidden_far, gain_far, out, spread, lengths, hidden, gain, arrived):
    copies = [
        pltpu.make_async_copy(far, near, arrived.at[at])
        for at, (far, near) in enumerate(((hidden_far, hidden), (gain_far, gain), (lengths_far, lengths)))
    ]
    for copy in copies:
        copy.start()
    copies[0].wait()
    states = hidden[...].astype(jnp.float32)
    scale = lax.rsqrt(jnp.mean(states * states, -1, keepdims=True) + EPSILON)
    copies[1].wait()
    normed = states * scale * gain[...].astype(jnp.float32).reshape(1, 1, gain.shape[0])
    steps, rows, width = normed.shape
    lines = [normed[step, row : row + 1] for row in range(rows) for step in range(steps)]
    out[:, :width] = jnp.concatenate(lines, 0).astype(out.dtype)
    line = lax.broadcasted_iota(jnp.int32, (steps * rows, TAG), 0)
    lane = lax.broadcasted_iota(jnp.int32, (steps * rows, TAG), 1)
    position = line % steps
    copies[2].wait()
    for row in range(rows):
        position = jnp.where(line // steps == row, position + lengths[row], position)
    tag = jnp.where(lane == 0, position // 32, position % 32)
    out[:, width:] = tag.astype(jnp.float32).astype(out.dtype)
    for row in range(spread.shape[0]):
        spread[row] = jnp.full(spread.shape[1:], lengths[row], spread.dtype)


def norm(hidden, gain, lengths):
    steps, rows, width = hidden.shape
    return pl.pallas_call(
        norm_kernel,
        out_shape=[
            jax.ShapeDtypeStruct((steps * rows, width + TAG), jnp.bfloat16),
            jax.ShapeDtypeStruct((rows, 8, HD), jnp.int32),
        ],
        in_specs=[HBM] * 3,
        out_specs=[VMEM] * 2,
        scratch_shapes=[
            pltpu.SMEM(lengths.shape, lengths.dtype),
            pltpu.VMEM(hidden.shape, hidden.dtype),
            pltpu.VMEM(gain.shape, gain.dtype),
            pltpu.SemaphoreType.DMA((3,)),
        ],
        compiler_params=pltpu.CompilerParams(vmem_limit_bytes=VMEM_LIMIT),
        cost_estimate=pl.CostEstimate(flops=6 * steps * rows * width, bytes_accessed=4 * steps * rows * width, transcendentals=0),
    )(*[pltpu.with_memory_space_constraint(array, pltpu.HBM) for array in (lengths, hidden, gain)])


def fetch_kernel(firsts, chunks, *refs):
    copies, count, arrived = [], len(firsts), refs[-1]
    refs[-2][...] = jnp.zeros_like(refs[-2])
    for first, far, near in zip(firsts, refs[:count], refs[count + 1 : 2 * count + 1]):
        size = near.shape[0] // min(chunks, near.shape[0])
        for at in range(0, near.shape[0], size):
            source = far.at[pl.ds(first + at, size)]
            copies.append(pltpu.make_async_copy(source, near.at[pl.ds(at, size)], arrived.at[len(copies)]))
            copies[-1].start()
    for copy in copies:
        copy.wait()


def fetch(ranges, after):
    chunks = 8
    arrays = [array for array, _, _ in ranges]
    shapes = [(count, *array.shape[1:]) for array, _, count in ranges]
    return pl.pallas_call(
        functools.partial(fetch_kernel, [first for _, first, _ in ranges], chunks),
        out_shape=[pltpu.VMEM(shape, array.dtype) for shape, array in zip(shapes, arrays)]
        + [jax.ShapeDtypeStruct((8, HD), jnp.float32)],
        in_specs=[HBM] * len(arrays) + [pl.BlockSpec(memory_space=pl.ANY)],
        out_specs=[VMEM] * (len(arrays) + 1),
        scratch_shapes=[pltpu.SemaphoreType.DMA((chunks * len(arrays),))],
        compiler_params=pltpu.CompilerParams(vmem_limit_bytes=VMEM_LIMIT),
        cost_estimate=pl.CostEstimate(
            flops=0, bytes_accessed=sum(2 * math.prod(shape) for shape in shapes), transcendentals=0
        ),
    )(*[pltpu.with_memory_space_constraint(array, pltpu.HBM) for array in arrays], after)


def slots_of(refs, counts):
    return [(ref, at) for ref, count in zip(refs, counts) for at in range(count)]


def assemble(slots, first, width):
    lanes = slice(first, first + width)
    return jnp.concatenate([ref[at, :, lanes] for ref, at in slots], 0)


def multiply(slots, weights, depth, total, kept):
    total[...] = jnp.zeros_like(total)
    chunk = 0
    for part in weights:
        for at in range(0, part.shape[0], depth):
            kept[chunk] = assemble(slots, chunk * depth, depth)
            total[...] += jnp.dot(kept[chunk], part[at : at + depth, :], preferred_element_type=jnp.float32)
            chunk += 1


def turns(positions):
    shape = (positions.shape[0], HD)
    lane = lax.broadcasted_iota(jnp.int32, shape, 1)
    pair = (lane // 2).astype(jnp.float32)
    angles = positions * jnp.exp(pair * (-2.0 * math.log(ROPE_BASE) / HD))
    return jnp.cos(angles), jnp.where(lane % 2 == 0, -1.0, 1.0) * jnp.sin(angles)


def turn(values, cosine, sine):
    lanes = values.shape[-1]
    even = lax.broadcasted_iota(jnp.int32, values.shape, 1) % 2 == 0
    swapped = jnp.where(even, pltpu.roll(values, lanes - 1, 1), pltpu.roll(values, 1, 1))
    return values * cosine + swapped * sine


def project_kernel(counts, crossed, width, *refs):
    slots = slots_of(refs, counts)
    first, second, keyval, *outs = refs[len(counts) : len(counts) + 7]
    kept, total, packed = refs[len(counts) + 7 :]
    queries, fresh = outs[:2], outs[2:]
    depth = keyval.shape[1]
    tags = jnp.concatenate([ref[at, :, width:].astype(jnp.float32) for ref, at in slots], 0)
    cosine, sine = turns(tags[:, 0:1] * 32.0 + tags[:, 1:2])
    multiply(slots, [first, second], depth, total, kept)
    own = kept[lax.axis_index("gx")]
    blocks = keyval.shape[2] // HD
    for which in range(2):
        term = jnp.dot(own, keyval[which], preferred_element_type=jnp.float32)
        for slot in range(len(slots)):
            for at in range(blocks):
                row = (which * blocks + at) * 4
                fresh[crossed[slot][0]][crossed[slot][1], row : row + 4, :] = term[
                    slot * 4 : slot * 4 + 4, at * HD : (at + 1) * HD
                ]
    heads = total.shape[1] // HD
    for head in range(heads):
        turned = turn(total[:, head * HD : (head + 1) * HD], cosine, sine)
        for slot in range(len(slots)):
            for row in range(2):
                line, at = row * 2 * heads + head * 2, slot * 4 + row * 2
                packed[slot, line : line + 2, :] = turned[at : at + 2, :]
    for slot in range(len(slots)):
        queries[crossed[slot][0]][crossed[slot][1]] = packed[slot].astype(jnp.bfloat16)


def group_shape(groups):
    counts = [len(group.sources) for group in groups]
    seen, order = [0, 0], []
    for group, count in zip(groups, counts):
        for _ in range(count):
            order.append((int(group.crossed), seen[group.crossed]))
            seen[group.crossed] += 1
    return counts, order


def project(groups, w_query, w_keyval, devices):
    counts, crossed = group_shape(groups)
    columns = w_query[0].shape[1]
    depth, kv_width = w_keyval.shape[1:]
    own, width = groups[0].blocks.shape[1], devices * depth
    rows, tile = devices * own, own * (columns // HD)
    query = jax.ShapeDtypeStruct((devices // 2, tile, HD), jnp.bfloat16)
    fresh = jax.ShapeDtypeStruct((devices // 2, own * 2 * kv_width // HD, HD), jnp.float32)
    return pl.pallas_call(
        functools.partial(project_kernel, counts, crossed, width),
        out_shape=[query, query, fresh, fresh],
        in_specs=[VMEM] * (len(groups) + 3),
        out_specs=[VMEM] * 4,
        scratch_shapes=[
            pltpu.VMEM((devices, rows, depth), jnp.bfloat16),
            pltpu.VMEM((rows, columns), jnp.float32),
            pltpu.VMEM((devices, tile, HD), jnp.float32),
        ],
        compiler_params=pltpu.CompilerParams(vmem_limit_bytes=VMEM_LIMIT),
        cost_estimate=pl.CostEstimate(
            flops=2 * rows * columns * width, bytes_accessed=2 * columns * width, transcendentals=2 * rows * HD
        ),
    )(*[group.blocks for group in groups], *w_query, w_keyval)


def pack_kernel(place, near, far, near_sum, far_sum, out):
    tile, lines = near.shape[1], near_sum.shape[1]
    for slot in range(near.shape[0]):
        chip = look_up(place[slot])
        out[chip, :tile, :] = near[slot]
        out[chip, tile : 2 * tile, :] = far[slot]
        total = near_sum[slot] + far_sum[slot]
        high = total.astype(jnp.bfloat16)
        out[chip, 2 * tile : 2 * tile + lines, :] = high
        out[chip, 2 * tile + lines :, :] = (total - high.astype(jnp.float32)).astype(jnp.bfloat16)


def pack(place, near, far, near_sum, far_sum):
    chips, tile, _ = near.shape
    return pl.pallas_call(
        functools.partial(pack_kernel, place),
        out_shape=jax.ShapeDtypeStruct((chips, 2 * tile + 2 * near_sum.shape[1], HD), jnp.bfloat16),
        in_specs=[VMEM] * 4,
        out_specs=VMEM,
        compiler_params=pltpu.CompilerParams(vmem_limit_bytes=VMEM_LIMIT),
    )(near, far, near_sum, far_sum)


def sort_kernel(place, near, far, out):
    core = lax.axis_index("gx") % 2
    for slot in range(near.shape[0]):
        chip = look_up(place[slot])
        out[2 * chip + core] = near[slot]
        out[2 * chip + 1 - core] = far[slot]


def sort(place, near, far):
    return pl.pallas_call(
        functools.partial(sort_kernel, place),
        out_shape=jax.ShapeDtypeStruct((2 * near.shape[0], *near.shape[1:]), near.dtype),
        in_specs=[VMEM] * 2,
        out_specs=VMEM,
        compiler_params=pltpu.CompilerParams(vmem_limit_bytes=VMEM_LIMIT),
    )(near, far)


def out_kernel(counts, crossed, *refs):
    slots = slots_of(refs, counts)
    *weights, near, far, kept, total = refs[len(counts) :]
    multiply(slots, weights, kept.shape[2], total, kept)
    own = near.shape[1]
    for slot in range(len(slots)):
        (near, far)[crossed[slot][0]][crossed[slot][1]] = total[slot * own : (slot + 1) * own].astype(near.dtype)


def project_out(groups, w_out, devices):
    counts, crossed = group_shape(groups)
    columns = w_out[0].shape[1]
    own, width = groups[0].blocks.shape[1:]
    chunks = devices // 2
    piece = jax.ShapeDtypeStruct((devices // 2, own, columns), jnp.bfloat16)
    return pl.pallas_call(
        functools.partial(out_kernel, counts, crossed),
        out_shape=[piece, piece],
        in_specs=[VMEM] * (len(groups) + len(w_out)),
        out_specs=[VMEM, VMEM],
        scratch_shapes=[
            pltpu.VMEM((chunks, devices * own, width // chunks), jnp.bfloat16),
            pltpu.VMEM((devices * own, columns), jnp.float32),
        ],
        compiler_params=pltpu.CompilerParams(vmem_limit_bytes=VMEM_LIMIT),
        cost_estimate=pl.CostEstimate(
            flops=2 * devices * own * columns * width, bytes_accessed=2 * columns * width, transcendentals=0
        ),
    )(*[group.blocks for group in groups], *w_out)


def attend_kernel(devices, kv_heads, tile, lengths, pieces, cache, out, fresh, queries, mixed):
    length, width = cache.shape[2:]
    extra = fresh.shape[2]
    half = tile // 2
    per_head = devices // kv_heads * half
    scale = 1.0 / math.sqrt(HD)
    for chip in range(devices // 2):
        for other in range(2):
            piece = pieces[chip, other * tile : (other + 1) * tile, :]
            queries[2 * chip + (lax.axis_index("gx") % 2 + other) % 2] = piece.astype(jnp.float32)
    line = lax.broadcasted_iota(jnp.int32, (8, 1), 0)
    first = jnp.where(line % 4 < 2, lengths[0, :, :1], lengths[1, :, :1])
    cosine, sine = turns((first + line % 2).astype(jnp.float32))
    total = jnp.sum(pieces[:, 2 * tile :, :].astype(jnp.float32), 0)
    total = total[: total.shape[0] // 2] + total[total.shape[0] // 2 :]
    twice = [jnp.concatenate([total[4 * at : 4 * at + 4]] * 2, 0) for at in range(2 * kv_heads)]
    new_keys = jnp.concatenate([turn(part, cosine, sine) for part in twice[:kv_heads]], 1)
    new_values = jnp.concatenate(twice[kv_heads:], 1)
    spot = lax.broadcasted_iota(jnp.int32, (extra, width), 0)
    for row in range(2):
        for which, new in enumerate((new_keys, new_values)):
            spread = jnp.where(spot == 0, new[2 * row : 2 * row + 1, :], 0.0)
            spread = jnp.where(spot == 1, new[2 * row + 1 : 2 * row + 2, :], spread)
            fresh[which, row] = spread.astype(fresh.dtype)
    every = queries[...]
    lines = kv_heads * per_head
    column = lax.broadcasted_iota(jnp.int32, (lines, length), 1)
    new_column = lax.broadcasted_iota(jnp.int32, (lines, extra), 1)
    step = lax.broadcasted_iota(jnp.int32, (lines, extra), 0) % 2
    across = (((1,), (1,)), ((), ()))
    for row in range(2):
        mine = every[:, row * half : row * half + half, :].reshape(lines, HD)
        spread = jnp.concatenate([mine] * kv_heads, 1)
        own_row = lax.broadcasted_iota(jnp.int32, spread.shape, 0) // per_head
        own_lane = lax.broadcasted_iota(jnp.int32, spread.shape, 1) // HD
        spread = jnp.where(own_row == own_lane, spread, 0.0).astype(jnp.bfloat16)
        scores = lax.dot_general(spread, cache[0, row], across, preferred_element_type=jnp.float32) * scale
        scores = jnp.where(column < lengths[row, :1, :1], scores, -jnp.inf)
        new_scores = lax.dot_general(spread, fresh[0, row], across, preferred_element_type=jnp.float32) * scale
        new_scores = jnp.where(new_column <= step, new_scores, -jnp.inf)
        peak = jnp.maximum(jnp.max(scores, 1, keepdims=True), jnp.max(new_scores, 1, keepdims=True))
        weight = jnp.exp(scores - peak)
        new_weight = jnp.exp(new_scores - peak)
        denominator = jnp.sum(weight, 1, keepdims=True) + jnp.sum(new_weight, 1, keepdims=True)
        result = jnp.dot(weight.astype(jnp.bfloat16), cache[1, row], preferred_element_type=jnp.float32)
        result += jnp.dot(new_weight.astype(jnp.bfloat16), fresh[1, row], preferred_element_type=jnp.float32)
        for head in range(kv_heads):
            rows = slice(head * per_head, (head + 1) * per_head)
            part = result[rows, head * HD : (head + 1) * HD] / denominator[rows]
            for query in range(per_head // 2):
                lanes = slice((head * per_head // 2 + query) * HD, (head * per_head // 2 + query + 1) * HD)
                for at in range(2):
                    mixed[at * 2 + row : at * 2 + row + 1, lanes] = part[2 * query + at : 2 * query + at + 1]
    out[...] = mixed[...].astype(out.dtype)


def attend(pieces, tile, cache, lengths, devices):
    length, width = cache.shape[2], cache.shape[3]
    columns = devices * tile // 4 * HD
    return pl.pallas_call(
        functools.partial(attend_kernel, devices, width // HD, tile),
        out_shape=jax.ShapeDtypeStruct((4, columns), jnp.bfloat16),
        in_specs=[VMEM] * 3,
        out_specs=VMEM,
        scratch_shapes=[
            pltpu.VMEM((2, 2, HD, width), cache.dtype),
            pltpu.VMEM((devices, tile, HD), jnp.float32),
            pltpu.VMEM((4, columns), jnp.float32),
        ],
        compiler_params=pltpu.CompilerParams(vmem_limit_bytes=VMEM_LIMIT),
        cost_estimate=pl.CostEstimate(
            flops=8 * 128 * length * width, bytes_accessed=8 * length * width, transcendentals=256 * length
        ),
    )(lengths, pieces, cache)


def finish_kernel(pieces, out):
    columns = pieces.shape[2]
    steps, rows = out.shape[:2]
    for source in range(pieces.shape[0]):
        piece = pieces[source].astype(jnp.float32)
        for step in range(steps):
            out[step, :, source * columns : (source + 1) * columns] = piece[step * rows : (step + 1) * rows].astype(out.dtype)


def finish(pieces, steps):
    devices, own, columns = pieces.shape
    return pl.pallas_call(
        finish_kernel,
        out_shape=jax.ShapeDtypeStruct((steps, own // steps, devices * columns), jnp.bfloat16),
        in_specs=[VMEM],
        out_specs=VMEM,
        compiler_params=pltpu.CompilerParams(vmem_limit_bytes=VMEM_LIMIT),
    )(pieces)


def body(hidden, norm_gain, w_query, w_keyval, w_out, kv_cache, lengths):
    steps = hidden.shape[0]
    devices = lax.axis_size("gx")

    normed, lengths = norm(hidden, norm_gain, lengths)
    cut = w_query.shape[0] * 3 // 4
    fetched = []

    def bring(*ranges):
        def start(after):
            *arrays, done = fetch(ranges, after)
            fetched.extend(arrays)
            return done

        return start

    part = w_out.shape[0] // 8
    waits = [
        bring((w_query, 0, cut)),
        bring((w_keyval, 0, 2), (kv_cache, 0, 2)),
        bring((w_query, cut, w_query.shape[0] - cut), (w_out, 0, 2 * part)),
    ]
    groups = gather(normed, devices, waits, inner_first=True)
    w_first, w_keyval, kv_cache, w_second, w_out_first = fetched
    place = places(groups)
    near, far, near_sum, far_sum = project(groups, [w_first, w_second], w_keyval, devices)
    pieces = pack(place, near, swap_cores(far, devices), near_sum, swap_cores(far_sum, devices))

    mixed = attend(exchange(pieces, devices), near.shape[1], kv_cache, lengths, devices)
    fetched = [w_out_first]
    waits = [bring((w_out, first * part, count * part)) for first, count in ((2, 2), (4, 4))]
    groups = gather_direct(mixed, devices, waits)
    near, far = project_out(groups, fetched, devices)
    pieces = sort(places(groups), near, far)
    return finish(lax.all_to_all(pieces, "gx", 0, 0, tiled=True), steps)


def rotate(values, positions):
    row_total, head_count, head_width = values.shape
    half_width = head_width // 2
    frequency = ROPE_BASE ** (-2.0 * jnp.arange(half_width, dtype=jnp.float32) / head_width)
    angles = positions[:, None, None] * frequency[None, None, :]
    cosine = jnp.cos(angles)
    sine_part = jnp.sin(angles)
    paired = values.reshape(row_total, head_count, half_width, 2)
    first_half = paired[..., 0]
    second_half = paired[..., 1]
    turned = jnp.stack(
        [
            first_half * cosine - second_half * sine_part,
            first_half * sine_part + second_half * cosine,
        ],
        -1,
    )
    return turned.reshape(row_total, head_count, head_width)


def attend_split_heads(queries, cache_keys, cache_values, lengths, fresh_keys, fresh_values):
    score_scale = 1.0 / math.sqrt(HD)
    fresh_scores = (
        jnp.einsum("rkgd,rskd->rkgs", queries, fresh_keys, preferred_element_type=jnp.float32)
        * score_scale
    )
    cached = (
        jnp.einsum("rkgd,rlkd->rkgl", queries, cache_keys, preferred_element_type=jnp.float32)
        * score_scale
    )
    in_range = jnp.arange(cache_keys.shape[1])[None, :] < lengths[:, None]
    cached = jnp.where(in_range[:, None, None, :], cached, -jnp.inf)
    row_peak = jnp.maximum(cached.max(-1), fresh_scores.max(-1))
    cached_exp = jnp.exp(cached - row_peak[..., None])
    fresh_exp = jnp.exp(fresh_scores - row_peak[..., None])
    denominator = cached_exp.sum(-1) + fresh_exp.sum(-1)
    mixed = jnp.einsum(
        "rkgl,rlkd->rkgd",
        cached_exp.astype(jnp.bfloat16),
        cache_values,
        preferred_element_type=jnp.float32,
    )
    mixed = mixed + jnp.einsum(
        "rkgs,rskd->rkgd",
        fresh_exp.astype(jnp.bfloat16),
        fresh_values,
        preferred_element_type=jnp.float32,
    )
    return (mixed / denominator[..., None]).astype(jnp.bfloat16)


def body_split_heads(hidden, norm_gain, w_query, w_keyval, w_out, kv_cache, lengths):
    step_count, rows_dev, model_width = hidden.shape
    devices = lax.axis_size("gx")
    device_index = lax.axis_index("gx")
    row_slab = w_keyval.shape[1]
    kv_width = w_keyval.shape[2]
    query_cols = w_query.shape[1]
    heads_width = query_cols * devices
    head_count = heads_width // HD
    kv_heads = kv_width // HD
    kv_both = jnp.concatenate([w_keyval[0], w_keyval[1]], 1)
    cache_keys = kv_cache[0].reshape(rows_dev, kv_cache.shape[2], kv_heads, HD)
    cache_values = kv_cache[1].reshape(rows_dev, kv_cache.shape[2], kv_heads, HD)
    states = hidden.astype(jnp.float32)
    scaled = states * lax.rsqrt(jnp.mean(states * states, -1, keepdims=True) + EPSILON)
    normed = (scaled * norm_gain.astype(jnp.float32)).astype(jnp.bfloat16)
    new_keys = []
    new_values = []
    outputs = []
    for step_index in range(step_count):
        shard_piece = lax.all_gather(normed[step_index], "gx", axis=0, tiled=True)
        queries = jnp.dot(shard_piece, w_query, preferred_element_type=jnp.float32)
        own_slab = lax.dynamic_slice_in_dim(shard_piece, device_index * row_slab, row_slab, 1)
        partial_kv = jnp.dot(own_slab, kv_both, preferred_element_type=jnp.float32)
        joined = jnp.concatenate([queries, partial_kv], 1)
        project_query_rows = lax.all_to_all(
            joined[:, :query_cols], "gx", split_axis=0, concat_axis=1, tiled=True
        )
        project_keyval = lax.psum_scatter(
            joined[:, query_cols:], "gx", scatter_dimension=0, tiled=True
        )
        positions = (lengths + step_index).astype(jnp.float32)
        prepare_queries = rotate(
            project_query_rows.reshape(rows_dev, head_count, HD), positions
        ).astype(jnp.bfloat16)
        prepare_queries = prepare_queries.reshape(rows_dev, kv_heads, head_count // kv_heads, HD)
        key_new = rotate(
            project_keyval[:, :kv_width].reshape(rows_dev, kv_heads, HD), positions
        ).astype(jnp.bfloat16)
        value_new = (
            project_keyval[:, kv_width:].reshape(rows_dev, kv_heads, HD).astype(jnp.bfloat16)
        )
        queries, key_new, value_new = (prepare_queries, key_new, value_new)
        new_keys.append(key_new)
        new_values.append(value_new)
        mixed = attend_split_heads(
            queries,
            cache_keys,
            cache_values,
            lengths,
            jnp.stack(new_keys, 1),
            jnp.stack(new_values, 1),
        )
        out_cols = jnp.dot(
            lax.all_gather(mixed.reshape(rows_dev, heads_width), "gx", axis=0, tiled=True),
            w_out,
            preferred_element_type=jnp.float32,
        ).astype(jnp.bfloat16)
        outputs.append(lax.all_to_all(out_cols, "gx", split_axis=0, concat_axis=1, tiled=True))
    return jnp.stack(outputs)


def solution(mesh):
    devices = mesh.shape["gx"]

    def run(*arrays):
        whole_heads = arrays[2].shape[1] % HD == 0 and devices % 2 == 0
        return (body if whole_heads else body_split_heads)(*arrays)

    in_specs = (
        P(None, ("group", "gx"), None),
        P(),
        P(None, "gx"),
        P(None, "gx", None),
        P(None, "gx"),
        P(None, ("group", "gx"), None, None),
        P(("group", "gx")),
    )
    out_specs = P(None, ("group", "gx"), None)
    return jax.shard_map(run, mesh=mesh, in_specs=in_specs, out_specs=out_specs, check_vma=False)
```

```python
import functools
import math

import jax
import jax.numpy as jnp
import numpy as np
from jax import lax
from jax.experimental import pallas as pl
from jax.experimental.pallas import tpu as pltpu
from jax.sharding import PartitionSpec as P

HD = 128
ROPE_BASE = 500000.0
EPSILON = 1e-05
TAG = 128
VMEM_LIMIT = 8 * 1024 * 1024
VMEM = pl.BlockSpec(memory_space=pltpu.VMEM)
SMEM = pl.BlockSpec(memory_space=pltpu.SMEM)
HBM = pl.BlockSpec(memory_space=pltpu.HBM)


def permute(block, target):
    return lax.ppermute(block, "gx", [(int(i), int(t)) for i, t in enumerate(target)])


def moved(source, target):
    result = np.empty_like(source)
    result[target] = source
    return result


class Group:
    def __init__(self, blocks, sources, crossed=False):
        self.blocks, self.sources, self.crossed = blocks, sources, crossed

    def send(self, target, crossed=False):
        return Group(permute(self.blocks, target), [moved(source, target) for source in self.sources], crossed)


def join(groups):
    if len(groups) == 1:
        return groups[0]
    return Group(jnp.concatenate([g.blocks for g in groups], 0), [source for g in groups for source in g.sources])


def ring_order(size):
    if size > 4:
        return list(range(size))
    return list(range(0, size, 2)) + list(range(1, size, 2))[::-1]


def axes_of(devices):
    chips, inner = devices // 2, 1
    while inner * inner * 4 <= chips and chips % (inner * 2) == 0:
        inner *= 2
    sizes = (chips // inner, inner, 2)
    place = np.arange(devices).reshape(sizes)
    result = []
    for axis, size in enumerate(sizes):
        order = ring_order(size)
        after = np.empty(size, int)
        for here, there in zip(order, order[1:] + order[:1]):
            after[here] = there
        before = np.argsort(after)
        result.append((size, np.take(place, after, axis).ravel(), np.take(place, before, axis).ravel()))
    return result


def ring(group, axis):
    size, following, preceding = axis
    groups = []
    forward = backward = group
    for step in range(1, size // 2 + 1):
        forward = forward.send(following)
        groups.append(forward)
        if 2 * step < size:
            backward = backward.send(preceding)
            groups.append(backward)
    return groups


def gather(block, devices, meanwhile=(), inner_first=False):
    (size, following, preceding), inner, core = axes_of(devices)
    own = Group(block[None], [np.arange(devices)])
    near = ring(own, inner)
    chip_pair = join([own] + near)
    groups = [own] + near + [chip_pair.send(core[1], crossed=True)]
    forward = backward = own
    for step in range(1, size // 2 + 1):
        before = forward.blocks
        arrived = [forward.send(following)] + ([backward.send(preceding)] if 2 * step < size else [])
        forward, backward = arrived[0], arrived[-1]
        if step <= len(meanwhile):
            onward = (step < size // 2) + (2 * step + 2 < size)
            chips, *alone = hold(arrived, 0 if inner_first else onward, meanwhile[step - 1](before))
            if inner_first:
                alone = [hold([group], 0, chip_pair.blocks)[0] for group in arrived[:onward]]
            forward, backward = (alone + [forward])[0], (alone + [backward])[-1]
        else:
            chips = join(arrived)
        reached = [chips] + ring(chips, inner)
        if step == size // 2 < len(meanwhile):
            reached[-1:] = hold(reached[-1:], 0, meanwhile[step](chips.blocks))
        groups += reached + [group.send(core[1], crossed=True) for group in reached]
    return groups


def gather_direct(block, devices, meanwhile):
    (size, following, _), inner, core = axes_of(devices)
    own = Group(block[None], [np.arange(devices)])
    near = ring(own, inner)
    groups = [own] + near + [join([own] + near).send(core[1], crossed=True)]
    arrived, target = [], following
    for _ in range(size - 1):
        arrived.append(own.send(target))
        target = following[target]
    reached = hold(arrived, 0, meanwhile[0](block), *[group.blocks for group in near])
    beside = ring(reached[0], inner)
    if beside:
        beside[-1:] = hold(beside[-1:], 0, meanwhile[1](reached[0].blocks), groups[-1].blocks)
    reached += beside
    return groups + reached + [group.send(core[1], crossed=True) for group in reached]


def hold_kernel(count, waits, *refs):
    stacked, *alone = refs[count + waits :]
    first = 0
    for ref in refs[:count]:
        for at in range(ref.shape[0]):
            stacked[first + at] = ref[at]
        first += ref.shape[0]
    for at in range(len(alone)):
        alone[at][...] = refs[at][...]


def hold(groups, onward, *after):
    blocks = [group.blocks for group in groups]
    stacked, *alone = pl.pallas_call(
        functools.partial(hold_kernel, len(blocks), len(after)),
        out_shape=[jax.ShapeDtypeStruct((sum(block.shape[0] for block in blocks), *blocks[0].shape[1:]), blocks[0].dtype)]
        + [jax.ShapeDtypeStruct(block.shape, block.dtype) for block in blocks[:onward]],
        in_specs=[VMEM] * len(blocks) + [pl.BlockSpec(memory_space=pl.ANY)] * len(after),
        out_specs=[VMEM] * (onward + 1),
        compiler_params=pltpu.CompilerParams(vmem_limit_bytes=VMEM_LIMIT),
    )(*blocks, *after)
    sources = [group.sources for group in groups]
    return [Group(stacked, sum(sources, []))] + [Group(block, source) for block, source in zip(alone, sources)]


def swap_cores(block, devices):
    return permute(block, np.arange(devices) ^ 1)


def exchange(pieces, devices):
    same_core = [list(range(core, devices, 2)) for core in range(2)]
    return lax.all_to_all(pieces, "gx", 0, 0, axis_index_groups=same_core, tiled=True)


def places(groups):
    return [(source // 2)[::2] for group in groups if not group.crossed for source in group.sources]


def look_up(values):
    chip = lax.axis_index("gx") // 2
    found = jnp.int32(int(values[0]))
    for at in range(1, len(values)):
        found = jnp.where(chip == at, jnp.int32(int(values[at])), found)
    return found


def norm_kernel(lengths_far, hidden_far, gain_far, out, spread, lengths, hidden, gain, arrived):
    copies = [
        pltpu.make_async_copy(far, near, arrived.at[at])
        for at, (far, near) in enumerate(((hidden_far, hidden), (gain_far, gain), (lengths_far, lengths)))
    ]
    for copy in copies:
        copy.start()
    copies[0].wait()
    states = hidden[...].astype(jnp.float32)
    scale = lax.rsqrt(jnp.mean(states * states, -1, keepdims=True) + EPSILON)
    copies[1].wait()
    normed = states * scale * gain[...].astype(jnp.float32).reshape(1, 1, gain.shape[0])
    steps, rows, width = normed.shape
    lines = [normed[step, row : row + 1] for row in range(rows) for step in range(steps)]
    out[:, :width] = jnp.concatenate(lines, 0).astype(out.dtype)
    line = lax.broadcasted_iota(jnp.int32, (steps * rows, TAG), 0)
    lane = lax.broadcasted_iota(jnp.int32, (steps * rows, TAG), 1)
    position = line % steps
    copies[2].wait()
    for row in range(rows):
        position = jnp.where(line // steps == row, position + lengths[row], position)
    tag = jnp.where(lane == 0, position // 32, position % 32)
    out[:, width:] = tag.astype(jnp.float32).astype(out.dtype)
    for row in range(spread.shape[0]):
        spread[row] = jnp.full(spread.shape[1:], lengths[row], spread.dtype)


def norm(hidden, gain, lengths):
    steps, rows, width = hidden.shape
    return pl.pallas_call(
        norm_kernel,
        out_shape=[
            jax.ShapeDtypeStruct((steps * rows, width + TAG), jnp.bfloat16),
            jax.ShapeDtypeStruct((rows, 8, HD), jnp.int32),
        ],
        in_specs=[HBM] * 3,
        out_specs=[VMEM] * 2,
        scratch_shapes=[
            pltpu.SMEM(lengths.shape, lengths.dtype),
            pltpu.VMEM(hidden.shape, hidden.dtype),
            pltpu.VMEM(gain.shape, gain.dtype),
            pltpu.SemaphoreType.DMA((3,)),
        ],
        compiler_params=pltpu.CompilerParams(vmem_limit_bytes=VMEM_LIMIT),
        cost_estimate=pl.CostEstimate(flops=6 * steps * rows * width, bytes_accessed=4 * steps * rows * width, transcendentals=0),
    )(*[pltpu.with_memory_space_constraint(array, pltpu.HBM) for array in (lengths, hidden, gain)])


def fetch_kernel(firsts, chunks, *refs):
    copies, count, arrived = [], len(firsts), refs[-1]
    refs[-2][...] = jnp.zeros_like(refs[-2])
    for first, far, near in zip(firsts, refs[:count], refs[count + 1 : 2 * count + 1]):
        size = near.shape[0] // min(chunks, near.shape[0])
        for at in range(0, near.shape[0], size):
            source = far.at[pl.ds(first + at, size)]
            copies.append(pltpu.make_async_copy(source, near.at[pl.ds(at, size)], arrived.at[len(copies)]))
            copies[-1].start()
    for copy in copies:
        copy.wait()


def fetch(ranges, after):
    chunks = 8
    arrays = [array for array, _, _ in ranges]
    shapes = [(count, *array.shape[1:]) for array, _, count in ranges]
    return pl.pallas_call(
        functools.partial(fetch_kernel, [first for _, first, _ in ranges], chunks),
        out_shape=[pltpu.VMEM(shape, array.dtype) for shape, array in zip(shapes, arrays)]
        + [jax.ShapeDtypeStruct((8, HD), jnp.float32)],
        in_specs=[HBM] * len(arrays) + [pl.BlockSpec(memory_space=pl.ANY)],
        out_specs=[VMEM] * (len(arrays) + 1),
        scratch_shapes=[pltpu.SemaphoreType.DMA((chunks * len(arrays),))],
        compiler_params=pltpu.CompilerParams(vmem_limit_bytes=VMEM_LIMIT),
        cost_estimate=pl.CostEstimate(
            flops=0, bytes_accessed=sum(2 * math.prod(shape) for shape in shapes), transcendentals=0
        ),
    )(*[pltpu.with_memory_space_constraint(array, pltpu.HBM) for array in arrays], after)


def slots_of(refs, counts):
    return [(ref, at) for ref, count in zip(refs, counts) for at in range(count)]


def assemble(slots, first, width):
    lanes = slice(first, first + width)
    return jnp.concatenate([ref[at, :, lanes] for ref, at in slots], 0)


def multiply(slots, weights, depth, total, kept):
    total[...] = jnp.zeros_like(total)
    chunk = 0
    for part in weights:
        for at in range(0, part.shape[0], depth):
            kept[chunk] = assemble(slots, chunk * depth, depth)
            total[...] += jnp.dot(kept[chunk], part[at : at + depth, :], preferred_element_type=jnp.float32)
            chunk += 1


def turns(positions):
    shape = (positions.shape[0], HD)
    lane = lax.broadcasted_iota(jnp.int32, shape, 1)
    pair = (lane // 2).astype(jnp.float32)
    angles = positions * jnp.exp(pair * (-2.0 * math.log(ROPE_BASE) / HD))
    return jnp.cos(angles), jnp.where(lane % 2 == 0, -1.0, 1.0) * jnp.sin(angles)


def turn(values, cosine, sine):
    lanes = values.shape[-1]
    even = lax.broadcasted_iota(jnp.int32, values.shape, 1) % 2 == 0
    swapped = jnp.where(even, pltpu.roll(values, lanes - 1, 1), pltpu.roll(values, 1, 1))
    return values * cosine + swapped * sine


def project_kernel(counts, crossed, width, *refs):
    slots = slots_of(refs, counts)
    first, second, keyval, *outs = refs[len(counts) : len(counts) + 7]
    kept, total, packed = refs[len(counts) + 7 :]
    queries, fresh = outs[:2], outs[2:]
    depth = keyval.shape[1]
    tags = jnp.concatenate([ref[at, :, width:].astype(jnp.float32) for ref, at in slots], 0)
    cosine, sine = turns(tags[:, 0:1] * 32.0 + tags[:, 1:2])
    multiply(slots, [first, second], depth, total, kept)
    own = kept[lax.axis_index("gx")]
    blocks = keyval.shape[2] // HD
    for which in range(2):
        term = jnp.dot(own, keyval[which], preferred_element_type=jnp.float32)
        for slot in range(len(slots)):
            for at in range(blocks):
                row = (which * blocks + at) * 4
                fresh[crossed[slot][0]][crossed[slot][1], row : row + 4, :] = term[
                    slot * 4 : slot * 4 + 4, at * HD : (at + 1) * HD
                ]
    heads = total.shape[1] // HD
    for head in range(heads):
        turned = turn(total[:, head * HD : (head + 1) * HD], cosine, sine)
        for slot in range(len(slots)):
            for row in range(2):
                line, at = row * 2 * heads + head * 2, slot * 4 + row * 2
                packed[slot, line : line + 2, :] = turned[at : at + 2, :]
    for slot in range(len(slots)):
        queries[crossed[slot][0]][crossed[slot][1]] = packed[slot].astype(jnp.bfloat16)


def group_shape(groups):
    counts = [len(group.sources) for group in groups]
    seen, order = [0, 0], []
    for group, count in zip(groups, counts):
        for _ in range(count):
            order.append((int(group.crossed), seen[group.crossed]))
            seen[group.crossed] += 1
    return counts, order


def project(groups, w_query, w_keyval, devices):
    counts, crossed = group_shape(groups)
    columns = w_query[0].shape[1]
    depth, kv_width = w_keyval.shape[1:]
    own, width = groups[0].blocks.shape[1], devices * depth
    rows, tile = devices * own, own * (columns // HD)
    query = jax.ShapeDtypeStruct((devices // 2, tile, HD), jnp.bfloat16)
    fresh = jax.ShapeDtypeStruct((devices // 2, own * 2 * kv_width // HD, HD), jnp.float32)
    return pl.pallas_call(
        functools.partial(project_kernel, counts, crossed, width),
        out_shape=[query, query, fresh, fresh],
        in_specs=[VMEM] * (len(groups) + 3),
        out_specs=[VMEM] * 4,
        scratch_shapes=[
            pltpu.VMEM((devices, rows, depth), jnp.bfloat16),
            pltpu.VMEM((rows, columns), jnp.float32),
            pltpu.VMEM((devices, tile, HD), jnp.float32),
        ],
        compiler_params=pltpu.CompilerParams(vmem_limit_bytes=VMEM_LIMIT),
        cost_estimate=pl.CostEstimate(
            flops=2 * rows * columns * width, bytes_accessed=2 * columns * width, transcendentals=2 * rows * HD
        ),
    )(*[group.blocks for group in groups], *w_query, w_keyval)


def pack_kernel(place, near, far, near_sum, far_sum, out):
    tile, lines = near.shape[1], near_sum.shape[1]
    for slot in range(near.shape[0]):
        chip = look_up(place[slot])
        out[chip, :tile, :] = near[slot]
        out[chip, tile : 2 * tile, :] = far[slot]
        total = near_sum[slot] + far_sum[slot]
        high = total.astype(jnp.bfloat16)
        out[chip, 2 * tile : 2 * tile + lines, :] = high
        out[chip, 2 * tile + lines :, :] = (total - high.astype(jnp.float32)).astype(jnp.bfloat16)


def pack(place, near, far, near_sum, far_sum):
    chips, tile, _ = near.shape
    return pl.pallas_call(
        functools.partial(pack_kernel, place),
        out_shape=jax.ShapeDtypeStruct((chips, 2 * tile + 2 * near_sum.shape[1], HD), jnp.bfloat16),
        in_specs=[VMEM] * 4,
        out_specs=VMEM,
        compiler_params=pltpu.CompilerParams(vmem_limit_bytes=VMEM_LIMIT),
    )(near, far, near_sum, far_sum)


def sort_kernel(place, near, far, out):
    core = lax.axis_index("gx") % 2
    for slot in range(near.shape[0]):
        chip = look_up(place[slot])
        out[2 * chip + core] = near[slot]
        out[2 * chip + 1 - core] = far[slot]


def sort(place, near, far):
    return pl.pallas_call(
        functools.partial(sort_kernel, place),
        out_shape=jax.ShapeDtypeStruct((2 * near.shape[0], *near.shape[1:]), near.dtype),
        in_specs=[VMEM] * 2,
        out_specs=VMEM,
        compiler_params=pltpu.CompilerParams(vmem_limit_bytes=VMEM_LIMIT),
    )(near, far)


def out_kernel(counts, crossed, *refs):
    slots = slots_of(refs, counts)
    *weights, near, far, kept, total = refs[len(counts) :]
    multiply(slots, weights, kept.shape[2], total, kept)
    own = near.shape[1]
    for slot in range(len(slots)):
        (near, far)[crossed[slot][0]][crossed[slot][1]] = total[slot * own : (slot + 1) * own].astype(near.dtype)


def project_out(groups, w_out, devices):
    counts, crossed = group_shape(groups)
    columns = w_out[0].shape[1]
    own, width = groups[0].blocks.shape[1:]
    chunks = devices // 2
    piece = jax.ShapeDtypeStruct((devices // 2, own, columns), jnp.bfloat16)
    return pl.pallas_call(
        functools.partial(out_kernel, counts, crossed),
        out_shape=[piece, piece],
        in_specs=[VMEM] * (len(groups) + len(w_out)),
        out_specs=[VMEM, VMEM],
        scratch_shapes=[
            pltpu.VMEM((chunks, devices * own, width // chunks), jnp.bfloat16),
            pltpu.VMEM((devices * own, columns), jnp.float32),
        ],
        compiler_params=pltpu.CompilerParams(vmem_limit_bytes=VMEM_LIMIT),
        cost_estimate=pl.CostEstimate(
            flops=2 * devices * own * columns * width, bytes_accessed=2 * columns * width, transcendentals=0
        ),
    )(*[group.blocks for group in groups], *w_out)


def attend_kernel(devices, kv_heads, tile, lengths, pieces, cache, out, fresh, queries, mixed):
    length, width = cache.shape[2:]
    extra = fresh.shape[2]
    half = tile // 2
    per_head = devices // kv_heads * half
    scale = 1.0 / math.sqrt(HD)
    for chip in range(devices // 2):
        for other in range(2):
            piece = pieces[chip, other * tile : (other + 1) * tile, :]
            queries[2 * chip + (lax.axis_index("gx") % 2 + other) % 2] = piece.astype(jnp.float32)
    line = lax.broadcasted_iota(jnp.int32, (8, 1), 0)
    first = jnp.where(line % 4 < 2, lengths[0, :, :1], lengths[1, :, :1])
    cosine, sine = turns((first + line % 2).astype(jnp.float32))
    total = jnp.sum(pieces[:, 2 * tile :, :].astype(jnp.float32), 0)
    total = total[: total.shape[0] // 2] + total[total.shape[0] // 2 :]
    twice = [jnp.concatenate([total[4 * at : 4 * at + 4]] * 2, 0) for at in range(2 * kv_heads)]
    new_keys = jnp.concatenate([turn(part, cosine, sine) for part in twice[:kv_heads]], 1)
    new_values = jnp.concatenate(twice[kv_heads:], 1)
    spot = lax.broadcasted_iota(jnp.int32, (extra, width), 0)
    for row in range(2):
        for which, new in enumerate((new_keys, new_values)):
            spread = jnp.where(spot == 0, new[2 * row : 2 * row + 1, :], 0.0)
            spread = jnp.where(spot == 1, new[2 * row + 1 : 2 * row + 2, :], spread)
            fresh[which, row] = spread.astype(fresh.dtype)
    every = queries[...]
    lines = kv_heads * per_head
    column = lax.broadcasted_iota(jnp.int32, (lines, length), 1)
    new_column = lax.broadcasted_iota(jnp.int32, (lines, extra), 1)
    step = lax.broadcasted_iota(jnp.int32, (lines, extra), 0) % 2
    across = (((1,), (1,)), ((), ()))
    for row in range(2):
        mine = every[:, row * half : row * half + half, :].reshape(lines, HD)
        spread = jnp.concatenate([mine] * kv_heads, 1)
        own_row = lax.broadcasted_iota(jnp.int32, spread.shape, 0) // per_head
        own_lane = lax.broadcasted_iota(jnp.int32, spread.shape, 1) // HD
        spread = jnp.where(own_row == own_lane, spread, 0.0).astype(jnp.bfloat16)
        scores = lax.dot_general(spread, cache[0, row], across, preferred_element_type=jnp.float32) * scale
        scores = jnp.where(column < lengths[row, :1, :1], scores, -jnp.inf)
        new_scores = lax.dot_general(spread, fresh[0, row], across, preferred_element_type=jnp.float32) * scale
        new_scores = jnp.where(new_column <= step, new_scores, -jnp.inf)
        peak = jnp.maximum(jnp.max(scores, 1, keepdims=True), jnp.max(new_scores, 1, keepdims=True))
        weight = jnp.exp(scores - peak)
        new_weight = jnp.exp(new_scores - peak)
        denominator = jnp.sum(weight, 1, keepdims=True) + jnp.sum(new_weight, 1, keepdims=True)
        result = jnp.dot(weight.astype(jnp.bfloat16), cache[1, row], preferred_element_type=jnp.float32)
        result += jnp.dot(new_weight.astype(jnp.bfloat16), fresh[1, row], preferred_element_type=jnp.float32)
        for head in range(kv_heads):
            rows = slice(head * per_head, (head + 1) * per_head)
            part = result[rows, head * HD : (head + 1) * HD] / denominator[rows]
            for query in range(per_head // 2):
                lanes = slice((head * per_head // 2 + query) * HD, (head * per_head // 2 + query + 1) * HD)
                for at in range(2):
                    mixed[at * 2 + row : at * 2 + row + 1, lanes] = part[2 * query + at : 2 * query + at + 1]
    out[...] = mixed[...].astype(out.dtype)


def attend(pieces, tile, cache, lengths, devices):
    length, width = cache.shape[2], cache.shape[3]
    columns = devices * tile // 4 * HD
    return pl.pallas_call(
        functools.partial(attend_kernel, devices, width // HD, tile),
        out_shape=jax.ShapeDtypeStruct((4, columns), jnp.bfloat16),
        in_specs=[VMEM] * 3,
        out_specs=VMEM,
        scratch_shapes=[
            pltpu.VMEM((2, 2, HD, width), cache.dtype),
            pltpu.VMEM((devices, tile, HD), jnp.float32),
            pltpu.VMEM((4, columns), jnp.float32),
        ],
        compiler_params=pltpu.CompilerParams(vmem_limit_bytes=VMEM_LIMIT),
        cost_estimate=pl.CostEstimate(
            flops=8 * 128 * length * width, bytes_accessed=8 * length * width, transcendentals=256 * length
        ),
    )(lengths, pieces, cache)


def finish_kernel(pieces, out):
    columns = pieces.shape[2]
    steps, rows = out.shape[:2]
    for source in range(pieces.shape[0]):
        piece = pieces[source].astype(jnp.float32)
        for step in range(steps):
            out[step, :, source * columns : (source + 1) * columns] = piece[step * rows : (step + 1) * rows].astype(out.dtype)


def finish(pieces, steps):
    devices, own, columns = pieces.shape
    return pl.pallas_call(
        finish_kernel,
        out_shape=jax.ShapeDtypeStruct((steps, own // steps, devices * columns), jnp.bfloat16),
        in_specs=[VMEM],
        out_specs=VMEM,
        compiler_params=pltpu.CompilerParams(vmem_limit_bytes=VMEM_LIMIT),
    )(pieces)


def body(hidden, norm_gain, w_query, w_keyval, w_out, kv_cache, lengths):
    steps = hidden.shape[0]
    devices = lax.axis_size("gx")

    normed, lengths = norm(hidden, norm_gain, lengths)
    cut = w_query.shape[0] * 3 // 4
    fetched = []

    def bring(*ranges):
        def start(after):
            *arrays, done = fetch(ranges, after)
            fetched.extend(arrays)
            return done

        return start

    part = w_out.shape[0] // 8
    waits = [
        bring((w_query, 0, cut)),
        bring((w_keyval, 0, 2), (kv_cache, 0, 2)),
        bring((w_query, cut, w_query.shape[0] - cut), (w_out, 0, 2 * part)),
    ]
    groups = gather(normed, devices, waits, inner_first=True)
    w_first, w_keyval, kv_cache, w_second, w_out_first = fetched
    place = places(groups)
    near, far, near_sum, far_sum = project(groups, [w_first, w_second], w_keyval, devices)
    pieces = pack(place, near, swap_cores(far, devices), near_sum, swap_cores(far_sum, devices))

    mixed = attend(exchange(pieces, devices), near.shape[1], kv_cache, lengths, devices)
    fetched = [w_out_first]
    waits = [bring((w_out, first * part, count * part)) for first, count in ((2, 3), (5, 3))]
    groups = gather_direct(mixed, devices, waits)
    near, far = project_out(groups, fetched, devices)
    pieces = sort(places(groups), near, far)
    return finish(lax.all_to_all(pieces, "gx", 0, 0, tiled=True), steps)


def rotate(values, positions):
    row_total, head_count, head_width = values.shape
    half_width = head_width // 2
    frequency = ROPE_BASE ** (-2.0 * jnp.arange(half_width, dtype=jnp.float32) / head_width)
    angles = positions[:, None, None] * frequency[None, None, :]
    cosine = jnp.cos(angles)
    sine_part = jnp.sin(angles)
    paired = values.reshape(row_total, head_count, half_width, 2)
    first_half = paired[..., 0]
    second_half = paired[..., 1]
    turned = jnp.stack(
        [
            first_half * cosine - second_half * sine_part,
            first_half * sine_part + second_half * cosine,
        ],
        -1,
    )
    return turned.reshape(row_total, head_count, head_width)


def attend_split_heads(queries, cache_keys, cache_values, lengths, fresh_keys, fresh_values):
    score_scale = 1.0 / math.sqrt(HD)
    fresh_scores = (
        jnp.einsum("rkgd,rskd->rkgs", queries, fresh_keys, preferred_element_type=jnp.float32)
        * score_scale
    )
    cached = (
        jnp.einsum("rkgd,rlkd->rkgl", queries, cache_keys, preferred_element_type=jnp.float32)
        * score_scale
    )
    in_range = jnp.arange(cache_keys.shape[1])[None, :] < lengths[:, None]
    cached = jnp.where(in_range[:, None, None, :], cached, -jnp.inf)
    row_peak = jnp.maximum(cached.max(-1), fresh_scores.max(-1))
    cached_exp = jnp.exp(cached - row_peak[..., None])
    fresh_exp = jnp.exp(fresh_scores - row_peak[..., None])
    denominator = cached_exp.sum(-1) + fresh_exp.sum(-1)
    mixed = jnp.einsum(
        "rkgl,rlkd->rkgd",
        cached_exp.astype(jnp.bfloat16),
        cache_values,
        preferred_element_type=jnp.float32,
    )
    mixed = mixed + jnp.einsum(
        "rkgs,rskd->rkgd",
        fresh_exp.astype(jnp.bfloat16),
        fresh_values,
        preferred_element_type=jnp.float32,
    )
    return (mixed / denominator[..., None]).astype(jnp.bfloat16)


def body_split_heads(hidden, norm_gain, w_query, w_keyval, w_out, kv_cache, lengths):
    step_count, rows_dev, model_width = hidden.shape
    devices = lax.axis_size("gx")
    device_index = lax.axis_index("gx")
    row_slab = w_keyval.shape[1]
    kv_width = w_keyval.shape[2]
    query_cols = w_query.shape[1]
    heads_width = query_cols * devices
    head_count = heads_width // HD
    kv_heads = kv_width // HD
    kv_both = jnp.concatenate([w_keyval[0], w_keyval[1]], 1)
    cache_keys = kv_cache[0].reshape(rows_dev, kv_cache.shape[2], kv_heads, HD)
    cache_values = kv_cache[1].reshape(rows_dev, kv_cache.shape[2], kv_heads, HD)
    states = hidden.astype(jnp.float32)
    scaled = states * lax.rsqrt(jnp.mean(states * states, -1, keepdims=True) + EPSILON)
    normed = (scaled * norm_gain.astype(jnp.float32)).astype(jnp.bfloat16)
    new_keys = []
    new_values = []
    outputs = []
    for step_index in range(step_count):
        shard_piece = lax.all_gather(normed[step_index], "gx", axis=0, tiled=True)
        queries = jnp.dot(shard_piece, w_query, preferred_element_type=jnp.float32)
        own_slab = lax.dynamic_slice_in_dim(shard_piece, device_index * row_slab, row_slab, 1)
        partial_kv = jnp.dot(own_slab, kv_both, preferred_element_type=jnp.float32)
        joined = jnp.concatenate([queries, partial_kv], 1)
        project_query_rows = lax.all_to_all(
            joined[:, :query_cols], "gx", split_axis=0, concat_axis=1, tiled=True
        )
        project_keyval = lax.psum_scatter(
            joined[:, query_cols:], "gx", scatter_dimension=0, tiled=True
        )
        positions = (lengths + step_index).astype(jnp.float32)
        prepare_queries = rotate(
            project_query_rows.reshape(rows_dev, head_count, HD), positions
        ).astype(jnp.bfloat16)
        prepare_queries = prepare_queries.reshape(rows_dev, kv_heads, head_count // kv_heads, HD)
        key_new = rotate(
            project_keyval[:, :kv_width].reshape(rows_dev, kv_heads, HD), positions
        ).astype(jnp.bfloat16)
        value_new = (
            project_keyval[:, kv_width:].reshape(rows_dev, kv_heads, HD).astype(jnp.bfloat16)
        )
        queries, key_new, value_new = (prepare_queries, key_new, value_new)
        new_keys.append(key_new)
        new_values.append(value_new)
        mixed = attend_split_heads(
            queries,
            cache_keys,
            cache_values,
            lengths,
            jnp.stack(new_keys, 1),
            jnp.stack(new_values, 1),
        )
        out_cols = jnp.dot(
            lax.all_gather(mixed.reshape(rows_dev, heads_width), "gx", axis=0, tiled=True),
            w_out,
            preferred_element_type=jnp.float32,
        ).astype(jnp.bfloat16)
        outputs.append(lax.all_to_all(out_cols, "gx", split_axis=0, concat_axis=1, tiled=True))
    return jnp.stack(outputs)


def solution(mesh):
    devices = mesh.shape["gx"]

    def run(*arrays):
        whole_heads = arrays[2].shape[1] % HD == 0 and devices % 2 == 0
        return (body if whole_heads else body_split_heads)(*arrays)

    in_specs = (
        P(None, ("group", "gx"), None),
        P(),
        P(None, "gx"),
        P(None, "gx", None),
        P(None, "gx"),
        P(None, ("group", "gx"), None, None),
        P(("group", "gx")),
    )
    out_specs = P(None, ("group", "gx"), None)
    return jax.shard_map(run, mesh=mesh, in_specs=in_specs, out_specs=out_specs, check_vma=False)
```

```python
import functools
import math

import jax
import jax.numpy as jnp
import numpy as np
from jax import lax
from jax.experimental import pallas as pl
from jax.experimental.pallas import tpu as pltpu
from jax.sharding import PartitionSpec as P

HD = 128
ROPE_BASE = 500000.0
EPSILON = 1e-05
TAG = 128
VMEM_LIMIT = 8 * 1024 * 1024
VMEM = pl.BlockSpec(memory_space=pltpu.VMEM)
SMEM = pl.BlockSpec(memory_space=pltpu.SMEM)
HBM = pl.BlockSpec(memory_space=pltpu.HBM)


def permute(block, target):
    return lax.ppermute(block, "gx", [(int(i), int(t)) for i, t in enumerate(target)])


def moved(source, target):
    result = np.empty_like(source)
    result[target] = source
    return result


class Group:
    def __init__(self, blocks, sources, crossed=False):
        self.blocks, self.sources, self.crossed = blocks, sources, crossed

    def send(self, target, crossed=False):
        return Group(permute(self.blocks, target), [moved(source, target) for source in self.sources], crossed)


def join(groups):
    if len(groups) == 1:
        return groups[0]
    return Group(jnp.concatenate([g.blocks for g in groups], 0), [source for g in groups for source in g.sources])


def ring_order(size):
    if size > 4:
        return list(range(size))
    return list(range(0, size, 2)) + list(range(1, size, 2))[::-1]


def axes_of(devices):
    chips, inner = devices // 2, 1
    while inner * inner * 4 <= chips and chips % (inner * 2) == 0:
        inner *= 2
    sizes = (chips // inner, inner, 2)
    place = np.arange(devices).reshape(sizes)
    result = []
    for axis, size in enumerate(sizes):
        order = ring_order(size)
        after = np.empty(size, int)
        for here, there in zip(order, order[1:] + order[:1]):
            after[here] = there
        before = np.argsort(after)
        result.append((size, np.take(place, after, axis).ravel(), np.take(place, before, axis).ravel()))
    return result


def ring(group, axis):
    size, following, preceding = axis
    groups = []
    forward = backward = group
    for step in range(1, size // 2 + 1):
        forward = forward.send(following)
        groups.append(forward)
        if 2 * step < size:
            backward = backward.send(preceding)
            groups.append(backward)
    return groups


def gather(block, devices, meanwhile=(), inner_first=False):
    (size, following, preceding), inner, core = axes_of(devices)
    own = Group(block[None], [np.arange(devices)])
    near = ring(own, inner)
    chip_pair = join([own] + near)
    groups = [own] + near + [chip_pair.send(core[1], crossed=True)]
    forward = backward = own
    for step in range(1, size // 2 + 1):
        before = forward.blocks
        arrived = [forward.send(following)] + ([backward.send(preceding)] if 2 * step < size else [])
        forward, backward = arrived[0], arrived[-1]
        if step <= len(meanwhile):
            onward = (step < size // 2) + (2 * step + 2 < size)
            chips, *alone = hold(arrived, 0 if inner_first else onward, meanwhile[step - 1](before))
            if inner_first:
                alone = [hold([group], 0, chip_pair.blocks)[0] for group in arrived[:onward]]
            forward, backward = (alone + [forward])[0], (alone + [backward])[-1]
        else:
            chips = join(arrived)
        reached = [chips] + ring(chips, inner)
        if step == size // 2 < len(meanwhile):
            reached[-1:] = hold(reached[-1:], 0, meanwhile[step](chips.blocks))
        groups += reached + [group.send(core[1], crossed=True) for group in reached]
    return groups


def gather_direct(block, devices, meanwhile):
    (size, following, _), inner, core = axes_of(devices)
    own = Group(block[None], [np.arange(devices)])
    near = ring(own, inner)
    groups = [own] + near + [join([own] + near).send(core[1], crossed=True)]
    arrived, target = [], following
    for _ in range(size - 1):
        arrived.append(own.send(target))
        target = following[target]
    reached = hold(arrived, 0, meanwhile[0](block), *[group.blocks for group in near])
    beside = ring(reached[0], inner)
    if beside:
        beside[-1:] = hold(beside[-1:], 0, meanwhile[1](reached[0].blocks), groups[-1].blocks)
    reached += beside
    return groups + reached + [group.send(core[1], crossed=True) for group in reached]


def hold_kernel(count, waits, *refs):
    stacked, *alone = refs[count + waits :]
    first = 0
    for ref in refs[:count]:
        for at in range(ref.shape[0]):
            stacked[first + at] = ref[at]
        first += ref.shape[0]
    for at in range(len(alone)):
        alone[at][...] = refs[at][...]


def hold(groups, onward, *after):
    blocks = [group.blocks for group in groups]
    stacked, *alone = pl.pallas_call(
        functools.partial(hold_kernel, len(blocks), len(after)),
        out_shape=[jax.ShapeDtypeStruct((sum(block.shape[0] for block in blocks), *blocks[0].shape[1:]), blocks[0].dtype)]
        + [jax.ShapeDtypeStruct(block.shape, block.dtype) for block in blocks[:onward]],
        in_specs=[VMEM] * len(blocks) + [pl.BlockSpec(memory_space=pl.ANY)] * len(after),
        out_specs=[VMEM] * (onward + 1),
        compiler_params=pltpu.CompilerParams(vmem_limit_bytes=VMEM_LIMIT),
    )(*blocks, *after)
    sources = [group.sources for group in groups]
    return [Group(stacked, sum(sources, []))] + [Group(block, source) for block, source in zip(alone, sources)]


def swap_cores(block, devices):
    return permute(block, np.arange(devices) ^ 1)


def exchange(pieces, devices):
    same_core = [list(range(core, devices, 2)) for core in range(2)]
    return lax.all_to_all(pieces, "gx", 0, 0, axis_index_groups=same_core, tiled=True)


def places(groups):
    return [(source // 2)[::2] for group in groups if not group.crossed for source in group.sources]


def look_up(values):
    chip = lax.axis_index("gx") // 2
    found = jnp.int32(int(values[0]))
    for at in range(1, len(values)):
        found = jnp.where(chip == at, jnp.int32(int(values[at])), found)
    return found


def norm_kernel(lengths_far, hidden_far, gain_far, out, spread, lengths, hidden, gain, arrived):
    copies = [
        pltpu.make_async_copy(far, near, arrived.at[at])
        for at, (far, near) in enumerate(((hidden_far, hidden), (gain_far, gain), (lengths_far, lengths)))
    ]
    for copy in copies:
        copy.start()
    copies[0].wait()
    states = hidden[...].astype(jnp.float32)
    scale = lax.rsqrt(jnp.mean(states * states, -1, keepdims=True) + EPSILON)
    copies[1].wait()
    normed = states * scale * gain[...].astype(jnp.float32).reshape(1, 1, gain.shape[0])
    steps, rows, width = normed.shape
    lines = [normed[step, row : row + 1] for row in range(rows) for step in range(steps)]
    out[:, :width] = jnp.concatenate(lines, 0).astype(out.dtype)
    line = lax.broadcasted_iota(jnp.int32, (steps * rows, TAG), 0)
    lane = lax.broadcasted_iota(jnp.int32, (steps * rows, TAG), 1)
    position = line % steps
    copies[2].wait()
    for row in range(rows):
        position = jnp.where(line // steps == row, position + lengths[row], position)
    tag = jnp.where(lane == 0, position // 32, position % 32)
    out[:, width:] = tag.astype(jnp.float32).astype(out.dtype)
    for row in range(spread.shape[0]):
        spread[row] = jnp.full(spread.shape[1:], lengths[row], spread.dtype)


def norm(hidden, gain, lengths):
    steps, rows, width = hidden.shape
    return pl.pallas_call(
        norm_kernel,
        out_shape=[
            jax.ShapeDtypeStruct((steps * rows, width + TAG), jnp.bfloat16),
            jax.ShapeDtypeStruct((rows, 8, HD), jnp.int32),
        ],
        in_specs=[HBM] * 3,
        out_specs=[VMEM] * 2,
        scratch_shapes=[
            pltpu.SMEM(lengths.shape, lengths.dtype),
            pltpu.VMEM(hidden.shape, hidden.dtype),
            pltpu.VMEM(gain.shape, gain.dtype),
            pltpu.SemaphoreType.DMA((3,)),
        ],
        compiler_params=pltpu.CompilerParams(vmem_limit_bytes=VMEM_LIMIT),
        cost_estimate=pl.CostEstimate(flops=6 * steps * rows * width, bytes_accessed=4 * steps * rows * width, transcendentals=0),
    )(*[pltpu.with_memory_space_constraint(array, pltpu.HBM) for array in (lengths, hidden, gain)])


def fetch_kernel(firsts, chunks, *refs):
    copies, count, arrived = [], len(firsts), refs[-1]
    refs[-2][...] = jnp.zeros_like(refs[-2])
    for first, far, near in zip(firsts, refs[:count], refs[count + 1 : 2 * count + 1]):
        size = near.shape[0] // min(chunks, near.shape[0])
        for at in range(0, near.shape[0], size):
            source = far.at[pl.ds(first + at, size)]
            copies.append(pltpu.make_async_copy(source, near.at[pl.ds(at, size)], arrived.at[len(copies)]))
            copies[-1].start()
    for copy in copies:
        copy.wait()


def fetch(ranges, after):
    chunks = 8
    arrays = [array for array, _, _ in ranges]
    shapes = [(count, *array.shape[1:]) for array, _, count in ranges]
    return pl.pallas_call(
        functools.partial(fetch_kernel, [first for _, first, _ in ranges], chunks),
        out_shape=[pltpu.VMEM(shape, array.dtype) for shape, array in zip(shapes, arrays)]
        + [jax.ShapeDtypeStruct((8, HD), jnp.float32)],
        in_specs=[HBM] * len(arrays) + [pl.BlockSpec(memory_space=pl.ANY)],
        out_specs=[VMEM] * (len(arrays) + 1),
        scratch_shapes=[pltpu.SemaphoreType.DMA((chunks * len(arrays),))],
        compiler_params=pltpu.CompilerParams(vmem_limit_bytes=VMEM_LIMIT),
        cost_estimate=pl.CostEstimate(
            flops=0, bytes_accessed=sum(2 * math.prod(shape) for shape in shapes), transcendentals=0
        ),
    )(*[pltpu.with_memory_space_constraint(array, pltpu.HBM) for array in arrays], after)


def slots_of(refs, counts):
    return [(ref, at) for ref, count in zip(refs, counts) for at in range(count)]


def assemble(slots, first, width):
    lanes = slice(first, first + width)
    return jnp.concatenate([ref[at, :, lanes] for ref, at in slots], 0)


def multiply(slots, weights, depth, total, kept):
    total[...] = jnp.zeros_like(total)
    chunk = 0
    for part in weights:
        for at in range(0, part.shape[0], depth):
            kept[chunk] = assemble(slots, chunk * depth, depth)
            total[...] += jnp.dot(kept[chunk], part[at : at + depth, :], preferred_element_type=jnp.float32)
            chunk += 1


def turns(positions):
    shape = (positions.shape[0], HD)
    lane = lax.broadcasted_iota(jnp.int32, shape, 1)
    pair = (lane // 2).astype(jnp.float32)
    angles = positions * jnp.exp(pair * (-2.0 * math.log(ROPE_BASE) / HD))
    return jnp.cos(angles), jnp.where(lane % 2 == 0, -1.0, 1.0) * jnp.sin(angles)


def turn(values, cosine, sine):
    lanes = values.shape[-1]
    even = lax.broadcasted_iota(jnp.int32, values.shape, 1) % 2 == 0
    swapped = jnp.where(even, pltpu.roll(values, lanes - 1, 1), pltpu.roll(values, 1, 1))
    return values * cosine + swapped * sine


def project_kernel(counts, crossed, width, *refs):
    slots = slots_of(refs, counts)
    first, second, keyval, *outs = refs[len(counts) : len(counts) + 7]
    kept, total, packed = refs[len(counts) + 7 :]
    queries, fresh = outs[:2], outs[2:]
    depth = keyval.shape[1]
    tags = jnp.concatenate([ref[at, :, width:].astype(jnp.float32) for ref, at in slots], 0)
    cosine, sine = turns(tags[:, 0:1] * 32.0 + tags[:, 1:2])
    multiply(slots, [first, second], depth, total, kept)
    own = kept[lax.axis_index("gx")]
    blocks = keyval.shape[2] // HD
    for which in range(2):
        term = jnp.dot(own, keyval[which], preferred_element_type=jnp.float32)
        for slot in range(len(slots)):
            for at in range(blocks):
                row = (which * blocks + at) * 4
                fresh[crossed[slot][0]][crossed[slot][1], row : row + 4, :] = term[
                    slot * 4 : slot * 4 + 4, at * HD : (at + 1) * HD
                ]
    heads = total.shape[1] // HD
    for head in range(heads):
        turned = turn(total[:, head * HD : (head + 1) * HD], cosine, sine)
        for slot in range(len(slots)):
            for row in range(2):
                line, at = row * 2 * heads + head * 2, slot * 4 + row * 2
                packed[slot, line : line + 2, :] = turned[at : at + 2, :]
    for slot in range(len(slots)):
        queries[crossed[slot][0]][crossed[slot][1]] = packed[slot].astype(jnp.bfloat16)


def group_shape(groups):
    counts = [len(group.sources) for group in groups]
    seen, order = [0, 0], []
    for group, count in zip(groups, counts):
        for _ in range(count):
            order.append((int(group.crossed), seen[group.crossed]))
            seen[group.crossed] += 1
    return counts, order


def project(groups, w_query, w_keyval, devices):
    counts, crossed = group_shape(groups)
    columns = w_query[0].shape[1]
    depth, kv_width = w_keyval.shape[1:]
    own, width = groups[0].blocks.shape[1], devices * depth
    rows, tile = devices * own, own * (columns // HD)
    query = jax.ShapeDtypeStruct((devices // 2, tile, HD), jnp.bfloat16)
    fresh = jax.ShapeDtypeStruct((devices // 2, own * 2 * kv_width // HD, HD), jnp.float32)
    return pl.pallas_call(
        functools.partial(project_kernel, counts, crossed, width),
        out_shape=[query, query, fresh, fresh],
        in_specs=[VMEM] * (len(groups) + 3),
        out_specs=[VMEM] * 4,
        scratch_shapes=[
            pltpu.VMEM((devices, rows, depth), jnp.bfloat16),
            pltpu.VMEM((rows, columns), jnp.float32),
            pltpu.VMEM((devices, tile, HD), jnp.float32),
        ],
        compiler_params=pltpu.CompilerParams(vmem_limit_bytes=VMEM_LIMIT),
        cost_estimate=pl.CostEstimate(
            flops=2 * rows * columns * width, bytes_accessed=2 * columns * width, transcendentals=2 * rows * HD
        ),
    )(*[group.blocks for group in groups], *w_query, w_keyval)


def pack_kernel(place, near, far, near_sum, far_sum, out):
    tile, lines = near.shape[1], near_sum.shape[1]
    for slot in range(near.shape[0]):
        chip = look_up(place[slot])
        out[chip, :tile, :] = near[slot]
        out[chip, tile : 2 * tile, :] = far[slot]
        total = near_sum[slot] + far_sum[slot]
        high = total.astype(jnp.bfloat16)
        out[chip, 2 * tile : 2 * tile + lines, :] = high
        out[chip, 2 * tile + lines :, :] = (total - high.astype(jnp.float32)).astype(jnp.bfloat16)


def pack(place, near, far, near_sum, far_sum):
    chips, tile, _ = near.shape
    return pl.pallas_call(
        functools.partial(pack_kernel, place),
        out_shape=jax.ShapeDtypeStruct((chips, 2 * tile + 2 * near_sum.shape[1], HD), jnp.bfloat16),
        in_specs=[VMEM] * 4,
        out_specs=VMEM,
        compiler_params=pltpu.CompilerParams(vmem_limit_bytes=VMEM_LIMIT),
    )(near, far, near_sum, far_sum)


def sort_kernel(place, near, far, out):
    core = lax.axis_index("gx") % 2
    for slot in range(near.shape[0]):
        chip = look_up(place[slot])
        out[2 * chip + core] = near[slot]
        out[2 * chip + 1 - core] = far[slot]


def sort(place, near, far):
    return pl.pallas_call(
        functools.partial(sort_kernel, place),
        out_shape=jax.ShapeDtypeStruct((2 * near.shape[0], *near.shape[1:]), near.dtype),
        in_specs=[VMEM] * 2,
        out_specs=VMEM,
        compiler_params=pltpu.CompilerParams(vmem_limit_bytes=VMEM_LIMIT),
    )(near, far)


def out_kernel(counts, crossed, *refs):
    slots = slots_of(refs, counts)
    *weights, near, far, kept, total = refs[len(counts) :]
    multiply(slots, weights, kept.shape[2], total, kept)
    own = near.shape[1]
    for slot in range(len(slots)):
        (near, far)[crossed[slot][0]][crossed[slot][1]] = total[slot * own : (slot + 1) * own].astype(near.dtype)


def project_out(groups, w_out, devices):
    counts, crossed = group_shape(groups)
    columns = w_out[0].shape[1]
    own, width = groups[0].blocks.shape[1:]
    chunks = devices // 2
    piece = jax.ShapeDtypeStruct((devices // 2, own, columns), jnp.bfloat16)
    return pl.pallas_call(
        functools.partial(out_kernel, counts, crossed),
        out_shape=[piece, piece],
        in_specs=[VMEM] * (len(groups) + len(w_out)),
        out_specs=[VMEM, VMEM],
        scratch_shapes=[
            pltpu.VMEM((chunks, devices * own, width // chunks), jnp.bfloat16),
            pltpu.VMEM((devices * own, columns), jnp.float32),
        ],
        compiler_params=pltpu.CompilerParams(vmem_limit_bytes=VMEM_LIMIT),
        cost_estimate=pl.CostEstimate(
            flops=2 * devices * own * columns * width, bytes_accessed=2 * columns * width, transcendentals=0
        ),
    )(*[group.blocks for group in groups], *w_out)


def attend_kernel(devices, kv_heads, tile, lengths, pieces, cache, out, fresh, queries, mixed):
    length, width = cache.shape[2:]
    extra = fresh.shape[2]
    half = tile // 2
    per_head = devices // kv_heads * half
    scale = 1.0 / math.sqrt(HD)
    for chip in range(devices // 2):
        for other in range(2):
            piece = pieces[chip, other * tile : (other + 1) * tile, :]
            queries[2 * chip + (lax.axis_index("gx") % 2 + other) % 2] = piece.astype(jnp.float32)
    line = lax.broadcasted_iota(jnp.int32, (8, 1), 0)
    first = jnp.where(line % 4 < 2, lengths[0, :, :1], lengths[1, :, :1])
    cosine, sine = turns((first + line % 2).astype(jnp.float32))
    total = jnp.sum(pieces[:, 2 * tile :, :].astype(jnp.float32), 0)
    total = total[: total.shape[0] // 2] + total[total.shape[0] // 2 :]
    twice = [jnp.concatenate([total[4 * at : 4 * at + 4]] * 2, 0) for at in range(2 * kv_heads)]
    new_keys = jnp.concatenate([turn(part, cosine, sine) for part in twice[:kv_heads]], 1)
    new_values = jnp.concatenate(twice[kv_heads:], 1)
    spot = lax.broadcasted_iota(jnp.int32, (extra, width), 0)
    for row in range(2):
        for which, new in enumerate((new_keys, new_values)):
            spread = jnp.where(spot == 0, new[2 * row : 2 * row + 1, :], 0.0)
            spread = jnp.where(spot == 1, new[2 * row + 1 : 2 * row + 2, :], spread)
            fresh[which, row] = spread.astype(fresh.dtype)
    every = queries[...]
    lines = kv_heads * per_head
    column = lax.broadcasted_iota(jnp.int32, (lines, length), 1)
    new_column = lax.broadcasted_iota(jnp.int32, (lines, extra), 1)
    step = lax.broadcasted_iota(jnp.int32, (lines, extra), 0) % 2
    across = (((1,), (1,)), ((), ()))
    for row in range(2):
        mine = every[:, row * half : row * half + half, :].reshape(lines, HD)
        spread = jnp.concatenate([mine] * kv_heads, 1)
        own_row = lax.broadcasted_iota(jnp.int32, spread.shape, 0) // per_head
        own_lane = lax.broadcasted_iota(jnp.int32, spread.shape, 1) // HD
        spread = jnp.where(own_row == own_lane, spread, 0.0).astype(jnp.bfloat16)
        scores = lax.dot_general(spread, cache[0, row], across, preferred_element_type=jnp.float32) * scale
        scores = jnp.where(column < lengths[row, :1, :1], scores, -jnp.inf)
        new_scores = lax.dot_general(spread, fresh[0, row], across, preferred_element_type=jnp.float32) * scale
        new_scores = jnp.where(new_column <= step, new_scores, -jnp.inf)
        peak = jnp.maximum(jnp.max(scores, 1, keepdims=True), jnp.max(new_scores, 1, keepdims=True))
        weight = jnp.exp(scores - peak)
        new_weight = jnp.exp(new_scores - peak)
        denominator = jnp.sum(weight, 1, keepdims=True) + jnp.sum(new_weight, 1, keepdims=True)
        result = jnp.dot(weight.astype(jnp.bfloat16), cache[1, row], preferred_element_type=jnp.float32)
        result += jnp.dot(new_weight.astype(jnp.bfloat16), fresh[1, row], preferred_element_type=jnp.float32)
        for head in range(kv_heads):
            rows = slice(head * per_head, (head + 1) * per_head)
            part = result[rows, head * HD : (head + 1) * HD] / denominator[rows]
            for query in range(per_head // 2):
                lanes = slice((head * per_head // 2 + query) * HD, (head * per_head // 2 + query + 1) * HD)
                for at in range(2):
                    mixed[at * 2 + row : at * 2 + row + 1, lanes] = part[2 * query + at : 2 * query + at + 1]
    out[...] = mixed[...].astype(out.dtype)


def attend(pieces, tile, cache, lengths, devices):
    length, width = cache.shape[2], cache.shape[3]
    columns = devices * tile // 4 * HD
    return pl.pallas_call(
        functools.partial(attend_kernel, devices, width // HD, tile),
        out_shape=jax.ShapeDtypeStruct((4, columns), jnp.bfloat16),
        in_specs=[VMEM] * 3,
        out_specs=VMEM,
        scratch_shapes=[
            pltpu.VMEM((2, 2, HD, width), cache.dtype),
            pltpu.VMEM((devices, tile, HD), jnp.float32),
            pltpu.VMEM((4, columns), jnp.float32),
        ],
        compiler_params=pltpu.CompilerParams(vmem_limit_bytes=VMEM_LIMIT),
        cost_estimate=pl.CostEstimate(
            flops=8 * 128 * length * width, bytes_accessed=8 * length * width, transcendentals=256 * length
        ),
    )(lengths, pieces, cache)


def finish_kernel(pieces, out):
    columns = pieces.shape[2]
    steps, rows = out.shape[:2]
    for source in range(pieces.shape[0]):
        piece = pieces[source].astype(jnp.float32)
        for step in range(steps):
            out[step, :, source * columns : (source + 1) * columns] = piece[step * rows : (step + 1) * rows].astype(out.dtype)


def finish(pieces, steps):
    devices, own, columns = pieces.shape
    return pl.pallas_call(
        finish_kernel,
        out_shape=jax.ShapeDtypeStruct((steps, own // steps, devices * columns), jnp.bfloat16),
        in_specs=[VMEM],
        out_specs=VMEM,
        compiler_params=pltpu.CompilerParams(vmem_limit_bytes=VMEM_LIMIT),
    )(pieces)


def body(hidden, norm_gain, w_query, w_keyval, w_out, kv_cache, lengths):
    steps = hidden.shape[0]
    devices = lax.axis_size("gx")

    normed, lengths = norm(hidden, norm_gain, lengths)
    cut = w_query.shape[0] * 11 // 16
    fetched = []

    def bring(*ranges):
        def start(after):
            *arrays, done = fetch(ranges, after)
            fetched.extend(arrays)
            return done

        return start

    part = w_out.shape[0] // 8
    waits = [
        bring((w_query, 0, cut)),
        bring((w_keyval, 0, 2), (kv_cache, 0, 2)),
        bring((w_query, cut, w_query.shape[0] - cut), (w_out, 0, 2 * part)),
    ]
    groups = gather(normed, devices, waits, inner_first=True)
    w_first, w_keyval, kv_cache, w_second, w_out_first = fetched
    place = places(groups)
    near, far, near_sum, far_sum = project(groups, [w_first, w_second], w_keyval, devices)
    pieces = pack(place, near, swap_cores(far, devices), near_sum, swap_cores(far_sum, devices))

    mixed = attend(exchange(pieces, devices), near.shape[1], kv_cache, lengths, devices)
    fetched = [w_out_first]
    waits = [bring((w_out, first * part, count * part)) for first, count in ((2, 3), (5, 3))]
    groups = gather_direct(mixed, devices, waits)
    near, far = project_out(groups, fetched, devices)
    pieces = sort(places(groups), near, far)
    return finish(lax.all_to_all(pieces, "gx", 0, 0, tiled=True), steps)


def rotate(values, positions):
    row_total, head_count, head_width = values.shape
    half_width = head_width // 2
    frequency = ROPE_BASE ** (-2.0 * jnp.arange(half_width, dtype=jnp.float32) / head_width)
    angles = positions[:, None, None] * frequency[None, None, :]
    cosine = jnp.cos(angles)
    sine_part = jnp.sin(angles)
    paired = values.reshape(row_total, head_count, half_width, 2)
    first_half = paired[..., 0]
    second_half = paired[..., 1]
    turned = jnp.stack(
        [
            first_half * cosine - second_half * sine_part,
            first_half * sine_part + second_half * cosine,
        ],
        -1,
    )
    return turned.reshape(row_total, head_count, head_width)


def attend_split_heads(queries, cache_keys, cache_values, lengths, fresh_keys, fresh_values):
    score_scale = 1.0 / math.sqrt(HD)
    fresh_scores = (
        jnp.einsum("rkgd,rskd->rkgs", queries, fresh_keys, preferred_element_type=jnp.float32)
        * score_scale
    )
    cached = (
        jnp.einsum("rkgd,rlkd->rkgl", queries, cache_keys, preferred_element_type=jnp.float32)
        * score_scale
    )
    in_range = jnp.arange(cache_keys.shape[1])[None, :] < lengths[:, None]
    cached = jnp.where(in_range[:, None, None, :], cached, -jnp.inf)
    row_peak = jnp.maximum(cached.max(-1), fresh_scores.max(-1))
    cached_exp = jnp.exp(cached - row_peak[..., None])
    fresh_exp = jnp.exp(fresh_scores - row_peak[..., None])
    denominator = cached_exp.sum(-1) + fresh_exp.sum(-1)
    mixed = jnp.einsum(
        "rkgl,rlkd->rkgd",
        cached_exp.astype(jnp.bfloat16),
        cache_values,
        preferred_element_type=jnp.float32,
    )
    mixed = mixed + jnp.einsum(
        "rkgs,rskd->rkgd",
        fresh_exp.astype(jnp.bfloat16),
        fresh_values,
        preferred_element_type=jnp.float32,
    )
    return (mixed / denominator[..., None]).astype(jnp.bfloat16)


def body_split_heads(hidden, norm_gain, w_query, w_keyval, w_out, kv_cache, lengths):
    step_count, rows_dev, model_width = hidden.shape
    devices = lax.axis_size("gx")
    device_index = lax.axis_index("gx")
    row_slab = w_keyval.shape[1]
    kv_width = w_keyval.shape[2]
    query_cols = w_query.shape[1]
    heads_width = query_cols * devices
    head_count = heads_width // HD
    kv_heads = kv_width // HD
    kv_both = jnp.concatenate([w_keyval[0], w_keyval[1]], 1)
    cache_keys = kv_cache[0].reshape(rows_dev, kv_cache.shape[2], kv_heads, HD)
    cache_values = kv_cache[1].reshape(rows_dev, kv_cache.shape[2], kv_heads, HD)
    states = hidden.astype(jnp.float32)
    scaled = states * lax.rsqrt(jnp.mean(states * states, -1, keepdims=True) + EPSILON)
    normed = (scaled * norm_gain.astype(jnp.float32)).astype(jnp.bfloat16)
    new_keys = []
    new_values = []
    outputs = []
    for step_index in range(step_count):
        shard_piece = lax.all_gather(normed[step_index], "gx", axis=0, tiled=True)
        queries = jnp.dot(shard_piece, w_query, preferred_element_type=jnp.float32)
        own_slab = lax.dynamic_slice_in_dim(shard_piece, device_index * row_slab, row_slab, 1)
        partial_kv = jnp.dot(own_slab, kv_both, preferred_element_type=jnp.float32)
        joined = jnp.concatenate([queries, partial_kv], 1)
        project_query_rows = lax.all_to_all(
            joined[:, :query_cols], "gx", split_axis=0, concat_axis=1, tiled=True
        )
        project_keyval = lax.psum_scatter(
            joined[:, query_cols:], "gx", scatter_dimension=0, tiled=True
        )
        positions = (lengths + step_index).astype(jnp.float32)
        prepare_queries = rotate(
            project_query_rows.reshape(rows_dev, head_count, HD), positions
        ).astype(jnp.bfloat16)
        prepare_queries = prepare_queries.reshape(rows_dev, kv_heads, head_count // kv_heads, HD)
        key_new = rotate(
            project_keyval[:, :kv_width].reshape(rows_dev, kv_heads, HD), positions
        ).astype(jnp.bfloat16)
        value_new = (
            project_keyval[:, kv_width:].reshape(rows_dev, kv_heads, HD).astype(jnp.bfloat16)
        )
        queries, key_new, value_new = (prepare_queries, key_new, value_new)
        new_keys.append(key_new)
        new_values.append(value_new)
        mixed = attend_split_heads(
            queries,
            cache_keys,
            cache_values,
            lengths,
            jnp.stack(new_keys, 1),
            jnp.stack(new_values, 1),
        )
        out_cols = jnp.dot(
            lax.all_gather(mixed.reshape(rows_dev, heads_width), "gx", axis=0, tiled=True),
            w_out,
            preferred_element_type=jnp.float32,
        ).astype(jnp.bfloat16)
        outputs.append(lax.all_to_all(out_cols, "gx", split_axis=0, concat_axis=1, tiled=True))
    return jnp.stack(outputs)


def solution(mesh):
    devices = mesh.shape["gx"]

    def run(*arrays):
        whole_heads = arrays[2].shape[1] % HD == 0 and devices % 2 == 0
        return (body if whole_heads else body_split_heads)(*arrays)

    in_specs = (
        P(None, ("group", "gx"), None),
        P(),
        P(None, "gx"),
        P(None, "gx", None),
        P(None, "gx"),
        P(None, ("group", "gx"), None, None),
        P(("group", "gx")),
    )
    out_specs = P(None, ("group", "gx"), None)
    return jax.shard_map(run, mesh=mesh, in_specs=in_specs, out_specs=out_specs, check_vma=False)
```
